32 devices in a mesh: rep: 4 (over z), fsdp: 8 (over y, x, core).
Axes of the slice: x: 2, y: 2, z: 4, core: 2. Of those that a mesh axis runs over, the one named last changes fastest.
Arguments:
- tokens: bfloat16 [8192, 2048], P(('rep', 'fsdp')), may hold values from -6 to 6
- cotangent: bfloat16 [8192, 2048], P(('rep', 'fsdp')), may hold values from -6 to 6
- lengths: int32 [32], replicated, may hold values from 64 to 256, as said below
- slot_owner: int32 [32], replicated, may hold values from 0 to 31, each once
- gain_in: bfloat16 [2048], P('fsdp'), may hold values from 0.5 to 1.5
- w_proj: bfloat16 [2048, 12288], P('fsdp'), may hold values from -0.125 to 0.125
- w_decay: bfloat16 [2048, 32], P('fsdp'), may hold values from -0.125 to 0.125
- conv_weight: bfloat16 [4, 8192], P(None, 'fsdp'), may hold values from -3 to 3
- a_log: bfloat16 [16], P('fsdp'), may hold values from -5.5 to -2.5
- dt_bias: bfloat16 [16], P('fsdp'), may hold values from -1 to 1
- o_gain: bfloat16 [256], P('fsdp'), may hold values from 0.5 to 1.5
- w_out: bfloat16 [4096, 2048], P('fsdp'), may hold values from -0.1875 to 0.1875
- gain_mid: bfloat16 [2048], P('fsdp'), may hold values from 0.5 to 1.5
- w_gate_up: bfloat16 [2048, 11264], P('fsdp'), may hold values from -0.125 to 0.125
- w_down: bfloat16 [5632, 2048], P('fsdp'), may hold values from -0.078125 to 0.078125
Outputs:
- output: bfloat16 [8192, 2048], P(('rep', 'fsdp'))
- grad_tokens: float32 [8192, 2048], P(('rep', 'fsdp'))
- grad_gain_in: float32 [2048], P('fsdp')
- grad_w_proj: float32 [2048, 12288], P('fsdp')
- grad_w_decay: float32 [2048, 32], P('fsdp')
- grad_conv: float32 [4, 8192], P(None, 'fsdp')
- grad_a_log: float32 [16], P('fsdp')
- grad_dt_bias: float32 [16], P('fsdp')
- grad_o_gain: float32 [256], P('fsdp')
- grad_w_out: float32 [4096, 2048], P('fsdp')
- grad_gain_mid: float32 [2048], P('fsdp')
- grad_w_gate_up: float32 [2048, 11264], P('fsdp')
- grad_w_down: float32 [5632, 2048], P('fsdp')
The draws below stay inside these ranges and needn't reach their ends.
Inputs may be any that keep to these rules, and one draw needn't show every extreme that they name: `lengths`: one slot holds 256 valid tokens in every draw. `slot_owner`: each device holds exactly one slot.
All inputs are finite; a program needn't handle non-finite values.
Results may differ from the reference program's by a relative error of at most 0.017.
Values may be sent and summed in bfloat16 or wider, within the bound.
No kernel may reach another device: no remote copies, remote signals or barrier semaphores. Data moves between devices by JAX's collectives and lax.ppermute only.
A program may use at most 704 MiB of HBM per device.

```python
import jax
import jax.numpy as jnp
from jax import lax

D = 2048
H = 16
DK = 128
DV = 256
FF = 5632
KCONV = 4
BLOCK = 64
TOK_DEV = 256
SLOTS = 32
TOKENS = 8192
CONV = 8192
HV = 4096
PROJ = 12288


def draw_lengths(key, part):
    key = jax.random.fold_in(key, 11)
    base_key, pick_key = jax.random.split(key)
    sampled = jax.random.randint(base_key, (SLOTS,), TOK_DEV // 4, TOK_DEV + 1)
    longest = jax.random.randint(pick_key, (), 0, SLOTS)
    return jnp.where(jnp.arange(SLOTS) == longest, TOK_DEV, sampled).astype(jnp.int32)


def shard_levels(stream_key, extent, shards, smallest, top_value):
    level = 1.0
    for dim, shards_of in shards:
        draws = jax.random.uniform(jax.random.fold_in(jax.random.fold_in(stream_key, 6), dim), (shards_of,), jnp.float32, smallest / len(shards), top_value / len(shards))
        level = level * jnp.repeat(jnp.exp(draws), extent[dim] // shards_of).reshape((-1,) + (1,) * (len(extent) - 1 - dim))
    return level


def noise(rng, extent, width, reach, shards=(), kind=jnp.bfloat16):
    values = jax.random.normal(rng, extent, jnp.float32) * width
    if len(shards) > 0:
        values = shard_levels(rng, extent, shards, -0.22, 0.18) * values
    return jnp.clip(values, min=-reach, max=reach).astype(kind)


def setup_inputs(seed: int = 0) -> dict:
    splits = jax.random.split(jax.random.key(seed), 16)
    tokens = noise(splits[0], (TOKENS, D), 1.0, 6.0, ((0, 32),))
    cotangent = noise(splits[1], (TOKENS, D), 1.0, 6.0, ((0, 32),))
    lengths = draw_lengths(jax.random.fold_in(splits[15], 71), 0)
    slot_owner = jax.random.permutation(splits[3], SLOTS).astype(jnp.int32)
    gain_in = jnp.clip(1.0 + 0.1 * jax.random.normal(splits[4], (D,), jnp.float32), 0.5, 1.5).astype(jnp.bfloat16)
    w_proj = noise(splits[5], (D, PROJ), D ** -0.5, 0.125, ((0, 8),))
    w_decay = noise(splits[6], (D, 2 * H), D ** -0.5, 0.125, ((0, 8),))
    conv_weight = noise(splits[7], (KCONV, CONV), KCONV ** -0.5, 3.0, ((1, 8),))
    a_log = jnp.clip(-5.5 + 3.0 * jax.random.uniform(splits[8], (H,), jnp.float32) ** shard_levels(splits[8], (H,), ((0, 8),), -0.2, 0.2), -5.5, -2.5).astype(jnp.bfloat16)
    dt_bias = jnp.clip(jax.random.uniform(splits[9], (H,), jnp.float32, -1.0, 1.0) * shard_levels(splits[9], (H,), ((0, 8),), -0.4, 0.0), -1.0, 1.0).astype(jnp.bfloat16)
    o_gain = jnp.clip(1.0 + 0.1 * jax.random.normal(splits[10], (DV,), jnp.float32), 0.5, 1.5).astype(jnp.bfloat16)
    w_out = noise(splits[11], (HV, D), (HV // 4) ** -0.5, 0.1875, ((0, 8),))
    gain_mid = jnp.clip(1.0 + 0.1 * jax.random.normal(splits[12], (D,), jnp.float32), 0.5, 1.5).astype(jnp.bfloat16)
    w_gate_up = noise(splits[13], (D, 2 * FF), D ** -0.5, 0.125, ((0, 8),))
    w_down = noise(splits[14], (FF, D), FF ** -0.5, 0.078125, ((0, 8),))
    return {"tokens": tokens, "cotangent": cotangent, "lengths": lengths, "slot_owner": slot_owner, "gain_in": gain_in, "w_proj": w_proj, "w_decay": w_decay, "conv_weight": conv_weight, "a_log": a_log, "dt_bias": dt_bias, "o_gain": o_gain, "w_out": w_out, "gain_mid": gain_mid, "w_gate_up": w_gate_up, "w_down": w_down}


eps_norm = 1e-05
eps_unit = 1e-06
highest_precision = lax.Precision.HIGHEST

@jax.custom_vjp
def low(v):
    return lax.optimization_barrier(v.astype(jnp.bfloat16)).astype(jnp.float32)

@jax.custom_vjp
def low_back(v):
    return v

def low_keep(v):
    return (low(v), None)

def low_pass(kept, grad):
    return (grad,)

def back_keep(v):
    return (v, None)

def back_low(kept, grad):
    return (low(grad),)
low.defvjp(low_keep, low_pass)
low_back.defvjp(back_keep, back_low)

def matmul(left, right):
    return jnp.dot(left, right, precision=highest_precision, preferred_element_type=jnp.float32)

def rms_scale(rows_in, gain):
    return rows_in * lax.rsqrt(lax.optimization_barrier(jnp.mean(rows_in * rows_in, axis=-1, keepdims=True)) + eps_norm) * gain

def mixer_inputs(mixed, decay_pre, conv_weight, a_log, dt_bias):
    row_count = mixed.shape[0]
    padded = jnp.pad(mixed, ((KCONV - 1, 0), (0, 0)))
    convolved = conv_weight[0] * padded[0:row_count]
    for offset in range(1, KCONV):
        convolved = convolved + conv_weight[offset] * padded[offset:offset + row_count]
    active = jax.nn.silu(convolved)
    query_rows = active[:, :H * DK].reshape(row_count, H, DK)
    key_matrix_rows = active[:, H * DK:2 * H * DK].reshape(row_count, H, DK)
    values = active[:, 2 * H * DK:]
    query_rows = query_rows * lax.rsqrt(lax.optimization_barrier(jnp.sum(query_rows * query_rows, axis=-1, keepdims=True)) + eps_unit) * DK ** (-0.5)
    key_matrix_rows = key_matrix_rows * lax.rsqrt(lax.optimization_barrier(jnp.sum(key_matrix_rows * key_matrix_rows, axis=-1, keepdims=True)) + eps_unit)
    beta_gate = jax.nn.sigmoid(decay_pre[:, H:])
    log_decay = -jnp.exp(a_log) * jax.nn.softplus(decay_pre[:, :H] + dt_bias)
    return (query_rows.reshape(row_count, H * DK), key_matrix_rows.reshape(row_count, H * DK), values, beta_gate, log_decay)

def gated_output(mixer_out, gate_pre, o_gain):
    row_count = mixer_out.shape[0]
    normed = mixer_out * lax.rsqrt(lax.optimization_barrier(jnp.mean(mixer_out * mixer_out, axis=-1, keepdims=True)) + eps_norm) * o_gain
    return (normed * jax.nn.silu(gate_pre.reshape(row_count, H, DV))).reshape(row_count, H * DV)

def swiglu(gate_up):
    return jax.nn.silu(gate_up[:, :FF]) * gate_up[:, FF:]

def token_step(carried_state, items):
    query_at_step, key_at_step, value_t, beta_t, decay_t = items
    carried_state = jnp.exp(decay_t)[:, None, None] * carried_state
    recalled_value = jnp.einsum('do,doy->dy', key_at_step, carried_state, precision=highest_precision)
    state_update = beta_t[:, None] * (value_t - recalled_value)
    carried_state = carried_state + key_at_step[:, :, None] * state_update[:, None, :]
    return (carried_state, jnp.einsum('do,doy->dy', query_at_step, carried_state, precision=highest_precision))

@jax.checkpoint
def block_step(carried_state, items):
    return lax.scan(token_step, carried_state, items)

def delta_rule(query_rows, key_matrix_rows, values, beta_gate, log_decay):
    row_count = query_rows.shape[0]
    blocks = row_count // BLOCK
    items = (query_rows.reshape(blocks, BLOCK, H, DK), key_matrix_rows.reshape(blocks, BLOCK, H, DK), values.reshape(blocks, BLOCK, H, DV), beta_gate.reshape(blocks, BLOCK, H), log_decay.reshape(blocks, BLOCK, H))
    final_state, output_rows = lax.scan(block_step, jnp.zeros((H, DK, DV), jnp.float32), items)
    return output_rows.reshape(row_count, H, DV)

def layer(params, slot_rows, live_rows):
    gain_in, w_proj, w_decay, conv_weight, a_log, dt_bias, o_gain, w_out, gain_mid, w_gate_up, w_down = params
    normed_in = low(rms_scale(slot_rows, gain_in))
    projected = low_back(matmul(normed_in, w_proj))
    decay_pre = low_back(matmul(normed_in, w_decay))
    query_rows, key_matrix_rows, values, beta_gate, log_decay = mixer_inputs(projected[:, :CONV], decay_pre, conv_weight, a_log, dt_bias)
    mixer_out = delta_rule(low(query_rows), low(key_matrix_rows), low(values), beta_gate, log_decay)
    gated = low(gated_output(mixer_out, projected[:, CONV:], o_gain))
    branch = low_back(matmul(gated, w_out))
    middle = slot_rows + live_rows * branch
    normed_mid = low(rms_scale(middle, gain_mid))
    gate_up = low_back(matmul(normed_mid, w_gate_up))
    hidden = low(swiglu(gate_up))
    ffn_branch = low_back(matmul(hidden, w_down))
    return middle + live_rows * ffn_branch

def reference(tokens, cotangent, lengths, slot_owner, gain_in, w_proj, w_decay, conv_weight, a_log, dt_bias, o_gain, w_out, gain_mid, w_gate_up, w_down):
    owned_by = slot_owner[None, :] == jnp.arange(SLOTS, dtype=jnp.int32)[:, None]
    slot_length = lax.optimization_barrier(jnp.sum(jnp.where(owned_by, lengths[None, :], 0), axis=1))
    live_rows = (jnp.arange(TOK_DEV, dtype=jnp.int32)[None, :] < slot_length[:, None]).astype(jnp.float32)[:, :, None]
    params = (gain_in.astype(jnp.float32), w_proj.astype(jnp.float32), w_decay.astype(jnp.float32), conv_weight.astype(jnp.float32), a_log.astype(jnp.float32), dt_bias.astype(jnp.float32), o_gain.astype(jnp.float32), w_out.astype(jnp.float32), gain_mid.astype(jnp.float32), w_gate_up.astype(jnp.float32), w_down.astype(jnp.float32))
    slot_rows = tokens.astype(jnp.float32).reshape(SLOTS, TOK_DEV, D)

    def forward(weights, inputs):

        def one_slot(items):
            return layer(weights, items[0], items[1])
        return lax.map(jax.checkpoint(one_slot), (inputs, live_rows))
    result, pull_back = jax.vjp(forward, params, slot_rows)
    seeded = cotangent.astype(jnp.float32).reshape(SLOTS, TOK_DEV, D) * live_rows
    gradients, grad_rows = pull_back(seeded)
    g_gain_in, g_proj, g_decay, g_conv, g_alog, g_bias, g_ogain, g_out, g_gain_mid, g_gate_up, g_down = gradients
    return (result.reshape(TOKENS, D).astype(jnp.bfloat16), grad_rows.reshape(TOKENS, D), g_gain_in, g_proj, g_decay, g_conv, g_alog, g_bias, g_ogain, g_out, g_gain_mid, g_gate_up, g_down)
```

```python
from functools import partial

import jax
import jax.numpy as jnp
from jax import lax
from jax.experimental import pallas as pl
from jax.experimental.pallas import tpu as pltpu
from jax.sharding import PartitionSpec as P

H = 16
DK = 128
DV = 256
KCONV = 4
BLOCK = 64
TOK_DEV = 256
eps_norm = 1e-05
eps_unit = 1e-06
bf16 = jnp.bfloat16
f32 = jnp.float32


def mm(a, b):
    return lax.dot_general(
        a.astype(bf16), b.astype(bf16), (((1,), (0,)), ((), ())), preferred_element_type=f32
    )


def mm_nt(a, b):
    return lax.dot_general(
        a.astype(bf16), b.astype(bf16), (((1,), (1,)), ((), ())), preferred_element_type=f32
    )


def mm_tn(a, b):
    return lax.dot_general(
        a.astype(bf16), b.astype(bf16), (((0,), (0,)), ((), ())), preferred_element_type=f32
    )


def mm_exact(a, b):
    return lax.dot_general(
        a, b, (((1,), (0,)), ((), ())), precision=lax.Precision.HIGHEST, preferred_element_type=f32
    )


def silu(v):
    return v * jax.nn.sigmoid(v)


def shifted_down(x, s):
    if s == 0:
        return x
    row = lax.broadcasted_iota(jnp.int32, x.shape, 0)
    return jnp.where(row >= s, pltpu.roll(x, s, 0), 0.0)


def shifted_up(x, s):
    if s == 0:
        return x
    n = x.shape[0]
    row = lax.broadcasted_iota(jnp.int32, x.shape, 0)
    return jnp.where(row < n - s, pltpu.roll(x, n - s, 0), 0.0)


def conv_forward(mixed, weight):
    out = weight[KCONV - 1 : KCONV, :] * mixed
    for s in range(1, KCONV):
        out = out + weight[KCONV - 1 - s : KCONV - s, :] * shifted_down(mixed, s)
    return out


def conv_backward(d_conv, mixed, weight):
    d_mixed = weight[KCONV - 1 : KCONV, :] * d_conv
    rows = [None] * KCONV
    rows[KCONV - 1] = jnp.sum(d_conv * mixed, axis=0, keepdims=True)
    for s in range(1, KCONV):
        up = shifted_up(d_conv, s)
        d_mixed = d_mixed + weight[KCONV - 1 - s : KCONV - s, :] * up
        rows[KCONV - 1 - s] = jnp.sum(up * mixed, axis=0, keepdims=True)
    return d_mixed, jnp.concatenate(rows, axis=0)


def block_masks(n):
    i = lax.broadcasted_iota(jnp.int32, (n, n), 0)
    j = lax.broadcasted_iota(jnp.int32, (n, n), 1)
    x = i ^ j
    same = x < BLOCK
    return x, i > j, jnp.logical_and(same, i >= j), jnp.logical_and(same, i > j), same


def decay_parts(dec, alog_row, bias_row):
    pre = dec + bias_row
    softplus = jnp.maximum(pre, 0.0) + jnp.log1p(jnp.exp(-jnp.abs(pre)))
    log_decay = -jnp.exp(alog_row) * softplus
    n = dec.shape[0]
    i = lax.broadcasted_iota(jnp.int32, (n, n), 0)
    j = lax.broadcasted_iota(jnp.int32, (n, n), 1)
    same = (i ^ j) < BLOCK
    lower = jnp.where(jnp.logical_and(same, i >= j), 1.0, 0.0)
    whole = jnp.where(same, 1.0, 0.0)
    running = mm_exact(lower, log_decay)
    total = mm_exact(whole, log_decay)
    return pre, log_decay, running, total


def lane_of(x, h):
    lane = lax.broadcasted_iota(jnp.int32, x.shape, 1)
    return jnp.sum(jnp.where(lane == h, x, 0.0), axis=1, keepdims=True)


def row_of(x, h):
    row = lax.broadcasted_iota(jnp.int32, x.shape, 0)
    return jnp.sum(jnp.where(row == h, x, 0.0), axis=0, keepdims=True)


def unit_rows(a, scale):
    r = lax.rsqrt(jnp.sum(a * a, axis=1, keepdims=True) + eps_unit)
    return a * r * scale, r


def inverse_blocks(lowers, x, below):
    eye = jnp.where(x == 0, 1.0, 0.0)
    inv = [eye - jnp.where(x == 1, low, 0.0) for low in lowers]
    level = 1
    while (2 << level) <= BLOCK:
        pick = lax.shift_right_logical(x, level) == 1
        half = [mm(jnp.where(pick, low, 0.0), t) for low, t in zip(lowers, inv)]
        inv = [t - mm(t, u) for t, u in zip(inv, half)]
        level += 1
    return inv


def forward_kernel(
    hl,
    pair,
    q_ref,
    k_ref,
    v_ref,
    g_ref,
    dec_ref,
    cq_ref,
    ck_ref,
    cv_ref,
    head_ref,
    gain_ref,
    gated_ref,
    o_ref,
    u_ref,
    w_ref,
    inv_ref,
    s_ref,
):
    p = pl.program_id(0)
    n = TOK_DEV
    blocks = n // BLOCK
    x, below, on_below, strict, same = block_masks(n)
    dec = dec_ref[...]
    pre, log_decay, running, total = decay_parts(dec, head_ref[0:1, :], head_ref[1:2, :])
    running_t = running.T
    heads = range(pair)
    q = silu(conv_forward(q_ref[...], cq_ref[...]))
    k = silu(conv_forward(k_ref[...], ck_ref[...]))
    v = silu(conv_forward(v_ref[...], cv_ref[...])).astype(bf16)
    qn, kn, vn, beta, b, tot, fade, low, score = [], [], [], [], [], [], [], [], []
    for i in heads:
        h = p * pair + i
        qn.append(unit_rows(q[:, i * DK : (i + 1) * DK], DK**-0.5)[0].astype(bf16))
        kn.append(unit_rows(k[:, i * DK : (i + 1) * DK], 1.0)[0].astype(bf16))
        vn.append(v[:, i * DV : (i + 1) * DV])
        beta.append(jax.nn.sigmoid(lane_of(dec, hl + h)))
        b.append(lane_of(running, h))
        tot.append(lane_of(total, h))
        d = jnp.where(on_below, jnp.exp(jnp.where(on_below, b[i] - row_of(running_t, h), 0.0)), 0.0)
        both = mm_nt(jnp.concatenate([kn[i], qn[i]], axis=0), kn[i])
        low.append(jnp.where(strict, beta[i] * d * both[:n], 0.0))
        score.append((both[n:] * d).astype(bf16))
    inv = inverse_blocks(low, x, below)
    e = [jnp.exp(b[i]) for i in heads]
    fin = [jnp.exp(tot[i] - b[i]) for i in heads]
    grow = [jnp.exp(tot[i]) for i in heads]
    inv = [t.astype(bf16) for t in inv]
    right = [
        jnp.concatenate(
            [beta[i] * vn[i].astype(f32), (beta[i] * e[i]) * kn[i].astype(f32)], axis=1
        ).astype(bf16)
        for i in heads
    ]
    uw = [mm(inv[i], right[i]) for i in heads]
    w = [uw[i][:, DV:].astype(bf16) for i in heads]
    state = [jnp.zeros((DK, DV), f32) for i in heads]
    u_parts = [[] for i in heads]
    o_parts = [[] for i in heads]
    for c in range(blocks):
        lo, hi = c * BLOCK, (c + 1) * BLOCK
        for i in heads:
            sb = state[i].astype(bf16)
            s_ref[0, i, c * DK : (c + 1) * DK, :] = sb
            got = mm(jnp.concatenate([w[i][lo:hi], qn[i][lo:hi]], axis=0), sb)
            u = uw[i][lo:hi, :DV] - got[:BLOCK]
            u_parts[i].append(u)
            o_parts[i].append(e[i][lo:hi] * got[BLOCK:])
            if c < blocks - 1:
                state[i] = grow[i][lo : lo + 1] * state[i] + mm_tn(
                    kn[i][lo:hi], fin[i][lo:hi] * u
                )
    gain = gain_ref[0:1, :]
    for i in heads:
        u = jnp.concatenate(u_parts[i], axis=0).astype(bf16)
        out = jnp.concatenate(o_parts[i], axis=0) + mm(score[i], u)
        cols = slice(i * DV, (i + 1) * DV)
        o_ref[:, cols] = out
        u_ref[:, cols] = u
        w_ref[:, i * DK : (i + 1) * DK] = w[i]
        inv_ref[0, i] = inv[i]
        r = lax.rsqrt(jnp.mean(out * out, axis=1, keepdims=True) + eps_norm)
        gated_ref[:, cols] = (out * r * gain * silu(g_ref[:, cols])).astype(bf16)


def mixer_forward(proj, conv, head_rows, gain_row, hl):
    tokens = proj.shape[0]
    slots = tokens // TOK_DEV
    pair = 2 if hl % 2 == 0 else 1
    groups = hl // pair
    qk = pair * DK
    vv = pair * DV
    spec = pl.BlockSpec
    n = TOK_DEV

    def body(*refs):
        forward_kernel(hl, pair, *refs)

    return pl.pallas_call(
        body,
        grid=(groups, slots),
        in_specs=[
            spec((n, qk), lambda p, s: (s, p)),
            spec((n, qk), lambda p, s: (s, groups + p)),
            spec((n, vv), lambda p, s: (s, groups + p)),
            spec((n, vv), lambda p, s: (s, 2 * groups + p)),
            spec((n, 128), lambda p, s: (s, hl * 6)),
            spec((8, qk), lambda p, s: (0, p)),
            spec((8, qk), lambda p, s: (0, groups + p)),
            spec((8, vv), lambda p, s: (0, groups + p)),
            spec((8, 128), lambda p, s: (0, 0)),
            spec((8, DV), lambda p, s: (0, 0)),
        ],
        out_specs=[
            spec((n, vv), lambda p, s: (s, p)),
            spec((n, vv), lambda p, s: (s, p)),
            spec((n, vv), lambda p, s: (s, p)),
            spec((n, qk), lambda p, s: (s, p)),
            spec((1, pair, n, n), lambda p, s: (s, p, 0, 0)),
            spec((1, pair, n // BLOCK * DK, DV), lambda p, s: (s, p, 0, 0)),
        ],
        out_shape=[
            jax.ShapeDtypeStruct((tokens, hl * DV), bf16),
            jax.ShapeDtypeStruct((tokens, hl * DV), f32),
            jax.ShapeDtypeStruct((tokens, hl * DV), bf16),
            jax.ShapeDtypeStruct((tokens, hl * DK), bf16),
            jax.ShapeDtypeStruct((slots, hl, n, n), bf16),
            jax.ShapeDtypeStruct((slots, hl, n // BLOCK * DK, DV), bf16),
        ],
        compiler_params=pltpu.CompilerParams(vmem_limit_bytes=56 * 1024 * 1024),
        cost_estimate=pl.CostEstimate(
            flops=slots * hl * 600_000_000,
            bytes_accessed=slots * hl * 2_500_000,
            transcendentals=slots * hl * 500_000,
        ),
        name="mixer_forward",
    )(proj, proj, proj, proj, proj, conv, conv, conv, head_rows, gain_row)


def backward_kernel(
    hl,
    pair,
    q_ref,
    k_ref,
    v_ref,
    g_ref,
    dec_ref,
    cq_ref,
    ck_ref,
    cv_ref,
    head_ref,
    gain_ref,
    o_ref,
    u_ref,
    w_ref,
    inv_ref,
    s_ref,
    dy_ref,
    dq_out,
    dk_out,
    dv_out,
    dg_out,
    ddec_out,
    gq_out,
    gk_out,
    gv_out,
    small_out,
):
    p = pl.program_id(0)
    slot = pl.program_id(1)
    n = TOK_DEV
    blocks = n // BLOCK
    x, below, on_below, strict, same = block_masks(n)
    dec = dec_ref[...]
    alog_row = head_ref[0:1, :]
    pre, log_decay, running, total = decay_parts(dec, alog_row, head_ref[1:2, :])
    running_t = running.T
    heads = range(pair)
    qc = conv_forward(q_ref[...], cq_ref[...])
    kc = conv_forward(k_ref[...], ck_ref[...])
    vc = conv_forward(v_ref[...], cv_ref[...])
    q_sig = jax.nn.sigmoid(qc)
    k_sig = jax.nn.sigmoid(kc)
    v_sig = jax.nn.sigmoid(vc)
    q = qc * q_sig
    k = kc * k_sig
    v = (vc * v_sig).astype(bf16)
    gain = gain_ref[0:1, :]
    qn, kn, vn, qr, kr, beta, b, tot, d, sim, low, score = ([] for _ in range(12))
    d_out, u = [], []
    gain_rows = jnp.zeros((1, DV), f32)
    for i in heads:
        h = p * pair + i
        cols = slice(i * DV, (i + 1) * DV)
        kcols = slice(i * DK, (i + 1) * DK)
        rows_q, r_q = unit_rows(q[:, kcols], DK**-0.5)
        rows_k, r_k = unit_rows(k[:, kcols], 1.0)
        qr.append((rows_q, r_q))
        kr.append((rows_k, r_k))
        qn.append(rows_q.astype(bf16))
        kn.append(rows_k.astype(bf16))
        vn.append(v[:, cols])
        beta.append(jax.nn.sigmoid(lane_of(dec, hl + h)))
        b.append(lane_of(running, h))
        tot.append(lane_of(total, h))
        d.append(
            jnp.where(on_below, jnp.exp(jnp.where(on_below, b[i] - row_of(running_t, h), 0.0)), 0.0)
        )
        both = mm_nt(jnp.concatenate([kn[i], qn[i]], axis=0), kn[i])
        sim.append(jnp.where(strict, d[i] * both[:n], 0.0))
        score.append(both[n:] * d[i])
        out = o_ref[:, cols]
        gate = g_ref[:, cols]
        dy = dy_ref[:, cols].astype(f32)
        r = lax.rsqrt(jnp.mean(out * out, axis=1, keepdims=True) + eps_norm)
        normed = out * r
        g_sig = jax.nn.sigmoid(gate)
        act = gate * g_sig
        d_act = dy * normed * gain
        dg_out[:, cols] = (d_act * (g_sig * (1.0 + gate * (1.0 - g_sig)))).astype(bf16)
        gain_rows = gain_rows + jnp.sum(dy * normed * act, axis=0, keepdims=True)
        d_normed = dy * gain * act
        d_out.append(r * (d_normed - normed * jnp.mean(d_normed * normed, axis=1, keepdims=True)))
        u.append(u_ref[:, cols])
    e = [jnp.exp(b[i]) for i in heads]
    fin = [jnp.exp(tot[i] - b[i]) for i in heads]
    grow = [jnp.exp(tot[i]) for i in heads]
    d_out16 = [d_out[i].astype(bf16) for i in heads]
    score16 = [score[i].astype(bf16) for i in heads]
    d_u0 = [mm_tn(score16[i], d_out16[i]) for i in heads]
    d_state = [jnp.zeros((DK, DV), f32) for i in heads]
    d_u = [[None] * blocks for i in heads]
    dq_s = [[None] * blocks for i in heads]
    dk_s = [[None] * blocks for i in heads]
    fin_col = [[None] * blocks for i in heads]
    grow_col = [[None] * blocks for i in heads]
    e_out = [(e[i] * d_out[i]).astype(bf16) for i in heads]
    for c in reversed(range(blocks)):
        lo, hi = c * BLOCK, (c + 1) * BLOCK
        for i in heads:
            ds16 = d_state[i].astype(bf16)
            s16 = s_ref[0, i, c * DK : (c + 1) * DK, :]
            u_c = u[i][lo:hi].astype(f32)
            if c == blocks - 1:
                d_u[i][c] = d_u0[i][lo:hi]
                fin_col[i][c] = jnp.zeros((BLOCK, 1), f32)
                grow_col[i][c] = jnp.zeros((1, 1), f32)
                dk_s[i][c] = jnp.zeros((BLOCK, DK), f32)
            else:
                k_ds = mm(kn[i][lo:hi], ds16)
                add = fin[i][lo:hi] * k_ds
                d_u[i][c] = d_u0[i][lo:hi] + add
                fin_col[i][c] = jnp.sum(add * u_c, axis=1, keepdims=True)
                grow_col[i][c] = grow[i][lo : lo + 1] * jnp.sum(
                    jnp.sum(d_state[i] * s16.astype(f32), axis=1, keepdims=True),
                    axis=0,
                    keepdims=True,
                )
                dk_s[i][c] = mm_nt(fin[i][lo:hi] * u_c, ds16)
            if c > 0:
                step = mm_tn(
                    jnp.concatenate([qn[i][lo:hi], w_ref[lo:hi, i * DK : (i + 1) * DK]], axis=0),
                    jnp.concatenate([e_out[i][lo:hi], (-d_u[i][c]).astype(bf16)], axis=0),
                )
                d_state[i] = grow[i][lo : lo + 1] * d_state[i] + step
    lane = lax.broadcasted_iota(jnp.int32, (n, 128), 1)
    d_dec = jnp.zeros((n, 128), f32)
    d_log = jnp.zeros((n, 128), f32)
    dq_all, dk_all, dv_all = [], [], []
    ones = jnp.ones((n, 128), bf16)
    upper_i = lax.broadcasted_iota(jnp.int32, (n, n), 0)
    upper_j = lax.broadcasted_iota(jnp.int32, (n, n), 1)
    upper = jnp.where(jnp.logical_and((upper_i ^ upper_j) < BLOCK, upper_i <= upper_j), 1.0, 0.0)
    for i in heads:
        h = p * pair + i
        du = jnp.concatenate(d_u[i], axis=0)
        d_right = mm_tn(inv_ref[0, i], du)
        dr16 = d_right.astype(bf16)
        outer = mm_nt(jnp.concatenate([d_out16[i], dr16], axis=0), u[i])
        d_score = jnp.where(on_below, outer[:n], 0.0)
        d_low = jnp.where(strict, -outer[n:], 0.0)
        z16 = (-(beta[i] * e[i]) * d_right).astype(bf16)
        recalled = []
        for c in range(blocks):
            lo, hi = c * BLOCK, (c + 1) * BLOCK
            s16 = s_ref[0, i, c * DK : (c + 1) * DK, :]
            if c == 0:
                dq_s[i][c] = jnp.zeros((BLOCK, DK), f32)
                recalled.append(jnp.zeros((BLOCK, 2 * DV), f32))
                continue
            back = mm_nt(jnp.concatenate([e_out[i][lo:hi], z16[lo:hi]], axis=0), s16)
            dq_s[i][c] = back[:BLOCK]
            dk_s[i][c] = dk_s[i][c] + back[BLOCK:]
            got = mm(jnp.concatenate([kn[i][lo:hi], qn[i][lo:hi]], axis=0), s16)
            recalled.append(jnp.concatenate([got[:BLOCK], got[BLOCK:]], axis=1))
        recalled = jnp.concatenate(recalled, axis=0)
        k_s = recalled[:, :DV]
        q_s = recalled[:, DV:]
        d_a = (d_score * d[i]).astype(bf16)
        d_g = d_low * beta[i] * d[i]
        d_g16 = (d_g + d_g.T).astype(bf16)
        dq = jnp.concatenate(dq_s[i], axis=0) + mm(d_a, kn[i])
        dk = jnp.concatenate(dk_s[i], axis=0) + mm_tn(d_a, qn[i]) + mm(d_g16, kn[i])
        dv = beta[i] * d_right
        row_sum = jnp.sum(d_low * sim[i], axis=1, keepdims=True)
        keep = vn[i].astype(f32) - e[i] * k_s
        d_beta = row_sum + jnp.sum(d_right * keep, axis=1, keepdims=True)
        moved = (d_score * score[i] + d_low * beta[i] * sim[i]).astype(bf16)
        d_b = mm(moved, ones) - mm_tn(moved, ones)
        d_b_col = e[i] * jnp.sum(
            d_out[i] * q_s - (beta[i] * d_right) * k_s, axis=1, keepdims=True
        )
        fin_all = jnp.concatenate(fin_col[i], axis=0)
        d_b = jnp.where(lane == h, d_b + (d_b_col - fin_all), 0.0)
        tail = jnp.concatenate(
            [
                jnp.broadcast_to(
                    grow_col[i][c] + jnp.sum(fin_col[i][c], axis=0, keepdims=True), (BLOCK, 1)
                )
                for c in range(blocks)
            ],
            axis=0,
        )
        d_log = d_log + mm_exact(upper, d_b) + jnp.where(lane == h, tail, 0.0)
        d_dec = d_dec + jnp.where(lane == hl + h, d_beta * beta[i] * (1.0 - beta[i]), 0.0)
        rows_q, r_q = qr[i]
        rows_k, r_k = kr[i]
        unit = rows_q * DK**0.5
        dq = (DK**-0.5) * r_q * (dq - unit * jnp.sum(dq * unit, axis=1, keepdims=True))
        dk = r_k * (dk - rows_k * jnp.sum(dk * rows_k, axis=1, keepdims=True))
        dq_all.append(dq)
        dk_all.append(dk)
        dv_all.append(dv)

    def through_conv(d_active, conv, sig, mixed, weight, out, grad):
        d_conv = d_active * (sig * (1.0 + conv * (1.0 - sig)))
        d_mixed, d_weight = conv_backward(d_conv, mixed, weight)
        out[...] = d_mixed.astype(bf16)

        @pl.when(slot == 0)
        def _():
            grad[...] = jnp.zeros_like(grad)

        grad[0:KCONV, :] += d_weight

    through_conv(
        jnp.concatenate(dq_all, axis=1), qc, q_sig, q_ref[...], cq_ref[...], dq_out, gq_out
    )
    through_conv(
        jnp.concatenate(dk_all, axis=1), kc, k_sig, k_ref[...], ck_ref[...], dk_out, gk_out
    )
    through_conv(
        jnp.concatenate(dv_all, axis=1), vc, v_sig, v_ref[...], cv_ref[...], dv_out, gv_out
    )
    mine = jnp.logical_and(lane >= p * pair, lane < (p + 1) * pair)
    d_pre = jnp.where(mine, -jnp.exp(alog_row) * jax.nn.sigmoid(pre) * d_log, 0.0)
    ddec_out[...] = d_dec + d_pre

    @pl.when(slot == 0)
    def _():
        small_out[...] = jnp.zeros_like(small_out)

    small_out[0:1, :] += gain_rows
    small_out[1:2, 0:128] += jnp.sum(jnp.where(mine, d_log * log_decay, 0.0), axis=0, keepdims=True)
    small_out[2:3, 0:128] += jnp.sum(d_pre, axis=0, keepdims=True)


def mixer_backward(proj, conv, head_rows, gain_row, saved, d_gated, hl):
    out, u, w, inv, states = saved
    tokens = proj.shape[0]
    slots = tokens // TOK_DEV
    pair = 2 if hl % 2 == 0 else 1
    groups = hl // pair
    qk = pair * DK
    vv = pair * DV
    spec = pl.BlockSpec
    n = TOK_DEV

    def body(*refs):
        backward_kernel(hl, pair, *refs)

    return pl.pallas_call(
        body,
        grid=(groups, slots),
        in_specs=[
            spec((n, qk), lambda p, s: (s, p)),
            spec((n, qk), lambda p, s: (s, groups + p)),
            spec((n, vv), lambda p, s: (s, groups + p)),
            spec((n, vv), lambda p, s: (s, 2 * groups + p)),
            spec((n, 128), lambda p, s: (s, hl * 6)),
            spec((8, qk), lambda p, s: (0, p)),
            spec((8, qk), lambda p, s: (0, groups + p)),
            spec((8, vv), lambda p, s: (0, groups + p)),
            spec((8, 128), lambda p, s: (0, 0)),
            spec((8, DV), lambda p, s: (0, 0)),
            spec((n, vv), lambda p, s: (s, p)),
            spec((n, vv), lambda p, s: (s, p)),
            spec((n, qk), lambda p, s: (s, p)),
            spec((1, pair, n, n), lambda p, s: (s, p, 0, 0)),
            spec((1, pair, n // BLOCK * DK, DV), lambda p, s: (s, p, 0, 0)),
            spec((n, vv), lambda p, s: (s, p)),
        ],
        out_specs=[
            spec((n, qk), lambda p, s: (s, p)),
            spec((n, qk), lambda p, s: (s, p)),
            spec((n, vv), lambda p, s: (s, p)),
            spec((n, vv), lambda p, s: (s, p)),
            spec((n, 128), lambda p, s: (p * slots + s, 0)),
            spec((8, qk), lambda p, s: (0, p)),
            spec((8, qk), lambda p, s: (0, p)),
            spec((8, vv), lambda p, s: (0, p)),
            spec((8, DV), lambda p, s: (p, 0)),
        ],
        out_shape=[
            jax.ShapeDtypeStruct((tokens, hl * DK), bf16),
            jax.ShapeDtypeStruct((tokens, hl * DK), bf16),
            jax.ShapeDtypeStruct((tokens, hl * DV), bf16),
            jax.ShapeDtypeStruct((tokens, hl * DV), bf16),
            jax.ShapeDtypeStruct((groups * tokens, 128), f32),
            jax.ShapeDtypeStruct((8, hl * DK), f32),
            jax.ShapeDtypeStruct((8, hl * DK), f32),
            jax.ShapeDtypeStruct((8, hl * DV), f32),
            jax.ShapeDtypeStruct((8 * groups, DV), f32),
        ],
        compiler_params=pltpu.CompilerParams(vmem_limit_bytes=56 * 1024 * 1024),
        cost_estimate=pl.CostEstimate(
            flops=slots * hl * 1_000_000_000,
            bytes_accessed=slots * hl * 3_500_000,
            transcendentals=slots * hl * 700_000,
        ),
        name="mixer_backward",
    )(proj, proj, proj, proj, proj, conv, conv, conv, head_rows, gain_row, out, u, w, inv, states, d_gated)


def relative(nf, j):
    return [(i, i ^ (2 * j)) for i in range(nf)]


def swap_core(a, nf):
    return lax.ppermute(a, "fsdp", [(i, i ^ 1) for i in range(nf)])


def to_chip(a, nf, j):
    return lax.ppermute(a, "fsdp", relative(nf, j))


def gather_rows(a, nf):
    chips = nf // 2
    if chips != 4:
        return jnp.concatenate([a] + [to_chip(a, nf, j) for j in range(1, chips)], axis=0)
    half = a.shape[0] // 2
    one = to_chip(a, nf, 1)
    two = to_chip(a, nf, 2)
    three = [to_chip(one[:half], nf, 2), to_chip(two[half:], nf, 1)]
    return jnp.concatenate([a, one, two] + three, axis=0)


def scatter_rows(a, nf):
    chips = nf // 2
    n = a.shape[0] // chips
    parts = [a[j * n : (j + 1) * n] for j in range(chips)]
    if chips != 4:
        total = parts[0].astype(f32)
        for j in range(1, chips):
            total = total + to_chip(parts[j], nf, j).astype(f32)
        return total
    half = n // 2
    low = to_chip(parts[3][:half], nf, 2)
    high = to_chip(parts[3][half:], nf, 1)
    one_high = to_chip(parts[1][half:], nf, 1)
    two_low = to_chip(parts[2][:half], nf, 2)
    one_low = to_chip((parts[1][:half].astype(f32) + low.astype(f32)).astype(bf16), nf, 1)
    two_high = to_chip((parts[2][half:].astype(f32) + high.astype(f32)).astype(bf16), nf, 2)
    own = parts[0].astype(f32)
    return jnp.concatenate(
        [
            own[:half] + one_low.astype(f32) + two_low.astype(f32),
            own[half:] + one_high.astype(f32) + two_high.astype(f32),
        ],
        axis=0,
    )


def sum_over_rep(a, nz):
    if nz != 4:
        return lax.psum(a, "rep")
    z = lax.axis_index("rep")
    first = lax.ppermute(a, "rep", [(0, 1), (3, 2)])
    pair = (a.astype(f32) + first.astype(f32)).astype(bf16)
    other = lax.ppermute(pair, "rep", [(1, 2), (2, 1)])
    total = (pair.astype(f32) + other.astype(f32)).astype(bf16)
    last = lax.ppermute(total, "rep", [(1, 0), (2, 3)])
    return jnp.where(jnp.logical_or(z == 1, z == 2), total, last)


def rms_rows(rows, gain):
    r = lax.rsqrt(jnp.mean(rows * rows, axis=1, keepdims=True) + eps_norm)
    return rows * r * gain, r


def rms_back(rows, r, gain, d_out):
    unit = rows * r
    d_unit = d_out * gain
    d_rows = r * (d_unit - unit * jnp.mean(d_unit * unit, axis=1, keepdims=True))
    return d_rows, jnp.sum(d_out * unit, axis=0)


def chip_ranges(chip, chips, widths):
    spans = []
    start = 0
    for width in widths:
        part = width // chips
        spans.append((start + chip * part, part))
        start += width
    return spans


def take_columns(w, spans):
    rows = w.shape[0]
    return jnp.concatenate(
        [lax.dynamic_slice(w, (0, start), (rows, width)) for start, width in spans], axis=1
    )


def redistribute(w, nf, widths):
    chips = nf // 2
    me = lax.axis_index("fsdp")
    chip, core = me // 2, me % 2
    rows = w.shape[0]
    width = sum(widths) // chips
    out = jnp.zeros((nf * rows, width), w.dtype)
    for j in range(chips):
        part = take_columns(w, chip_ranges(chip ^ j, chips, widths))
        if j:
            part = to_chip(part, nf, j)
        other = swap_core(part, nf)
        base = 2 * (chip ^ j) * rows
        out = lax.dynamic_update_slice(out, part, (base + core * rows, 0))
        out = lax.dynamic_update_slice(out, other, (base + (1 - core) * rows, 0))
    return out


def both_cores(w, nf):
    core = lax.axis_index("fsdp") % 2
    rows = w.shape[0]
    out = jnp.zeros((2 * rows, w.shape[1]), w.dtype)
    out = lax.dynamic_update_slice(out, w, (core * rows, 0))
    return lax.dynamic_update_slice(out, swap_core(w, nf), ((1 - core) * rows, 0))


def sum_cores(a, nf):
    core = lax.axis_index("fsdp") % 2
    rows = a.shape[0] // 2
    mine = lax.dynamic_slice(a, (core * rows, 0), (rows, a.shape[1]))
    theirs = lax.dynamic_slice(a, ((1 - core) * rows, 0), (rows, a.shape[1]))
    return (mine.astype(f32) + swap_core(theirs, nf).astype(f32)).astype(bf16)


def column_gradient(left, right, nf, nz, widths):
    chips = nf // 2
    chip = lax.axis_index("fsdp") // 2
    rows = left.shape[1] // chips
    out = jnp.zeros((rows // 2, sum(widths)), f32)
    for j in reversed(range(chips)):
        part = lax.dynamic_slice(left, (0, (chip ^ j) * rows), (left.shape[0], rows))
        term = sum_cores(mm_tn(part, right).astype(bf16), nf)
        if j:
            term = to_chip(term, nf, j)
        term = sum_over_rep(term, nz).astype(f32)
        at = 0
        for start, width in chip_ranges(chip ^ j, chips, widths):
            out = lax.dynamic_update_slice(out, term[:, at : at + width], (0, start))
            at += width
    return out


def as_rows(a):
    flat = a.reshape(-1)
    return jnp.pad(flat, (0, -flat.shape[0] % 128)).reshape(-1, 128)


def local(
    tokens,
    cotangent,
    lengths,
    slot_owner,
    gain_in,
    w_proj,
    w_decay,
    conv_weight,
    a_log,
    dt_bias,
    o_gain,
    w_out,
    gain_mid,
    w_gate_up,
    w_down,
    *,
    nf,
    nz,
):
    chips = nf // 2
    hl = H // chips
    me = lax.axis_index("fsdp")
    rep = lax.axis_index("rep")
    chip = me // 2
    d_model = tokens.shape[1]
    shard = gain_in.shape[0]
    conv_shard = conv_weight.shape[1]
    channels = conv_shard * nf
    hv = w_out.shape[0] * nf
    hk = (channels - hv) // 2
    ff = w_down.shape[0] * nf
    proj_widths = (hk, hk, hv, hv)
    up_widths = (ff, ff)

    device = rep * nf + (me ^ (2 * jnp.arange(chips, dtype=jnp.int32)))
    held = jnp.sum(
        jnp.where(slot_owner[None, :] == device[:, None], lengths[None, :], 0), axis=1
    )
    live_all = (jnp.arange(TOK_DEV, dtype=jnp.int32)[None, :] < held[:, None]).astype(f32)
    live_own = live_all[0][:, None]
    live_all = live_all.reshape(chips * TOK_DEV, 1)

    pieces = [conv_weight, w_decay.T, gain_in, gain_mid, o_gain, a_log, dt_bias]
    rows = [as_rows(p) for p in pieces]
    counts = [r.shape[0] for r in rows]
    packed = jnp.concatenate(rows, axis=0)
    packed = jnp.pad(packed, ((0, -packed.shape[0] % 16), (0, 0)))
    small = lax.all_gather(packed, "fsdp", axis=0).astype(f32)
    split = []
    at = 0
    for p, count in zip(pieces, counts):
        split.append(
            small[:, at : at + count].reshape(nf, count * 128)[:, : p.size].reshape((nf,) + p.shape)
        )
        at += count
    conv_full = split[0].transpose(1, 0, 2).reshape(KCONV, channels)
    decay_full = split[1].transpose(1, 0, 2).reshape(2 * H, d_model).T
    gain_in_full, gain_mid_full, ogain_full, alog_full, bias_full = (
        s.reshape(-1) for s in split[2:]
    )
    conv_chip = take_columns(conv_full, chip_ranges(chip, chips, proj_widths[:3]))
    conv_chip = jnp.pad(conv_chip, ((0, 8 - KCONV), (0, 0)))
    decay_chip = take_columns(decay_full, chip_ranges(chip, chips, (H, H)))
    decay_chip = jnp.pad(decay_chip, ((0, 0), (0, 128 - 2 * hl))).astype(bf16)
    head_rows = jnp.stack([alog_full, bias_full])
    head_rows = lax.dynamic_slice(head_rows, (0, chip * hl), (2, hl))
    head_rows = jnp.pad(head_rows, ((0, 6), (0, 128 - hl)))
    gain_row = jnp.pad(ogain_full[None, :], ((0, 7), (0, 0)))

    rows_in = gather_rows(tokens, nf).astype(f32)
    normed_in = rms_rows(rows_in, gain_in_full)[0].astype(bf16)
    proj_chip = redistribute(w_proj, nf, proj_widths)
    weight_in = jnp.concatenate([proj_chip, decay_chip], axis=1)
    projected = mm(normed_in, weight_in)
    gated, *saved = mixer_forward(projected, conv_chip, head_rows, gain_row, hl)
    out_chip = both_cores(w_out, nf)
    branch = scatter_rows(mm(gated, out_chip).astype(bf16), nf)

    tokens32 = tokens.astype(f32)
    middle = tokens32 + live_own * branch
    normed_own, r_mid = rms_rows(middle, gain_mid_full)
    normed_mid = gather_rows(normed_own.astype(bf16), nf)
    up_chip = redistribute(w_gate_up, nf, up_widths)
    down_chip = both_cores(w_down, nf)
    seeded = cotangent.astype(f32) * live_own
    d_ffn = gather_rows(seeded.astype(bf16), nf)
    d_hidden = mm_nt(d_ffn, down_chip)
    gate_up = mm(normed_mid, up_chip)
    wide = ff // chips
    gate, up = gate_up[:, :wide], gate_up[:, wide:]
    sig = jax.nn.sigmoid(gate)
    act = gate * sig
    hidden = (act * up).astype(bf16)
    d_gate_up = jnp.concatenate(
        [d_hidden * up * (sig * (1.0 + gate * (1.0 - sig))), d_hidden * act], axis=1
    ).astype(bf16)
    ffn_branch = scatter_rows(mm(hidden, down_chip).astype(bf16), nf)
    output = (middle + live_own * ffn_branch).astype(bf16)

    d_normed_mid = scatter_rows(mm_nt(d_gate_up, up_chip).astype(bf16), nf)
    grad_down = sum_over_rep(sum_cores(mm_tn(hidden, d_ffn).astype(bf16), nf), nz).astype(f32)
    grad_up = column_gradient(normed_mid, d_gate_up, nf, nz, up_widths)
    d_mid, g_gain_mid = rms_back(middle, r_mid, gain_mid_full, d_normed_mid)
    d_middle = seeded + d_mid
    d_branch = gather_rows((live_own * d_middle).astype(bf16), nf)

    d_gated = mm_nt(d_branch, out_chip)
    grad_out = sum_over_rep(sum_cores(mm_tn(gated, d_branch).astype(bf16), nf), nz).astype(f32)
    dq, dk, dv, dg, d_dec, gq, gk, gv, g_small = mixer_backward(
        projected, conv_chip, head_rows, gain_row, saved, d_gated, hl
    )
    groups = g_small.shape[0] // 8
    d_dec = jnp.sum(d_dec.reshape(groups, -1, 128), axis=0).astype(bf16)
    d_proj = jnp.concatenate([dq, dk, dv, dg], axis=1)
    d_normed_in = scatter_rows(
        mm_nt(jnp.concatenate([d_proj, d_dec], axis=1), weight_in).astype(bf16), nf
    )
    grad_proj = column_gradient(normed_in, d_proj, nf, nz, proj_widths)
    g_decay = mm_tn(normed_in, d_dec)[:, : 2 * hl]
    r_in = lax.rsqrt(jnp.mean(tokens32 * tokens32, axis=1, keepdims=True) + eps_norm)
    d_rows, g_gain_in = rms_back(tokens32, r_in, gain_in_full, d_normed_in)
    grad_tokens = d_middle + d_rows

    def spread(values, widths):
        out = jnp.zeros((values.shape[0], sum(widths)), f32)
        at = 0
        for start, width in chip_ranges(chip, chips, widths):
            out = lax.dynamic_update_slice(out, values[:, at : at + width], (0, start))
            at += width
        return out

    g_small = jnp.sum(g_small.reshape(groups, 8, DV), axis=0)
    g_conv = spread(jnp.concatenate([gq, gk, gv], axis=1)[:KCONV], proj_widths[:3])
    g_decay = spread(g_decay, (H, H)).T
    g_alog = spread(g_small[1:2, :hl], (H,))
    g_bias = spread(g_small[2:3, :hl], (H,))
    parts = [
        g_conv.reshape(KCONV, nf, conv_shard).transpose(1, 0, 2),
        g_decay.reshape(2 * H, nf, shard).transpose(1, 0, 2),
        g_gain_in.reshape(nf, shard),
        g_gain_mid.reshape(nf, shard),
        g_small[0].reshape(nf, -1),
        g_alog.reshape(nf, -1),
        g_bias.reshape(nf, -1),
    ]
    flat = []
    for part in parts:
        part = part.reshape(nf, -1)
        flat.append(jnp.pad(part, ((0, 0), (0, -part.shape[1] % 128))))
    flat = jnp.concatenate(flat, axis=1)
    count = flat.shape[1]
    summed = lax.psum_scatter(
        flat.reshape(nf * count // 128, 128), "fsdp", scatter_dimension=0, tiled=True
    )
    summed = lax.psum(summed, "rep").reshape(-1)
    grads = []
    at = 0
    for p in pieces:
        grads.append(summed[at : at + p.size].reshape(p.shape))
        at += p.size + (-p.size % 128)
    s_conv, s_decay, s_gain_in, s_gain_mid, s_ogain, s_alog, s_bias = grads
    return (
        output,
        grad_tokens,
        s_gain_in,
        grad_proj,
        s_decay.T,
        s_conv,
        s_alog,
        s_bias,
        s_ogain,
        grad_out,
        s_gain_mid,
        grad_up,
        grad_down,
    )


def solution(mesh):
    rows = P(("rep", "fsdp"), None)
    one = P("fsdp")
    two = P("fsdp", None)
    columns = P(None, "fsdp")
    in_specs = (rows, rows, P(), P(), one, two, two, columns, one, one, one, two, one, two, two)
    out_specs = (rows, rows, one, two, two, columns, one, one, one, two, one, two, two)
    body = partial(local, nf=mesh.shape["fsdp"], nz=mesh.shape["rep"])
    return jax.shard_map(body, mesh=mesh, in_specs=in_specs, out_specs=out_specs, check_vma=False)
```

```python
from functools import partial

import jax
import jax.numpy as jnp
from jax import lax
from jax.experimental import pallas as pl
from jax.experimental.pallas import tpu as pltpu
from jax.sharding import PartitionSpec as P

H = 16
DK = 128
DV = 256
KCONV = 4
BLOCK = 64
TOK_DEV = 256
eps_norm = 1e-05
eps_unit = 1e-06
bf16 = jnp.bfloat16
f32 = jnp.float32


def mm(a, b):
    return lax.dot_general(
        a.astype(bf16), b.astype(bf16), (((1,), (0,)), ((), ())), preferred_element_type=f32
    )


def mm_nt(a, b):
    return lax.dot_general(
        a.astype(bf16), b.astype(bf16), (((1,), (1,)), ((), ())), preferred_element_type=f32
    )


def mm_tn(a, b):
    return lax.dot_general(
        a.astype(bf16), b.astype(bf16), (((0,), (0,)), ((), ())), preferred_element_type=f32
    )


def mm_exact(a, b):
    return lax.dot_general(
        a, b, (((1,), (0,)), ((), ())), precision=lax.Precision.HIGHEST, preferred_element_type=f32
    )


def silu(v):
    return v * jax.nn.sigmoid(v)


def shifted_down(x, s):
    if s == 0:
        return x
    row = lax.broadcasted_iota(jnp.int32, x.shape, 0)
    return jnp.where(row >= s, pltpu.roll(x, s, 0), 0.0)


def shifted_up(x, s):
    if s == 0:
        return x
    n = x.shape[0]
    row = lax.broadcasted_iota(jnp.int32, x.shape, 0)
    return jnp.where(row < n - s, pltpu.roll(x, n - s, 0), 0.0)


def conv_forward(mixed, weight):
    out = weight[KCONV - 1 : KCONV, :] * mixed
    for s in range(1, KCONV):
        out = out + weight[KCONV - 1 - s : KCONV - s, :] * shifted_down(mixed, s)
    return out


def conv_backward(d_conv, mixed, weight):
    d_mixed = weight[KCONV - 1 : KCONV, :] * d_conv
    rows = [None] * KCONV
    rows[KCONV - 1] = jnp.sum(d_conv * mixed, axis=0, keepdims=True)
    for s in range(1, KCONV):
        up = shifted_up(d_conv, s)
        d_mixed = d_mixed + weight[KCONV - 1 - s : KCONV - s, :] * up
        rows[KCONV - 1 - s] = jnp.sum(up * mixed, axis=0, keepdims=True)
    return d_mixed, jnp.concatenate(rows, axis=0)


def block_masks(n):
    i = lax.broadcasted_iota(jnp.int32, (n, n), 0)
    j = lax.broadcasted_iota(jnp.int32, (n, n), 1)
    x = i ^ j
    same = x < BLOCK
    return x, i > j, jnp.logical_and(same, i >= j), jnp.logical_and(same, i > j), same


def decay_parts(dec, alog_row, bias_row):
    pre = dec + bias_row
    softplus = jnp.maximum(pre, 0.0) + jnp.log1p(jnp.exp(-jnp.abs(pre)))
    log_decay = -jnp.exp(alog_row) * softplus
    n = dec.shape[0]
    i = lax.broadcasted_iota(jnp.int32, (n, n), 0)
    j = lax.broadcasted_iota(jnp.int32, (n, n), 1)
    same = (i ^ j) < BLOCK
    lower = jnp.where(jnp.logical_and(same, i >= j), 1.0, 0.0)
    whole = jnp.where(same, 1.0, 0.0)
    running = mm_exact(lower, log_decay)
    total = mm_exact(whole, log_decay)
    return pre, log_decay, running, total


def lane_of(x, h):
    lane = lax.broadcasted_iota(jnp.int32, x.shape, 1)
    return jnp.sum(jnp.where(lane == h, x, 0.0), axis=1, keepdims=True)


def row_of(x, h):
    row = lax.broadcasted_iota(jnp.int32, x.shape, 0)
    return jnp.sum(jnp.where(row == h, x, 0.0), axis=0, keepdims=True)


def unit_rows(a, scale):
    r = lax.rsqrt(jnp.sum(a * a, axis=1, keepdims=True) + eps_unit)
    return a * r * scale, r


def inverse_blocks(lowers, x, below):
    eye = jnp.where(x == 0, 1.0, 0.0)
    inv = [eye - jnp.where(x == 1, low, 0.0) for low in lowers]
    level = 1
    while (2 << level) <= BLOCK:
        pick = lax.shift_right_logical(x, level) == 1
        half = [mm(jnp.where(pick, low, 0.0), t) for low, t in zip(lowers, inv)]
        inv = [t - mm(t, u) for t, u in zip(inv, half)]
        level += 1
    return inv


def forward_kernel(
    hl,
    pair,
    p,
    ids_ref,
    x_ref,
    dec_ref,
    conv_ref,
    head_ref,
    gain_ref,
    gated_ref,
    o_ref,
    u_ref,
    w_ref,
    inv_ref,
    s_ref,
):
    n = TOK_DEV
    qk, vv = pair * DK, pair * DV
    blocks = n // BLOCK
    x, below, on_below, strict, same = block_masks(n)
    dec = dec_ref[...]
    pre, log_decay, running, total = decay_parts(dec, head_ref[0:1, :], head_ref[1:2, :])
    running_t = running.T
    heads = range(pair)
    q = silu(conv_forward(x_ref[:, :qk], conv_ref[:, :qk]))
    k = silu(conv_forward(x_ref[:, qk : 2 * qk], conv_ref[:, qk : 2 * qk]))
    v = silu(conv_forward(x_ref[:, 2 * qk : 2 * qk + vv], conv_ref[:, 2 * qk :])).astype(bf16)
    qn, kn, vn, beta, b, tot, fade, low, score = [], [], [], [], [], [], [], [], []
    for i in heads:
        h = ids_ref[0] * hl + p * pair + i
        qn.append(unit_rows(q[:, i * DK : (i + 1) * DK], DK**-0.5)[0].astype(bf16))
        kn.append(unit_rows(k[:, i * DK : (i + 1) * DK], 1.0)[0].astype(bf16))
        vn.append(v[:, i * DV : (i + 1) * DV])
        beta.append(jax.nn.sigmoid(lane_of(dec, H + h)))
        b.append(lane_of(running, h))
        tot.append(lane_of(total, h))
        d = jnp.where(on_below, jnp.exp(jnp.where(on_below, b[i] - row_of(running_t, h), 0.0)), 0.0)
        both = mm_nt(jnp.concatenate([kn[i], qn[i]], axis=0), kn[i])
        low.append(jnp.where(strict, beta[i] * d * both[:n], 0.0))
        score.append((both[n:] * d).astype(bf16))
    inv = inverse_blocks(low, x, below)
    e = [jnp.exp(b[i]) for i in heads]
    fin = [jnp.exp(tot[i] - b[i]) for i in heads]
    grow = [jnp.exp(tot[i]) for i in heads]
    inv = [t.astype(bf16) for t in inv]
    right = [
        jnp.concatenate(
            [beta[i] * vn[i].astype(f32), (beta[i] * e[i]) * kn[i].astype(f32)], axis=1
        ).astype(bf16)
        for i in heads
    ]
    uw = [mm(inv[i], right[i]) for i in heads]
    w = [uw[i][:, DV:].astype(bf16) for i in heads]
    state = [jnp.zeros((DK, DV), f32) for i in heads]
    u_parts = [[] for i in heads]
    o_parts = [[] for i in heads]
    for c in range(blocks):
        lo, hi = c * BLOCK, (c + 1) * BLOCK
        for i in heads:
            sb = state[i].astype(bf16)
            s_ref[0, i, c * DK : (c + 1) * DK, :] = sb
            got = mm(jnp.concatenate([w[i][lo:hi], qn[i][lo:hi]], axis=0), sb)
            u = uw[i][lo:hi, :DV] - got[:BLOCK]
            u_parts[i].append(u)
            o_parts[i].append(e[i][lo:hi] * got[BLOCK:])
            if c < blocks - 1:
                state[i] = grow[i][lo : lo + 1] * state[i] + mm_tn(
                    kn[i][lo:hi], fin[i][lo:hi] * u
                )
    gain = gain_ref[0:1, :]
    for i in heads:
        u = jnp.concatenate(u_parts[i], axis=0).astype(bf16)
        out = jnp.concatenate(o_parts[i], axis=0) + mm(score[i], u)
        cols = slice(i * DV, (i + 1) * DV)
        o_ref[:, cols] = out
        u_ref[:, cols] = u
        w_ref[:, i * DK : (i + 1) * DK] = w[i]
        inv_ref[0, i] = inv[i]
        r = lax.rsqrt(jnp.mean(out * out, axis=1, keepdims=True) + eps_norm)
        gated_ref[:, cols] = (out * r * gain * silu(x_ref[:, 2 * qk + vv + i * DV : 2 * qk + vv + (i + 1) * DV])).astype(bf16)


def mixer_forward(ids, proj, dec, conv, head_rows, gain_row, hl, pair, p):
    tokens = proj.shape[0]
    slots = tokens // TOK_DEV
    qk = pair * DK
    vv = pair * DV
    spec = pl.BlockSpec
    n = TOK_DEV

    def body(*refs):
        forward_kernel(hl, pair, p, *refs)

    return pl.pallas_call(
        body,
        grid=(slots,),
        in_specs=[
            pl.BlockSpec(memory_space=pltpu.SMEM),
            spec((n, 2 * qk + 2 * vv), lambda s: (s, 0)),
            spec((n, 128), lambda s: (s, dec.shape[1] // 128 - 1)),
            spec((8, 2 * qk + vv), lambda s: (0, 0)),
            spec((8, 128), lambda s: (0, 0)),
            spec((8, DV), lambda s: (0, 0)),
        ],
        out_specs=[
            spec((n, vv), lambda s: (s, 0)),
            spec((n, vv), lambda s: (s, 0)),
            spec((n, vv), lambda s: (s, 0)),
            spec((n, qk), lambda s: (s, 0)),
            spec((1, pair, n, n), lambda s: (s, 0, 0, 0)),
            spec((1, pair, n // BLOCK * DK, DV), lambda s: (s, 0, 0, 0)),
        ],
        out_shape=[
            jax.ShapeDtypeStruct((tokens, vv), bf16),
            jax.ShapeDtypeStruct((tokens, vv), f32),
            jax.ShapeDtypeStruct((tokens, vv), bf16),
            jax.ShapeDtypeStruct((tokens, qk), bf16),
            jax.ShapeDtypeStruct((slots, pair, n, n), bf16),
            jax.ShapeDtypeStruct((slots, pair, n // BLOCK * DK, DV), bf16),
        ],
        compiler_params=pltpu.CompilerParams(vmem_limit_bytes=56 * 1024 * 1024),
        cost_estimate=pl.CostEstimate(flops=1, bytes_accessed=1, transcendentals=0),
        name="mixer_forward",
    )(ids, proj, dec, conv, head_rows, gain_row)


def backward_kernel(
    hl,
    pair,
    p,
    ids_ref,
    x_ref,
    dec_ref,
    conv_ref,
    head_ref,
    gain_ref,
    o_ref,
    u_ref,
    w_ref,
    inv_ref,
    s_ref,
    dy_ref,
    dx_out,
    ddec_out,
    conv_out,
    small_out,
):
    slot = pl.program_id(0)
    n = TOK_DEV
    qk, vv = pair * DK, pair * DV
    q_at = slice(0, qk)
    k_at = slice(qk, 2 * qk)
    v_at = slice(2 * qk, 2 * qk + vv)
    blocks = n // BLOCK
    x, below, on_below, strict, same = block_masks(n)
    dec = dec_ref[...]
    alog_row = head_ref[0:1, :]
    pre, log_decay, running, total = decay_parts(dec, alog_row, head_ref[1:2, :])
    running_t = running.T
    heads = range(pair)
    qc = conv_forward(x_ref[:, q_at], conv_ref[:, q_at])
    kc = conv_forward(x_ref[:, k_at], conv_ref[:, k_at])
    vc = conv_forward(x_ref[:, v_at], conv_ref[:, v_at])
    q_sig = jax.nn.sigmoid(qc)
    k_sig = jax.nn.sigmoid(kc)
    v_sig = jax.nn.sigmoid(vc)
    q = qc * q_sig
    k = kc * k_sig
    v = (vc * v_sig).astype(bf16)
    gain = gain_ref[0:1, :]
    qn, kn, vn, qr, kr, beta, b, tot, d, sim, low, score = ([] for _ in range(12))
    d_out, u = [], []
    gain_rows = jnp.zeros((1, DV), f32)
    for i in heads:
        h = ids_ref[0] * hl + p * pair + i
        cols = slice(i * DV, (i + 1) * DV)
        kcols = slice(i * DK, (i + 1) * DK)
        rows_q, r_q = unit_rows(q[:, kcols], DK**-0.5)
        rows_k, r_k = unit_rows(k[:, kcols], 1.0)
        qr.append((rows_q, r_q))
        kr.append((rows_k, r_k))
        qn.append(rows_q.astype(bf16))
        kn.append(rows_k.astype(bf16))
        vn.append(v[:, cols])
        beta.append(jax.nn.sigmoid(lane_of(dec, H + h)))
        b.append(lane_of(running, h))
        tot.append(lane_of(total, h))
        d.append(
            jnp.where(on_below, jnp.exp(jnp.where(on_below, b[i] - row_of(running_t, h), 0.0)), 0.0)
        )
        both = mm_nt(jnp.concatenate([kn[i], qn[i]], axis=0), kn[i])
        sim.append(jnp.where(strict, d[i] * both[:n], 0.0))
        score.append(both[n:] * d[i])
        out = o_ref[:, cols]
        g_at = slice(2 * qk + vv + i * DV, 2 * qk + vv + (i + 1) * DV)
        gate = x_ref[:, g_at]
        dy = dy_ref[:, cols].astype(f32)
        r = lax.rsqrt(jnp.mean(out * out, axis=1, keepdims=True) + eps_norm)
        normed = out * r
        g_sig = jax.nn.sigmoid(gate)
        act = gate * g_sig
        d_act = dy * normed * gain
        dx_out[:, g_at] = (d_act * (g_sig * (1.0 + gate * (1.0 - g_sig)))).astype(bf16)
        gain_rows = gain_rows + jnp.sum(dy * normed * act, axis=0, keepdims=True)
        d_normed = dy * gain * act
        d_out.append(r * (d_normed - normed * jnp.mean(d_normed * normed, axis=1, keepdims=True)))
        u.append(u_ref[:, cols])
    e = [jnp.exp(b[i]) for i in heads]
    fin = [jnp.exp(tot[i] - b[i]) for i in heads]
    grow = [jnp.exp(tot[i]) for i in heads]
    d_out16 = [d_out[i].astype(bf16) for i in heads]
    score16 = [score[i].astype(bf16) for i in heads]
    d_u0 = [mm_tn(score16[i], d_out16[i]) for i in heads]
    d_state = [jnp.zeros((DK, DV), f32) for i in heads]
    d_u = [[None] * blocks for i in heads]
    dq_s = [[None] * blocks for i in heads]
    dk_s = [[None] * blocks for i in heads]
    fin_col = [[None] * blocks for i in heads]
    grow_col = [[None] * blocks for i in heads]
    e_out = [(e[i] * d_out[i]).astype(bf16) for i in heads]
    for c in reversed(range(blocks)):
        lo, hi = c * BLOCK, (c + 1) * BLOCK
        for i in heads:
            ds16 = d_state[i].astype(bf16)
            s16 = s_ref[0, i, c * DK : (c + 1) * DK, :]
            u_c = u[i][lo:hi].astype(f32)
            if c == blocks - 1:
                d_u[i][c] = d_u0[i][lo:hi]
                fin_col[i][c] = jnp.zeros((BLOCK, 1), f32)
                grow_col[i][c] = jnp.zeros((1, 1), f32)
                dk_s[i][c] = jnp.zeros((BLOCK, DK), f32)
            else:
                k_ds = mm(kn[i][lo:hi], ds16)
                add = fin[i][lo:hi] * k_ds
                d_u[i][c] = d_u0[i][lo:hi] + add
                fin_col[i][c] = jnp.sum(add * u_c, axis=1, keepdims=True)
                grow_col[i][c] = grow[i][lo : lo + 1] * jnp.sum(
                    jnp.sum(d_state[i] * s16.astype(f32), axis=1, keepdims=True),
                    axis=0,
                    keepdims=True,
                )
                dk_s[i][c] = mm_nt(fin[i][lo:hi] * u_c, ds16)
            if c > 0:
                step = mm_tn(
                    jnp.concatenate([qn[i][lo:hi], w_ref[lo:hi, i * DK : (i + 1) * DK]], axis=0),
                    jnp.concatenate([e_out[i][lo:hi], (-d_u[i][c]).astype(bf16)], axis=0),
                )
                d_state[i] = grow[i][lo : lo + 1] * d_state[i] + step
    lane = lax.broadcasted_iota(jnp.int32, (n, 128), 1)
    d_dec = jnp.zeros((n, 128), f32)
    d_log = jnp.zeros((n, 128), f32)
    dq_all, dk_all, dv_all = [], [], []
    ones = jnp.ones((n, 128), bf16)
    upper_i = lax.broadcasted_iota(jnp.int32, (n, n), 0)
    upper_j = lax.broadcasted_iota(jnp.int32, (n, n), 1)
    upper = jnp.where(jnp.logical_and((upper_i ^ upper_j) < BLOCK, upper_i <= upper_j), 1.0, 0.0)
    for i in heads:
        h = ids_ref[0] * hl + p * pair + i
        du = jnp.concatenate(d_u[i], axis=0)
        d_right = mm_tn(inv_ref[0, i], du)
        dr16 = d_right.astype(bf16)
        outer = mm_nt(jnp.concatenate([d_out16[i], dr16], axis=0), u[i])
        d_score = jnp.where(on_below, outer[:n], 0.0)
        d_low = jnp.where(strict, -outer[n:], 0.0)
        z16 = (-(beta[i] * e[i]) * d_right).astype(bf16)
        recalled = []
        for c in range(blocks):
            lo, hi = c * BLOCK, (c + 1) * BLOCK
            s16 = s_ref[0, i, c * DK : (c + 1) * DK, :]
            if c == 0:
                dq_s[i][c] = jnp.zeros((BLOCK, DK), f32)
                recalled.append(jnp.zeros((BLOCK, 2 * DV), f32))
                continue
            back = mm_nt(jnp.concatenate([e_out[i][lo:hi], z16[lo:hi]], axis=0), s16)
            dq_s[i][c] = back[:BLOCK]
            dk_s[i][c] = dk_s[i][c] + back[BLOCK:]
            got = mm(jnp.concatenate([kn[i][lo:hi], qn[i][lo:hi]], axis=0), s16)
            recalled.append(jnp.concatenate([got[:BLOCK], got[BLOCK:]], axis=1))
        recalled = jnp.concatenate(recalled, axis=0)
        k_s = recalled[:, :DV]
        q_s = recalled[:, DV:]
        d_a = (d_score * d[i]).astype(bf16)
        d_g = d_low * beta[i] * d[i]
        d_g16 = (d_g + d_g.T).astype(bf16)
        dq = jnp.concatenate(dq_s[i], axis=0) + mm(d_a, kn[i])
        dk = jnp.concatenate(dk_s[i], axis=0) + mm_tn(d_a, qn[i]) + mm(d_g16, kn[i])
        dv = beta[i] * d_right
        row_sum = jnp.sum(d_low * sim[i], axis=1, keepdims=True)
        keep = vn[i].astype(f32) - e[i] * k_s
        d_beta = row_sum + jnp.sum(d_right * keep, axis=1, keepdims=True)
        moved = (d_score * score[i] + d_low * beta[i] * sim[i]).astype(bf16)
        d_b = mm(moved, ones) - mm_tn(moved, ones)
        d_b_col = e[i] * jnp.sum(
            d_out[i] * q_s - (beta[i] * d_right) * k_s, axis=1, keepdims=True
        )
        fin_all = jnp.concatenate(fin_col[i], axis=0)
        d_b = jnp.where(lane == h, d_b + (d_b_col - fin_all), 0.0)
        tail = jnp.concatenate(
            [
                jnp.broadcast_to(
                    grow_col[i][c] + jnp.sum(fin_col[i][c], axis=0, keepdims=True), (BLOCK, 1)
                )
                for c in range(blocks)
            ],
            axis=0,
        )
        d_log = d_log + mm_exact(upper, d_b) + jnp.where(lane == h, tail, 0.0)
        d_dec = d_dec + jnp.where(lane == H + h, d_beta * beta[i] * (1.0 - beta[i]), 0.0)
        rows_q, r_q = qr[i]
        rows_k, r_k = kr[i]
        unit = rows_q * DK**0.5
        dq = (DK**-0.5) * r_q * (dq - unit * jnp.sum(dq * unit, axis=1, keepdims=True))
        dk = r_k * (dk - rows_k * jnp.sum(dk * rows_k, axis=1, keepdims=True))
        dq_all.append(dq)
        dk_all.append(dk)
        dv_all.append(dv)

    @pl.when(slot == 0)
    def _():
        conv_out[...] = jnp.zeros_like(conv_out)
        small_out[...] = jnp.zeros_like(small_out)

    def through_conv(d_active, conv, sig, at):
        d_conv = d_active * (sig * (1.0 + conv * (1.0 - sig)))
        d_mixed, d_weight = conv_backward(d_conv, x_ref[:, at], conv_ref[:, at])
        dx_out[:, at] = d_mixed.astype(bf16)
        conv_out[0:KCONV, at] += d_weight

    through_conv(jnp.concatenate(dq_all, axis=1), qc, q_sig, q_at)
    through_conv(jnp.concatenate(dk_all, axis=1), kc, k_sig, k_at)
    through_conv(jnp.concatenate(dv_all, axis=1), vc, v_sig, v_at)
    first = ids_ref[0] * hl + p * pair
    mine = jnp.logical_and(lane >= first, lane < first + pair)
    d_pre = jnp.where(mine, -jnp.exp(alog_row) * jax.nn.sigmoid(pre) * d_log, 0.0)
    ddec_out[...] = d_dec + d_pre

    small_out[0:1, :] += gain_rows
    small_out[1:2, 0:128] += jnp.sum(jnp.where(mine, d_log * log_decay, 0.0), axis=0, keepdims=True)
    small_out[2:3, 0:128] += jnp.sum(d_pre, axis=0, keepdims=True)


def mixer_backward(ids, proj, dec, conv, head_rows, gain_row, saved, d_gated, hl, pair, p):
    out, u, w, inv, states = saved
    tokens = proj.shape[0]
    slots = tokens // TOK_DEV
    qk = pair * DK
    vv = pair * DV
    spec = pl.BlockSpec
    n = TOK_DEV

    def body(*refs):
        backward_kernel(hl, pair, p, *refs)

    return pl.pallas_call(
        body,
        grid=(slots,),
        in_specs=[
            pl.BlockSpec(memory_space=pltpu.SMEM),
            spec((n, 2 * qk + 2 * vv), lambda s: (s, 0)),
            spec((n, 128), lambda s: (s, dec.shape[1] // 128 - 1)),
            spec((8, 2 * qk + vv), lambda s: (0, 0)),
            spec((8, 128), lambda s: (0, 0)),
            spec((8, DV), lambda s: (0, 0)),
            spec((n, vv), lambda s: (s, 0)),
            spec((n, vv), lambda s: (s, 0)),
            spec((n, qk), lambda s: (s, 0)),
            spec((1, pair, n, n), lambda s: (s, 0, 0, 0)),
            spec((1, pair, n // BLOCK * DK, DV), lambda s: (s, 0, 0, 0)),
            spec((n, vv), lambda s: (s, 0)),
        ],
        out_specs=[
            spec((n, 2 * qk + 2 * vv), lambda s: (s, 0)),
            spec((n, 128), lambda s: (s, 0)),
            spec((8, 2 * qk + vv), lambda s: (0, 0)),
            spec((8, DV), lambda s: (0, 0)),
        ],
        out_shape=[
            jax.ShapeDtypeStruct((tokens, 2 * qk + 2 * vv), bf16),
            jax.ShapeDtypeStruct((tokens, 128), f32),
            jax.ShapeDtypeStruct((8, 2 * qk + vv), f32),
            jax.ShapeDtypeStruct((8, DV), f32),
        ],
        compiler_params=pltpu.CompilerParams(vmem_limit_bytes=56 * 1024 * 1024),
        cost_estimate=pl.CostEstimate(flops=1, bytes_accessed=1, transcendentals=0),
        name="mixer_backward",
    )(ids, proj, dec, conv, head_rows, gain_row, out, u, w, inv, states, d_gated)


VMEM_LIMIT = 58 * 1024 * 1024
ANY = pl.BlockSpec(memory_space=pl.ANY)
SMEM = pl.BlockSpec(memory_space=pltpu.SMEM)


def params(**more):
    return pltpu.CompilerParams(vmem_limit_bytes=VMEM_LIMIT, **more)


def cost(flops, moved):
    return pl.CostEstimate(flops=1, bytes_accessed=1, transcendentals=0)


def pack_columns(w, extra, table, rows, plane, ids):
    chips = len(table)
    width = sum(size for _, size in table[0])
    more = 0 if extra is None else extra.shape[1]

    def body(ids_ref, w_ref, *refs):
        out = refs[-1]
        for c in range(chips):
            at = 0
            for start, size in table[c]:
                out[c, :, at : at + size] = w_ref[:, start : start + size]
                at += size
            if more:
                out[c, :, at : at + more] = refs[0][...]

    def block(i, ids_ref):
        return (ids_ref[2] if plane else 0, 0)

    def whole(i, ids_ref):
        return (0, 0)

    return pl.pallas_call(
        body,
        grid_spec=pltpu.PrefetchScalarGridSpec(
            num_scalar_prefetch=1,
            grid=(1,),
            in_specs=[pl.BlockSpec((rows, w.shape[1]), block)]
            + ([pl.BlockSpec((rows, more), whole)] if more else []),
            out_specs=pl.BlockSpec((chips, rows, width + more), lambda i, ids_ref: (0, 0, 0)),
        ),
        out_shape=jax.ShapeDtypeStruct((chips, rows, width + more), bf16),
        compiler_params=params(),
        cost_estimate=cost(0, 2 * rows * w.shape[1] + 2 * chips * rows * (width + more)),
        name="pack_columns",
    )(ids, w, *([extra] if more else []))


def pack_relative(w, extra, table, plane, ids):
    rows = w.shape[0] // 4 if plane else w.shape[0]
    chips = len(table)
    more = 0 if extra is None else extra.shape[1]
    width = sum(size for _, size in table[0]) + more

    def body(ids_ref, w_ref, *refs):
        outs = refs[-chips:]
        for j in range(chips):
            c = jnp.bitwise_xor(ids_ref[0], j)
            at = 0
            for r, (start, size) in enumerate(table[0]):
                step = table[1][r][0] - start
                lane = pl.multiple_of(start + c * step, 128)
                outs[j][:, at : at + size] = w_ref[:, pl.ds(lane, size)]
                at += size
            if more:
                outs[j][:, at : at + more] = refs[0][...]

    def block(i, ids_ref):
        return (ids_ref[2] if plane else 0, 0)

    def whole(i, ids_ref):
        return (0, 0)

    return pl.pallas_call(
        body,
        grid_spec=pltpu.PrefetchScalarGridSpec(
            num_scalar_prefetch=1,
            grid=(1,),
            in_specs=[pl.BlockSpec((rows, w.shape[1]), block)]
            + ([pl.BlockSpec((rows, more), block)] if more else []),
            out_specs=[pl.BlockSpec((rows, width), whole)] * chips,
        ),
        out_shape=[jax.ShapeDtypeStruct((rows, width), bf16)] * chips,
        compiler_params=params(),
        cost_estimate=cost(0, 4 * rows * w.shape[1]),
        name="pack_relative",
    )(ids, w, *([extra] if more else []))


def join_cores(mine, theirs, ids):
    rows, n = mine.shape
    tile = 512

    def body(ids_ref, mine_ref, theirs_ref, o_ref):
        core = ids_ref[1]
        o_ref[pl.ds(pl.multiple_of(core * rows, 16), rows), :] = mine_ref[...]
        o_ref[pl.ds(pl.multiple_of((1 - core) * rows, 16), rows), :] = theirs_ref[...]

    return pl.pallas_call(
        body,
        grid=(n // tile,),
        in_specs=[SMEM] + [pl.BlockSpec((rows, tile), lambda i: (0, i))] * 2,
        out_specs=pl.BlockSpec((2 * rows, tile), lambda i: (0, i)),
        out_shape=jax.ShapeDtypeStruct((2 * rows, n), bf16),
        compiler_params=params(),
        cost_estimate=cost(0, 8 * rows * n),
        name="join_cores",
    )(ids, mine, theirs)


def norm_rows(parts, gain):
    d = parts[0].shape[1]
    total = sum(p.shape[0] for p in parts)

    def body(gain_ref, *refs):
        out = refs[-1]
        at = 0
        for ref in refs[:-1]:
            for m in range(0, ref.shape[0], 128):
                rows = ref[m : m + 128, :].astype(f32)
                r = lax.rsqrt(jnp.mean(rows * rows, axis=1, keepdims=True) + eps_norm)
                out[at : at + 128, :] = (rows * r * gain_ref[0:1, :]).astype(bf16)
                at += 128

    return pl.pallas_call(
        body,
        out_shape=jax.ShapeDtypeStruct((total, d), bf16),
        compiler_params=params(),
        cost_estimate=cost(8 * total * d, 4 * total * d),
        name="norm_rows",
    )(gain, *parts)


def small_layout(shapes):
    lanes = []
    at = 0
    for size in shapes:
        lanes.append(at)
        at += size + (-size % 128)
    return lanes, at


def pack_small(conv, vectors, nf):
    lanes, used = small_layout([v.shape[1] for v in vectors])
    channels = conv.shape[1]

    def body(conv_ref, *refs):
        out = refs[-1]
        out[...] = jnp.zeros_like(out)
        for d in range(nf):
            out[d, 0:KCONV, :] = conv_ref[...].astype(f32)
            for ref, lane in zip(refs[:-1], lanes):
                out[d, KCONV : KCONV + 1, lane : lane + ref.shape[1]] = ref[...].astype(f32)

    out = pl.pallas_call(
        body,
        out_shape=jax.ShapeDtypeStruct((nf, 8, channels), f32),
        compiler_params=params(),
        cost_estimate=cost(0, 0),
        name="pack_small",
    )(conv, *vectors)
    return out.astype(bf16)


def small_ranges(chip, hk, qk, vv, groups, p, conv_shard):
    at = chip * groups + p
    found = []
    for start, size in ((at * qk, qk), (hk + at * qk, qk), (2 * hk + at * vv, vv)):
        lane = pl.multiple_of(lax.rem(start, conv_shard), 128)
        found.append((lax.div(start, conv_shard), lane, size))
    return found


def unpack_small(gathered, sizes, ids, hk, qk, vv, groups):
    nf, _, conv_shard = gathered.shape
    lanes, _ = small_layout(sizes)
    d = nf * sizes[0]

    def body(ids_ref, g_ref, gains_ref, heads_ref, ogain_ref, *convs):
        gains_ref[...] = jnp.zeros_like(gains_ref)
        heads_ref[...] = jnp.zeros_like(heads_ref)
        ogain_ref[...] = jnp.zeros_like(ogain_ref)
        for n, out, row in (
            (0, gains_ref, 0),
            (1, gains_ref, 1),
            (2, ogain_ref, 0),
            (3, heads_ref, 0),
            (4, heads_ref, 1),
        ):
            size = sizes[n]
            for i in range(nf):
                out[row : row + 1, i * size : (i + 1) * size] = g_ref[
                    i, KCONV : KCONV + 1, lanes[n] : lanes[n] + size
                ]
        for p, out in enumerate(convs):
            at = 0
            for dev, lane, size in small_ranges(ids_ref[0], hk, qk, vv, groups, p, conv_shard):
                out[:, at : at + size] = g_ref[dev, :, pl.ds(lane, size)]
                at += size

    return pl.pallas_call(
        body,
        in_specs=[SMEM, pl.BlockSpec(memory_space=pltpu.VMEM)],
        out_shape=[
            jax.ShapeDtypeStruct((8, d), f32),
            jax.ShapeDtypeStruct((8, 128), f32),
            jax.ShapeDtypeStruct((8, nf * sizes[2]), f32),
        ]
        + [jax.ShapeDtypeStruct((8, 2 * qk + vv), f32)] * groups,
        compiler_params=params(),
        name="unpack_small",
    )(ids, gathered.astype(f32))


def pack_small_grads(g_conv, g_heads, gain_in, gain_mid, sizes, ids, nf, conv_shard, hk, qk, vv):
    lanes, _ = small_layout(sizes)
    groups = len(g_conv)

    def body(ids_ref, gin_ref, gmid_ref, *refs):
        out = refs[-1]
        out[...] = jnp.zeros_like(out)
        heads = refs[groups][...]
        for ref in refs[groups + 1 : -1]:
            heads = heads + ref[...]
        for n, row in (
            (0, gin_ref[0:1, :]),
            (1, gmid_ref[0:1, :]),
            (2, heads[0:1, :]),
            (3, heads[1:2, :]),
            (4, heads[2:3, :]),
        ):
            size = sizes[n]
            for i in range(nf):
                out[i, KCONV : KCONV + 1, lanes[n] : lanes[n] + size] = row[
                    :, i * size : (i + 1) * size
                ]
        for p in range(groups):
            at = 0
            for dev, lane, size in small_ranges(ids_ref[0], hk, qk, vv, groups, p, conv_shard):
                out[dev, 0:KCONV, pl.ds(lane, size)] = refs[p][0:KCONV, at : at + size]
                at += size

    vmem = pl.BlockSpec(memory_space=pltpu.VMEM)
    return pl.pallas_call(
        body,
        in_specs=[SMEM] + [vmem] * (2 + 2 * groups),
        out_shape=jax.ShapeDtypeStruct((nf, 8, conv_shard), f32),
        compiler_params=params(),
        name="pack_small_grads",
    )(ids, gain_in, gain_mid, *g_conv, *g_heads)


def place_blocks(whole, pair_values, ids, c, shape):
    t, last = pair_values
    rows, n = t.shape
    old = [] if whole is None else [whole]

    def body(ids_ref, t_ref, last_ref, *refs):
        middle = jnp.logical_or(ids_ref[2] == 1, ids_ref[2] == 2)
        refs[-1][0] = jnp.where(middle, t_ref[...], last_ref[...])

    half = n // 2
    return pl.pallas_call(
        body,
        grid=(2,),
        in_specs=[SMEM]
        + [pl.BlockSpec((rows, half), lambda i: (0, i))] * 2
        + [ANY] * len(old),
        out_specs=pl.BlockSpec((1, rows, half), lambda i: (c, 0, i)),
        out_shape=jax.ShapeDtypeStruct(shape, bf16),
        input_output_aliases={3: 0} if old else {},
        compiler_params=params(),
        cost_estimate=cost(0, 6 * rows * n),
        name="place_blocks",
    )(ids, t, last, *old)


def finish_projection(whole, pair_values, ids, chunk, p, groups, shape, widths):
    t, last = pair_values
    rows = shape[0]
    unit = 256
    starts = []
    for c in chunk:
        base = 0
        for width in widths:
            size = width // (4 * groups)
            starts.append([base + (c * groups + p) * size + s for s in range(0, size, unit)])
            base += width
    starts = sum(starts, [])
    each = len(starts) // len(chunk)
    old = [] if whole is None else [whole]

    def body(ids_ref, t_ref, last_ref, *refs):
        middle = jnp.logical_or(ids_ref[2] == 1, ids_ref[2] == 2)
        refs[-1][...] = jnp.where(middle, t_ref[...], last_ref[...]).astype(f32)

    def column(i):
        at = starts[-1] // unit
        for n in reversed(range(len(starts) - 1)):
            at = jnp.where(i == n, starts[n] // unit, at)
        return (0, at)

    return pl.pallas_call(
        body,
        grid=(len(starts),),
        in_specs=[SMEM]
        + [pl.BlockSpec((rows, unit), lambda i: (lax.div(i, each), lax.rem(i, each)))] * 2
        + [ANY] * len(old),
        out_specs=pl.BlockSpec((rows, unit), column),
        out_shape=jax.ShapeDtypeStruct(shape, f32),
        input_output_aliases={3: 0} if old else {},
        compiler_params=params(),
        cost_estimate=cost(0, 8 * rows * unit * len(starts)),
        name="finish_projection",
    )(ids, t, last, *old)


def finish_feed_forward(blocks):
    chips, rows, n = blocks.shape
    wide = n // 2

    def body(x_ref, o_ref):
        which = pl.program_id(1)
        for s in range(2):

            @pl.when(which == s)
            def _():
                for at in range(0, wide, 128):
                    start = 2 * at + 128 * s
                    o_ref[:, at : at + 128] = x_ref[0, :, start : start + 128].astype(f32)

    return pl.pallas_call(
        body,
        grid=(chips, 2),
        in_specs=[pl.BlockSpec((1, rows, n), lambda c, s: (c, 0, 0))],
        out_specs=pl.BlockSpec((rows, wide), lambda c, s: (0, s * chips + c)),
        out_shape=jax.ShapeDtypeStruct((rows, chips * n), f32),
        compiler_params=params(),
        cost_estimate=cost(0, 6 * chips * rows * n),
        name="finish_feed_forward",
    )(blocks)


def fill_rows(w_ref, own_ref, other_ref, core, chip=0):
    planes, chips, rows, _ = own_ref.shape
    for z in range(planes):
        for j in range(chips):
            c = jnp.bitwise_xor(chip, j)
            for ref, k in ((own_ref, core), (other_ref, 1 - core)):
                at = pl.multiple_of((2 * c + k) * planes * rows + z * rows, rows)
                w_ref[pl.ds(at, rows), :] = ref[z, j]


def project_planes(x, own, other, ids):
    tokens, k = x.shape
    planes, chips, rows, n = own.shape
    tile = 256

    def body(ids_ref, x_ref, own_ref, other_ref, o_ref, w_ref):
        fill_rows(w_ref, own_ref, other_ref, ids_ref[1], ids_ref[0])
        o_ref[...] = jnp.dot(x_ref[...], w_ref[...], preferred_element_type=f32)

    return pl.pallas_call(
        body,
        grid=(pl.cdiv(n, tile),),
        in_specs=[SMEM, pl.BlockSpec((tokens, k), lambda i: (0, 0))]
        + [pl.BlockSpec((planes, chips, rows, tile), lambda i: (0, 0, 0, i))] * 2,
        out_specs=pl.BlockSpec((tokens, tile), lambda i: (0, i)),
        out_shape=jax.ShapeDtypeStruct((tokens, n), f32),
        scratch_shapes=[pltpu.VMEM((k, tile), bf16)],
        compiler_params=params(),
        cost_estimate=cost(2 * tokens * k * n, 2 * tokens * k + 2 * k * n + 4 * tokens * n),
        name="project",
    )(ids, x, own, other)


def project(x, own, other, ids):
    tokens, k = x.shape
    rows, n = own[0].shape
    chips = len(own)
    tile = 256

    def body(ids_ref, x_ref, *refs):
        o_ref, w_ref = refs[2 * chips :]
        for j in range(chips):
            c = jnp.bitwise_xor(ids_ref[0], j)
            for ref, core in ((refs[j], ids_ref[1]), (refs[chips + j], 1 - ids_ref[1])):
                at = pl.multiple_of((2 * c + core) * rows, rows)
                w_ref[pl.ds(at, rows), :] = ref[...]
        o_ref[...] = jnp.dot(x_ref[...], w_ref[...], preferred_element_type=f32)

    return pl.pallas_call(
        body,
        grid=(pl.cdiv(n, tile),),
        in_specs=[SMEM, pl.BlockSpec((tokens, k), lambda i: (0, 0))]
        + [pl.BlockSpec((rows, tile), lambda i: (0, i))] * (2 * chips),
        out_specs=pl.BlockSpec((tokens, tile), lambda i: (0, i)),
        out_shape=jax.ShapeDtypeStruct((tokens, n), f32),
        scratch_shapes=[pltpu.VMEM((k, tile), bf16)],
        compiler_params=params(),
        cost_estimate=cost(2 * tokens * k * n, 2 * tokens * k + 2 * k * n + 4 * tokens * n),
        name="project",
    )(ids, x, *own, *other)


def feed_forward(x, own, other, down, d_ffn, ids):
    tokens, k = x.shape
    planes, chips, rows, n = own.shape
    wide = n // 2
    tile = 512

    def body(ids_ref, x_ref, own_ref, other_ref, down_ref, d_ref, h_ref, g_ref, w_ref):
        fill_rows(w_ref, own_ref, other_ref, ids_ref[1])
        for m in range(0, tokens, 256):
            rows_at = slice(m, m + 256)
            both = jnp.dot(x_ref[rows_at, :], w_ref[...], preferred_element_type=f32)
            d_hidden = mm_nt(d_ref[rows_at, :], down_ref[...])
            for s in range(tile // 256):
                gate = both[:, 256 * s : 256 * s + 128]
                up = both[:, 256 * s + 128 : 256 * s + 256]
                dh = d_hidden[:, 128 * s : 128 * s + 128]
                sig = jax.nn.sigmoid(gate)
                act = gate * sig
                h_ref[rows_at, 128 * s : 128 * s + 128] = (act * up).astype(bf16)
                g_ref[rows_at, 256 * s : 256 * s + 128] = (
                    dh * up * (sig * (1.0 + gate * (1.0 - sig)))
                ).astype(bf16)
                g_ref[rows_at, 256 * s + 128 : 256 * s + 256] = (dh * act).astype(bf16)

    return pl.pallas_call(
        body,
        grid=(pl.cdiv(n, tile),),
        in_specs=[
            SMEM,
            pl.BlockSpec((tokens, k), lambda i: (0, 0)),
            pl.BlockSpec((planes, chips, rows, tile), lambda i: (0, 0, 0, i)),
            pl.BlockSpec((planes, chips, rows, tile), lambda i: (0, 0, 0, i)),
            pl.BlockSpec((tile // 2, k), lambda i: (i, 0)),
            pl.BlockSpec((tokens, k), lambda i: (0, 0)),
        ],
        out_specs=[
            pl.BlockSpec((tokens, tile // 2), lambda i: (0, i)),
            pl.BlockSpec((tokens, tile), lambda i: (0, i)),
        ],
        out_shape=[
            jax.ShapeDtypeStruct((tokens, wide), bf16),
            jax.ShapeDtypeStruct((tokens, n), bf16),
        ],
        scratch_shapes=[pltpu.VMEM((k, tile), bf16)],
        compiler_params=params(),
        cost_estimate=cost(3 * tokens * k * n, 4 * tokens * k + 3 * k * n + 3 * tokens * n),
        name="feed_forward",
    )(ids, x, own, other, down, d_ffn)


def halves_of(i, tiles):
    half = tiles // 2
    return jnp.minimum(i, half - 1), jnp.maximum(i - half, 0)


def scatter_outputs(tokens, n, tile, refs=None):
    size = tokens // 2
    tiles = n // tile
    first = pl.BlockSpec((size, tile), lambda i, *ids: (0, halves_of(i, tiles)[0]))
    second = pl.BlockSpec((size, tile), lambda i, *ids: (0, halves_of(i, tiles)[1]))
    return [first, first, second, second], [jax.ShapeDtypeStruct((size, n // 2), bf16)] * 4


def write_scattered(outs, total_ref, tiles):
    size = total_ref.shape[0] // 4
    i = pl.program_id(0)

    for half, rows in ((0, ((1, 3), (0, 2))), (1, ((2, 3), (0, 1)))):

        @pl.when((i < tiles // 2) if half == 0 else (i >= tiles // 2))
        def _():
            for out, chips in zip(outs[2 * half : 2 * half + 2], rows):
                for n, m in enumerate(chips):
                    out[n * size : (n + 1) * size, :] = total_ref[m * size : (m + 1) * size, :]


def times_rows(lefts, mine, theirs, ids):
    tokens = lefts[0].shape[0]
    half, n = mine.shape
    tile = 256
    specs, shapes = scatter_outputs(tokens, n, tile)

    def body(ids_ref, *refs):
        left_refs = refs[: len(lefts)]
        mine_ref, theirs_ref = refs[len(lefts) : len(lefts) + 2]
        outs = refs[len(lefts) + 2 : -2]
        right_ref, total_ref = refs[-2:]
        core = ids_ref[1]
        right_ref[pl.ds(pl.multiple_of(core * half, 16), half), :] = mine_ref[...]
        right_ref[pl.ds(pl.multiple_of((1 - core) * half, 16), half), :] = theirs_ref[...]
        total = None
        at = 0
        for ref in left_refs:
            width = ref.shape[1]
            term = jnp.dot(ref[...], right_ref[at : at + width, :], preferred_element_type=f32)
            total = term if total is None else total + term
            at += width
        total_ref[...] = total.astype(bf16)
        write_scattered(outs, total_ref, n // tile)

    return pl.pallas_call(
        body,
        grid=(n // tile,),
        in_specs=[SMEM]
        + [pl.BlockSpec(a.shape, lambda i: (0, 0)) for a in lefts]
        + [pl.BlockSpec((half, tile), lambda i: (0, i))] * 2,
        out_specs=specs,
        out_shape=shapes,
        scratch_shapes=[pltpu.VMEM((2 * half, tile), bf16), pltpu.VMEM((tokens, tile), bf16)],
        compiler_params=params(),
        cost_estimate=cost(4 * tokens * half * n, 2 * (tokens * half + half * n + tokens * n)),
        name="times_rows",
    )(ids, *lefts, mine, theirs)


def times_transposed(pairs, ids, relative):
    tokens = pairs[0][0].shape[0]
    planes, chips, rows, _ = pairs[0][1].shape
    rows *= planes
    total_n = sum(left.shape[1] for left, own, other in pairs)
    k = 2 * chips * rows
    specs_out, shapes = scatter_outputs(tokens, k, rows)

    def body(ids_ref, *refs):
        count = len(pairs)
        outs = refs[3 * count : 3 * count + 4]
        piece_refs = refs[3 * count + 4 : -1]
        total_ref = refs[-1]
        mine = pl.program_id(0) % 2 == ids_ref[1]

        def choose(which):
            for n in range(count):
                piece = refs[3 * n + which][:, 0]
                piece_refs[n][...] = piece.reshape(rows, piece.shape[2])

        @pl.when(mine)
        def _():
            choose(1)

        @pl.when(jnp.logical_not(mine))
        def _():
            choose(2)

        total = None
        for n in range(count):
            term = mm_nt(refs[3 * n][...], piece_refs[n][...])
            total = term if total is None else total + term
        total_ref[...] = total.astype(bf16)
        write_scattered(outs, total_ref, 2 * chips)

    def piece_at(i, ids_ref):
        c = lax.div(i, 2)
        if relative:
            c = jnp.bitwise_xor(c, ids_ref[0])
        return (0, c, 0, 0)

    specs = []
    args = []
    for left, own, other in pairs:
        specs.append(pl.BlockSpec(left.shape, lambda i, ids_ref: (0, 0)))
        block = (own.shape[0], 1) + own.shape[2:]
        specs += [pl.BlockSpec(block, piece_at)] * 2
        args += [left, own, other]
    return pl.pallas_call(
        body,
        grid_spec=pltpu.PrefetchScalarGridSpec(
            num_scalar_prefetch=1,
            grid=(2 * chips,),
            in_specs=specs,
            out_specs=specs_out,
            scratch_shapes=[pltpu.VMEM((rows, own.shape[3]), bf16) for _, own, _ in pairs]
            + [pltpu.VMEM((tokens, rows), bf16)],
        ),
        out_shape=shapes,
        compiler_params=params(),
        cost_estimate=cost(
            2 * tokens * k * total_n, 2 * (tokens * k + k * total_n + tokens * total_n)
        ),
        name="times_transposed",
    )(ids, *args)


def column_terms(lefts, rights, ids):
    tokens, k = lefts[0].shape
    n = rights[0].shape[1]
    chips = 4
    rows = k // (2 * chips)

    def body(ids_ref, a_ref, b_ref, ra_ref, rb_ref, o_ref):
        total = mm_tn(a_ref[...], ra_ref[...]) + mm_tn(b_ref[...], rb_ref[...])
        o_ref[0] = total.astype(bf16)

    def column(i, ids_ref):
        return (0, 2 * i + ids_ref[1])

    def whole(i, ids_ref):
        return (0, 0)

    return pl.pallas_call(
        body,
        grid_spec=pltpu.PrefetchScalarGridSpec(
            num_scalar_prefetch=1,
            grid=(chips,),
            in_specs=[pl.BlockSpec((tokens, rows), column)] * 2
            + [pl.BlockSpec((tokens, n), whole)] * 2,
            out_specs=pl.BlockSpec((1, rows, n), lambda i, ids_ref: (i, 0, 0)),
        ),
        out_shape=jax.ShapeDtypeStruct((chips, rows, n), bf16),
        compiler_params=params(),
        cost_estimate=cost(2 * tokens * k * n, 4 * (tokens * k + tokens * n + k * n)),
        name="column_terms",
    )(ids, *lefts, *rights)


def row_terms(lefts, right, ids):
    tokens, n = right.shape
    k = sum(a.shape[1] for a in lefts)
    tile = 512
    half = k // 2

    def body(ids_ref, *refs):
        left_refs = refs[: len(lefts)]
        right_ref, mine_ref, theirs_ref, acc = refs[len(lefts) :]
        core = ids_ref[1]
        at = 0
        for ref in left_refs:
            width = ref.shape[1]
            acc[at : at + width, :] = mm_tn(ref[...], right_ref[...])
            at += width
        mine_ref[...] = acc[pl.ds(pl.multiple_of(core * half, 16), half), :].astype(bf16)
        theirs_ref[...] = acc[pl.ds(pl.multiple_of((1 - core) * half, 16), half), :].astype(bf16)

    out = pl.BlockSpec((half, tile), lambda i: (0, i))
    return pl.pallas_call(
        body,
        grid=(n // tile,),
        in_specs=[SMEM]
        + [pl.BlockSpec(a.shape, lambda i: (0, 0)) for a in lefts]
        + [pl.BlockSpec((tokens, tile), lambda i: (0, i))],
        out_specs=[out, out],
        out_shape=[jax.ShapeDtypeStruct((half, n), bf16)] * 2,
        scratch_shapes=[pltpu.VMEM((k, tile), f32)],
        compiler_params=params(),
        cost_estimate=cost(2 * tokens * k * n, 2 * (tokens * k + tokens * n + k * n)),
        name="row_terms",
    )(ids, *lefts, right)


def after(values, *earlier):
    if not earlier:
        return values
    return lax.optimization_barrier((values, earlier))[0]


def to_chip(a, nf, j):
    return lax.ppermute(a, "fsdp", [(i, i ^ (2 * j)) for i in range(nf)])


def swap_core(a, nf):
    return lax.ppermute(a, "fsdp", [(i, i ^ 1) for i in range(nf)])


RIGHT = [(0, 1), (1, 2), (2, 3)]
LEFT = [(1, 0), (2, 1), (3, 2)]
INWARD = [(0, 1), (3, 2)]
MIDDLE = [(1, 2), (2, 1)]
OUTWARD = [(1, 0), (2, 3)]
SWAP = [(0, 1), (1, 0), (2, 3), (3, 2)]


def along(a, pairs):
    return lax.ppermute(a, "rep", pairs)


def add16(a, b):
    return (a.astype(f32) + b.astype(f32)).astype(bf16)


def gather_small(a, nf):
    me = lax.axis_index("fsdp")
    out = a[None]
    bit = 1
    while bit < nf:
        other = lax.ppermute(out, "fsdp", [(i, i ^ bit) for i in range(nf)])
        upper = (me & bit) != 0
        out = jnp.concatenate(
            [jnp.where(upper, other, out), jnp.where(upper, out, other)], axis=0
        )
        bit *= 2
    return out


def sum_small(a, nf):
    me = lax.axis_index("fsdp")
    bit = nf // 2
    while bit:
        half = a.shape[0] // 2
        upper = (me & bit) != 0
        keep = jnp.where(upper, a[half:], a[:half])
        send = jnp.where(upper, a[:half], a[half:])
        a = keep + lax.ppermute(send, "fsdp", [(i, i ^ bit) for i in range(nf)])
        bit //= 2
    return a[0]


class Line:
    def __init__(self, nz):
        self.nz = nz
        self.tokens = ()
        self.first = None
        self.second = None
        z = lax.axis_index("rep")
        self.middle = jnp.logical_or(z == 1, z == 2)

    def step(self, new, *earlier):
        if self.nz != 4:
            return new and (new[0], (lax.psum(new[1], "rep"),) * 2)
        chunk = None if new is None else new[1]
        first = None if self.first is None else self.first[1:]
        second = None if self.second is None else self.second[1:]
        chunk, first, second, _, _ = lax.optimization_barrier(
            (chunk, first, second, self.tokens, earlier)
        )
        outward = None if second is None else second[0] + second[1]
        across = None if first is None else first[0] + first[1]
        finished = next_first = next_second = None
        tokens = []
        if chunk is not None and outward is not None and outward.shape != chunk.shape:
            got = along(chunk, INWARD)
            last = along(outward, OUTWARD)
            tokens += [got, last]
            finished = (self.second[0], (outward, last))
            next_first = (new[0], chunk, got)
        elif chunk is not None or outward is not None:
            send = chunk if outward is None else outward
            if chunk is not None and outward is not None:
                send = jnp.where(self.middle, outward, chunk)
            got = along(send, SWAP)
            tokens.append(got)
            if outward is not None:
                finished = (self.second[0], (send, got))
            if chunk is not None:
                next_first = (new[0], chunk, got)
        if across is not None:
            met = along(across, MIDDLE)
            tokens.append(met)
            next_second = (self.first[0], across, met)
        self.first, self.second, self.tokens = next_first, next_second, tuple(tokens)
        return finished


def gather_first(a, nf, *earlier):
    chips = nf // 2
    a = after(a, *earlier)
    if chips != 4:
        return [a] + [to_chip(a, nf, j) for j in range(1, chips)]
    return [a, to_chip(a, nf, 1), to_chip(a, nf, 2)]


def gather_second(parts, nf, *earlier):
    if nf != 8:
        return jnp.concatenate(parts, axis=0)
    a, one, two = parts
    half = a.shape[0] // 2
    low, high = after((one[:half], two[half:]), *earlier)
    return jnp.concatenate([a, one, two, to_chip(low, nf, 2), to_chip(high, nf, 1)], axis=0)


def scatter_first(a, nf, *earlier):
    chips = nf // 2
    n = a.shape[0] // chips
    parts = [a[j * n : (j + 1) * n] for j in range(chips)]
    if chips != 4:
        return [parts[0]] + [to_chip(parts[j], nf, j) for j in range(1, chips)]
    half = n // 2
    low, high, one, two = after(
        (parts[3][:half], parts[3][half:], parts[1][half:], parts[2][:half]), *earlier
    )
    low = to_chip(low, nf, 2)
    high = to_chip(high, nf, 1)
    one = to_chip(one, nf, 1)
    two = to_chip(two, nf, 2)
    return [
        parts[0],
        one,
        two,
        add16(parts[1][:half], low),
        add16(parts[2][half:], high),
    ]


def scatter_second(parts, nf, *earlier):
    if nf != 8:
        total = parts[0].astype(f32)
        for part in parts[1:]:
            total = total + part.astype(f32)
        return total
    own, one, two, one_low, two_high = parts
    one_low, two_high = after((one_low, two_high), *earlier)
    one_low = to_chip(one_low, nf, 1)
    two_high = to_chip(two_high, nf, 2)
    own = own.astype(f32)
    half = own.shape[0] // 2
    return jnp.concatenate(
        [
            own[:half] + one_low.astype(f32) + two.astype(f32),
            own[half:] + one.astype(f32) + two_high.astype(f32),
        ],
        axis=0,
    )


def rms_back(rows, r, gain, d_out):
    unit = rows * r
    d_unit = d_out * gain
    d_rows = r * (d_unit - unit * jnp.mean(d_unit * unit, axis=1, keepdims=True))
    return d_rows, jnp.sum(d_out * unit, axis=0)


def scale_of(rows):
    return lax.rsqrt(jnp.mean(rows * rows, axis=1, keepdims=True) + eps_norm)


def exchange(a, nf):
    groups = [[2 * c + k for c in range(nf // 2)] for k in range(2)]
    return lax.all_to_all(a, "fsdp", 0, 0, axis_index_groups=groups, tiled=True)


def column_blocks(w, widths, chips, groups, p):
    rows = w.shape[0]
    start = 0
    parts = []
    for width in widths:
        part = w[:, start : start + width].reshape(rows, chips, groups, width // (chips * groups))
        parts.append(part[:, :, p].transpose(1, 0, 2))
        start += width
    return jnp.concatenate(parts, axis=2)


def from_column_blocks(blocks, widths):
    chips, rows, _ = blocks.shape
    parts = []
    at = 0
    for width in widths:
        part = blocks[:, :, at : at + width // chips]
        parts.append(part.transpose(1, 0, 2).reshape(rows, width))
        at += width // chips
    return parts


def both_core_rows(own, nf):
    core = lax.axis_index("fsdp") % 2
    other = swap_core(own, nf)
    first = core == 0
    chips, rows, width = own.shape
    both = jnp.stack([jnp.where(first, own, other), jnp.where(first, other, own)], axis=1)
    return both.reshape(chips * 2 * rows, width)


def core_half(x, chips, which):
    tokens, width = x.shape
    x = x.reshape(tokens, chips, 2, width // (2 * chips))
    x = lax.dynamic_index_in_dim(x, which, 2, keepdims=False)
    return x.reshape(tokens, width // 2)


def column_gradient(left, right, nf, *earlier):
    core = lax.axis_index("fsdp") % 2
    chips = nf // 2
    theirs = mm_tn(core_half(left, chips, 1 - core), right).astype(bf16)
    got = swap_core(theirs, nf)
    mine = mm_tn(core_half(left, chips, core), right) + got.astype(f32)
    return mine.astype(bf16).reshape(chips, -1, right.shape[1])


def both_cores(w, nf, *earlier):
    core = lax.axis_index("fsdp") % 2
    other = swap_core(after(w, *earlier), nf)
    first = core == 0
    return jnp.concatenate([jnp.where(first, w, other), jnp.where(first, other, w)], axis=0)


def halves(a):
    core = lax.axis_index("fsdp") % 2
    rows = a.shape[0] // 2
    mine = lax.dynamic_slice(a, (core * rows, 0), (rows, a.shape[1]))
    theirs = lax.dynamic_slice(a, ((1 - core) * rows, 0), (rows, a.shape[1]))
    return mine, theirs


def sum_cores(a, nf):
    mine, theirs = halves(a)
    return add16(mine, swap_core(theirs, nf))


def as_rows(a):
    flat = a.reshape(-1)
    return jnp.pad(flat, (0, -flat.shape[0] % 128)).reshape(-1, 128)


def gather_pieces(parts, nf, *earlier):
    a, one, two = parts
    half = a.shape[0] // 2
    low, high = after((one[:half], two[half:]), *earlier)
    return [a, one, two, to_chip(low, nf, 2), to_chip(high, nf, 1)]


def scatter_start(parts, nf, *earlier):
    over_x, over_y = after((parts[0], parts[2]), *earlier)
    return [parts[1], to_chip(over_x, nf, 1), parts[3], to_chip(over_y, nf, 2)]


def scatter_middle(parts, nf, *earlier):
    stay_x, got_x, stay_y, got_y = after(parts, *earlier)
    size = stay_x.shape[0] // 2
    over_y = to_chip(stay_x[size:] + got_x[size:], nf, 2)
    over_x = to_chip(stay_y[size:] + got_y[size:], nf, 1)
    return [stay_x[:size], got_x[:size], over_y, stay_y[:size], got_y[:size], over_x]


def scatter_end(parts):
    parts = [p.astype(f32) for p in parts]
    return jnp.concatenate([sum(parts[:3]), sum(parts[3:])], axis=1)


def local_fast(
    tokens,
    cotangent,
    lengths,
    slot_owner,
    gain_in,
    w_proj,
    w_decay,
    conv_weight,
    a_log,
    dt_bias,
    o_gain,
    w_out,
    gain_mid,
    w_gate_up,
    w_down,
    *,
    nf,
    nz,
):
    chips = nf // 2
    hl = H // chips
    pair = 2
    groups = hl // pair
    me = lax.axis_index("fsdp")
    rep = lax.axis_index("rep")
    ids = jnp.stack([me // 2, me % 2, rep, me]).astype(jnp.int32)
    shard = gain_in.shape[0]
    conv_shard = conv_weight.shape[1]
    hv = w_out.shape[0] * nf
    hk = (conv_shard * nf - hv) // 2
    ff = w_down.shape[0] * nf
    wide = ff // chips
    qk, vv = pair * DK, pair * DV
    span = 2 * qk + 2 * vv
    proj_widths = (hk, hk, hv, hv)

    def proj_table(p):
        table = []
        for c in range(chips):
            at = c * groups + p
            table.append(
                [
                    (at * qk, qk),
                    (hk + at * qk, qk),
                    (2 * hk + at * vv, vv),
                    (2 * hk + hv + at * vv, vv),
                ]
            )
        return table

    up_table = [
        [(s * ff + c * wide + at, 128) for at in range(0, wide, 128) for s in range(2)]
        for c in range(chips)
    ]
    plane = shard // nz

    vectors = [v.reshape(1, -1) for v in (gain_in, gain_mid, o_gain, a_log, dt_bias)]
    sizes = [v.shape[1] for v in vectors]
    small = lax.all_to_all(pack_small(conv_weight, vectors, nf), "fsdp", 0, 0, tiled=True)
    decay_pad = jnp.pad(w_decay, ((0, 0), (0, 128 - 2 * H)))
    plane_rows = pack_relative(w_proj, decay_pad, proj_table(0), True, ids)
    packed = pack_relative(w_proj, None, proj_table(1), False, ids)

    def spread(own, *earlier):
        sends = after(own[1:], *earlier)
        return [own[0]] + [to_chip(a, nf, j + 1) for j, a in enumerate(sends)]

    def swap_all(own, *earlier):
        return [swap_core(a, nf) for a in after(own, *earlier)]

    out_other = swap_core(w_out, nf)
    down_other = swap_core(w_down, nf)
    first = jnp.stack(after(spread(plane_rows), packed))
    tok = gather_first(tokens, nf, small, first)
    first = lax.all_gather(first, "rep", axis=0)
    gains, head_rows, gain_row, *conv_pair = unpack_small(small, sizes, ids, hk, qk, vv, groups)
    tok = gather_pieces(tok, nf, gains, out_other, down_other)
    own = spread(packed, tok)

    held = jnp.sum(jnp.where(slot_owner == rep * nf + me, lengths, 0))
    live_own = (jnp.arange(TOK_DEV, dtype=jnp.int32) < held).astype(f32)[:, None]
    tokens32 = tokens.astype(f32)
    seeded = cotangent.astype(f32) * live_own
    d_ffn_own = seeded.astype(bf16)
    up_plane = pack_columns(after(w_gate_up, packed), None, up_table, plane, True, ids)

    normed_in = norm_rows(after(tok, up_plane, d_ffn_own), gains)
    first_other = swap_core(after(first, tok), nf)
    projected = [project_planes(normed_in, first, first_other, ids)]
    up_plane = exchange(after(up_plane, own, projected[0]), nf)
    ffn_parts = gather_first(d_ffn_own, nf, own, projected[0])

    def forward(p, *before):
        return mixer_forward(
            ids, after(projected[p], *before), projected[0], conv_pair[p], head_rows, gain_row,
            hl, pair, p,
        )

    gated0, *saved0 = forward(0, own)
    other = swap_all(own, projected[0])
    up_own = lax.all_gather(after(up_plane, gated0), "rep", axis=0)
    projected.append(project(after(normed_in, gated0), own, other, ids))
    ffn_parts = gather_pieces(ffn_parts, nf, projected[1])
    gated1, *saved1 = forward(1, ffn_parts[:3])
    gated = [gated0, gated1]
    saved = [saved0, saved1]
    branch_parts = scatter_start(
        times_rows(after(gated, ffn_parts), w_out, out_other, ids), nf
    )
    d_ffn = jnp.concatenate(after(ffn_parts, branch_parts[0]), axis=0)
    pieces_in = [
        (first, first_other),
        (jnp.stack(after(own, branch_parts[0]))[None], jnp.stack(after(other, branch_parts[0]))[None]),
    ]
    down_chip = join_cores(w_down, after(down_other, branch_parts[0]), ids)
    out_chip = join_cores(w_out, after(out_other, branch_parts[0]), ids)
    branch_parts = scatter_middle(branch_parts, nf, d_ffn, pieces_in[1], down_chip)
    branch = scatter_end(branch_parts)
    up_own = after(up_own, branch_parts)
    up_other = swap_core(up_own, nf)
    in_other = swap_core(after(normed_in, up_other), nf)

    middle = tokens32 + live_own * branch
    r_mid = scale_of(middle)
    normed_own = (middle * r_mid * gains[1]).astype(bf16)
    normed_mid = gather_first(normed_own, nf)
    normed_mid = jnp.concatenate(gather_pieces(normed_mid, nf), axis=0)
    hidden, d_gate_up = feed_forward(normed_mid, up_own, up_other, down_chip, d_ffn, ids)

    line = Line(nz)
    done = {}

    def step(new, *earlier):
        got = line.step(new, *earlier)
        if got is not None:
            done[got[0]] = got[1]

    d_up_other = swap_core(d_gate_up, nf)
    mid_other = swap_core(normed_mid, nf)
    mine, theirs = row_terms([hidden], after(d_ffn, mid_other), ids)
    theirs = swap_core(theirs, nf)
    half = mine.shape[0] // 2
    down0 = mine[:half] + theirs[:half]
    down1 = mine[half:] + theirs[half:]
    step(("down0", down0), down1)
    z = line.tokens
    partial_mid = times_transposed(
        [(after(d_gate_up, down0, down1, d_up_other), up_own, up_other)], ids, False
    )
    mid_parts = scatter_start(partial_mid, nf)
    partial_ffn = times_rows(after([hidden], partial_mid, z), w_down, down_other, ids)
    step(("down1", down1), partial_mid)
    mid_first = mid_parts
    mid_parts = scatter_middle(mid_parts, nf, partial_ffn)
    grad_up = column_terms(
        [normed_mid, mid_other],
        [after(d_gate_up, partial_ffn, mid_first[1], mid_first[3]), d_up_other],
        ids,
    )
    z = line.tokens
    step(("up0", grad_up[0]))
    d_normed_mid = scatter_end(after(mid_parts, grad_up, z))
    z = line.tokens
    d_mid, g_gain_mid = rms_back(middle, r_mid, gains[1], d_normed_mid)
    d_middle = seeded + d_mid
    d_branch_own = (live_own * d_middle).astype(bf16)
    branch_parts = gather_first(d_branch_own, nf)
    ffn_first = scatter_start(partial_ffn, nf, mid_parts, grad_up)
    d_branch = gather_pieces(branch_parts, nf, z, ffn_first)
    step(("up1", grad_up[1]))
    z = line.tokens
    ffn_sends = scatter_middle(ffn_first, nf, d_branch)
    d_branch = jnp.concatenate(d_branch, axis=0)
    d_gated = [mm_nt(d_branch, out_chip[p * vv : (p + 1) * vv]) for p in range(groups)]

    def backward(p, *before):
        return mixer_backward(
            ids, projected[p], projected[0], conv_pair[p], head_rows, gain_row, saved[p],
            after(d_gated[p], *before), hl, pair, p,
        )

    step(("up2", grad_up[2]))
    d_x1, d_dec, g_conv1, g_heads1 = backward(1, d_gated, z, ffn_sends)
    z = line.tokens
    d_x1_other = swap_core(after(d_x1, line.tokens), nf)
    step(("up3", grad_up[3]), d_x1)
    mine, theirs = row_terms(gated, after(d_branch, d_x1, z), ids)
    half = mine.shape[0] // 2
    theirs = [swap_core(theirs[:half], nf), swap_core(theirs[half:], nf)]
    cols1 = column_terms([normed_in, in_other], [after(d_x1, mine), d_x1_other], ids)
    z = line.tokens
    grad_out = [after(mine, cols1)[:half] + theirs[0], mine[half:] + theirs[1]]
    cols1_all = exchange(after(cols1, z), nf)
    step(("out0", grad_out[0]), cols1)
    d_x0, dec, g_conv0, g_heads0 = backward(0, cols1, z, grad_out)
    z = line.tokens
    d_x0 = jnp.concatenate([after(d_x0, z, cols1_all), (d_dec + dec).astype(bf16)], axis=1)
    d_x0_other = swap_core(d_x0, nf)
    step(("out1", grad_out[1]), d_x0)
    z = line.tokens
    cols0 = column_terms([normed_in, in_other], [d_x0, d_x0_other], ids)
    queue = [(1, (0, 1)), (1, (2, 3))] + [(0, (c,)) for c in range(chips)]
    grad_cols = [exchange(after(cols0, z), nf), cols1_all]

    def chunk_of(key):
        p, chunk = key
        block = grad_cols[p][chunk[0] : chunk[-1] + 1]
        return (key, block.reshape(len(chunk) * shard, block.shape[2]))

    grad_proj = None

    def place(grad_proj, key, *before):
        return finish_projection(
            grad_proj, after(done[key], *before), ids, key[1], key[0], groups, w_proj.shape,
            proj_widths,
        )

    right = [d_x0, d_x1]
    step(chunk_of(queue[0]), cols0)
    partial_in = times_transposed(
        [(after(right[p], cols0, z),) + pieces_in[p] for p in range(groups)], ids, True
    )
    in_first = scatter_start(partial_in, nf)
    g_conv = [g_conv0, g_conv1]
    g_heads = [g_heads0, g_heads1]
    z = line.tokens
    step(chunk_of(queue[1]), partial_in, grad_cols[0])
    grad_up = None
    for j in range(chips):
        grad_up = place_blocks(
            grad_up, after(done["up%d" % j], z), ids, j, (chips, shard, 2 * wide)
        )
    in_sends = scatter_middle(in_first, nf, grad_up)
    output = (middle + live_own * scatter_end(after(ffn_sends, z))).astype(bf16)
    z = line.tokens
    step(chunk_of(queue[2]))
    d_normed_in = scatter_end(after(in_sends, z))
    d_rows, g_gain_in = rms_back(tokens32, scale_of(tokens32), gains[0], d_normed_in)
    grad_tokens = d_middle + d_rows
    blocks = pack_small_grads(
        g_conv,
        g_heads,
        g_gain_in.reshape(1, -1),
        g_gain_mid.reshape(1, -1),
        sizes,
        ids,
        nf,
        conv_shard,
        hk,
        qk,
        vv,
    )
    small_sum = sum_small(blocks, nf)
    grad_up_all = exchange(after(grad_up, small_sum), nf)
    z = line.tokens
    step(chunk_of(queue[3]), grad_tokens)
    grad_proj = place(grad_proj, queue[0], z)
    z = line.tokens
    step(chunk_of(queue[4]), grad_proj)
    grad_proj = place(grad_proj, queue[1], z)
    z = line.tokens
    key, chunk = chunk_of(queue[5])
    small_sum = jnp.pad(
        small_sum.astype(bf16), ((0, 16 - small_sum.shape[0]), (0, chunk.shape[1] - small_sum.shape[1]))
    )
    step((key, jnp.concatenate([chunk, small_sum], axis=0)), grad_proj)
    grad_proj = place(grad_proj, queue[2], z)
    z = line.tokens
    step(None, grad_proj)
    grad_proj = place(grad_proj, queue[3], z)
    z = line.tokens
    step(None, grad_proj)
    grad_up = finish_feed_forward(after(grad_up_all, z))
    for key in queue[4:]:
        grad_proj = place(grad_proj, key)
    summed = [v[shard : shard + 8] for v in done[queue[5]]]
    middle_two = jnp.logical_or(rep == 1, rep == 2)

    def pick(name):
        return jnp.where(middle_two, *done[name])

    summed = jnp.where(middle_two, *summed).astype(f32)
    lanes, _ = small_layout(sizes)
    s_gain_in, s_gain_mid, s_ogain, s_alog, s_bias = (
        summed[KCONV, lane : lane + size] for lane, size in zip(lanes, sizes)
    )
    grad_decay = sum(
        jnp.where(middle_two, *(v[:shard, span : span + 2 * H] for v in done[(0, (c,))])).astype(f32)
        for c in range(chips)
    )
    grad_down = jnp.concatenate([pick("down0"), pick("down1")], axis=0).astype(f32)
    grad_out = jnp.concatenate([pick("out0"), pick("out1")], axis=0).astype(f32)
    return (
        output,
        grad_tokens,
        s_gain_in,
        grad_proj,
        grad_decay,
        summed[:KCONV, :conv_shard],
        s_alog,
        s_bias,
        s_ogain,
        grad_out,
        s_gain_mid,
        grad_up,
        grad_down,
    )


def local_general(
    tokens,
    cotangent,
    lengths,
    slot_owner,
    gain_in,
    w_proj,
    w_decay,
    conv_weight,
    a_log,
    dt_bias,
    o_gain,
    w_out,
    gain_mid,
    w_gate_up,
    w_down,
    *,
    nf,
    nz,
):
    chips = nf // 2
    hl = H // chips
    pair = 2 if hl % 2 == 0 else 1
    groups = hl // pair
    me = lax.axis_index("fsdp")
    rep = lax.axis_index("rep")
    chip, core = me // 2, me % 2
    ids = jnp.stack([chip, core, rep, rep]).astype(jnp.int32)
    d_model = tokens.shape[1]
    shard = gain_in.shape[0]
    conv_shard = conv_weight.shape[1]
    channels = conv_shard * nf
    hv = w_out.shape[0] * nf
    hk = (channels - hv) // 2
    ff = w_down.shape[0] * nf
    wide = ff // chips
    qk, vv = pair * DK, pair * DV
    span = 2 * qk + 2 * vv
    proj_widths = (hk, hk, hv, hv)
    up_widths = (ff, ff)

    def proj_blocks(w, dec, p):
        blocks = column_blocks(w, proj_widths, chips, groups, p)
        if p:
            return blocks
        extra = jnp.pad(dec, ((0, 0), (0, 128 - 2 * H)))
        extra = jnp.broadcast_to(extra, (chips,) + extra.shape)
        return jnp.concatenate([blocks, extra], axis=2)

    def plane_rows(w):
        rows = w.shape[0] // nz
        return lax.dynamic_slice(w, (rep * rows, 0), (rows, w.shape[1]))

    def over_planes(blocks):
        got = lax.all_gather(blocks, "rep", axis=0)
        return got.transpose(1, 0, 2, 3).reshape(chips, -1, blocks.shape[2])

    pieces = [conv_weight, gain_in, gain_mid, o_gain, a_log, dt_bias]
    rows = [as_rows(p) for p in pieces]
    counts = [r.shape[0] for r in rows]
    packed = jnp.concatenate(rows, axis=0)
    packed = jnp.pad(packed, ((0, -packed.shape[0] % 16), (0, 0)))

    plane_proj = plane_rows(w_proj)
    rest = [exchange(proj_blocks(plane_proj, None, p), nf) for p in range(1, groups)]
    first = exchange(proj_blocks(w_proj, w_decay, 0), nf)
    tok = gather_first(tokens, nf)
    small = gather_small(packed, nf)
    tokens_all = gather_second(tok, nf)
    rest = [over_planes(r) for r in rest]
    up_plane = exchange(
        after(column_blocks(plane_rows(w_gate_up), up_widths, chips, 1, 0), first), nf
    )
    up_own = over_planes(after(up_plane, *rest))

    device = rep * nf + me
    held = jnp.sum(jnp.where(slot_owner == device, lengths, 0))
    live_own = (jnp.arange(TOK_DEV, dtype=jnp.int32) < held).astype(f32)[:, None]

    small = small.astype(f32)
    split = []
    at = 0
    for p, count in zip(pieces, counts):
        split.append(
            small[:, at : at + count].reshape(nf, count * 128)[:, : p.size].reshape((nf,) + p.shape)
        )
        at += count
    conv_full = split[0].transpose(1, 0, 2).reshape(KCONV, channels)
    gain_in_full, gain_mid_full, ogain_full, alog_full, bias_full = (
        s.reshape(-1) for s in split[1:]
    )
    conv_pair = []
    for p in range(groups):
        blocks = column_blocks(conv_full, proj_widths[:3], chips, groups, p)
        mine = lax.dynamic_index_in_dim(blocks, chip, 0, keepdims=False)
        conv_pair.append(jnp.pad(mine, ((0, 8 - KCONV), (0, 0))))
    head_rows = jnp.stack([alog_full, bias_full])
    head_rows = jnp.pad(head_rows, ((0, 6), (0, 128 - H)))
    gain_row = jnp.pad(ogain_full[None, :], ((0, 7), (0, 0)))

    rows_in = tokens_all.astype(f32)
    normed_in = (rows_in * scale_of(rows_in) * gain_in_full).astype(bf16)
    seeded = cotangent.astype(f32) * live_own
    weight_in = [both_core_rows(first, nf)]
    out_chip = both_cores(w_out, nf, weight_in[0])
    down_chip = both_cores(w_down, nf, weight_in[0])
    weight_in += [both_core_rows(r, nf) for r in rest]
    ffn_parts = gather_first(seeded.astype(bf16), nf, up_plane)
    d_ffn = gather_second(ffn_parts, nf)
    projected = []
    gated = []
    saved = []
    for p in range(groups):
        projected.append(mm(normed_in, weight_in[p]))
        got = mixer_forward(
            ids, projected[p], projected[0], conv_pair[p], head_rows, gain_row, hl, pair, p
        )
        gated.append(got[0])
        saved.append(got[1:])
    gated = jnp.concatenate(gated, axis=1)
    branch_parts = scatter_first(mm(gated, out_chip).astype(bf16), nf, d_ffn)
    d_hidden = mm_nt(after(d_ffn, gated), down_chip)
    up_chip = both_core_rows(after(up_own, gated), nf)
    branch = scatter_second(branch_parts, nf)

    tokens32 = tokens.astype(f32)
    middle = tokens32 + live_own * branch
    r_mid = scale_of(middle)
    normed_own = (middle * r_mid * gain_mid_full).astype(bf16)
    normed_mid = gather_second(gather_first(normed_own, nf), nf)
    gate_up = mm(normed_mid, up_chip)
    gate, up = gate_up[:, :wide], gate_up[:, wide:]
    sig = jax.nn.sigmoid(gate)
    act = gate * sig
    hidden = (act * up).astype(bf16)
    d_gate_up = jnp.concatenate(
        [d_hidden * up * (sig * (1.0 + gate * (1.0 - sig))), d_hidden * act], axis=1
    ).astype(bf16)

    line = Line(nz)
    done = {}

    def step(new, *earlier):
        for item in new or [None]:
            got = line.step(item, *earlier)
            if got is not None:
                done[got[0]] = got[1][0]

    grad_down = sum_cores(mm_tn(hidden, d_ffn).astype(bf16), nf)
    down_parts = jnp.split(grad_down, 2, axis=0)
    step([("down0", down_parts[0])])
    partial_mid = mm_nt(after(d_gate_up, down_parts[0]), up_chip).astype(bf16)
    mid_parts = scatter_first(partial_mid, nf)
    grad_up = column_gradient(normed_mid, after(d_gate_up, partial_mid), nf)
    step([("down1", down_parts[1])], grad_up)
    d_normed_mid = scatter_second(mid_parts, nf)
    d_mid, g_gain_mid = rms_back(middle, r_mid, gain_mid_full, d_normed_mid)
    d_middle = seeded + d_mid
    d_branch_own = (live_own * d_middle).astype(bf16)
    branch_parts = gather_first(d_branch_own, nf)
    partial_ffn = mm(after(hidden, d_branch_own), down_chip).astype(bf16)
    step([("up0", grad_up[0])], partial_ffn)
    d_branch = gather_second(branch_parts, nf)
    step([("up1", grad_up[1])], d_branch)
    d_gated = [mm_nt(d_branch, out_chip[p * vv : (p + 1) * vv]) for p in range(groups)]
    grad_out = sum_cores(mm_tn(gated, d_branch).astype(bf16), nf)
    d_x = [None] * groups
    d_dec = None
    g_conv = [None] * groups
    g_heads = None
    ups = [("up%d" % j, grad_up[j]) for j in range(2, chips)]
    for n, p in enumerate(reversed(range(groups))):
        d_x[p], dec, g_conv[p], heads = mixer_backward(
            ids, projected[p], projected[0], conv_pair[p], head_rows, gain_row, saved[p],
            d_gated[p], hl, pair, p,
        )
        d_dec = dec if d_dec is None else d_dec + dec
        g_heads = heads if g_heads is None else g_heads + heads
        step(ups[n : n + 1] if n + 1 < groups else ups[n:], d_x[p])
        if p:
            d_gated[p - 1] = after(d_gated[p - 1], d_x[p])
    d_dec = d_dec.astype(bf16)
    right = [jnp.concatenate([d_x[0], d_dec], axis=1)] + d_x[1:]
    grad_cols = [None] * groups
    for p in reversed(range(groups)):
        grad_cols[p] = exchange(column_gradient(normed_in, right[p], nf), nf)
    ffn_parts = scatter_first(partial_ffn, nf, grad_cols[0])
    step([("out", grad_out)], right[0])
    partial_in = mm_nt(right[0], weight_in[0])
    for p in range(1, groups):
        partial_in = partial_in + mm_nt(right[p], weight_in[p])
    partial_in = partial_in.astype(bf16)
    queue = []
    for p in reversed(range(groups)):
        size = 1 if p == 0 else 2
        for c in range(0, chips, size):
            queue.append(((p, c), grad_cols[p][c : c + size]))
    for n, item in enumerate(queue):
        if n == 1:
            ffn_branch = scatter_second(ffn_parts, nf, line.tokens)
            output = (middle + live_own * ffn_branch).astype(bf16)
            in_parts = scatter_first(partial_in, nf, ffn_branch)
        if n == 2:
            d_normed_in = scatter_second(in_parts, nf, line.tokens)
            d_rows, g_gain_in = rms_back(tokens32, scale_of(tokens32), gain_in_full, d_normed_in)
            grad_tokens = d_middle + d_rows
            ups = jnp.stack([done["up%d" % j] for j in range(chips)])
            grad_up = exchange(after(ups, d_normed_in), nf)
        step([item])

    g_conv = [g[:KCONV] for g in g_conv]
    blocks = jnp.concatenate(
        [g[:, a:b] for a, b in ((0, qk), (qk, 2 * qk), (2 * qk, 2 * qk + vv)) for g in g_conv],
        axis=1,
    )
    conv_grad = jnp.zeros((KCONV, chips, channels // chips), f32)
    conv_grad = lax.dynamic_update_slice(conv_grad, blocks[:, None], (0, chip, 0))
    conv_grad = jnp.concatenate(from_column_blocks(conv_grad.transpose(1, 0, 2), proj_widths[:3]), axis=1)
    heads_grad = g_heads[1:3, :H]
    parts = [
        conv_grad.reshape(KCONV, nf, conv_shard).transpose(1, 0, 2),
        g_gain_in.reshape(nf, shard),
        g_gain_mid.reshape(nf, shard),
        g_heads[0].reshape(nf, -1),
        heads_grad[0].reshape(nf, -1),
        heads_grad[1].reshape(nf, -1),
    ]
    flat = []
    for part in parts:
        part = part.reshape(nf, -1)
        flat.append(jnp.pad(part, ((0, 0), (0, -part.shape[1] % 128))))
    flat = jnp.concatenate(flat, axis=1)
    summed = lax.psum(sum_small(flat.reshape(nf, -1, 128), nf), "rep").reshape(-1)
    grads = []
    at = 0
    for p in pieces:
        grads.append(summed[at : at + p.size].reshape(p.shape))
        at += p.size + (-p.size % 128)
    s_conv, s_gain_in, s_gain_mid, s_ogain, s_alog, s_bias = grads

    step([])
    step([])
    grad_up = jnp.concatenate(from_column_blocks(grad_up, up_widths), axis=1).astype(f32)
    wholes = []
    for p in range(groups):
        size = 1 if p == 0 else 2
        wholes.append(jnp.concatenate([done[(p, c)] for c in range(0, chips, size)], axis=0))
    parts = []
    at = 0
    for width in (qk, qk, vv, vv):
        part = jnp.stack([w[:, :, at : at + width] for w in wholes], axis=1)
        parts.append(part.transpose(2, 0, 1, 3).reshape(shard, -1))
        at += width
    grad_proj = jnp.concatenate(parts, axis=1).astype(f32)
    grad_decay = jnp.sum(wholes[0][:, :, span : span + 2 * H].astype(f32), axis=0)
    grad_down = jnp.concatenate([done["down0"], done["down1"]], axis=0).astype(f32)
    grad_out = done["out"].astype(f32)
    return (
        output,
        grad_tokens,
        s_gain_in,
        grad_proj,
        grad_decay,
        s_conv,
        s_alog,
        s_bias,
        s_ogain,
        grad_out,
        s_gain_mid,
        grad_up,
        grad_down,
    )


def solution(mesh):
    rows = P(("rep", "fsdp"), None)
    one = P("fsdp")
    two = P("fsdp", None)
    columns = P(None, "fsdp")
    in_specs = (rows, rows, P(), P(), one, two, two, columns, one, one, one, two, one, two, two)
    out_specs = (rows, rows, one, two, two, columns, one, one, one, two, one, two, two)
    nf, nz = mesh.shape["fsdp"], mesh.shape["rep"]
    body = partial(local_fast if (nf, nz) == (8, 4) else local_general, nf=nf, nz=nz)
    return jax.shard_map(body, mesh=mesh, in_specs=in_specs, out_specs=out_specs, check_vma=False)
```

```python
from functools import partial

import jax
import jax.numpy as jnp
from jax import lax
from jax.experimental import pallas as pl
from jax.experimental.pallas import tpu as pltpu
from jax.sharding import PartitionSpec as P

H = 16
DK = 128
DV = 256
KCONV = 4
BLOCK = 64
TOK_DEV = 256
eps_norm = 1e-05
eps_unit = 1e-06
bf16 = jnp.bfloat16
f32 = jnp.float32


def mm(a, b):
    return lax.dot_general(
        a.astype(bf16), b.astype(bf16), (((1,), (0,)), ((), ())), preferred_element_type=f32
    )


def mm_nt(a, b):
    return lax.dot_general(
        a.astype(bf16), b.astype(bf16), (((1,), (1,)), ((), ())), preferred_element_type=f32
    )


def mm_tn(a, b):
    return lax.dot_general(
        a.astype(bf16), b.astype(bf16), (((0,), (0,)), ((), ())), preferred_element_type=f32
    )


def mm_exact(a, b):
    return lax.dot_general(
        a, b, (((1,), (0,)), ((), ())), precision=lax.Precision.HIGHEST, preferred_element_type=f32
    )


def silu(v):
    return v * jax.nn.sigmoid(v)


def shifted_down(x, s):
    if s == 0:
        return x
    row = lax.broadcasted_iota(jnp.int32, x.shape, 0)
    return jnp.where(row >= s, pltpu.roll(x, s, 0), 0.0)


def shifted_up(x, s):
    if s == 0:
        return x
    n = x.shape[0]
    row = lax.broadcasted_iota(jnp.int32, x.shape, 0)
    return jnp.where(row < n - s, pltpu.roll(x, n - s, 0), 0.0)


def conv_forward(mixed, weight):
    out = weight[KCONV - 1 : KCONV, :] * mixed
    for s in range(1, KCONV):
        out = out + weight[KCONV - 1 - s : KCONV - s, :] * shifted_down(mixed, s)
    return out


def conv_backward(d_conv, mixed, weight):
    d_mixed = weight[KCONV - 1 : KCONV, :] * d_conv
    rows = [None] * KCONV
    rows[KCONV - 1] = jnp.sum(d_conv * mixed, axis=0, keepdims=True)
    for s in range(1, KCONV):
        up = shifted_up(d_conv, s)
        d_mixed = d_mixed + weight[KCONV - 1 - s : KCONV - s, :] * up
        rows[KCONV - 1 - s] = jnp.sum(up * mixed, axis=0, keepdims=True)
    return d_mixed, jnp.concatenate(rows, axis=0)


def block_masks(n):
    i = lax.broadcasted_iota(jnp.int32, (n, n), 0)
    j = lax.broadcasted_iota(jnp.int32, (n, n), 1)
    x = i ^ j
    same = x < BLOCK
    return x, i > j, jnp.logical_and(same, i >= j), jnp.logical_and(same, i > j), same


def decay_parts(dec, alog_row, bias_row):
    pre = dec + bias_row
    softplus = jnp.maximum(pre, 0.0) + jnp.log1p(jnp.exp(-jnp.abs(pre)))
    log_decay = -jnp.exp(alog_row) * softplus
    n = dec.shape[0]
    i = lax.broadcasted_iota(jnp.int32, (n, n), 0)
    j = lax.broadcasted_iota(jnp.int32, (n, n), 1)
    same = (i ^ j) < BLOCK
    lower = jnp.where(jnp.logical_and(same, i >= j), 1.0, 0.0)
    whole = jnp.where(same, 1.0, 0.0)
    running = mm_exact(lower, log_decay)
    total = mm_exact(whole, log_decay)
    return pre, log_decay, running, total


def lane_of(x, h):
    lane = lax.broadcasted_iota(jnp.int32, x.shape, 1)
    return jnp.sum(jnp.where(lane == h, x, 0.0), axis=1, keepdims=True)


def row_of(x, h):
    row = lax.broadcasted_iota(jnp.int32, x.shape, 0)
    return jnp.sum(jnp.where(row == h, x, 0.0), axis=0, keepdims=True)


def unit_rows(a, scale):
    r = lax.rsqrt(jnp.sum(a * a, axis=1, keepdims=True) + eps_unit)
    return a * r * scale, r


def inverse_blocks(lowers, x, below):
    eye = jnp.where(x == 0, 1.0, 0.0)
    inv = [eye - jnp.where(x == 1, low, 0.0) for low in lowers]
    level = 1
    while (2 << level) <= BLOCK:
        pick = lax.shift_right_logical(x, level) == 1
        half = [mm(jnp.where(pick, low, 0.0), t) for low, t in zip(lowers, inv)]
        inv = [t - mm(t, u) for t, u in zip(inv, half)]
        level += 1
    return inv


def forward_kernel(
    hl,
    pair,
    p,
    ids_ref,
    x_ref,
    dec_ref,
    conv_ref,
    head_ref,
    gain_ref,
    gated_ref,
    o_ref,
    u_ref,
    w_ref,
    inv_ref,
    s_ref,
):
    n = TOK_DEV
    qk, vv = pair * DK, pair * DV
    blocks = n // BLOCK
    x, below, on_below, strict, same = block_masks(n)
    dec = dec_ref[...]
    pre, log_decay, running, total = decay_parts(dec, head_ref[0:1, :], head_ref[1:2, :])
    running_t = running.T
    heads = range(pair)
    q = silu(conv_forward(x_ref[:, :qk], conv_ref[:, :qk]))
    k = silu(conv_forward(x_ref[:, qk : 2 * qk], conv_ref[:, qk : 2 * qk]))
    v = silu(conv_forward(x_ref[:, 2 * qk : 2 * qk + vv], conv_ref[:, 2 * qk :])).astype(bf16)
    qn, kn, vn, beta, b, tot, fade, low, score = [], [], [], [], [], [], [], [], []
    for i in heads:
        h = ids_ref[0] * hl + p * pair + i
        qn.append(unit_rows(q[:, i * DK : (i + 1) * DK], DK**-0.5)[0].astype(bf16))
        kn.append(unit_rows(k[:, i * DK : (i + 1) * DK], 1.0)[0].astype(bf16))
        vn.append(v[:, i * DV : (i + 1) * DV])
        beta.append(jax.nn.sigmoid(lane_of(dec, H + h)))
        b.append(lane_of(running, h))
        tot.append(lane_of(total, h))
        d = jnp.where(on_below, jnp.exp(jnp.where(on_below, b[i] - row_of(running_t, h), 0.0)), 0.0)
        both = mm_nt(jnp.concatenate([kn[i], qn[i]], axis=0), kn[i])
        low.append(jnp.where(strict, beta[i] * d * both[:n], 0.0))
        score.append((both[n:] * d).astype(bf16))
    inv = inverse_blocks(low, x, below)
    e = [jnp.exp(b[i]) for i in heads]
    fin = [jnp.exp(tot[i] - b[i]) for i in heads]
    grow = [jnp.exp(tot[i]) for i in heads]
    inv = [t.astype(bf16) for t in inv]
    right = [
        jnp.concatenate(
            [beta[i] * vn[i].astype(f32), (beta[i] * e[i]) * kn[i].astype(f32)], axis=1
        ).astype(bf16)
        for i in heads
    ]
    uw = [mm(inv[i], right[i]) for i in heads]
    w = [uw[i][:, DV:].astype(bf16) for i in heads]
    state = [jnp.zeros((DK, DV), f32) for i in heads]
    u_parts = [[] for i in heads]
    o_parts = [[] for i in heads]
    for c in range(blocks):
        lo, hi = c * BLOCK, (c + 1) * BLOCK
        for i in heads:
            sb = state[i].astype(bf16)
            s_ref[0, i, c * DK : (c + 1) * DK, :] = sb
            got = mm(jnp.concatenate([w[i][lo:hi], qn[i][lo:hi]], axis=0), sb)
            u = uw[i][lo:hi, :DV] - got[:BLOCK]
            u_parts[i].append(u)
            o_parts[i].append(e[i][lo:hi] * got[BLOCK:])
            if c < blocks - 1:
                state[i] = grow[i][lo : lo + 1] * state[i] + mm_tn(
                    kn[i][lo:hi], fin[i][lo:hi] * u
                )
    gain = gain_ref[0:1, :]
    for i in heads:
        u = jnp.concatenate(u_parts[i], axis=0).astype(bf16)
        out = jnp.concatenate(o_parts[i], axis=0) + mm(score[i], u)
        cols = slice(i * DV, (i + 1) * DV)
        o_ref[:, cols] = out
        u_ref[:, cols] = u
        w_ref[:, i * DK : (i + 1) * DK] = w[i]
        inv_ref[0, i] = inv[i]
        r = lax.rsqrt(jnp.mean(out * out, axis=1, keepdims=True) + eps_norm)
        gated_ref[:, cols] = (out * r * gain * silu(x_ref[:, 2 * qk + vv + i * DV : 2 * qk + vv + (i + 1) * DV])).astype(bf16)


def mixer_forward(ids, proj, dec, conv, head_rows, gain_row, hl, pair, p):
    tokens = proj.shape[0]
    slots = tokens // TOK_DEV
    qk = pair * DK
    vv = pair * DV
    spec = pl.BlockSpec
    n = TOK_DEV

    def body(*refs):
        forward_kernel(hl, pair, p, *refs)

    return pl.pallas_call(
        body,
        grid=(slots,),
        in_specs=[
            pl.BlockSpec(memory_space=pltpu.SMEM),
            spec((n, 2 * qk + 2 * vv), lambda s: (s, 0)),
            spec((n, 128), lambda s: (s, dec.shape[1] // 128 - 1)),
            spec((8, 2 * qk + vv), lambda s: (0, 0)),
            spec((8, 128), lambda s: (0, 0)),
            spec((8, DV), lambda s: (0, 0)),
        ],
        out_specs=[
            spec((n, vv), lambda s: (s, 0)),
            spec((n, vv), lambda s: (s, 0)),
            spec((n, vv), lambda s: (s, 0)),
            spec((n, qk), lambda s: (s, 0)),
            spec((1, pair, n, n), lambda s: (s, 0, 0, 0)),
            spec((1, pair, n // BLOCK * DK, DV), lambda s: (s, 0, 0, 0)),
        ],
        out_shape=[
            jax.ShapeDtypeStruct((tokens, vv), bf16),
            jax.ShapeDtypeStruct((tokens, vv), f32),
            jax.ShapeDtypeStruct((tokens, vv), bf16),
            jax.ShapeDtypeStruct((tokens, qk), bf16),
            jax.ShapeDtypeStruct((slots, pair, n, n), bf16),
            jax.ShapeDtypeStruct((slots, pair, n // BLOCK * DK, DV), bf16),
        ],
        compiler_params=pltpu.CompilerParams(vmem_limit_bytes=56 * 1024 * 1024),
        cost_estimate=pl.CostEstimate(flops=1, bytes_accessed=1, transcendentals=0),
        name="mixer_forward",
    )(ids, proj, dec, conv, head_rows, gain_row)


def backward_kernel(
    hl,
    pair,
    p,
    ids_ref,
    x_ref,
    dec_ref,
    conv_ref,
    head_ref,
    gain_ref,
    o_ref,
    u_ref,
    w_ref,
    inv_ref,
    s_ref,
    dy_ref,
    *refs,
):
    more_ref = refs[0] if len(refs) == 5 else None
    dx_out, ddec_out, conv_out, small_out = refs[-4:]
    slot = pl.program_id(0)
    n = TOK_DEV
    qk, vv = pair * DK, pair * DV
    q_at = slice(0, qk)
    k_at = slice(qk, 2 * qk)
    v_at = slice(2 * qk, 2 * qk + vv)
    blocks = n // BLOCK
    x, below, on_below, strict, same = block_masks(n)
    dec = dec_ref[...]
    alog_row = head_ref[0:1, :]
    pre, log_decay, running, total = decay_parts(dec, alog_row, head_ref[1:2, :])
    running_t = running.T
    heads = range(pair)
    qc = conv_forward(x_ref[:, q_at], conv_ref[:, q_at])
    kc = conv_forward(x_ref[:, k_at], conv_ref[:, k_at])
    vc = conv_forward(x_ref[:, v_at], conv_ref[:, v_at])
    q_sig = jax.nn.sigmoid(qc)
    k_sig = jax.nn.sigmoid(kc)
    v_sig = jax.nn.sigmoid(vc)
    q = qc * q_sig
    k = kc * k_sig
    v = (vc * v_sig).astype(bf16)
    gain = gain_ref[0:1, :]
    qn, kn, vn, qr, kr, beta, b, tot, d, sim, low, score = ([] for _ in range(12))
    d_out, u = [], []
    gain_rows = jnp.zeros((1, DV), f32)
    for i in heads:
        h = ids_ref[0] * hl + p * pair + i
        cols = slice(i * DV, (i + 1) * DV)
        kcols = slice(i * DK, (i + 1) * DK)
        rows_q, r_q = unit_rows(q[:, kcols], DK**-0.5)
        rows_k, r_k = unit_rows(k[:, kcols], 1.0)
        qr.append((rows_q, r_q))
        kr.append((rows_k, r_k))
        qn.append(rows_q.astype(bf16))
        kn.append(rows_k.astype(bf16))
        vn.append(v[:, cols])
        beta.append(jax.nn.sigmoid(lane_of(dec, H + h)))
        b.append(lane_of(running, h))
        tot.append(lane_of(total, h))
        d.append(
            jnp.where(on_below, jnp.exp(jnp.where(on_below, b[i] - row_of(running_t, h), 0.0)), 0.0)
        )
        both = mm_nt(jnp.concatenate([kn[i], qn[i]], axis=0), kn[i])
        sim.append(jnp.where(strict, d[i] * both[:n], 0.0))
        score.append(both[n:] * d[i])
        out = o_ref[:, cols]
        g_at = slice(2 * qk + vv + i * DV, 2 * qk + vv + (i + 1) * DV)
        gate = x_ref[:, g_at]
        dy = dy_ref[:, cols].astype(f32)
        r = lax.rsqrt(jnp.mean(out * out, axis=1, keepdims=True) + eps_norm)
        normed = out * r
        g_sig = jax.nn.sigmoid(gate)
        act = gate * g_sig
        d_act = dy * normed * gain
        dx_out[:, g_at] = (d_act * (g_sig * (1.0 + gate * (1.0 - g_sig)))).astype(bf16)
        gain_rows = gain_rows + jnp.sum(dy * normed * act, axis=0, keepdims=True)
        d_normed = dy * gain * act
        d_out.append(r * (d_normed - normed * jnp.mean(d_normed * normed, axis=1, keepdims=True)))
        u.append(u_ref[:, cols])
    e = [jnp.exp(b[i]) for i in heads]
    fin = [jnp.exp(tot[i] - b[i]) for i in heads]
    grow = [jnp.exp(tot[i]) for i in heads]
    d_out16 = [d_out[i].astype(bf16) for i in heads]
    score16 = [score[i].astype(bf16) for i in heads]
    d_u0 = [mm_tn(score16[i], d_out16[i]) for i in heads]
    d_state = [jnp.zeros((DK, DV), f32) for i in heads]
    d_u = [[None] * blocks for i in heads]
    dq_s = [[None] * blocks for i in heads]
    dk_s = [[None] * blocks for i in heads]
    fin_col = [[None] * blocks for i in heads]
    grow_col = [[None] * blocks for i in heads]
    e_out = [(e[i] * d_out[i]).astype(bf16) for i in heads]
    for c in reversed(range(blocks)):
        lo, hi = c * BLOCK, (c + 1) * BLOCK
        for i in heads:
            ds16 = d_state[i].astype(bf16)
            s16 = s_ref[0, i, c * DK : (c + 1) * DK, :]
            u_c = u[i][lo:hi].astype(f32)
            if c == blocks - 1:
                d_u[i][c] = d_u0[i][lo:hi]
                fin_col[i][c] = jnp.zeros((BLOCK, 1), f32)
                grow_col[i][c] = jnp.zeros((1, 1), f32)
                dk_s[i][c] = jnp.zeros((BLOCK, DK), f32)
            else:
                k_ds = mm(kn[i][lo:hi], ds16)
                add = fin[i][lo:hi] * k_ds
                d_u[i][c] = d_u0[i][lo:hi] + add
                fin_col[i][c] = jnp.sum(add * u_c, axis=1, keepdims=True)
                grow_col[i][c] = grow[i][lo : lo + 1] * jnp.sum(
                    jnp.sum(d_state[i] * s16.astype(f32), axis=1, keepdims=True),
                    axis=0,
                    keepdims=True,
                )
                dk_s[i][c] = mm_nt(fin[i][lo:hi] * u_c, ds16)
            if c > 0:
                step = mm_tn(
                    jnp.concatenate([qn[i][lo:hi], w_ref[lo:hi, i * DK : (i + 1) * DK]], axis=0),
                    jnp.concatenate([e_out[i][lo:hi], (-d_u[i][c]).astype(bf16)], axis=0),
                )
                d_state[i] = grow[i][lo : lo + 1] * d_state[i] + step
    lane = lax.broadcasted_iota(jnp.int32, (n, 128), 1)
    d_dec = jnp.zeros((n, 128), f32)
    d_log = jnp.zeros((n, 128), f32)
    dq_all, dk_all, dv_all = [], [], []
    ones = jnp.ones((n, 128), bf16)
    upper_i = lax.broadcasted_iota(jnp.int32, (n, n), 0)
    upper_j = lax.broadcasted_iota(jnp.int32, (n, n), 1)
    upper = jnp.where(jnp.logical_and((upper_i ^ upper_j) < BLOCK, upper_i <= upper_j), 1.0, 0.0)
    for i in heads:
        h = ids_ref[0] * hl + p * pair + i
        du = jnp.concatenate(d_u[i], axis=0)
        d_right = mm_tn(inv_ref[0, i], du)
        dr16 = d_right.astype(bf16)
        outer = mm_nt(jnp.concatenate([d_out16[i], dr16], axis=0), u[i])
        d_score = jnp.where(on_below, outer[:n], 0.0)
        d_low = jnp.where(strict, -outer[n:], 0.0)
        z16 = (-(beta[i] * e[i]) * d_right).astype(bf16)
        recalled = []
        for c in range(blocks):
            lo, hi = c * BLOCK, (c + 1) * BLOCK
            s16 = s_ref[0, i, c * DK : (c + 1) * DK, :]
            if c == 0:
                dq_s[i][c] = jnp.zeros((BLOCK, DK), f32)
                recalled.append(jnp.zeros((BLOCK, 2 * DV), f32))
                continue
            back = mm_nt(jnp.concatenate([e_out[i][lo:hi], z16[lo:hi]], axis=0), s16)
            dq_s[i][c] = back[:BLOCK]
            dk_s[i][c] = dk_s[i][c] + back[BLOCK:]
            got = mm(jnp.concatenate([kn[i][lo:hi], qn[i][lo:hi]], axis=0), s16)
            recalled.append(jnp.concatenate([got[:BLOCK], got[BLOCK:]], axis=1))
        recalled = jnp.concatenate(recalled, axis=0)
        k_s = recalled[:, :DV]
        q_s = recalled[:, DV:]
        d_a = (d_score * d[i]).astype(bf16)
        d_g = d_low * beta[i] * d[i]
        d_g16 = (d_g + d_g.T).astype(bf16)
        dq = jnp.concatenate(dq_s[i], axis=0) + mm(d_a, kn[i])
        dk = jnp.concatenate(dk_s[i], axis=0) + mm_tn(d_a, qn[i]) + mm(d_g16, kn[i])
        dv = beta[i] * d_right
        row_sum = jnp.sum(d_low * sim[i], axis=1, keepdims=True)
        keep = vn[i].astype(f32) - e[i] * k_s
        d_beta = row_sum + jnp.sum(d_right * keep, axis=1, keepdims=True)
        moved = (d_score * score[i] + d_low * beta[i] * sim[i]).astype(bf16)
        d_b = mm(moved, ones) - mm_tn(moved, ones)
        d_b_col = e[i] * jnp.sum(
            d_out[i] * q_s - (beta[i] * d_right) * k_s, axis=1, keepdims=True
        )
        fin_all = jnp.concatenate(fin_col[i], axis=0)
        d_b = jnp.where(lane == h, d_b + (d_b_col - fin_all), 0.0)
        tail = jnp.concatenate(
            [
                jnp.broadcast_to(
                    grow_col[i][c] + jnp.sum(fin_col[i][c], axis=0, keepdims=True), (BLOCK, 1)
                )
                for c in range(blocks)
            ],
            axis=0,
        )
        d_log = d_log + mm_exact(upper, d_b) + jnp.where(lane == h, tail, 0.0)
        d_dec = d_dec + jnp.where(lane == H + h, d_beta * beta[i] * (1.0 - beta[i]), 0.0)
        rows_q, r_q = qr[i]
        rows_k, r_k = kr[i]
        unit = rows_q * DK**0.5
        dq = (DK**-0.5) * r_q * (dq - unit * jnp.sum(dq * unit, axis=1, keepdims=True))
        dk = r_k * (dk - rows_k * jnp.sum(dk * rows_k, axis=1, keepdims=True))
        dq_all.append(dq)
        dk_all.append(dk)
        dv_all.append(dv)

    @pl.when(slot == 0)
    def _():
        conv_out[...] = jnp.zeros_like(conv_out)
        small_out[...] = jnp.zeros_like(small_out)

    def through_conv(d_active, conv, sig, at):
        d_conv = d_active * (sig * (1.0 + conv * (1.0 - sig)))
        d_mixed, d_weight = conv_backward(d_conv, x_ref[:, at], conv_ref[:, at])
        dx_out[:, at] = d_mixed.astype(bf16)
        conv_out[0:KCONV, at] += d_weight

    through_conv(jnp.concatenate(dq_all, axis=1), qc, q_sig, q_at)
    through_conv(jnp.concatenate(dk_all, axis=1), kc, k_sig, k_at)
    through_conv(jnp.concatenate(dv_all, axis=1), vc, v_sig, v_at)
    first = ids_ref[0] * hl + p * pair
    mine = jnp.logical_and(lane >= first, lane < first + pair)
    d_pre = jnp.where(mine, -jnp.exp(alog_row) * jax.nn.sigmoid(pre) * d_log, 0.0)
    ddec_out[...] = d_dec + d_pre
    if more_ref is not None:
        dx_out[:, 2 * qk + 2 * vv :] = (more_ref[...] + (d_dec + d_pre)).astype(bf16)

    small_out[0:1, :] += gain_rows
    small_out[1:2, 0:128] += jnp.sum(jnp.where(mine, d_log * log_decay, 0.0), axis=0, keepdims=True)
    small_out[2:3, 0:128] += jnp.sum(d_pre, axis=0, keepdims=True)


def mixer_backward(ids, proj, dec, conv, head_rows, gain_row, saved, d_gated, hl, pair, p, more=None):
    out, u, w, inv, states = saved
    tokens = proj.shape[0]
    slots = tokens // TOK_DEV
    qk = pair * DK
    vv = pair * DV
    spec = pl.BlockSpec
    n = TOK_DEV
    width = 2 * qk + 2 * vv + (128 if more is not None else 0)

    def body(*refs):
        backward_kernel(hl, pair, p, *refs)

    return pl.pallas_call(
        body,
        grid=(slots,),
        in_specs=[
            pl.BlockSpec(memory_space=pltpu.SMEM),
            spec((n, 2 * qk + 2 * vv), lambda s: (s, 0)),
            spec((n, 128), lambda s: (s, dec.shape[1] // 128 - 1)),
            spec((8, 2 * qk + vv), lambda s: (0, 0)),
            spec((8, 128), lambda s: (0, 0)),
            spec((8, DV), lambda s: (0, 0)),
            spec((n, vv), lambda s: (s, 0)),
            spec((n, vv), lambda s: (s, 0)),
            spec((n, qk), lambda s: (s, 0)),
            spec((1, pair, n, n), lambda s: (s, 0, 0, 0)),
            spec((1, pair, n // BLOCK * DK, DV), lambda s: (s, 0, 0, 0)),
            spec((n, vv), lambda s: (s, 0)),
        ]
        + ([spec((n, 128), lambda s: (s, 0))] if more is not None else []),
        out_specs=[
            spec((n, width), lambda s: (s, 0)),
            spec((n, 128), lambda s: (s, 0)),
            spec((8, 2 * qk + vv), lambda s: (0, 0)),
            spec((8, DV), lambda s: (0, 0)),
        ],
        out_shape=[
            jax.ShapeDtypeStruct((tokens, width), bf16),
            jax.ShapeDtypeStruct((tokens, 128), f32),
            jax.ShapeDtypeStruct((8, 2 * qk + vv), f32),
            jax.ShapeDtypeStruct((8, DV), f32),
        ],
        compiler_params=pltpu.CompilerParams(vmem_limit_bytes=56 * 1024 * 1024),
        cost_estimate=pl.CostEstimate(flops=1, bytes_accessed=1, transcendentals=0),
        name="mixer_backward",
    )(ids, proj, dec, conv, head_rows, gain_row, out, u, w, inv, states, d_gated, *([more] if more is not None else []))


VMEM_LIMIT = 58 * 1024 * 1024
ANY = pl.BlockSpec(memory_space=pl.ANY)
SMEM = pl.BlockSpec(memory_space=pltpu.SMEM)


def params(**more):
    return pltpu.CompilerParams(vmem_limit_bytes=VMEM_LIMIT, **more)


def cost(flops, moved):
    return pl.CostEstimate(flops=1, bytes_accessed=1, transcendentals=0)


def pack_columns(w, extra, table, rows, plane, ids):
    chips = len(table)
    width = sum(size for _, size in table[0])
    more = 0 if extra is None else extra.shape[1]

    def body(ids_ref, w_ref, *refs):
        out = refs[-1]
        for c in range(chips):
            at = 0
            for start, size in table[c]:
                out[c, :, at : at + size] = w_ref[:, start : start + size]
                at += size
            if more:
                out[c, :, at : at + more] = refs[0][...]

    def block(i, ids_ref):
        return (ids_ref[2] if plane else 0, 0)

    def whole(i, ids_ref):
        return (0, 0)

    return pl.pallas_call(
        body,
        grid_spec=pltpu.PrefetchScalarGridSpec(
            num_scalar_prefetch=1,
            grid=(1,),
            in_specs=[pl.BlockSpec((rows, w.shape[1]), block)]
            + ([pl.BlockSpec((rows, more), whole)] if more else []),
            out_specs=pl.BlockSpec((chips, rows, width + more), lambda i, ids_ref: (0, 0, 0)),
        ),
        out_shape=jax.ShapeDtypeStruct((chips, rows, width + more), bf16),
        compiler_params=params(),
        cost_estimate=cost(0, 2 * rows * w.shape[1] + 2 * chips * rows * (width + more)),
        name="pack_columns",
    )(ids, w, *([extra] if more else []))


def pack_relative(w, extra, table, plane, ids):
    rows = w.shape[0] // 4 if plane else w.shape[0]
    chips = len(table)
    more = 0 if extra is None else extra.shape[1]
    width = sum(size for _, size in table[0]) + more

    def body(ids_ref, w_ref, *refs):
        outs = refs[-chips:]
        for j in range(chips):
            c = jnp.bitwise_xor(ids_ref[0], j)
            at = 0
            for r, (start, size) in enumerate(table[0]):
                step = table[1][r][0] - start
                lane = pl.multiple_of(start + c * step, 128)
                outs[j][:, at : at + size] = w_ref[:, pl.ds(lane, size)]
                at += size
            if more:
                outs[j][:, at : at + more] = refs[0][...]

    def block(i, ids_ref):
        return (ids_ref[2] if plane else 0, 0)

    def whole(i, ids_ref):
        return (0, 0)

    return pl.pallas_call(
        body,
        grid_spec=pltpu.PrefetchScalarGridSpec(
            num_scalar_prefetch=1,
            grid=(1,),
            in_specs=[pl.BlockSpec((rows, w.shape[1]), block)]
            + ([pl.BlockSpec((rows, more), block)] if more else []),
            out_specs=[pl.BlockSpec((rows, width), whole)] * chips,
        ),
        out_shape=[jax.ShapeDtypeStruct((rows, width), bf16)] * chips,
        compiler_params=params(),
        cost_estimate=cost(0, 4 * rows * w.shape[1]),
        name="pack_relative",
    )(ids, w, *([extra] if more else []))


def scatter_add(stay_x, got_x, stay_y, got_y):
    rows, n = stay_x.shape
    block = pl.BlockSpec((rows // 2, n), lambda i: (1, 0))
    out = pl.BlockSpec((rows // 2, n), lambda i: (0, 0))

    def body(a_ref, b_ref, c_ref, d_ref, x_ref, y_ref):
        x_ref[...] = a_ref[...] + b_ref[...]
        y_ref[...] = c_ref[...] + d_ref[...]

    return pl.pallas_call(
        body,
        grid=(1,),
        in_specs=[block] * 4,
        out_specs=[out] * 2,
        out_shape=[jax.ShapeDtypeStruct((rows // 2, n), bf16)] * 2,
        compiler_params=params(),
        cost_estimate=cost(0, 0),
        name="scatter_add",
    )(stay_x, got_x, stay_y, got_y)


def parts_specs(parts):
    rows = parts[2].shape[0]
    return [pl.BlockSpec((rows, p.shape[1]), lambda i: (0, 0)) for p in parts]


def sum_parts(refs):
    halves = []
    for h in range(2):
        a, b, c = refs[3 * h : 3 * h + 3]
        halves.append(a[...].astype(f32) + b[...].astype(f32) + c[...].astype(f32))
    return jnp.concatenate(halves, axis=1)


def live_rows(ids_ref, rows):
    return lax.broadcasted_iota(jnp.int32, (rows, 1), 0) < ids_ref[3]


def middle_rows(parts, tokens, gains, ids):
    rows, d = tokens.shape

    def body(ids_ref, t_ref, g_ref, *refs):
        mid_ref, out_ref = refs[-2:]
        branch = jnp.where(live_rows(ids_ref, rows), sum_parts(refs[:6]), 0.0)
        mid = t_ref[...].astype(f32) + branch
        mid_ref[...] = mid
        r = lax.rsqrt(jnp.mean(mid * mid, axis=1, keepdims=True) + eps_norm)
        out_ref[...] = (mid * r * g_ref[1:2, :]).astype(bf16)

    whole = pl.BlockSpec((rows, d), lambda i: (0, 0))
    return pl.pallas_call(
        body,
        grid=(1,),
        in_specs=[SMEM, whole, pl.BlockSpec((8, d), lambda i: (0, 0))] + parts_specs(parts),
        out_specs=[whole, whole],
        out_shape=[jax.ShapeDtypeStruct((rows, d), f32), jax.ShapeDtypeStruct((rows, d), bf16)],
        compiler_params=params(),
        cost_estimate=cost(0, 0),
        name="middle_rows",
    )(ids, tokens, gains, *parts)


def rms_parts(unit, r, gain, d_out):
    d_unit = d_out * gain
    d_rows = r * (d_unit - unit * jnp.mean(d_unit * unit, axis=1, keepdims=True))
    return d_rows, jnp.sum(d_out * unit, axis=0, keepdims=True)


def middle_back(parts, middle, cotangent, gains, ids):
    rows, d = middle.shape

    def body(ids_ref, m_ref, c_ref, g_ref, *refs):
        d_ref, b_ref, s_ref = refs[-3:]
        mid = m_ref[...]
        r = lax.rsqrt(jnp.mean(mid * mid, axis=1, keepdims=True) + eps_norm)
        d_rows, s_ref[...] = rms_parts(mid * r, r, g_ref[1:2, :], sum_parts(refs[:6]))
        live = live_rows(ids_ref, rows)
        total = jnp.where(live, c_ref[...].astype(f32), 0.0) + d_rows
        d_ref[...] = total
        b_ref[...] = jnp.where(live, total, 0.0).astype(bf16)

    whole = pl.BlockSpec((rows, d), lambda i: (0, 0))
    return pl.pallas_call(
        body,
        grid=(1,),
        in_specs=[SMEM, whole, whole, pl.BlockSpec((8, d), lambda i: (0, 0))]
        + parts_specs(parts),
        out_specs=[whole, whole, pl.BlockSpec((1, d), lambda i: (0, 0))],
        out_shape=[
            jax.ShapeDtypeStruct((rows, d), f32),
            jax.ShapeDtypeStruct((rows, d), bf16),
            jax.ShapeDtypeStruct((1, d), f32),
        ],
        compiler_params=params(),
        cost_estimate=cost(0, 0),
        name="middle_back",
    )(ids, middle, cotangent, gains, *parts)


def tokens_back(parts, tokens, d_middle, gains):
    rows, d = tokens.shape

    def body(t_ref, m_ref, g_ref, *refs):
        d_ref, s_ref = refs[-2:]
        x = t_ref[...].astype(f32)
        r = lax.rsqrt(jnp.mean(x * x, axis=1, keepdims=True) + eps_norm)
        d_rows, s_ref[...] = rms_parts(x * r, r, g_ref[0:1, :], sum_parts(refs[:6]))
        d_ref[...] = m_ref[...] + d_rows

    whole = pl.BlockSpec((rows, d), lambda i: (0, 0))
    return pl.pallas_call(
        body,
        grid=(1,),
        in_specs=[whole, whole, pl.BlockSpec((8, d), lambda i: (0, 0))] + parts_specs(parts),
        out_specs=[whole, pl.BlockSpec((1, d), lambda i: (0, 0))],
        out_shape=[jax.ShapeDtypeStruct((rows, d), f32), jax.ShapeDtypeStruct((1, d), f32)],
        compiler_params=params(),
        cost_estimate=cost(0, 0),
        name="tokens_back",
    )(tokens, d_middle, gains, *parts)


def stack_blocks(parts):
    rows, n = parts[0].shape
    tile = n // 2

    def body(*refs):
        for j in range(len(parts)):
            refs[-1][0, j] = refs[j][...]

    return pl.pallas_call(
        body,
        grid=(2,),
        in_specs=[pl.BlockSpec((rows, tile), lambda i: (0, i))] * len(parts),
        out_specs=pl.BlockSpec((1, len(parts), rows, tile), lambda i: (0, 0, 0, i)),
        out_shape=jax.ShapeDtypeStruct((1, len(parts), rows, n), bf16),
        compiler_params=params(),
        cost_estimate=cost(0, 0),
        name="stack_blocks",
    )(*parts)


def join_cores(mine, theirs, ids):
    rows, n = mine.shape
    tile = 512

    def body(ids_ref, mine_ref, theirs_ref, o_ref):
        core = ids_ref[1]
        o_ref[pl.ds(pl.multiple_of(core * rows, 16), rows), :] = mine_ref[...]
        o_ref[pl.ds(pl.multiple_of((1 - core) * rows, 16), rows), :] = theirs_ref[...]

    return pl.pallas_call(
        body,
        grid=(n // tile,),
        in_specs=[SMEM] + [pl.BlockSpec((rows, tile), lambda i: (0, i))] * 2,
        out_specs=pl.BlockSpec((2 * rows, tile), lambda i: (0, i)),
        out_shape=jax.ShapeDtypeStruct((2 * rows, n), bf16),
        compiler_params=params(),
        cost_estimate=cost(0, 8 * rows * n),
        name="join_cores",
    )(ids, mine, theirs)


def norm_rows(parts, gain):
    d = parts[0].shape[1]
    total = sum(p.shape[0] for p in parts)

    def body(gain_ref, *refs):
        out = refs[-1]
        at = 0
        for ref in refs[:-1]:
            for m in range(0, ref.shape[0], 128):
                rows = ref[m : m + 128, :].astype(f32)
                r = lax.rsqrt(jnp.mean(rows * rows, axis=1, keepdims=True) + eps_norm)
                out[at : at + 128, :] = (rows * r * gain_ref[0:1, :]).astype(bf16)
                at += 128

    return pl.pallas_call(
        body,
        out_shape=jax.ShapeDtypeStruct((total, d), bf16),
        compiler_params=params(),
        cost_estimate=cost(8 * total * d, 4 * total * d),
        name="norm_rows",
    )(gain, *parts)


def small_layout(shapes):
    lanes = []
    at = 0
    for size in shapes:
        lanes.append(at)
        at += size + (-size % 128)
    return lanes, at


def pack_small(conv, vectors, nf):
    lanes, used = small_layout([v.shape[1] for v in vectors])
    channels = conv.shape[1]

    def body(conv_ref, *refs):
        out = refs[-1]
        out[...] = jnp.zeros_like(out)
        for d in range(nf):
            out[d, 0:KCONV, :] = conv_ref[...].astype(f32)
            for ref, lane in zip(refs[:-1], lanes):
                out[d, KCONV : KCONV + 1, lane : lane + ref.shape[1]] = ref[...].astype(f32)

    out = pl.pallas_call(
        body,
        out_shape=jax.ShapeDtypeStruct((nf, 8, channels), f32),
        compiler_params=params(),
        cost_estimate=cost(0, 0),
        name="pack_small",
    )(conv, *vectors)
    return out.astype(bf16)


def small_ranges(chip, hk, qk, vv, groups, p, conv_shard):
    at = chip * groups + p
    found = []
    for start, size in ((at * qk, qk), (hk + at * qk, qk), (2 * hk + at * vv, vv)):
        lane = pl.multiple_of(lax.rem(start, conv_shard), 128)
        found.append((lax.div(start, conv_shard), lane, size))
    return found


def unpack_small(gathered, sizes, ids, hk, qk, vv, groups):
    nf, _, conv_shard = gathered.shape
    lanes, _ = small_layout(sizes)
    d = nf * sizes[0]

    def body(ids_ref, g_ref, gains_ref, heads_ref, ogain_ref, *convs):
        gains_ref[...] = jnp.zeros_like(gains_ref)
        heads_ref[...] = jnp.zeros_like(heads_ref)
        ogain_ref[...] = jnp.zeros_like(ogain_ref)
        for n, out, row in (
            (0, gains_ref, 0),
            (1, gains_ref, 1),
            (2, ogain_ref, 0),
            (3, heads_ref, 0),
            (4, heads_ref, 1),
        ):
            size = sizes[n]
            for i in range(nf):
                out[row : row + 1, i * size : (i + 1) * size] = g_ref[
                    i, KCONV : KCONV + 1, lanes[n] : lanes[n] + size
                ]
        for p, out in enumerate(convs):
            at = 0
            for dev, lane, size in small_ranges(ids_ref[0], hk, qk, vv, groups, p, conv_shard):
                out[:, at : at + size] = g_ref[dev, :, pl.ds(lane, size)]
                at += size

    return pl.pallas_call(
        body,
        in_specs=[SMEM, pl.BlockSpec(memory_space=pltpu.VMEM)],
        out_shape=[
            jax.ShapeDtypeStruct((8, d), f32),
            jax.ShapeDtypeStruct((8, 128), f32),
            jax.ShapeDtypeStruct((8, nf * sizes[2]), f32),
        ]
        + [jax.ShapeDtypeStruct((8, 2 * qk + vv), f32)] * groups,
        compiler_params=params(),
        name="unpack_small",
    )(ids, gathered.astype(f32))


def pack_small_grads(g_conv, g_heads, gain_in, gain_mid, sizes, ids, nf, conv_shard, hk, qk, vv):
    lanes, _ = small_layout(sizes)
    groups = len(g_conv)

    def body(ids_ref, gin_ref, gmid_ref, *refs):
        out = refs[-1]
        out[...] = jnp.zeros_like(out)
        heads = refs[groups][...]
        for ref in refs[groups + 1 : -1]:
            heads = heads + ref[...]
        for n, row in (
            (0, gin_ref[0:1, :]),
            (1, gmid_ref[0:1, :]),
            (2, heads[0:1, :]),
            (3, heads[1:2, :]),
            (4, heads[2:3, :]),
        ):
            size = sizes[n]
            for i in range(nf):
                out[i, KCONV : KCONV + 1, lanes[n] : lanes[n] + size] = row[
                    :, i * size : (i + 1) * size
                ]
        for p in range(groups):
            at = 0
            for dev, lane, size in small_ranges(ids_ref[0], hk, qk, vv, groups, p, conv_shard):
                out[dev, 0:KCONV, pl.ds(lane, size)] = refs[p][0:KCONV, at : at + size]
                at += size

    vmem = pl.BlockSpec(memory_space=pltpu.VMEM)
    return pl.pallas_call(
        body,
        in_specs=[SMEM] + [vmem] * (2 + 2 * groups),
        out_shape=jax.ShapeDtypeStruct((nf, 8, conv_shard), f32),
        compiler_params=params(),
        name="pack_small_grads",
    )(ids, gain_in, gain_mid, *g_conv, *g_heads)


def line_values(ids, chunk, got, pair, met, new):
    rows, n = chunk.shape if chunk is not None else (new if new is not None else pair).shape
    steps = 2
    args = [a for a in (chunk, got, pair, met, new) if a is not None]
    count = (pair is not None or new is not None) + (chunk is not None)

    def body(ids_ref, *refs):
        refs = list(refs)
        outs = refs[len(args) :]
        if chunk is not None:
            outs[-1][...] = refs.pop(0)[...] + refs.pop(0)[...]
        if pair is not None:
            total = refs.pop(0)[...] + refs.pop(0)[...]
            if new is not None:
                middle = jnp.logical_or(ids_ref[2] == 1, ids_ref[2] == 2)
                total = jnp.where(middle, total, refs.pop(0)[...])
            outs[0][...] = total

    block = pl.BlockSpec((rows // steps, n), lambda i: (i, 0))
    return list(pl.pallas_call(
        body,
        grid=(steps,),
        in_specs=[SMEM] + [block] * len(args),
        out_specs=[block] * count,
        out_shape=[jax.ShapeDtypeStruct((rows, n), bf16)] * count,
        compiler_params=params(),
        cost_estimate=cost(0, 0),
        name="line_values",
    )(ids, *args))


def place_blocks(whole, pair_values, ids, c, shape):
    t, last = pair_values
    rows, n = shape[1:]
    old = [] if whole is None else [whole]
    tiles = n // 128

    def body(ids_ref, t_ref, last_ref, *refs):
        out = refs[-1]
        middle = jnp.logical_or(ids_ref[2] == 1, ids_ref[2] == 2)
        for k in range(tiles):
            band = slice(16 * k, 16 * k + 16)
            value = jnp.where(middle, t_ref[band, :], last_ref[band, :])
            for s in range(rows // 16):
                out[0, 16 * s : 16 * s + 16, 128 * k : 128 * k + 128] = value[
                    :, 128 * s : 128 * s + 128
                ]

    vmem = pl.BlockSpec(t.shape, lambda i: (0, 0))
    return pl.pallas_call(
        body,
        grid=(1,),
        in_specs=[SMEM, vmem, vmem] + [ANY] * len(old),
        out_specs=pl.BlockSpec((1, rows, n), lambda i: (c, 0, 0)),
        out_shape=jax.ShapeDtypeStruct(shape, bf16),
        input_output_aliases={3: 0} if old else {},
        compiler_params=params(),
        cost_estimate=cost(0, 6 * rows * n),
        name="place_blocks",
    )(ids, t, last, *old)


def finish_projection(whole, pair_values, ids, bands, shape):
    t, last = pair_values
    rows = shape[0]
    old = [] if whole is None else [whole]
    table = jnp.array([b for b, _ in bands] + [c // 2 for _, c in bands], jnp.int32)
    count = len(bands)

    def body(table_ref, ids_ref, t_ref, last_ref, *refs):
        middle = jnp.logical_or(ids_ref[2] == 1, ids_ref[2] == 2)
        at = pl.multiple_of(16 * table_ref[pl.program_id(0)], 16)
        value = jnp.where(middle, t_ref[pl.ds(at, 32), :], last_ref[pl.ds(at, 32), :])
        for k in range(2):
            for s in range(rows // 16):
                refs[-1][16 * s : 16 * s + 16, 128 * k : 128 * k + 128] = value[
                    16 * k : 16 * k + 16, 128 * s : 128 * s + 128
                ].astype(f32)

    def whole_chunk(i, table_ref):
        return (0, 0)

    return pl.pallas_call(
        body,
        grid_spec=pltpu.PrefetchScalarGridSpec(
            num_scalar_prefetch=1,
            grid=(count,),
            in_specs=[SMEM] + [pl.BlockSpec(t.shape, whole_chunk)] * 2 + [ANY] * len(old),
            out_specs=pl.BlockSpec((rows, 256), lambda i, table_ref: (0, table_ref[count + i])),
        ),
        out_shape=jax.ShapeDtypeStruct(shape, f32),
        input_output_aliases={4: 0} if old else {},
        compiler_params=params(),
        cost_estimate=cost(0, 8 * rows * 256 * count),
        name="finish_projection",
    )(table, ids, t, last, *old)


def finish_feed_forward(blocks):
    chips, rows, n = blocks.shape
    wide = n // 2

    def body(x_ref, o_ref):
        which = pl.program_id(1)
        for s in range(2):

            @pl.when(which == s)
            def _():
                for at in range(0, wide, 128):
                    start = 2 * at + 128 * s
                    o_ref[:, at : at + 128] = x_ref[0, :, start : start + 128].astype(f32)

    return pl.pallas_call(
        body,
        grid=(chips, 2),
        in_specs=[pl.BlockSpec((1, rows, n), lambda c, s: (c, 0, 0))],
        out_specs=pl.BlockSpec((rows, wide), lambda c, s: (0, s * chips + c)),
        out_shape=jax.ShapeDtypeStruct((rows, chips * n), f32),
        compiler_params=params(),
        cost_estimate=cost(0, 6 * chips * rows * n),
        name="finish_feed_forward",
    )(blocks)


def fill_rows(w_ref, own_ref, other_ref, core, chip=0):
    planes, chips, rows, _ = own_ref.shape
    for z in range(planes):
        for j in range(chips):
            c = jnp.bitwise_xor(chip, j)
            for ref, k in ((own_ref, core), (other_ref, 1 - core)):
                at = pl.multiple_of((2 * c + k) * planes * rows + z * rows, rows)
                w_ref[pl.ds(at, rows), :] = ref[z, j]


def project_planes(x, own, other, ids):
    tokens, k = x.shape
    planes, chips, rows, n = own.shape
    tile = 256

    def body(ids_ref, x_ref, own_ref, other_ref, o_ref, w_ref):
        fill_rows(w_ref, own_ref, other_ref, ids_ref[1], ids_ref[0])
        o_ref[...] = jnp.dot(x_ref[...], w_ref[...], preferred_element_type=f32)

    return pl.pallas_call(
        body,
        grid=(pl.cdiv(n, tile),),
        in_specs=[SMEM, pl.BlockSpec((tokens, k), lambda i: (0, 0))]
        + [pl.BlockSpec((planes, chips, rows, tile), lambda i: (0, 0, 0, i))] * 2,
        out_specs=pl.BlockSpec((tokens, tile), lambda i: (0, i)),
        out_shape=jax.ShapeDtypeStruct((tokens, n), f32),
        scratch_shapes=[pltpu.VMEM((k, tile), bf16)],
        compiler_params=params(),
        cost_estimate=cost(2 * tokens * k * n, 2 * tokens * k + 2 * k * n + 4 * tokens * n),
        name="project",
    )(ids, x, own, other)


def project(x, own, other, ids):
    tokens, k = x.shape
    rows, n = own[0].shape
    chips = len(own)
    tile = 256

    def body(ids_ref, x_ref, *refs):
        o_ref, w_ref = refs[2 * chips :]
        for j in range(chips):
            c = jnp.bitwise_xor(ids_ref[0], j)
            for ref, core in ((refs[j], ids_ref[1]), (refs[chips + j], 1 - ids_ref[1])):
                at = pl.multiple_of((2 * c + core) * rows, rows)
                w_ref[pl.ds(at, rows), :] = ref[...]
        o_ref[...] = jnp.dot(x_ref[...], w_ref[...], preferred_element_type=f32)

    return pl.pallas_call(
        body,
        grid=(pl.cdiv(n, tile),),
        in_specs=[SMEM, pl.BlockSpec((tokens, k), lambda i: (0, 0))]
        + [pl.BlockSpec((rows, tile), lambda i: (0, i))] * (2 * chips),
        out_specs=pl.BlockSpec((tokens, tile), lambda i: (0, i)),
        out_shape=jax.ShapeDtypeStruct((tokens, n), f32),
        scratch_shapes=[pltpu.VMEM((k, tile), bf16)],
        compiler_params=params(),
        cost_estimate=cost(2 * tokens * k * n, 2 * tokens * k + 2 * k * n + 4 * tokens * n),
        name="project",
    )(ids, x, *own, *other)


def feed_forward(x, own, other, down, d_ffn, ids):
    tokens, k = x.shape
    planes, chips, rows, n = own.shape
    wide = n // 2
    tile = 512

    def body(ids_ref, x_ref, own_ref, other_ref, down_ref, d_ref, h_ref, g_ref, w_ref):
        fill_rows(w_ref, own_ref, other_ref, ids_ref[1])
        for m in range(0, tokens, 256):
            rows_at = slice(m, m + 256)
            both = jnp.dot(x_ref[rows_at, :], w_ref[...], preferred_element_type=f32)
            d_hidden = mm_nt(d_ref[rows_at, :], down_ref[...])
            for s in range(tile // 256):
                gate = both[:, 256 * s : 256 * s + 128]
                up = both[:, 256 * s + 128 : 256 * s + 256]
                dh = d_hidden[:, 128 * s : 128 * s + 128]
                sig = jax.nn.sigmoid(gate)
                act = gate * sig
                h_ref[rows_at, 128 * s : 128 * s + 128] = (act * up).astype(bf16)
                g_ref[rows_at, 256 * s : 256 * s + 128] = (
                    dh * up * (sig * (1.0 + gate * (1.0 - sig)))
                ).astype(bf16)
                g_ref[rows_at, 256 * s + 128 : 256 * s + 256] = (dh * act).astype(bf16)

    return pl.pallas_call(
        body,
        grid=(pl.cdiv(n, tile),),
        in_specs=[
            SMEM,
            pl.BlockSpec((tokens, k), lambda i: (0, 0)),
            pl.BlockSpec((planes, chips, rows, tile), lambda i: (0, 0, 0, i)),
            pl.BlockSpec((planes, chips, rows, tile), lambda i: (0, 0, 0, i)),
            pl.BlockSpec((tile // 2, k), lambda i: (i, 0)),
            pl.BlockSpec((tokens, k), lambda i: (0, 0)),
        ],
        out_specs=[
            pl.BlockSpec((tokens, tile // 2), lambda i: (0, i)),
            pl.BlockSpec((tokens, tile), lambda i: (0, i)),
        ],
        out_shape=[
            jax.ShapeDtypeStruct((tokens, wide), bf16),
            jax.ShapeDtypeStruct((tokens, n), bf16),
        ],
        scratch_shapes=[pltpu.VMEM((k, tile), bf16)],
        compiler_params=params(),
        cost_estimate=cost(3 * tokens * k * n, 4 * tokens * k + 3 * k * n + 3 * tokens * n),
        name="feed_forward",
    )(ids, x, own, other, down, d_ffn)


def halves_of(i, tiles):
    half = tiles // 2
    return jnp.minimum(i, half - 1), jnp.maximum(i - half, 0)


def scatter_outputs(tokens, n, tile, refs=None):
    size = tokens // 2
    tiles = n // tile
    first = pl.BlockSpec((size, tile), lambda i, *ids: (0, halves_of(i, tiles)[0]))
    second = pl.BlockSpec((size, tile), lambda i, *ids: (0, halves_of(i, tiles)[1]))
    return [first, first, second, second], [jax.ShapeDtypeStruct((size, n // 2), bf16)] * 4


def write_scattered(outs, total_ref, tiles):
    size = total_ref.shape[0] // 4
    i = pl.program_id(0)

    for half, rows in ((0, ((1, 3), (0, 2))), (1, ((2, 3), (0, 1)))):

        @pl.when((i < tiles // 2) if half == 0 else (i >= tiles // 2))
        def _():
            for out, chips in zip(outs[2 * half : 2 * half + 2], rows):
                for n, m in enumerate(chips):
                    out[n * size : (n + 1) * size, :] = total_ref[m * size : (m + 1) * size, :]


def times_rows(lefts, mine, theirs, ids):
    tokens = lefts[0].shape[0]
    half, n = mine.shape
    tile = 256
    specs, shapes = scatter_outputs(tokens, n, tile)

    def body(ids_ref, *refs):
        left_refs = refs[: len(lefts)]
        mine_ref, theirs_ref = refs[len(lefts) : len(lefts) + 2]
        outs = refs[len(lefts) + 2 : -2]
        right_ref, total_ref = refs[-2:]
        core = ids_ref[1]
        right_ref[pl.ds(pl.multiple_of(core * half, 16), half), :] = mine_ref[...]
        right_ref[pl.ds(pl.multiple_of((1 - core) * half, 16), half), :] = theirs_ref[...]
        total = None
        at = 0
        for ref in left_refs:
            width = ref.shape[1]
            term = jnp.dot(ref[...], right_ref[at : at + width, :], preferred_element_type=f32)
            total = term if total is None else total + term
            at += width
        total_ref[...] = total.astype(bf16)
        write_scattered(outs, total_ref, n // tile)

    return pl.pallas_call(
        body,
        grid=(n // tile,),
        in_specs=[SMEM]
        + [pl.BlockSpec(a.shape, lambda i: (0, 0)) for a in lefts]
        + [pl.BlockSpec((half, tile), lambda i: (0, i))] * 2,
        out_specs=specs,
        out_shape=shapes,
        scratch_shapes=[pltpu.VMEM((2 * half, tile), bf16), pltpu.VMEM((tokens, tile), bf16)],
        compiler_params=params(),
        cost_estimate=cost(4 * tokens * half * n, 2 * (tokens * half + half * n + tokens * n)),
        name="times_rows",
    )(ids, *lefts, mine, theirs)


def times_transposed(pairs, ids, relative):
    tokens = pairs[0][0].shape[0]
    planes, chips, rows, _ = pairs[0][1].shape
    rows *= planes
    total_n = sum(left.shape[1] for left, own, other in pairs)
    k = 2 * chips * rows
    specs_out, shapes = scatter_outputs(tokens, k, rows)

    def body(ids_ref, *refs):
        count = len(pairs)
        outs = refs[3 * count : 3 * count + 4]
        piece_refs = refs[3 * count + 4 : -1]
        total_ref = refs[-1]
        mine = pl.program_id(0) % 2 == ids_ref[1]

        def choose(which):
            for n in range(count):
                piece = refs[3 * n + which][:, 0]
                piece_refs[n][...] = piece.reshape(rows, piece.shape[2])

        @pl.when(mine)
        def _():
            choose(1)

        @pl.when(jnp.logical_not(mine))
        def _():
            choose(2)

        total = None
        for n in range(count):
            term = mm_nt(refs[3 * n][...], piece_refs[n][...])
            total = term if total is None else total + term
        total_ref[...] = total.astype(bf16)
        write_scattered(outs, total_ref, 2 * chips)

    def piece_at(i, ids_ref):
        c = lax.div(i, 2)
        if relative:
            c = jnp.bitwise_xor(c, ids_ref[0])
        return (0, c, 0, 0)

    specs = []
    args = []
    for left, own, other in pairs:
        specs.append(pl.BlockSpec(left.shape, lambda i, ids_ref: (0, 0)))
        block = (own.shape[0], 1) + own.shape[2:]
        specs += [pl.BlockSpec(block, piece_at)] * 2
        args += [left, own, other]
    return pl.pallas_call(
        body,
        grid_spec=pltpu.PrefetchScalarGridSpec(
            num_scalar_prefetch=1,
            grid=(2 * chips,),
            in_specs=specs,
            out_specs=specs_out,
            scratch_shapes=[pltpu.VMEM((rows, own.shape[3]), bf16) for _, own, _ in pairs]
            + [pltpu.VMEM((tokens, rows), bf16)],
        ),
        out_shape=shapes,
        compiler_params=params(),
        cost_estimate=cost(
            2 * tokens * k * total_n, 2 * (tokens * k + k * total_n + tokens * total_n)
        ),
        name="times_transposed",
    )(ids, *args)


STREAM = 2048


def pack_bands(value, out, rows, tiles):
    for t in range(tiles):
        for s in range(rows // 16):
            out[16 * t : 16 * t + 16, 128 * s : 128 * s + 128] = value[
                16 * s : 16 * s + 16, 128 * t : 128 * t + 128
            ]


def column_terms(lefts, rights, ids, split):
    tokens, k = lefts[0].shape
    n = rights[0].shape[1]
    chips = 4
    rows = k // (2 * chips)
    tiles = n // 128

    def body(ids_ref, a_ref, b_ref, ra_ref, rb_ref, *refs):
        total_ref = refs[-1]
        total = mm_tn(a_ref[...], ra_ref[...]) + mm_tn(b_ref[...], rb_ref[...])
        if not split:
            total_ref[...] = total.astype(bf16)
            pack_bands(total_ref, refs[0].at[0], rows, tiles)
            return
        total_ref[...] = total.astype(bf16)
        for c in range(chips):

            @pl.when(pl.program_id(0) == c)
            def _():
                pack_bands(total_ref, refs[c], rows, tiles)

    def column(i, ids_ref):
        return (0, 2 * i + ids_ref[1])

    def whole(i, ids_ref):
        return (0, 0)

    if split:
        out_specs = [pl.BlockSpec((16 * tiles, STREAM), whole)] * chips
        out_shape = [jax.ShapeDtypeStruct((16 * tiles, STREAM), bf16)] * chips
    else:
        out_specs = pl.BlockSpec((1, 16 * tiles, STREAM), lambda i, ids_ref: (i, 0, 0))
        out_shape = jax.ShapeDtypeStruct((chips, 16 * tiles, STREAM), bf16)
    return pl.pallas_call(
        body,
        grid_spec=pltpu.PrefetchScalarGridSpec(
            num_scalar_prefetch=1,
            grid=(chips,),
            in_specs=[pl.BlockSpec((tokens, rows), column)] * 2
            + [pl.BlockSpec((tokens, n), whole)] * 2,
            out_specs=out_specs,
            scratch_shapes=[pltpu.VMEM((rows, n), bf16)],
        ),
        out_shape=out_shape,
        compiler_params=params(),
        cost_estimate=cost(2 * tokens * k * n, 4 * (tokens * k + tokens * n + k * n)),
        name="column_terms",
    )(ids, *lefts, *rights)


def row_terms(lefts, right, ids, in_order=False):
    tokens, n = right.shape
    k = sum(a.shape[1] for a in lefts)
    tile = 512
    half = k // 2

    def body(ids_ref, *refs):
        left_refs = refs[: len(lefts)]
        right_ref, mine_ref, theirs_ref, acc = refs[len(lefts) :]
        core = ids_ref[1]
        at = 0
        for ref in left_refs:
            width = ref.shape[1]
            if not in_order:
                acc[at : at + width, :] = mm_tn(ref[...], right_ref[...])
            else:
                total = None
                size = tokens // 4
                for m in range(4):
                    chip = jnp.bitwise_xor(ids_ref[0], m)
                    rows = right_ref[pl.ds(pl.multiple_of(chip * size, size), size), :]
                    term = mm_tn(ref[m * size : (m + 1) * size, :], rows)
                    total = term if total is None else total + term
                acc[at : at + width, :] = total
            at += width
        mine_ref[...] = acc[pl.ds(pl.multiple_of(core * half, 16), half), :].astype(bf16)
        theirs_ref[...] = acc[pl.ds(pl.multiple_of((1 - core) * half, 16), half), :].astype(bf16)

    out = pl.BlockSpec((half, tile), lambda i: (0, i))
    return pl.pallas_call(
        body,
        grid=(n // tile,),
        in_specs=[SMEM]
        + [pl.BlockSpec(a.shape, lambda i: (0, 0)) for a in lefts]
        + [pl.BlockSpec((tokens, tile), lambda i: (0, i))],
        out_specs=[out, out],
        out_shape=[jax.ShapeDtypeStruct((half, n), bf16)] * 2,
        scratch_shapes=[pltpu.VMEM((k, tile), f32)],
        compiler_params=params(),
        cost_estimate=cost(2 * tokens * k * n, 2 * (tokens * k + tokens * n + k * n)),
        name="row_terms",
    )(ids, *lefts, right)


def after(values, *earlier):
    if not earlier:
        return values
    return lax.optimization_barrier((values, earlier))[0]


def to_chip(a, nf, j):
    return lax.ppermute(a, "fsdp", [(i, i ^ (2 * j)) for i in range(nf)])


def swap_core(a, nf):
    return lax.ppermute(a, "fsdp", [(i, i ^ 1) for i in range(nf)])


RIGHT = [(0, 1), (1, 2), (2, 3)]
LEFT = [(1, 0), (2, 1), (3, 2)]
INWARD = [(0, 1), (3, 2)]
MIDDLE = [(1, 2), (2, 1)]
OUTWARD = [(1, 0), (2, 3)]
SWAP = [(0, 1), (1, 0), (2, 3), (3, 2)]


def along(a, pairs):
    return lax.ppermute(a, "rep", pairs)


def add16(a, b):
    return (a.astype(f32) + b.astype(f32)).astype(bf16)


def gather_small(a, nf):
    me = lax.axis_index("fsdp")
    out = a[None]
    bit = 1
    while bit < nf:
        other = lax.ppermute(out, "fsdp", [(i, i ^ bit) for i in range(nf)])
        upper = (me & bit) != 0
        out = jnp.concatenate(
            [jnp.where(upper, other, out), jnp.where(upper, out, other)], axis=0
        )
        bit *= 2
    return out


def sum_small(a, nf):
    me = lax.axis_index("fsdp")
    bit = nf // 2
    while bit:
        half = a.shape[0] // 2
        upper = (me & bit) != 0
        keep = jnp.where(upper, a[half:], a[:half])
        send = jnp.where(upper, a[:half], a[half:])
        got = lax.ppermute(send, "fsdp", [(i, i ^ bit) for i in range(nf)])
        a = keep + got
        bit //= 2
    return a[0], got


def sum_line(a):
    z = lax.axis_index("rep")
    a = a + along(a, INWARD)
    a = a + along(a, MIDDLE)
    return jnp.where(jnp.logical_or(z == 1, z == 2), a, along(a, OUTWARD))


class Line:
    def __init__(self, nz, ids):
        self.nz = nz
        self.ids = ids
        self.tokens = ()
        self.first = None
        self.second = None

    def step(self, new, *earlier):
        if self.nz != 4:
            return new and (new[0], (lax.psum(new[1], "rep"),) * 2)
        chunk = None if new is None else new[1]
        first = (None, None) if self.first is None else self.first[1:]
        second = (None, None) if self.second is None else self.second[1:]
        chunk, first, second, _, _ = lax.optimization_barrier(
            (chunk, first, second, self.tokens, earlier)
        )
        finished = next_first = next_second = None
        tokens = []
        values = []
        if self.first is not None or self.second is not None:
            if chunk is not None and self.second is None:
                values = [chunk] + line_values(self.ids, *first, None, None, None)
            else:
                values = line_values(self.ids, *first, *second, chunk)
        elif chunk is not None:
            values = [chunk]
        if chunk is not None or self.second is not None:
            got = along(values[0], OUTWARD if chunk is None else SWAP)
            tokens.append(got)
            if self.second is not None:
                finished = (self.second[0], (values[0], got))
            if chunk is not None:
                next_first = (new[0], chunk, got)
        if self.first is not None:
            met = along(values[-1], MIDDLE)
            tokens.append(met)
            next_second = (self.first[0], values[-1], met)
        self.first, self.second, self.tokens = next_first, next_second, tuple(tokens)
        self.sent = tuple(values)
        return finished


def gather_first(a, nf, *earlier):
    chips = nf // 2
    a = after(a, *earlier)
    if chips != 4:
        return [a] + [to_chip(a, nf, j) for j in range(1, chips)]
    return [a, to_chip(a, nf, 1), to_chip(a, nf, 2)]


def gather_second(parts, nf, *earlier):
    if nf != 8:
        return jnp.concatenate(parts, axis=0)
    a, one, two = parts
    half = a.shape[0] // 2
    low, high = after((one[:half], two[half:]), *earlier)
    return jnp.concatenate([a, one, two, to_chip(low, nf, 2), to_chip(high, nf, 1)], axis=0)


def scatter_first(a, nf, *earlier):
    chips = nf // 2
    n = a.shape[0] // chips
    parts = [a[j * n : (j + 1) * n] for j in range(chips)]
    if chips != 4:
        return [parts[0]] + [to_chip(parts[j], nf, j) for j in range(1, chips)]
    half = n // 2
    low, high, one, two = after(
        (parts[3][:half], parts[3][half:], parts[1][half:], parts[2][:half]), *earlier
    )
    low = to_chip(low, nf, 2)
    high = to_chip(high, nf, 1)
    one = to_chip(one, nf, 1)
    two = to_chip(two, nf, 2)
    return [
        parts[0],
        one,
        two,
        add16(parts[1][:half], low),
        add16(parts[2][half:], high),
    ]


def scatter_second(parts, nf, *earlier):
    if nf != 8:
        total = parts[0].astype(f32)
        for part in parts[1:]:
            total = total + part.astype(f32)
        return total
    own, one, two, one_low, two_high = parts
    one_low, two_high = after((one_low, two_high), *earlier)
    one_low = to_chip(one_low, nf, 1)
    two_high = to_chip(two_high, nf, 2)
    own = own.astype(f32)
    half = own.shape[0] // 2
    return jnp.concatenate(
        [
            own[:half] + one_low.astype(f32) + two.astype(f32),
            own[half:] + one.astype(f32) + two_high.astype(f32),
        ],
        axis=0,
    )


def rms_back(rows, r, gain, d_out):
    unit = rows * r
    d_unit = d_out * gain
    d_rows = r * (d_unit - unit * jnp.mean(d_unit * unit, axis=1, keepdims=True))
    return d_rows, jnp.sum(d_out * unit, axis=0)


def scale_of(rows):
    return lax.rsqrt(jnp.mean(rows * rows, axis=1, keepdims=True) + eps_norm)


def exchange(a, nf):
    groups = [[2 * c + k for c in range(nf // 2)] for k in range(2)]
    return lax.all_to_all(a, "fsdp", 0, 0, axis_index_groups=groups, tiled=True)


def column_blocks(w, widths, chips, groups, p):
    rows = w.shape[0]
    start = 0
    parts = []
    for width in widths:
        part = w[:, start : start + width].reshape(rows, chips, groups, width // (chips * groups))
        parts.append(part[:, :, p].transpose(1, 0, 2))
        start += width
    return jnp.concatenate(parts, axis=2)


def from_column_blocks(blocks, widths):
    chips, rows, _ = blocks.shape
    parts = []
    at = 0
    for width in widths:
        part = blocks[:, :, at : at + width // chips]
        parts.append(part.transpose(1, 0, 2).reshape(rows, width))
        at += width // chips
    return parts


def both_core_rows(own, nf):
    core = lax.axis_index("fsdp") % 2
    other = swap_core(own, nf)
    first = core == 0
    chips, rows, width = own.shape
    both = jnp.stack([jnp.where(first, own, other), jnp.where(first, other, own)], axis=1)
    return both.reshape(chips * 2 * rows, width)


def core_half(x, chips, which):
    tokens, width = x.shape
    x = x.reshape(tokens, chips, 2, width // (2 * chips))
    x = lax.dynamic_index_in_dim(x, which, 2, keepdims=False)
    return x.reshape(tokens, width // 2)


def column_gradient(left, right, nf, *earlier):
    core = lax.axis_index("fsdp") % 2
    chips = nf // 2
    theirs = mm_tn(core_half(left, chips, 1 - core), right).astype(bf16)
    got = swap_core(theirs, nf)
    mine = mm_tn(core_half(left, chips, core), right) + got.astype(f32)
    return mine.astype(bf16).reshape(chips, -1, right.shape[1])


def both_cores(w, nf, *earlier):
    core = lax.axis_index("fsdp") % 2
    other = swap_core(after(w, *earlier), nf)
    first = core == 0
    return jnp.concatenate([jnp.where(first, w, other), jnp.where(first, other, w)], axis=0)


def halves(a):
    core = lax.axis_index("fsdp") % 2
    rows = a.shape[0] // 2
    mine = lax.dynamic_slice(a, (core * rows, 0), (rows, a.shape[1]))
    theirs = lax.dynamic_slice(a, ((1 - core) * rows, 0), (rows, a.shape[1]))
    return mine, theirs


def sum_cores(a, nf):
    mine, theirs = halves(a)
    return add16(mine, swap_core(theirs, nf))


def as_rows(a):
    flat = a.reshape(-1)
    return jnp.pad(flat, (0, -flat.shape[0] % 128)).reshape(-1, 128)


def gather_pieces(parts, nf, *earlier):
    a, one, two = parts
    half = a.shape[0] // 2
    low, high = after((one[:half], two[half:]), *earlier)
    return [a, one, two, to_chip(low, nf, 2), to_chip(high, nf, 1)]


def scatter_start(parts, nf, *earlier):
    over_x, over_y = after((parts[0], parts[2]), *earlier)
    return [parts[1], to_chip(over_x, nf, 1), parts[3], to_chip(over_y, nf, 2)]


def scatter_middle(parts, nf, *earlier):
    stay_x, got_x, stay_y, got_y = after(parts, *earlier)
    over_y, over_x = scatter_add(stay_x, got_x, stay_y, got_y)
    return [stay_x, got_x, to_chip(over_y, nf, 2), stay_y, got_y, to_chip(over_x, nf, 1)]


def scatter_end(parts):
    size = parts[2].shape[0]
    parts = [p[:size].astype(f32) for p in parts]
    return jnp.concatenate([sum(parts[:3]), sum(parts[3:])], axis=1)


def local_fast(
    tokens,
    cotangent,
    lengths,
    slot_owner,
    gain_in,
    w_proj,
    w_decay,
    conv_weight,
    a_log,
    dt_bias,
    o_gain,
    w_out,
    gain_mid,
    w_gate_up,
    w_down,
    *,
    nf,
    nz,
):
    chips = nf // 2
    hl = H // chips
    pair = 2
    groups = hl // pair
    me = lax.axis_index("fsdp")
    rep = lax.axis_index("rep")
    held = jnp.sum(jnp.where(slot_owner == rep * nf + me, lengths, 0))
    ids = jnp.stack([me // 2, me % 2, rep, held]).astype(jnp.int32)
    shard = gain_in.shape[0]
    conv_shard = conv_weight.shape[1]
    hv = w_out.shape[0] * nf
    hk = (conv_shard * nf - hv) // 2
    ff = w_down.shape[0] * nf
    wide = ff // chips
    qk, vv = pair * DK, pair * DV
    span = 2 * qk + 2 * vv
    proj_widths = (hk, hk, hv, hv)

    def proj_table(p):
        table = []
        for c in range(chips):
            at = c * groups + p
            table.append(
                [
                    (at * qk, qk),
                    (hk + at * qk, qk),
                    (2 * hk + at * vv, vv),
                    (2 * hk + hv + at * vv, vv),
                ]
            )
        return table

    up_table = [
        [(s * ff + c * wide + at, 128) for at in range(0, wide, 128) for s in range(2)]
        for c in range(chips)
    ]
    plane = shard // nz

    vectors = [v.reshape(1, -1) for v in (gain_in, gain_mid, o_gain, a_log, dt_bias)]
    sizes = [v.shape[1] for v in vectors]
    small = lax.all_to_all(pack_small(conv_weight, vectors, nf), "fsdp", 0, 0, tiled=True)
    decay_pad = jnp.pad(w_decay, ((0, 0), (0, 128 - 2 * H)))
    plane_rows = pack_relative(w_proj, decay_pad, proj_table(0), True, ids)
    packed = pack_relative(w_proj, None, proj_table(1), False, ids)

    def spread(own, *earlier):
        sends = after(own[1:], *earlier)
        return [own[0]] + [to_chip(a, nf, j + 1) for j, a in enumerate(sends)]

    def swap_all(own, *earlier):
        return [swap_core(a, nf) for a in after(own, *earlier)]

    out_other = swap_core(w_out, nf)
    down_other = swap_core(w_down, nf)
    first_rows = spread(plane_rows)
    first = jnp.stack(after(first_rows, packed))
    tok = gather_first(tokens, nf, small, first_rows, out_other, down_other)
    sends = after(packed[1:], first_rows, out_other, down_other)
    own = [packed[0], to_chip(sends[0], nf, 1), to_chip(sends[1], nf, 2)]
    first = lax.all_gather(first, "rep", axis=0)
    gains, head_rows, gain_row, *conv_pair = unpack_small(small, sizes, ids, hk, qk, vv, groups)
    tok = gather_pieces(tok, nf, gains)
    own.append(to_chip(after(sends[2], tok[3:]), nf, 3))
    up_plane = pack_columns(after(w_gate_up, packed), None, up_table, plane, True, ids)
    up_plane = exchange(after(up_plane, tok[3:]), nf)

    live_own = (jnp.arange(TOK_DEV, dtype=jnp.int32) < held).astype(f32)[:, None]
    seeded = cotangent.astype(f32) * live_own
    d_ffn_own = seeded.astype(bf16)

    normed_in = norm_rows(after(tok, d_ffn_own), gains)
    first_other = swap_core(after(first, tok, own[1], own[2]), nf)
    projected = [project_planes(normed_in, first, first_other, ids)]
    own = stack_blocks(after(own, projected[0]))
    other = swap_core(own, nf)
    ffn_parts = gather_first(d_ffn_own, nf, own)
    up_own = lax.all_gather(after(up_plane, own), "rep", axis=0)

    def forward(p, *before):
        return mixer_forward(
            ids, after(projected[p], *before), projected[0], conv_pair[p], head_rows, gain_row,
            hl, pair, p,
        )

    gated0, *saved0 = forward(0, own)
    projected.append(project_planes(after(normed_in, gated0, ffn_parts), own, other, ids))
    ffn_parts = gather_pieces(ffn_parts, nf, gated0)
    gated1, *saved1 = forward(1)
    gated = [gated0, gated1]
    saved = [saved0, saved1]
    branch_parts = scatter_start(
        times_rows(after(gated, ffn_parts), w_out, out_other, ids), nf
    )
    d_ffn = jnp.concatenate(after(ffn_parts, branch_parts[0]), axis=0)
    pieces_in = [(first, first_other), (own, other)]
    down_chip = join_cores(w_down, after(down_other, branch_parts[0]), ids)
    out_chip = join_cores(w_out, after(out_other, branch_parts[0]), ids)
    branch_parts = scatter_middle(branch_parts, nf, d_ffn, down_chip, out_chip)
    up_own = after(up_own, branch_parts)
    up_other = swap_core(up_own, nf)
    in_other = swap_core(after(normed_in, up_other), nf)

    middle, normed_own = middle_rows(branch_parts, tokens, gains, ids)
    normed_mid = gather_first(normed_own, nf)
    normed_mid = jnp.concatenate(gather_pieces(normed_mid, nf), axis=0)
    hidden, d_gate_up = feed_forward(normed_mid, up_own, up_other, down_chip, d_ffn, ids)

    line = Line(nz, ids)
    done = {}

    def step(new, *earlier):
        got = line.step(new, *earlier)
        if got is not None:
            done[got[0]] = got[1]

    d_up_other = swap_core(d_gate_up, nf)
    mid_other = swap_core(normed_mid, nf)
    mine, theirs = row_terms([hidden], after(d_ffn, mid_other), ids)
    theirs = swap_core(theirs, nf)
    half = mine.shape[0] // 2
    down0 = mine[:half] + theirs[:half]
    down1 = mine[half:] + theirs[half:]
    step(("down0", down0), down1)
    z = line.tokens
    partial_mid = times_transposed(
        [(after(d_gate_up, down0, down1, d_up_other), up_own, up_other)], ids, False
    )
    mid_parts = scatter_start(partial_mid, nf)
    partial_ffn = times_rows(after([hidden], partial_mid), w_down, down_other, ids)
    step(("down1", down1), partial_ffn, mid_parts[1], mid_parts[3])
    mid_first = mid_parts
    grad_up = column_terms(
        [normed_mid, mid_other],
        [after(d_gate_up, line.sent, mid_first[1], mid_first[3]), d_up_other],
        ids,
        True,
    )
    mid_parts = scatter_middle(mid_parts, nf)
    z = line.tokens
    step(("up0", grad_up[0]))
    d_middle, d_branch_own, g_gain_mid = middle_back(
        after(mid_parts, line.sent), middle, cotangent, gains, ids
    )
    z = line.tokens
    branch_parts = gather_first(d_branch_own, nf)
    d_branch = gather_pieces(branch_parts, nf, z)
    step(("up1", grad_up[1]))
    z = line.tokens
    d_branch = jnp.concatenate(d_branch, axis=0)
    d_gated = [mm_nt(d_branch, out_chip[p * vv : (p + 1) * vv]) for p in range(groups)]

    def backward(p, *before, more=None):
        return mixer_backward(
            ids, projected[p], projected[0], conv_pair[p], head_rows, gain_row, saved[p],
            after(d_gated[p], *before), hl, pair, p, more,
        )

    mine, theirs = row_terms(gated, after(d_branch, d_gated), ids)
    half = mine.shape[0] // 2
    theirs = [swap_core(theirs[:half], nf), swap_core(theirs[half:], nf)]
    step(("up2", grad_up[2]), mine)
    ffn_first = scatter_start(partial_ffn, nf, line.sent)
    d_x1, d_dec, g_conv1, g_heads1 = backward(1, line.sent)
    d_x1_other = swap_core(after(d_x1, line.tokens, ffn_first, theirs), nf)
    grad_out = mine + jnp.concatenate(theirs, axis=0)
    step(("up3", grad_up[3]), d_x1)
    ffn_sends = scatter_middle(ffn_first, nf, line.sent)
    cols1 = column_terms([normed_in, in_other], [after(d_x1, line.sent, ffn_sends[2], ffn_sends[5]), d_x1_other], ids, False)
    cols1_all = exchange(cols1, nf)
    size = down0.shape[0]
    rest = grad_out.shape[0] - size
    step(("out0", grad_out[:size]), cols1)
    d_x0, dec, g_conv0, g_heads0 = backward(0, line.sent, more=d_dec)
    z = line.tokens
    d_x0_other = swap_core(after(d_x0, z, cols1_all), nf)
    bands1 = cols1_all.reshape(-1, STREAM)
    at1 = size - rest
    step(("mix0", jnp.concatenate([grad_out[size:], bands1[:at1]], axis=0)), d_x0)
    cols0 = column_terms([normed_in, in_other], [after(d_x0, line.sent), d_x0_other], ids, False)
    z = line.tokens
    step(("p1", bands1[at1 : at1 + size]), cols0)
    bands0_all = exchange(cols0, nf)
    bands0 = bands0_all.reshape(-1, STREAM)
    right = [d_x0, d_x1]
    partial_in = times_transposed(
        [(after(right[p], line.sent),) + pieces_in[p] for p in range(groups)], ids, True
    )
    at1 += size
    left = bands1.shape[0] - at1
    at0 = size - left
    step(("mix1", jnp.concatenate([bands1[at1:], bands0[:at0]], axis=0)), partial_in)
    in_first = scatter_start(partial_in, nf, line.sent)
    grad_up = None
    for j in range(2):
        grad_up = place_blocks(
            grad_up, after(done["up%d" % j], line.sent), ids, j, (chips, shard, 2 * wide)
        )
    step(("p0", bands0[at0 : at0 + size]), grad_up)
    for j in range(2, chips):
        grad_up = place_blocks(
            grad_up, after(done["up%d" % j], line.sent), ids, j, (chips, shard, 2 * wide)
        )
    in_sends = scatter_middle(in_first, nf, grad_up)
    output = (middle + live_own * scatter_end(after(ffn_sends, line.sent))).astype(bf16)
    grad_up_all = exchange(after(grad_up, in_sends[2], in_sends[5]), nf)
    step(("p0last", bands0[at0 + size :]))
    grad_tokens, g_gain_in = tokens_back(after(in_sends, line.sent), tokens, d_middle, gains)
    blocks = pack_small_grads(
        [g_conv0, g_conv1],
        [g_heads0, g_heads1],
        g_gain_in,
        g_gain_mid,
        sizes,
        ids,
        nf,
        conv_shard,
        hk,
        qk,
        vv,
    )
    def tile_of(p, c, t):
        at = c * groups + p
        q_tiles, v_tiles = qk // 128, vv // 128
        if t < q_tiles:
            return at * q_tiles + t
        if t < 2 * q_tiles:
            return hk // 128 + at * q_tiles + t - q_tiles
        if t < 2 * q_tiles + v_tiles:
            return 2 * hk // 128 + at * v_tiles + t - 2 * q_tiles
        return (2 * hk + hv) // 128 + at * v_tiles + t - 2 * q_tiles - v_tiles

    each = span // 128
    bands = [(1, c, t) for c in range(chips) for t in range(each)]
    bands += [(0, c, t) for c in range(chips) for t in range(each + 1)]
    slots = [("mix0", n) for n in range(rest // 16, size // 16)]
    slots += [("p1", n) for n in range(size // 16)]
    slots += [("mix1", n) for n in range(size // 16)]
    slots += [("p0", n) for n in range(size // 16)]
    slots += [("p0last", n) for n in range(size // 16)]
    where = dict(zip(bands, slots))

    def place(grad_proj, name, *before):
        pairs = [
            (where[key][1], tile_of(*key))
            for key in bands
            if where[key][0] == name and key[2] < each and key[2] % 2 == 0
        ]
        return finish_projection(grad_proj, after(done[name], *before), ids, pairs, w_proj.shape)

    step(None, grad_tokens)
    grad_proj = place(None, "mix0", line.sent)
    grad_proj = place(grad_proj, "p1", line.sent)
    grad_proj = place(grad_proj, "mix1")
    small_sum = lax.all_to_all(after(blocks, grad_proj, grad_up_all), "fsdp", 0, 0, tiled=True)
    step(None, grad_proj)
    grad_up = finish_feed_forward(after(grad_up_all, line.sent))
    grad_proj = place(grad_proj, "p0", grad_up)
    small_sum = lax.all_gather(jnp.sum(after(small_sum, grad_proj), axis=0), "rep", axis=0)
    small_sum = jnp.sum(small_sum, axis=0)
    done["p0last"] = after(done["p0last"], grad_proj)
    grad_proj = place(grad_proj, "p0last")
    middle_two = jnp.logical_or(rep == 1, rep == 2)

    def pick(name):
        return jnp.where(middle_two, *done[name])

    tail = pick("p0last")
    summed = small_sum
    lanes, _ = small_layout(sizes)
    s_gain_in, s_gain_mid, s_ogain, s_alog, s_bias = (
        summed[KCONV, lane : lane + width] for lane, width in zip(lanes, sizes)
    )
    grad_decay = 0.0
    for c in range(chips):
        name, n = where[(0, c, each)]
        band = tail if name == "p0last" else pick(name)
        band = band[16 * n : 16 * n + 16].astype(f32).reshape(16, shard // 16, 128)
        grad_decay = grad_decay + band.transpose(1, 0, 2).reshape(shard, 128)
    grad_decay = grad_decay[:, : 2 * H]
    grad_down = jnp.concatenate([pick("down0"), pick("down1")], axis=0).astype(f32)
    grad_out = jnp.concatenate([pick("out0"), pick("mix0")[:rest]], axis=0).astype(f32)
    return (
        output,
        grad_tokens,
        s_gain_in,
        grad_proj,
        grad_decay,
        summed[:KCONV, :conv_shard],
        s_alog,
        s_bias,
        s_ogain,
        grad_out,
        s_gain_mid,
        grad_up,
        grad_down,
    )


def local_general(
    tokens,
    cotangent,
    lengths,
    slot_owner,
    gain_in,
    w_proj,
    w_decay,
    conv_weight,
    a_log,
    dt_bias,
    o_gain,
    w_out,
    gain_mid,
    w_gate_up,
    w_down,
    *,
    nf,
    nz,
):
    chips = nf // 2
    hl = H // chips
    pair = 2 if hl % 2 == 0 else 1
    groups = hl // pair
    me = lax.axis_index("fsdp")
    rep = lax.axis_index("rep")
    chip, core = me // 2, me % 2
    ids = jnp.stack([chip, core, rep, rep]).astype(jnp.int32)
    d_model = tokens.shape[1]
    shard = gain_in.shape[0]
    conv_shard = conv_weight.shape[1]
    channels = conv_shard * nf
    hv = w_out.shape[0] * nf
    hk = (channels - hv) // 2
    ff = w_down.shape[0] * nf
    wide = ff // chips
    qk, vv = pair * DK, pair * DV
    span = 2 * qk + 2 * vv
    proj_widths = (hk, hk, hv, hv)
    up_widths = (ff, ff)

    def proj_blocks(w, dec, p):
        blocks = column_blocks(w, proj_widths, chips, groups, p)
        if p:
            return blocks
        extra = jnp.pad(dec, ((0, 0), (0, 128 - 2 * H)))
        extra = jnp.broadcast_to(extra, (chips,) + extra.shape)
        return jnp.concatenate([blocks, extra], axis=2)

    def plane_rows(w):
        rows = w.shape[0] // nz
        return lax.dynamic_slice(w, (rep * rows, 0), (rows, w.shape[1]))

    def over_planes(blocks):
        got = lax.all_gather(blocks, "rep", axis=0)
        return got.transpose(1, 0, 2, 3).reshape(chips, -1, blocks.shape[2])

    pieces = [conv_weight, gain_in, gain_mid, o_gain, a_log, dt_bias]
    rows = [as_rows(p) for p in pieces]
    counts = [r.shape[0] for r in rows]
    packed = jnp.concatenate(rows, axis=0)
    packed = jnp.pad(packed, ((0, -packed.shape[0] % 16), (0, 0)))

    plane_proj = plane_rows(w_proj)
    rest = [exchange(proj_blocks(plane_proj, None, p), nf) for p in range(1, groups)]
    first = exchange(proj_blocks(w_proj, w_decay, 0), nf)
    tok = gather_first(tokens, nf)
    small = gather_small(packed, nf)
    tokens_all = gather_second(tok, nf)
    rest = [over_planes(r) for r in rest]
    up_plane = exchange(
        after(column_blocks(plane_rows(w_gate_up), up_widths, chips, 1, 0), first), nf
    )
    up_own = over_planes(after(up_plane, *rest))

    device = rep * nf + me
    held = jnp.sum(jnp.where(slot_owner == device, lengths, 0))
    live_own = (jnp.arange(TOK_DEV, dtype=jnp.int32) < held).astype(f32)[:, None]

    small = small.astype(f32)
    split = []
    at = 0
    for p, count in zip(pieces, counts):
        split.append(
            small[:, at : at + count].reshape(nf, count * 128)[:, : p.size].reshape((nf,) + p.shape)
        )
        at += count
    conv_full = split[0].transpose(1, 0, 2).reshape(KCONV, channels)
    gain_in_full, gain_mid_full, ogain_full, alog_full, bias_full = (
        s.reshape(-1) for s in split[1:]
    )
    conv_pair = []
    for p in range(groups):
        blocks = column_blocks(conv_full, proj_widths[:3], chips, groups, p)
        mine = lax.dynamic_index_in_dim(blocks, chip, 0, keepdims=False)
        conv_pair.append(jnp.pad(mine, ((0, 8 - KCONV), (0, 0))))
    head_rows = jnp.stack([alog_full, bias_full])
    head_rows = jnp.pad(head_rows, ((0, 6), (0, 128 - H)))
    gain_row = jnp.pad(ogain_full[None, :], ((0, 7), (0, 0)))

    rows_in = tokens_all.astype(f32)
    normed_in = (rows_in * scale_of(rows_in) * gain_in_full).astype(bf16)
    seeded = cotangent.astype(f32) * live_own
    weight_in = [both_core_rows(first, nf)]
    out_chip = both_cores(w_out, nf, weight_in[0])
    down_chip = both_cores(w_down, nf, weight_in[0])
    weight_in += [both_core_rows(r, nf) for r in rest]
    ffn_parts = gather_first(seeded.astype(bf16), nf, up_plane)
    d_ffn = gather_second(ffn_parts, nf)
    projected = []
    gated = []
    saved = []
    for p in range(groups):
        projected.append(mm(normed_in, weight_in[p]))
        got = mixer_forward(
            ids, projected[p], projected[0], conv_pair[p], head_rows, gain_row, hl, pair, p
        )
        gated.append(got[0])
        saved.append(got[1:])
    gated = jnp.concatenate(gated, axis=1)
    branch_parts = scatter_first(mm(gated, out_chip).astype(bf16), nf, d_ffn)
    d_hidden = mm_nt(after(d_ffn, gated), down_chip)
    up_chip = both_core_rows(after(up_own, gated), nf)
    branch = scatter_second(branch_parts, nf)

    tokens32 = tokens.astype(f32)
    middle = tokens32 + live_own * branch
    r_mid = scale_of(middle)
    normed_own = (middle * r_mid * gain_mid_full).astype(bf16)
    normed_mid = gather_second(gather_first(normed_own, nf), nf)
    gate_up = mm(normed_mid, up_chip)
    gate, up = gate_up[:, :wide], gate_up[:, wide:]
    sig = jax.nn.sigmoid(gate)
    act = gate * sig
    hidden = (act * up).astype(bf16)
    d_gate_up = jnp.concatenate(
        [d_hidden * up * (sig * (1.0 + gate * (1.0 - sig))), d_hidden * act], axis=1
    ).astype(bf16)

    line = Line(nz, ids)
    done = {}

    def step(new, *earlier):
        for item in new or [None]:
            got = line.step(item, *earlier)
            if got is not None:
                done[got[0]] = got[1][0]

    grad_down = sum_cores(mm_tn(hidden, d_ffn).astype(bf16), nf)
    down_parts = jnp.split(grad_down, 2, axis=0)
    step([("down0", down_parts[0])])
    partial_mid = mm_nt(after(d_gate_up, down_parts[0]), up_chip).astype(bf16)
    mid_parts = scatter_first(partial_mid, nf)
    grad_up = column_gradient(normed_mid, after(d_gate_up, partial_mid), nf)
    step([("down1", down_parts[1])], grad_up)
    d_normed_mid = scatter_second(mid_parts, nf)
    d_mid, g_gain_mid = rms_back(middle, r_mid, gain_mid_full, d_normed_mid)
    d_middle = seeded + d_mid
    d_branch_own = (live_own * d_middle).astype(bf16)
    branch_parts = gather_first(d_branch_own, nf)
    partial_ffn = mm(after(hidden, d_branch_own), down_chip).astype(bf16)
    step([("up0", grad_up[0])], partial_ffn)
    d_branch = gather_second(branch_parts, nf)
    step([("up1", grad_up[1])], d_branch)
    d_gated = [mm_nt(d_branch, out_chip[p * vv : (p + 1) * vv]) for p in range(groups)]
    grad_out = sum_cores(mm_tn(gated, d_branch).astype(bf16), nf)
    d_x = [None] * groups
    d_dec = None
    g_conv = [None] * groups
    g_heads = None
    ups = [("up%d" % j, grad_up[j]) for j in range(2, chips)]
    for n, p in enumerate(reversed(range(groups))):
        d_x[p], dec, g_conv[p], heads = mixer_backward(
            ids, projected[p], projected[0], conv_pair[p], head_rows, gain_row, saved[p],
            d_gated[p], hl, pair, p,
        )
        d_dec = dec if d_dec is None else d_dec + dec
        g_heads = heads if g_heads is None else g_heads + heads
        step(ups[n : n + 1] if n + 1 < groups else ups[n:], d_x[p])
        if p:
            d_gated[p - 1] = after(d_gated[p - 1], d_x[p])
    d_dec = d_dec.astype(bf16)
    right = [jnp.concatenate([d_x[0], d_dec], axis=1)] + d_x[1:]
    grad_cols = [None] * groups
    for p in reversed(range(groups)):
        grad_cols[p] = exchange(column_gradient(normed_in, right[p], nf), nf)
    ffn_parts = scatter_first(partial_ffn, nf, grad_cols[0])
    step([("out", grad_out)], right[0])
    partial_in = mm_nt(right[0], weight_in[0])
    for p in range(1, groups):
        partial_in = partial_in + mm_nt(right[p], weight_in[p])
    partial_in = partial_in.astype(bf16)
    queue = []
    for p in reversed(range(groups)):
        size = 1 if p == 0 else 2
        for c in range(0, chips, size):
            queue.append(((p, c), grad_cols[p][c : c + size]))
    for n, item in enumerate(queue):
        if n == 1:
            ffn_branch = scatter_second(ffn_parts, nf, line.tokens)
            output = (middle + live_own * ffn_branch).astype(bf16)
            in_parts = scatter_first(partial_in, nf, ffn_branch)
        if n == 2:
            d_normed_in = scatter_second(in_parts, nf, line.tokens)
            d_rows, g_gain_in = rms_back(tokens32, scale_of(tokens32), gain_in_full, d_normed_in)
            grad_tokens = d_middle + d_rows
            ups = jnp.stack([done["up%d" % j] for j in range(chips)])
            grad_up = exchange(after(ups, d_normed_in), nf)
        step([item])

    g_conv = [g[:KCONV] for g in g_conv]
    blocks = jnp.concatenate(
        [g[:, a:b] for a, b in ((0, qk), (qk, 2 * qk), (2 * qk, 2 * qk + vv)) for g in g_conv],
        axis=1,
    )
    conv_grad = jnp.zeros((KCONV, chips, channels // chips), f32)
    conv_grad = lax.dynamic_update_slice(conv_grad, blocks[:, None], (0, chip, 0))
    conv_grad = jnp.concatenate(from_column_blocks(conv_grad.transpose(1, 0, 2), proj_widths[:3]), axis=1)
    heads_grad = g_heads[1:3, :H]
    parts = [
        conv_grad.reshape(KCONV, nf, conv_shard).transpose(1, 0, 2),
        g_gain_in.reshape(nf, shard),
        g_gain_mid.reshape(nf, shard),
        g_heads[0].reshape(nf, -1),
        heads_grad[0].reshape(nf, -1),
        heads_grad[1].reshape(nf, -1),
    ]
    flat = []
    for part in parts:
        part = part.reshape(nf, -1)
        flat.append(jnp.pad(part, ((0, 0), (0, -part.shape[1] % 128))))
    flat = jnp.concatenate(flat, axis=1)
    summed = lax.psum(sum_small(flat.reshape(nf, -1, 128), nf)[0], "rep").reshape(-1)
    grads = []
    at = 0
    for p in pieces:
        grads.append(summed[at : at + p.size].reshape(p.shape))
        at += p.size + (-p.size % 128)
    s_conv, s_gain_in, s_gain_mid, s_ogain, s_alog, s_bias = grads

    step([])
    step([])
    grad_up = jnp.concatenate(from_column_blocks(grad_up, up_widths), axis=1).astype(f32)
    wholes = []
    for p in range(groups):
        size = 1 if p == 0 else 2
        wholes.append(jnp.concatenate([done[(p, c)] for c in range(0, chips, size)], axis=0))
    parts = []
    at = 0
    for width in (qk, qk, vv, vv):
        part = jnp.stack([w[:, :, at : at + width] for w in wholes], axis=1)
        parts.append(part.transpose(2, 0, 1, 3).reshape(shard, -1))
        at += width
    grad_proj = jnp.concatenate(parts, axis=1).astype(f32)
    grad_decay = jnp.sum(wholes[0][:, :, span : span + 2 * H].astype(f32), axis=0)
    grad_down = jnp.concatenate([done["down0"], done["down1"]], axis=0).astype(f32)
    grad_out = done["out"].astype(f32)
    return (
        output,
        grad_tokens,
        s_gain_in,
        grad_proj,
        grad_decay,
        s_conv,
        s_alog,
        s_bias,
        s_ogain,
        grad_out,
        s_gain_mid,
        grad_up,
        grad_down,
    )


def solution(mesh):
    rows = P(("rep", "fsdp"), None)
    one = P("fsdp")
    two = P("fsdp", None)
    columns = P(None, "fsdp")
    in_specs = (rows, rows, P(), P(), one, two, two, columns, one, one, one, two, one, two, two)
    out_specs = (rows, rows, one, two, two, columns, one, one, one, two, one, two, two)
    nf, nz = mesh.shape["fsdp"], mesh.shape["rep"]
    body = partial(local_fast if (nf, nz) == (8, 4) else local_general, nf=nf, nz=nz)
    return jax.shard_map(body, mesh=mesh, in_specs=in_specs, out_specs=out_specs, check_vma=False)
```

```python
from functools import partial

import jax
import jax.numpy as jnp
from jax import lax
from jax.experimental import pallas as pl
from jax.experimental.pallas import tpu as pltpu
from jax.sharding import PartitionSpec as P

H = 16
DK = 128
DV = 256
KCONV = 4
BLOCK = 64
TOK_DEV = 256
eps_norm = 1e-05
eps_unit = 1e-06
bf16 = jnp.bfloat16
f32 = jnp.float32


def mm(a, b):
    return lax.dot_general(
        a.astype(bf16), b.astype(bf16), (((1,), (0,)), ((), ())), preferred_element_type=f32
    )


def mm_nt(a, b):
    return lax.dot_general(
        a.astype(bf16), b.astype(bf16), (((1,), (1,)), ((), ())), preferred_element_type=f32
    )


def mm_tn(a, b):
    return lax.dot_general(
        a.astype(bf16), b.astype(bf16), (((0,), (0,)), ((), ())), preferred_element_type=f32
    )


def mm_exact(a, b):
    return lax.dot_general(
        a, b, (((1,), (0,)), ((), ())), precision=lax.Precision.HIGHEST, preferred_element_type=f32
    )


def silu(v):
    return v * jax.nn.sigmoid(v)


def shifted_down(x, s):
    if s == 0:
        return x
    row = lax.broadcasted_iota(jnp.int32, x.shape, 0)
    return jnp.where(row >= s, pltpu.roll(x, s, 0), 0.0)


def shifted_up(x, s):
    if s == 0:
        return x
    n = x.shape[0]
    row = lax.broadcasted_iota(jnp.int32, x.shape, 0)
    return jnp.where(row < n - s, pltpu.roll(x, n - s, 0), 0.0)


def conv_forward(mixed, weight):
    out = weight[KCONV - 1 : KCONV, :] * mixed
    for s in range(1, KCONV):
        out = out + weight[KCONV - 1 - s : KCONV - s, :] * shifted_down(mixed, s)
    return out


def conv_backward(d_conv, mixed, weight):
    d_mixed = weight[KCONV - 1 : KCONV, :] * d_conv
    rows = [None] * KCONV
    rows[KCONV - 1] = jnp.sum(d_conv * mixed, axis=0, keepdims=True)
    for s in range(1, KCONV):
        up = shifted_up(d_conv, s)
        d_mixed = d_mixed + weight[KCONV - 1 - s : KCONV - s, :] * up
        rows[KCONV - 1 - s] = jnp.sum(up * mixed, axis=0, keepdims=True)
    return d_mixed, jnp.concatenate(rows, axis=0)


def block_masks(n):
    i = lax.broadcasted_iota(jnp.int32, (n, n), 0)
    j = lax.broadcasted_iota(jnp.int32, (n, n), 1)
    x = i ^ j
    same = x < BLOCK
    return x, i > j, jnp.logical_and(same, i >= j), jnp.logical_and(same, i > j), same


def decay_parts(dec, alog_row, bias_row):
    pre = dec + bias_row
    softplus = jnp.maximum(pre, 0.0) + jnp.log1p(jnp.exp(-jnp.abs(pre)))
    log_decay = -jnp.exp(alog_row) * softplus
    n = dec.shape[0]
    i = lax.broadcasted_iota(jnp.int32, (n, n), 0)
    j = lax.broadcasted_iota(jnp.int32, (n, n), 1)
    same = (i ^ j) < BLOCK
    lower = jnp.where(jnp.logical_and(same, i >= j), 1.0, 0.0)
    whole = jnp.where(same, 1.0, 0.0)
    running = mm_exact(lower, log_decay)
    total = mm_exact(whole, log_decay)
    return pre, log_decay, running, total


def lane_of(x, h):
    lane = lax.broadcasted_iota(jnp.int32, x.shape, 1)
    return jnp.sum(jnp.where(lane == h, x, 0.0), axis=1, keepdims=True)


def row_of(x, h):
    row = lax.broadcasted_iota(jnp.int32, x.shape, 0)
    return jnp.sum(jnp.where(row == h, x, 0.0), axis=0, keepdims=True)


def unit_rows(a, scale):
    r = lax.rsqrt(jnp.sum(a * a, axis=1, keepdims=True) + eps_unit)
    return a * r * scale, r


def inverse_blocks(lowers, x, below):
    eye = jnp.where(x == 0, 1.0, 0.0)
    inv = [eye - jnp.where(x == 1, low, 0.0) for low in lowers]
    level = 1
    while (2 << level) <= BLOCK:
        pick = lax.shift_right_logical(x, level) == 1
        half = [mm(jnp.where(pick, low, 0.0), t) for low, t in zip(lowers, inv)]
        inv = [t - mm(t, u) for t, u in zip(inv, half)]
        level += 1
    return inv


def forward_kernel(
    hl,
    pair,
    p,
    ids_ref,
    x_ref,
    dec_ref,
    conv_ref,
    head_ref,
    gain_ref,
    gated_ref,
    o_ref,
    u_ref,
    w_ref,
    inv_ref,
    s_ref,
):
    n = TOK_DEV
    qk, vv = pair * DK, pair * DV
    blocks = n // BLOCK
    x, below, on_below, strict, same = block_masks(n)
    dec = dec_ref[...]
    pre, log_decay, running, total = decay_parts(dec, head_ref[0:1, :], head_ref[1:2, :])
    running_t = running.T
    heads = range(pair)
    q = silu(conv_forward(x_ref[:, :qk], conv_ref[:, :qk]))
    k = silu(conv_forward(x_ref[:, qk : 2 * qk], conv_ref[:, qk : 2 * qk]))
    v = silu(conv_forward(x_ref[:, 2 * qk : 2 * qk + vv], conv_ref[:, 2 * qk :])).astype(bf16)
    qn, kn, vn, beta, b, tot, fade, low, score = [], [], [], [], [], [], [], [], []
    for i in heads:
        h = ids_ref[0] * hl + p * pair + i
        qn.append(unit_rows(q[:, i * DK : (i + 1) * DK], DK**-0.5)[0].astype(bf16))
        kn.append(unit_rows(k[:, i * DK : (i + 1) * DK], 1.0)[0].astype(bf16))
        vn.append(v[:, i * DV : (i + 1) * DV])
        beta.append(jax.nn.sigmoid(lane_of(dec, H + h)))
        b.append(lane_of(running, h))
        tot.append(lane_of(total, h))
        d = jnp.where(on_below, jnp.exp(jnp.where(on_below, b[i] - row_of(running_t, h), 0.0)), 0.0)
        both = mm_nt(jnp.concatenate([kn[i], qn[i]], axis=0), kn[i])
        low.append(jnp.where(strict, beta[i] * d * both[:n], 0.0))
        score.append((both[n:] * d).astype(bf16))
    inv = inverse_blocks(low, x, below)
    e = [jnp.exp(b[i]) for i in heads]
    fin = [jnp.exp(tot[i] - b[i]) for i in heads]
    grow = [jnp.exp(tot[i]) for i in heads]
    inv = [t.astype(bf16) for t in inv]
    right = [
        jnp.concatenate(
            [beta[i] * vn[i].astype(f32), (beta[i] * e[i]) * kn[i].astype(f32)], axis=1
        ).astype(bf16)
        for i in heads
    ]
    uw = [mm(inv[i], right[i]) for i in heads]
    w = [uw[i][:, DV:].astype(bf16) for i in heads]
    state = [jnp.zeros((DK, DV), f32) for i in heads]
    u_parts = [[] for i in heads]
    o_parts = [[] for i in heads]
    for c in range(blocks):
        lo, hi = c * BLOCK, (c + 1) * BLOCK
        for i in heads:
            sb = state[i].astype(bf16)
            s_ref[0, i, c * DK : (c + 1) * DK, :] = sb
            got = mm(jnp.concatenate([w[i][lo:hi], qn[i][lo:hi]], axis=0), sb)
            u = uw[i][lo:hi, :DV] - got[:BLOCK]
            u_parts[i].append(u)
            o_parts[i].append(e[i][lo:hi] * got[BLOCK:])
            if c < blocks - 1:
                state[i] = grow[i][lo : lo + 1] * state[i] + mm_tn(
                    kn[i][lo:hi], fin[i][lo:hi] * u
                )
    gain = gain_ref[0:1, :]
    for i in heads:
        u = jnp.concatenate(u_parts[i], axis=0).astype(bf16)
        out = jnp.concatenate(o_parts[i], axis=0) + mm(score[i], u)
        cols = slice(i * DV, (i + 1) * DV)
        o_ref[:, cols] = out
        u_ref[:, cols] = u
        w_ref[:, i * DK : (i + 1) * DK] = w[i]
        inv_ref[0, i] = inv[i]
        r = lax.rsqrt(jnp.mean(out * out, axis=1, keepdims=True) + eps_norm)
        gated_ref[:, cols] = (out * r * gain * silu(x_ref[:, 2 * qk + vv + i * DV : 2 * qk + vv + (i + 1) * DV])).astype(bf16)


def mixer_forward(ids, proj, dec, conv, head_rows, gain_row, hl, pair, p):
    tokens = proj.shape[0]
    slots = tokens // TOK_DEV
    qk = pair * DK
    vv = pair * DV
    spec = pl.BlockSpec
    n = TOK_DEV

    def body(*refs):
        forward_kernel(hl, pair, p, *refs)

    return pl.pallas_call(
        body,
        grid=(slots,),
        in_specs=[
            pl.BlockSpec(memory_space=pltpu.SMEM),
            spec((n, 2 * qk + 2 * vv), lambda s: (s, 0)),
            spec((n, 128), lambda s: (s, dec.shape[1] // 128 - 1)),
            spec((8, 2 * qk + vv), lambda s: (0, 0)),
            spec((8, 128), lambda s: (0, 0)),
            spec((8, DV), lambda s: (0, 0)),
        ],
        out_specs=[
            spec((n, vv), lambda s: (s, 0)),
            spec((n, vv), lambda s: (s, 0)),
            spec((n, vv), lambda s: (s, 0)),
            spec((n, qk), lambda s: (s, 0)),
            spec((1, pair, n, n), lambda s: (s, 0, 0, 0)),
            spec((1, pair, n // BLOCK * DK, DV), lambda s: (s, 0, 0, 0)),
        ],
        out_shape=[
            jax.ShapeDtypeStruct((tokens, vv), bf16),
            jax.ShapeDtypeStruct((tokens, vv), f32),
            jax.ShapeDtypeStruct((tokens, vv), bf16),
            jax.ShapeDtypeStruct((tokens, qk), bf16),
            jax.ShapeDtypeStruct((slots, pair, n, n), bf16),
            jax.ShapeDtypeStruct((slots, pair, n // BLOCK * DK, DV), bf16),
        ],
        compiler_params=pltpu.CompilerParams(vmem_limit_bytes=56 * 1024 * 1024),
        cost_estimate=pl.CostEstimate(flops=1, bytes_accessed=1, transcendentals=0),
        name="mixer_forward",
    )(ids, proj, dec, conv, head_rows, gain_row)


def backward_kernel(
    hl,
    pair,
    p,
    ids_ref,
    x_ref,
    dec_ref,
    conv_ref,
    head_ref,
    gain_ref,
    o_ref,
    u_ref,
    w_ref,
    inv_ref,
    s_ref,
    dy_ref,
    *refs,
):
    more_ref = refs[0] if len(refs) == 5 else None
    dx_out, ddec_out, conv_out, small_out = refs[-4:]
    slot = pl.program_id(0)
    n = TOK_DEV
    qk, vv = pair * DK, pair * DV
    q_at = slice(0, qk)
    k_at = slice(qk, 2 * qk)
    v_at = slice(2 * qk, 2 * qk + vv)
    blocks = n // BLOCK
    x, below, on_below, strict, same = block_masks(n)
    dec = dec_ref[...]
    alog_row = head_ref[0:1, :]
    pre, log_decay, running, total = decay_parts(dec, alog_row, head_ref[1:2, :])
    running_t = running.T
    heads = range(pair)
    qc = conv_forward(x_ref[:, q_at], conv_ref[:, q_at])
    kc = conv_forward(x_ref[:, k_at], conv_ref[:, k_at])
    vc = conv_forward(x_ref[:, v_at], conv_ref[:, v_at])
    q_sig = jax.nn.sigmoid(qc)
    k_sig = jax.nn.sigmoid(kc)
    v_sig = jax.nn.sigmoid(vc)
    q = qc * q_sig
    k = kc * k_sig
    v = (vc * v_sig).astype(bf16)
    gain = gain_ref[0:1, :]
    qn, kn, vn, qr, kr, beta, b, tot, d, sim, low, score = ([] for _ in range(12))
    d_out, u = [], []
    gain_rows = jnp.zeros((1, DV), f32)
    for i in heads:
        h = ids_ref[0] * hl + p * pair + i
        cols = slice(i * DV, (i + 1) * DV)
        kcols = slice(i * DK, (i + 1) * DK)
        rows_q, r_q = unit_rows(q[:, kcols], DK**-0.5)
        rows_k, r_k = unit_rows(k[:, kcols], 1.0)
        qr.append((rows_q, r_q))
        kr.append((rows_k, r_k))
        qn.append(rows_q.astype(bf16))
        kn.append(rows_k.astype(bf16))
        vn.append(v[:, cols])
        beta.append(jax.nn.sigmoid(lane_of(dec, H + h)))
        b.append(lane_of(running, h))
        tot.append(lane_of(total, h))
        d.append(
            jnp.where(on_below, jnp.exp(jnp.where(on_below, b[i] - row_of(running_t, h), 0.0)), 0.0)
        )
        both = mm_nt(jnp.concatenate([kn[i], qn[i]], axis=0), kn[i])
        sim.append(jnp.where(strict, d[i] * both[:n], 0.0))
        score.append(both[n:] * d[i])
        out = o_ref[:, cols]
        g_at = slice(2 * qk + vv + i * DV, 2 * qk + vv + (i + 1) * DV)
        gate = x_ref[:, g_at]
        dy = dy_ref[:, cols].astype(f32)
        r = lax.rsqrt(jnp.mean(out * out, axis=1, keepdims=True) + eps_norm)
        normed = out * r
        g_sig = jax.nn.sigmoid(gate)
        act = gate * g_sig
        d_act = dy * normed * gain
        dx_out[:, g_at] = (d_act * (g_sig * (1.0 + gate * (1.0 - g_sig)))).astype(bf16)
        gain_rows = gain_rows + jnp.sum(dy * normed * act, axis=0, keepdims=True)
        d_normed = dy * gain * act
        d_out.append(r * (d_normed - normed * jnp.mean(d_normed * normed, axis=1, keepdims=True)))
        u.append(u_ref[:, cols])
    e = [jnp.exp(b[i]) for i in heads]
    fin = [jnp.exp(tot[i] - b[i]) for i in heads]
    grow = [jnp.exp(tot[i]) for i in heads]
    d_out16 = [d_out[i].astype(bf16) for i in heads]
    score16 = [score[i].astype(bf16) for i in heads]
    d_u0 = [mm_tn(score16[i], d_out16[i]) for i in heads]
    d_state = [jnp.zeros((DK, DV), f32) for i in heads]
    d_u = [[None] * blocks for i in heads]
    dq_s = [[None] * blocks for i in heads]
    dk_s = [[None] * blocks for i in heads]
    fin_col = [[None] * blocks for i in heads]
    grow_col = [[None] * blocks for i in heads]
    e_out = [(e[i] * d_out[i]).astype(bf16) for i in heads]
    for c in reversed(range(blocks)):
        lo, hi = c * BLOCK, (c + 1) * BLOCK
        for i in heads:
            ds16 = d_state[i].astype(bf16)
            s16 = s_ref[0, i, c * DK : (c + 1) * DK, :]
            u_c = u[i][lo:hi].astype(f32)
            if c == blocks - 1:
                d_u[i][c] = d_u0[i][lo:hi]
                fin_col[i][c] = jnp.zeros((BLOCK, 1), f32)
                grow_col[i][c] = jnp.zeros((1, 1), f32)
                dk_s[i][c] = jnp.zeros((BLOCK, DK), f32)
            else:
                k_ds = mm(kn[i][lo:hi], ds16)
                add = fin[i][lo:hi] * k_ds
                d_u[i][c] = d_u0[i][lo:hi] + add
                fin_col[i][c] = jnp.sum(add * u_c, axis=1, keepdims=True)
                grow_col[i][c] = grow[i][lo : lo + 1] * jnp.sum(
                    jnp.sum(d_state[i] * s16.astype(f32), axis=1, keepdims=True),
                    axis=0,
                    keepdims=True,
                )
                dk_s[i][c] = mm_nt(fin[i][lo:hi] * u_c, ds16)
            if c > 0:
                step = mm_tn(
                    jnp.concatenate([qn[i][lo:hi], w_ref[lo:hi, i * DK : (i + 1) * DK]], axis=0),
                    jnp.concatenate([e_out[i][lo:hi], (-d_u[i][c]).astype(bf16)], axis=0),
                )
                d_state[i] = grow[i][lo : lo + 1] * d_state[i] + step
    lane = lax.broadcasted_iota(jnp.int32, (n, 128), 1)
    d_dec = jnp.zeros((n, 128), f32)
    d_log = jnp.zeros((n, 128), f32)
    dq_all, dk_all, dv_all = [], [], []
    ones = jnp.ones((n, 128), bf16)
    upper_i = lax.broadcasted_iota(jnp.int32, (n, n), 0)
    upper_j = lax.broadcasted_iota(jnp.int32, (n, n), 1)
    upper = jnp.where(jnp.logical_and((upper_i ^ upper_j) < BLOCK, upper_i <= upper_j), 1.0, 0.0)
    for i in heads:
        h = ids_ref[0] * hl + p * pair + i
        du = jnp.concatenate(d_u[i], axis=0)
        d_right = mm_tn(inv_ref[0, i], du)
        dr16 = d_right.astype(bf16)
        outer = mm_nt(jnp.concatenate([d_out16[i], dr16], axis=0), u[i])
        d_score = jnp.where(on_below, outer[:n], 0.0)
        d_low = jnp.where(strict, -outer[n:], 0.0)
        z16 = (-(beta[i] * e[i]) * d_right).astype(bf16)
        recalled = []
        for c in range(blocks):
            lo, hi = c * BLOCK, (c + 1) * BLOCK
            s16 = s_ref[0, i, c * DK : (c + 1) * DK, :]
            if c == 0:
                dq_s[i][c] = jnp.zeros((BLOCK, DK), f32)
                recalled.append(jnp.zeros((BLOCK, 2 * DV), f32))
                continue
            back = mm_nt(jnp.concatenate([e_out[i][lo:hi], z16[lo:hi]], axis=0), s16)
            dq_s[i][c] = back[:BLOCK]
            dk_s[i][c] = dk_s[i][c] + back[BLOCK:]
            got = mm(jnp.concatenate([kn[i][lo:hi], qn[i][lo:hi]], axis=0), s16)
            recalled.append(jnp.concatenate([got[:BLOCK], got[BLOCK:]], axis=1))
        recalled = jnp.concatenate(recalled, axis=0)
        k_s = recalled[:, :DV]
        q_s = recalled[:, DV:]
        d_a = (d_score * d[i]).astype(bf16)
        d_g = d_low * beta[i] * d[i]
        d_g16 = (d_g + d_g.T).astype(bf16)
        dq = jnp.concatenate(dq_s[i], axis=0) + mm(d_a, kn[i])
        dk = jnp.concatenate(dk_s[i], axis=0) + mm_tn(d_a, qn[i]) + mm(d_g16, kn[i])
        dv = beta[i] * d_right
        row_sum = jnp.sum(d_low * sim[i], axis=1, keepdims=True)
        keep = vn[i].astype(f32) - e[i] * k_s
        d_beta = row_sum + jnp.sum(d_right * keep, axis=1, keepdims=True)
        moved = (d_score * score[i] + d_low * beta[i] * sim[i]).astype(bf16)
        d_b = mm(moved, ones) - mm_tn(moved, ones)
        d_b_col = e[i] * jnp.sum(
            d_out[i] * q_s - (beta[i] * d_right) * k_s, axis=1, keepdims=True
        )
        fin_all = jnp.concatenate(fin_col[i], axis=0)
        d_b = jnp.where(lane == h, d_b + (d_b_col - fin_all), 0.0)
        tail = jnp.concatenate(
            [
                jnp.broadcast_to(
                    grow_col[i][c] + jnp.sum(fin_col[i][c], axis=0, keepdims=True), (BLOCK, 1)
                )
                for c in range(blocks)
            ],
            axis=0,
        )
        d_log = d_log + mm_exact(upper, d_b) + jnp.where(lane == h, tail, 0.0)
        d_dec = d_dec + jnp.where(lane == H + h, d_beta * beta[i] * (1.0 - beta[i]), 0.0)
        rows_q, r_q = qr[i]
        rows_k, r_k = kr[i]
        unit = rows_q * DK**0.5
        dq = (DK**-0.5) * r_q * (dq - unit * jnp.sum(dq * unit, axis=1, keepdims=True))
        dk = r_k * (dk - rows_k * jnp.sum(dk * rows_k, axis=1, keepdims=True))
        dq_all.append(dq)
        dk_all.append(dk)
        dv_all.append(dv)

    @pl.when(slot == 0)
    def _():
        conv_out[...] = jnp.zeros_like(conv_out)
        small_out[...] = jnp.zeros_like(small_out)

    def through_conv(d_active, conv, sig, at):
        d_conv = d_active * (sig * (1.0 + conv * (1.0 - sig)))
        d_mixed, d_weight = conv_backward(d_conv, x_ref[:, at], conv_ref[:, at])
        dx_out[:, at] = d_mixed.astype(bf16)
        conv_out[0:KCONV, at] += d_weight

    through_conv(jnp.concatenate(dq_all, axis=1), qc, q_sig, q_at)
    through_conv(jnp.concatenate(dk_all, axis=1), kc, k_sig, k_at)
    through_conv(jnp.concatenate(dv_all, axis=1), vc, v_sig, v_at)
    first = ids_ref[0] * hl + p * pair
    mine = jnp.logical_and(lane >= first, lane < first + pair)
    d_pre = jnp.where(mine, -jnp.exp(alog_row) * jax.nn.sigmoid(pre) * d_log, 0.0)
    ddec_out[...] = d_dec + d_pre
    if more_ref is not None:
        dx_out[:, 2 * qk + 2 * vv :] = (more_ref[...] + (d_dec + d_pre)).astype(bf16)

    small_out[0:1, :] += gain_rows
    small_out[1:2, 0:128] += jnp.sum(jnp.where(mine, d_log * log_decay, 0.0), axis=0, keepdims=True)
    small_out[2:3, 0:128] += jnp.sum(d_pre, axis=0, keepdims=True)


def mixer_backward(ids, proj, dec, conv, head_rows, gain_row, saved, d_gated, hl, pair, p, more=None):
    out, u, w, inv, states = saved
    tokens = proj.shape[0]
    slots = tokens // TOK_DEV
    qk = pair * DK
    vv = pair * DV
    spec = pl.BlockSpec
    n = TOK_DEV
    width = 2 * qk + 2 * vv + (128 if more is not None else 0)

    def body(*refs):
        backward_kernel(hl, pair, p, *refs)

    return pl.pallas_call(
        body,
        grid=(slots,),
        in_specs=[
            pl.BlockSpec(memory_space=pltpu.SMEM),
            spec((n, 2 * qk + 2 * vv), lambda s: (s, 0)),
            spec((n, 128), lambda s: (s, dec.shape[1] // 128 - 1)),
            spec((8, 2 * qk + vv), lambda s: (0, 0)),
            spec((8, 128), lambda s: (0, 0)),
            spec((8, DV), lambda s: (0, 0)),
            spec((n, vv), lambda s: (s, 0)),
            spec((n, vv), lambda s: (s, 0)),
            spec((n, qk), lambda s: (s, 0)),
            spec((1, pair, n, n), lambda s: (s, 0, 0, 0)),
            spec((1, pair, n // BLOCK * DK, DV), lambda s: (s, 0, 0, 0)),
            spec((n, vv), lambda s: (s, 0)),
        ]
        + ([spec((n, 128), lambda s: (s, 0))] if more is not None else []),
        out_specs=[
            spec((n, width), lambda s: (s, 0)),
            spec((n, 128), lambda s: (s, 0)),
            spec((8, 2 * qk + vv), lambda s: (0, 0)),
            spec((8, DV), lambda s: (0, 0)),
        ],
        out_shape=[
            jax.ShapeDtypeStruct((tokens, width), bf16),
            jax.ShapeDtypeStruct((tokens, 128), f32),
            jax.ShapeDtypeStruct((8, 2 * qk + vv), f32),
            jax.ShapeDtypeStruct((8, DV), f32),
        ],
        compiler_params=pltpu.CompilerParams(vmem_limit_bytes=56 * 1024 * 1024),
        cost_estimate=pl.CostEstimate(flops=1, bytes_accessed=1, transcendentals=0),
        name="mixer_backward",
    )(ids, proj, dec, conv, head_rows, gain_row, out, u, w, inv, states, d_gated, *([more] if more is not None else []))


VMEM_LIMIT = 58 * 1024 * 1024
ANY = pl.BlockSpec(memory_space=pl.ANY)
SMEM = pl.BlockSpec(memory_space=pltpu.SMEM)


def params(**more):
    return pltpu.CompilerParams(vmem_limit_bytes=VMEM_LIMIT, **more)


def cost(flops, moved):
    return pl.CostEstimate(flops=1, bytes_accessed=1, transcendentals=0)


def pack_columns(w, extra, table, rows, plane, ids):
    chips = len(table)
    width = sum(size for _, size in table[0])
    more = 0 if extra is None else extra.shape[1]

    def body(ids_ref, w_ref, *refs):
        out = refs[-1]
        for c in range(chips):
            at = 0
            for start, size in table[c]:
                out[c, :, at : at + size] = w_ref[:, start : start + size]
                at += size
            if more:
                out[c, :, at : at + more] = refs[0][...]

    def block(i, ids_ref):
        return (ids_ref[2] if plane else 0, 0)

    def whole(i, ids_ref):
        return (0, 0)

    return pl.pallas_call(
        body,
        grid_spec=pltpu.PrefetchScalarGridSpec(
            num_scalar_prefetch=1,
            grid=(1,),
            in_specs=[pl.BlockSpec((rows, w.shape[1]), block)]
            + ([pl.BlockSpec((rows, more), whole)] if more else []),
            out_specs=pl.BlockSpec((chips, rows, width + more), lambda i, ids_ref: (0, 0, 0)),
        ),
        out_shape=jax.ShapeDtypeStruct((chips, rows, width + more), bf16),
        compiler_params=params(),
        cost_estimate=cost(0, 2 * rows * w.shape[1] + 2 * chips * rows * (width + more)),
        name="pack_columns",
    )(ids, w, *([extra] if more else []))


def pack_relative(w, extra, table, plane, ids):
    rows = w.shape[0] // 4 if plane else w.shape[0]
    chips = len(table)
    more = 0 if extra is None else extra.shape[1]
    width = sum(size for _, size in table[0]) + more

    def body(ids_ref, w_ref, *refs):
        outs = refs[-chips:]
        for j in range(chips):
            c = jnp.bitwise_xor(ids_ref[0], j)
            at = 0
            for r, (start, size) in enumerate(table[0]):
                step = table[1][r][0] - start
                lane = pl.multiple_of(start + c * step, 128)
                outs[j][:, at : at + size] = w_ref[:, pl.ds(lane, size)]
                at += size
            if more:
                outs[j][:, at : at + more] = refs[0][...]

    def block(i, ids_ref):
        return (ids_ref[2] if plane else 0, 0)

    def whole(i, ids_ref):
        return (0, 0)

    return pl.pallas_call(
        body,
        grid_spec=pltpu.PrefetchScalarGridSpec(
            num_scalar_prefetch=1,
            grid=(1,),
            in_specs=[pl.BlockSpec((rows, w.shape[1]), block)]
            + ([pl.BlockSpec((rows, more), block)] if more else []),
            out_specs=[pl.BlockSpec((rows, width), whole)] * chips,
        ),
        out_shape=[jax.ShapeDtypeStruct((rows, width), bf16)] * chips,
        compiler_params=params(),
        cost_estimate=cost(0, 4 * rows * w.shape[1]),
        name="pack_relative",
    )(ids, w, *([extra] if more else []))


def scatter_add(stay_x, got_x, stay_y, got_y):
    rows, n = stay_x.shape
    block = pl.BlockSpec((rows // 2, n), lambda i: (1, 0))
    out = pl.BlockSpec((rows // 2, n), lambda i: (0, 0))

    def body(a_ref, b_ref, c_ref, d_ref, x_ref, y_ref):
        x_ref[...] = a_ref[...] + b_ref[...]
        y_ref[...] = c_ref[...] + d_ref[...]

    return pl.pallas_call(
        body,
        grid=(1,),
        in_specs=[block] * 4,
        out_specs=[out] * 2,
        out_shape=[jax.ShapeDtypeStruct((rows // 2, n), bf16)] * 2,
        compiler_params=params(),
        cost_estimate=cost(0, 0),
        name="scatter_add",
    )(stay_x, got_x, stay_y, got_y)


def parts_specs(parts):
    rows = parts[2].shape[0]
    return [pl.BlockSpec((rows, p.shape[1]), lambda i: (0, 0)) for p in parts]


def sum_parts(refs):
    halves = []
    for h in range(2):
        a, b, c = refs[3 * h : 3 * h + 3]
        halves.append(a[...].astype(f32) + b[...].astype(f32) + c[...].astype(f32))
    return jnp.concatenate(halves, axis=1)


def live_rows(ids_ref, rows):
    return lax.broadcasted_iota(jnp.int32, (rows, 1), 0) < ids_ref[3]


def middle_rows(parts, tokens, gains, ids):
    rows, d = tokens.shape

    def body(ids_ref, t_ref, g_ref, *refs):
        mid_ref, out_ref = refs[-2:]
        branch = jnp.where(live_rows(ids_ref, rows), sum_parts(refs[:6]), 0.0)
        mid = t_ref[...].astype(f32) + branch
        mid_ref[...] = mid
        r = lax.rsqrt(jnp.mean(mid * mid, axis=1, keepdims=True) + eps_norm)
        out_ref[...] = (mid * r * g_ref[1:2, :]).astype(bf16)

    whole = pl.BlockSpec((rows, d), lambda i: (0, 0))
    return pl.pallas_call(
        body,
        grid=(1,),
        in_specs=[SMEM, whole, pl.BlockSpec((8, d), lambda i: (0, 0))] + parts_specs(parts),
        out_specs=[whole, whole],
        out_shape=[jax.ShapeDtypeStruct((rows, d), f32), jax.ShapeDtypeStruct((rows, d), bf16)],
        compiler_params=params(),
        cost_estimate=cost(0, 0),
        name="middle_rows",
    )(ids, tokens, gains, *parts)


def rms_parts(unit, r, gain, d_out):
    d_unit = d_out * gain
    d_rows = r * (d_unit - unit * jnp.mean(d_unit * unit, axis=1, keepdims=True))
    return d_rows, jnp.sum(d_out * unit, axis=0, keepdims=True)


def middle_back(parts, middle, cotangent, gains, ids):
    rows, d = middle.shape

    def body(ids_ref, m_ref, c_ref, g_ref, *refs):
        d_ref, b_ref, s_ref = refs[-3:]
        mid = m_ref[...]
        r = lax.rsqrt(jnp.mean(mid * mid, axis=1, keepdims=True) + eps_norm)
        d_rows, s_ref[...] = rms_parts(mid * r, r, g_ref[1:2, :], sum_parts(refs[:6]))
        live = live_rows(ids_ref, rows)
        total = jnp.where(live, c_ref[...].astype(f32), 0.0) + d_rows
        d_ref[...] = total
        b_ref[...] = jnp.where(live, total, 0.0).astype(bf16)

    whole = pl.BlockSpec((rows, d), lambda i: (0, 0))
    return pl.pallas_call(
        body,
        grid=(1,),
        in_specs=[SMEM, whole, whole, pl.BlockSpec((8, d), lambda i: (0, 0))]
        + parts_specs(parts),
        out_specs=[whole, whole, pl.BlockSpec((1, d), lambda i: (0, 0))],
        out_shape=[
            jax.ShapeDtypeStruct((rows, d), f32),
            jax.ShapeDtypeStruct((rows, d), bf16),
            jax.ShapeDtypeStruct((1, d), f32),
        ],
        compiler_params=params(),
        cost_estimate=cost(0, 0),
        name="middle_back",
    )(ids, middle, cotangent, gains, *parts)


def tokens_back(parts, tokens, d_middle, gains):
    rows, d = tokens.shape

    def body(t_ref, m_ref, g_ref, *refs):
        d_ref, s_ref = refs[-2:]
        x = t_ref[...].astype(f32)
        r = lax.rsqrt(jnp.mean(x * x, axis=1, keepdims=True) + eps_norm)
        d_rows, s_ref[...] = rms_parts(x * r, r, g_ref[0:1, :], sum_parts(refs[:6]))
        d_ref[...] = m_ref[...] + d_rows

    whole = pl.BlockSpec((rows, d), lambda i: (0, 0))
    return pl.pallas_call(
        body,
        grid=(1,),
        in_specs=[whole, whole, pl.BlockSpec((8, d), lambda i: (0, 0))] + parts_specs(parts),
        out_specs=[whole, pl.BlockSpec((1, d), lambda i: (0, 0))],
        out_shape=[jax.ShapeDtypeStruct((rows, d), f32), jax.ShapeDtypeStruct((1, d), f32)],
        compiler_params=params(),
        cost_estimate=cost(0, 0),
        name="tokens_back",
    )(tokens, d_middle, gains, *parts)


def stack_blocks(parts):
    rows, n = parts[0].shape
    tile = n // 2

    def body(*refs):
        for j in range(len(parts)):
            refs[-1][0, j] = refs[j][...]

    return pl.pallas_call(
        body,
        grid=(2,),
        in_specs=[pl.BlockSpec((rows, tile), lambda i: (0, i))] * len(parts),
        out_specs=pl.BlockSpec((1, len(parts), rows, tile), lambda i: (0, 0, 0, i)),
        out_shape=jax.ShapeDtypeStruct((1, len(parts), rows, n), bf16),
        compiler_params=params(),
        cost_estimate=cost(0, 0),
        name="stack_blocks",
    )(*parts)


def join_cores(mine, theirs, ids):
    rows, n = mine.shape
    tile = 512

    def body(ids_ref, mine_ref, theirs_ref, o_ref):
        core = ids_ref[1]
        o_ref[pl.ds(pl.multiple_of(core * rows, 16), rows), :] = mine_ref[...]
        o_ref[pl.ds(pl.multiple_of((1 - core) * rows, 16), rows), :] = theirs_ref[...]

    return pl.pallas_call(
        body,
        grid=(n // tile,),
        in_specs=[SMEM] + [pl.BlockSpec((rows, tile), lambda i: (0, i))] * 2,
        out_specs=pl.BlockSpec((2 * rows, tile), lambda i: (0, i)),
        out_shape=jax.ShapeDtypeStruct((2 * rows, n), bf16),
        compiler_params=params(),
        cost_estimate=cost(0, 8 * rows * n),
        name="join_cores",
    )(ids, mine, theirs)


def norm_rows(parts, gain):
    d = parts[0].shape[1]
    total = sum(p.shape[0] for p in parts)

    def body(gain_ref, *refs):
        out = refs[-1]
        at = 0
        for ref in refs[:-1]:
            for m in range(0, ref.shape[0], 128):
                rows = ref[m : m + 128, :].astype(f32)
                r = lax.rsqrt(jnp.mean(rows * rows, axis=1, keepdims=True) + eps_norm)
                out[at : at + 128, :] = (rows * r * gain_ref[0:1, :]).astype(bf16)
                at += 128

    return pl.pallas_call(
        body,
        out_shape=jax.ShapeDtypeStruct((total, d), bf16),
        compiler_params=params(),
        cost_estimate=cost(8 * total * d, 4 * total * d),
        name="norm_rows",
    )(gain, *parts)


def small_layout(shapes):
    lanes = []
    at = 0
    for size in shapes:
        lanes.append(at)
        at += size + (-size % 128)
    return lanes, at


def pack_small(conv, vectors, nf):
    lanes, used = small_layout([v.shape[1] for v in vectors])
    channels = conv.shape[1]

    def body(conv_ref, *refs):
        out = refs[-1]
        out[...] = jnp.zeros_like(out)
        for d in range(nf):
            out[d, 0:KCONV, :] = conv_ref[...].astype(f32)
            for ref, lane in zip(refs[:-1], lanes):
                out[d, KCONV : KCONV + 1, lane : lane + ref.shape[1]] = ref[...].astype(f32)

    out = pl.pallas_call(
        body,
        out_shape=jax.ShapeDtypeStruct((nf, 8, channels), f32),
        compiler_params=params(),
        cost_estimate=cost(0, 0),
        name="pack_small",
    )(conv, *vectors)
    return out.astype(bf16)


def small_ranges(chip, hk, qk, vv, groups, p, conv_shard):
    at = chip * groups + p
    found = []
    for start, size in ((at * qk, qk), (hk + at * qk, qk), (2 * hk + at * vv, vv)):
        lane = pl.multiple_of(lax.rem(start, conv_shard), 128)
        found.append((lax.div(start, conv_shard), lane, size))
    return found


def unpack_small(gathered, sizes, ids, hk, qk, vv, groups):
    nf, _, conv_shard = gathered.shape
    lanes, _ = small_layout(sizes)
    d = nf * sizes[0]

    def body(ids_ref, g_ref, gains_ref, heads_ref, ogain_ref, *convs):
        gains_ref[...] = jnp.zeros_like(gains_ref)
        heads_ref[...] = jnp.zeros_like(heads_ref)
        ogain_ref[...] = jnp.zeros_like(ogain_ref)
        for n, out, row in (
            (0, gains_ref, 0),
            (1, gains_ref, 1),
            (2, ogain_ref, 0),
            (3, heads_ref, 0),
            (4, heads_ref, 1),
        ):
            size = sizes[n]
            for i in range(nf):
                out[row : row + 1, i * size : (i + 1) * size] = g_ref[
                    i, KCONV : KCONV + 1, lanes[n] : lanes[n] + size
                ]
        for p, out in enumerate(convs):
            at = 0
            for dev, lane, size in small_ranges(ids_ref[0], hk, qk, vv, groups, p, conv_shard):
                out[:, at : at + size] = g_ref[dev, :, pl.ds(lane, size)]
                at += size

    return pl.pallas_call(
        body,
        in_specs=[SMEM, pl.BlockSpec(memory_space=pltpu.VMEM)],
        out_shape=[
            jax.ShapeDtypeStruct((8, d), f32),
            jax.ShapeDtypeStruct((8, 128), f32),
            jax.ShapeDtypeStruct((8, nf * sizes[2]), f32),
        ]
        + [jax.ShapeDtypeStruct((8, 2 * qk + vv), f32)] * groups,
        compiler_params=params(),
        name="unpack_small",
    )(ids, gathered.astype(f32))


def pack_small_grads(g_conv, g_heads, gain_in, gain_mid, sizes, ids, nf, conv_shard, hk, qk, vv):
    lanes, _ = small_layout(sizes)
    groups = len(g_conv)

    def body(ids_ref, gin_ref, gmid_ref, *refs):
        out = refs[-1]
        out[...] = jnp.zeros_like(out)
        heads = refs[groups][...]
        for ref in refs[groups + 1 : -1]:
            heads = heads + ref[...]
        for n, row in (
            (0, gin_ref[0:1, :]),
            (1, gmid_ref[0:1, :]),
            (2, heads[0:1, :]),
            (3, heads[1:2, :]),
            (4, heads[2:3, :]),
        ):
            size = sizes[n]
            for i in range(nf):
                out[i, KCONV : KCONV + 1, lanes[n] : lanes[n] + size] = row[
                    :, i * size : (i + 1) * size
                ]
        for p in range(groups):
            at = 0
            for dev, lane, size in small_ranges(ids_ref[0], hk, qk, vv, groups, p, conv_shard):
                out[dev, 0:KCONV, pl.ds(lane, size)] = refs[p][0:KCONV, at : at + size]
                at += size

    vmem = pl.BlockSpec(memory_space=pltpu.VMEM)
    return pl.pallas_call(
        body,
        in_specs=[SMEM] + [vmem] * (2 + 2 * groups),
        out_shape=jax.ShapeDtypeStruct((nf, 8, conv_shard), f32),
        compiler_params=params(),
        name="pack_small_grads",
    )(ids, gain_in, gain_mid, *g_conv, *g_heads)


def line_values(ids, chunk, got, pair, met, new):
    rows, n = chunk.shape if chunk is not None else (new if new is not None else pair).shape
    steps = 2
    args = [a for a in (chunk, got, pair, met, new) if a is not None]
    count = (pair is not None or new is not None) + (chunk is not None)

    def body(ids_ref, *refs):
        refs = list(refs)
        outs = refs[len(args) :]
        if chunk is not None:
            outs[-1][...] = refs.pop(0)[...] + refs.pop(0)[...]
        if pair is not None:
            total = refs.pop(0)[...] + refs.pop(0)[...]
            if new is not None:
                middle = jnp.logical_or(ids_ref[2] == 1, ids_ref[2] == 2)
                total = jnp.where(middle, total, refs.pop(0)[...])
            outs[0][...] = total

    block = pl.BlockSpec((rows // steps, n), lambda i: (i, 0))
    return list(pl.pallas_call(
        body,
        grid=(steps,),
        in_specs=[SMEM] + [block] * len(args),
        out_specs=[block] * count,
        out_shape=[jax.ShapeDtypeStruct((rows, n), bf16)] * count,
        compiler_params=params(),
        cost_estimate=cost(0, 0),
        name="line_values",
    )(ids, *args))


def place_blocks(whole, pair_values, ids, c, shape):
    t, last = pair_values
    rows, n = shape[1:]
    old = [] if whole is None else [whole]
    tiles = n // 128

    def body(ids_ref, t_ref, last_ref, *refs):
        out = refs[-1]
        middle = jnp.logical_or(ids_ref[2] == 1, ids_ref[2] == 2)
        for k in range(tiles):
            band = slice(16 * k, 16 * k + 16)
            value = jnp.where(middle, t_ref[band, :], last_ref[band, :])
            for s in range(rows // 16):
                out[0, 16 * s : 16 * s + 16, 128 * k : 128 * k + 128] = value[
                    :, 128 * s : 128 * s + 128
                ]

    vmem = pl.BlockSpec(t.shape, lambda i: (0, 0))
    return pl.pallas_call(
        body,
        grid=(1,),
        in_specs=[SMEM, vmem, vmem] + [ANY] * len(old),
        out_specs=pl.BlockSpec((1, rows, n), lambda i: (c, 0, 0)),
        out_shape=jax.ShapeDtypeStruct(shape, bf16),
        input_output_aliases={3: 0} if old else {},
        compiler_params=params(),
        cost_estimate=cost(0, 6 * rows * n),
        name="place_blocks",
    )(ids, t, last, *old)


def finish_projection(whole, pair_values, ids, bands, shape):
    t, last = pair_values
    rows = shape[0]
    old = [] if whole is None else [whole]
    table = jnp.array([b for b, _ in bands] + [c // 2 for _, c in bands], jnp.int32)
    count = len(bands)

    def body(table_ref, ids_ref, t_ref, last_ref, *refs):
        middle = jnp.logical_or(ids_ref[2] == 1, ids_ref[2] == 2)
        at = pl.multiple_of(16 * table_ref[pl.program_id(0)], 16)
        value = jnp.where(middle, t_ref[pl.ds(at, 32), :], last_ref[pl.ds(at, 32), :])
        for k in range(2):
            for s in range(rows // 16):
                refs[-1][16 * s : 16 * s + 16, 128 * k : 128 * k + 128] = value[
                    16 * k : 16 * k + 16, 128 * s : 128 * s + 128
                ].astype(f32)

    def whole_chunk(i, table_ref):
        return (0, 0)

    return pl.pallas_call(
        body,
        grid_spec=pltpu.PrefetchScalarGridSpec(
            num_scalar_prefetch=1,
            grid=(count,),
            in_specs=[SMEM] + [pl.BlockSpec(t.shape, whole_chunk)] * 2 + [ANY] * len(old),
            out_specs=pl.BlockSpec((rows, 256), lambda i, table_ref: (0, table_ref[count + i])),
        ),
        out_shape=jax.ShapeDtypeStruct(shape, f32),
        input_output_aliases={4: 0} if old else {},
        compiler_params=params(),
        cost_estimate=cost(0, 8 * rows * 256 * count),
        name="finish_projection",
    )(table, ids, t, last, *old)


def finish_feed_forward(blocks):
    chips, rows, n = blocks.shape
    wide = n // 2

    def body(x_ref, o_ref):
        which = pl.program_id(1)
        for s in range(2):

            @pl.when(which == s)
            def _():
                for at in range(0, wide, 128):
                    start = 2 * at + 128 * s
                    o_ref[:, at : at + 128] = x_ref[0, :, start : start + 128].astype(f32)

    return pl.pallas_call(
        body,
        grid=(chips, 2),
        in_specs=[pl.BlockSpec((1, rows, n), lambda c, s: (c, 0, 0))],
        out_specs=pl.BlockSpec((rows, wide), lambda c, s: (0, s * chips + c)),
        out_shape=jax.ShapeDtypeStruct((rows, chips * n), f32),
        compiler_params=params(),
        cost_estimate=cost(0, 6 * chips * rows * n),
        name="finish_feed_forward",
    )(blocks)


def fill_rows(w_ref, own_ref, other_ref, core, chip=0):
    planes, chips, rows, _ = own_ref.shape
    for z in range(planes):
        for j in range(chips):
            c = jnp.bitwise_xor(chip, j)
            for ref, k in ((own_ref, core), (other_ref, 1 - core)):
                at = pl.multiple_of((2 * c + k) * planes * rows + z * rows, rows)
                w_ref[pl.ds(at, rows), :] = ref[z, j]


def project_planes(x, own, other, ids):
    tokens, k = x.shape
    planes, chips, rows, n = own.shape
    tile = 256

    def body(ids_ref, x_ref, own_ref, other_ref, o_ref, w_ref):
        fill_rows(w_ref, own_ref, other_ref, ids_ref[1], ids_ref[0])
        o_ref[...] = jnp.dot(x_ref[...], w_ref[...], preferred_element_type=f32)

    return pl.pallas_call(
        body,
        grid=(pl.cdiv(n, tile),),
        in_specs=[SMEM, pl.BlockSpec((tokens, k), lambda i: (0, 0))]
        + [pl.BlockSpec((planes, chips, rows, tile), lambda i: (0, 0, 0, i))] * 2,
        out_specs=pl.BlockSpec((tokens, tile), lambda i: (0, i)),
        out_shape=jax.ShapeDtypeStruct((tokens, n), f32),
        scratch_shapes=[pltpu.VMEM((k, tile), bf16)],
        compiler_params=params(),
        cost_estimate=cost(2 * tokens * k * n, 2 * tokens * k + 2 * k * n + 4 * tokens * n),
        name="project",
    )(ids, x, own, other)


def project(x, own, other, ids):
    tokens, k = x.shape
    rows, n = own[0].shape
    chips = len(own)
    tile = 256

    def body(ids_ref, x_ref, *refs):
        o_ref, w_ref = refs[2 * chips :]
        for j in range(chips):
            c = jnp.bitwise_xor(ids_ref[0], j)
            for ref, core in ((refs[j], ids_ref[1]), (refs[chips + j], 1 - ids_ref[1])):
                at = pl.multiple_of((2 * c + core) * rows, rows)
                w_ref[pl.ds(at, rows), :] = ref[...]
        o_ref[...] = jnp.dot(x_ref[...], w_ref[...], preferred_element_type=f32)

    return pl.pallas_call(
        body,
        grid=(pl.cdiv(n, tile),),
        in_specs=[SMEM, pl.BlockSpec((tokens, k), lambda i: (0, 0))]
        + [pl.BlockSpec((rows, tile), lambda i: (0, i))] * (2 * chips),
        out_specs=pl.BlockSpec((tokens, tile), lambda i: (0, i)),
        out_shape=jax.ShapeDtypeStruct((tokens, n), f32),
        scratch_shapes=[pltpu.VMEM((k, tile), bf16)],
        compiler_params=params(),
        cost_estimate=cost(2 * tokens * k * n, 2 * tokens * k + 2 * k * n + 4 * tokens * n),
        name="project",
    )(ids, x, *own, *other)


def feed_forward(x, own, other, down, d_ffn, ids):
    tokens, k = x.shape
    planes, chips, rows, n = own.shape
    wide = n // 2
    tile = 512

    def body(ids_ref, x_ref, own_ref, other_ref, down_ref, d_ref, h_ref, g_ref, w_ref):
        fill_rows(w_ref, own_ref, other_ref, ids_ref[1])
        for m in range(0, tokens, 256):
            rows_at = slice(m, m + 256)
            both = jnp.dot(x_ref[rows_at, :], w_ref[...], preferred_element_type=f32)
            d_hidden = mm_nt(d_ref[rows_at, :], down_ref[...])
            for s in range(tile // 256):
                gate = both[:, 256 * s : 256 * s + 128]
                up = both[:, 256 * s + 128 : 256 * s + 256]
                dh = d_hidden[:, 128 * s : 128 * s + 128]
                sig = jax.nn.sigmoid(gate)
                act = gate * sig
                h_ref[rows_at, 128 * s : 128 * s + 128] = (act * up).astype(bf16)
                g_ref[rows_at, 256 * s : 256 * s + 128] = (
                    dh * up * (sig * (1.0 + gate * (1.0 - sig)))
                ).astype(bf16)
                g_ref[rows_at, 256 * s + 128 : 256 * s + 256] = (dh * act).astype(bf16)

    return pl.pallas_call(
        body,
        grid=(pl.cdiv(n, tile),),
        in_specs=[
            SMEM,
            pl.BlockSpec((tokens, k), lambda i: (0, 0)),
            pl.BlockSpec((planes, chips, rows, tile), lambda i: (0, 0, 0, i)),
            pl.BlockSpec((planes, chips, rows, tile), lambda i: (0, 0, 0, i)),
            pl.BlockSpec((tile // 2, k), lambda i: (i, 0)),
            pl.BlockSpec((tokens, k), lambda i: (0, 0)),
        ],
        out_specs=[
            pl.BlockSpec((tokens, tile // 2), lambda i: (0, i)),
            pl.BlockSpec((tokens, tile), lambda i: (0, i)),
        ],
        out_shape=[
            jax.ShapeDtypeStruct((tokens, wide), bf16),
            jax.ShapeDtypeStruct((tokens, n), bf16),
        ],
        scratch_shapes=[pltpu.VMEM((k, tile), bf16)],
        compiler_params=params(),
        cost_estimate=cost(3 * tokens * k * n, 4 * tokens * k + 3 * k * n + 3 * tokens * n),
        name="feed_forward",
    )(ids, x, own, other, down, d_ffn)


def halves_of(i, tiles):
    half = tiles // 2
    return jnp.minimum(i, half - 1), jnp.maximum(i - half, 0)


def scatter_outputs(tokens, n, tile, refs=None):
    size = tokens // 2
    tiles = n // tile
    first = pl.BlockSpec((size, tile), lambda i, *ids: (0, halves_of(i, tiles)[0]))
    second = pl.BlockSpec((size, tile), lambda i, *ids: (0, halves_of(i, tiles)[1]))
    return [first, first, second, second], [jax.ShapeDtypeStruct((size, n // 2), bf16)] * 4


def write_scattered(outs, total_ref, tiles):
    size = total_ref.shape[0] // 4
    i = pl.program_id(0)

    for half, rows in ((0, ((1, 3), (0, 2))), (1, ((2, 3), (0, 1)))):

        @pl.when((i < tiles // 2) if half == 0 else (i >= tiles // 2))
        def _():
            for out, chips in zip(outs[2 * half : 2 * half + 2], rows):
                for n, m in enumerate(chips):
                    out[n * size : (n + 1) * size, :] = total_ref[m * size : (m + 1) * size, :]


def times_rows(lefts, mine, theirs, ids):
    tokens = lefts[0].shape[0]
    half, n = mine.shape
    tile = 256
    specs, shapes = scatter_outputs(tokens, n, tile)

    def body(ids_ref, *refs):
        left_refs = refs[: len(lefts)]
        mine_ref, theirs_ref = refs[len(lefts) : len(lefts) + 2]
        outs = refs[len(lefts) + 2 : -2]
        right_ref, total_ref = refs[-2:]
        core = ids_ref[1]
        right_ref[pl.ds(pl.multiple_of(core * half, 16), half), :] = mine_ref[...]
        right_ref[pl.ds(pl.multiple_of((1 - core) * half, 16), half), :] = theirs_ref[...]
        total = None
        at = 0
        for ref in left_refs:
            width = ref.shape[1]
            term = jnp.dot(ref[...], right_ref[at : at + width, :], preferred_element_type=f32)
            total = term if total is None else total + term
            at += width
        total_ref[...] = total.astype(bf16)
        write_scattered(outs, total_ref, n // tile)

    return pl.pallas_call(
        body,
        grid=(n // tile,),
        in_specs=[SMEM]
        + [pl.BlockSpec(a.shape, lambda i: (0, 0)) for a in lefts]
        + [pl.BlockSpec((half, tile), lambda i: (0, i))] * 2,
        out_specs=specs,
        out_shape=shapes,
        scratch_shapes=[pltpu.VMEM((2 * half, tile), bf16), pltpu.VMEM((tokens, tile), bf16)],
        compiler_params=params(),
        cost_estimate=cost(4 * tokens * half * n, 2 * (tokens * half + half * n + tokens * n)),
        name="times_rows",
    )(ids, *lefts, mine, theirs)


def times_transposed(pairs, ids, relative):
    tokens = pairs[0][0].shape[0]
    planes, chips, rows, _ = pairs[0][1].shape
    rows *= planes
    total_n = sum(left.shape[1] for left, own, other in pairs)
    k = 2 * chips * rows
    specs_out, shapes = scatter_outputs(tokens, k, rows)

    def body(ids_ref, *refs):
        count = len(pairs)
        outs = refs[3 * count : 3 * count + 4]
        piece_refs = refs[3 * count + 4 : -1]
        total_ref = refs[-1]
        mine = pl.program_id(0) % 2 == ids_ref[1]

        def choose(which):
            for n in range(count):
                piece = refs[3 * n + which][:, 0]
                piece_refs[n][...] = piece.reshape(rows, piece.shape[2])

        @pl.when(mine)
        def _():
            choose(1)

        @pl.when(jnp.logical_not(mine))
        def _():
            choose(2)

        total = None
        for n in range(count):
            term = mm_nt(refs[3 * n][...], piece_refs[n][...])
            total = term if total is None else total + term
        total_ref[...] = total.astype(bf16)
        write_scattered(outs, total_ref, 2 * chips)

    def piece_at(i, ids_ref):
        c = lax.div(i, 2)
        if relative:
            c = jnp.bitwise_xor(c, ids_ref[0])
        return (0, c, 0, 0)

    specs = []
    args = []
    for left, own, other in pairs:
        specs.append(pl.BlockSpec(left.shape, lambda i, ids_ref: (0, 0)))
        block = (own.shape[0], 1) + own.shape[2:]
        specs += [pl.BlockSpec(block, piece_at)] * 2
        args += [left, own, other]
    return pl.pallas_call(
        body,
        grid_spec=pltpu.PrefetchScalarGridSpec(
            num_scalar_prefetch=1,
            grid=(2 * chips,),
            in_specs=specs,
            out_specs=specs_out,
            scratch_shapes=[pltpu.VMEM((rows, own.shape[3]), bf16) for _, own, _ in pairs]
            + [pltpu.VMEM((tokens, rows), bf16)],
        ),
        out_shape=shapes,
        compiler_params=params(),
        cost_estimate=cost(
            2 * tokens * k * total_n, 2 * (tokens * k + k * total_n + tokens * total_n)
        ),
        name="times_transposed",
    )(ids, *args)


STREAM = 2048


def pack_bands(value, out, rows, tiles):
    for t in range(tiles):
        for s in range(rows // 16):
            out[16 * t : 16 * t + 16, 128 * s : 128 * s + 128] = value[
                16 * s : 16 * s + 16, 128 * t : 128 * t + 128
            ]


def column_terms(lefts, rights, ids, split):
    tokens, k = lefts[0].shape
    n = rights[0].shape[1]
    chips = 4
    rows = k // (2 * chips)
    tiles = n // 128

    def body(ids_ref, a_ref, b_ref, ra_ref, rb_ref, *refs):
        total_ref = refs[-1]
        total = mm_tn(a_ref[...], ra_ref[...]) + mm_tn(b_ref[...], rb_ref[...])
        if not split:
            total_ref[...] = total.astype(bf16)
            pack_bands(total_ref, refs[0].at[0], rows, tiles)
            return
        total_ref[...] = total.astype(bf16)
        for c in range(chips):

            @pl.when(pl.program_id(0) == c)
            def _():
                pack_bands(total_ref, refs[c], rows, tiles)

    def column(i, ids_ref):
        return (0, 2 * i + ids_ref[1])

    def whole(i, ids_ref):
        return (0, 0)

    if split:
        out_specs = [pl.BlockSpec((16 * tiles, STREAM), whole)] * chips
        out_shape = [jax.ShapeDtypeStruct((16 * tiles, STREAM), bf16)] * chips
    else:
        out_specs = pl.BlockSpec((1, 16 * tiles, STREAM), lambda i, ids_ref: (i, 0, 0))
        out_shape = jax.ShapeDtypeStruct((chips, 16 * tiles, STREAM), bf16)
    return pl.pallas_call(
        body,
        grid_spec=pltpu.PrefetchScalarGridSpec(
            num_scalar_prefetch=1,
            grid=(chips,),
            in_specs=[pl.BlockSpec((tokens, rows), column)] * 2
            + [pl.BlockSpec((tokens, n), whole)] * 2,
            out_specs=out_specs,
            scratch_shapes=[pltpu.VMEM((rows, n), bf16)],
        ),
        out_shape=out_shape,
        compiler_params=params(),
        cost_estimate=cost(2 * tokens * k * n, 4 * (tokens * k + tokens * n + k * n)),
        name="column_terms",
    )(ids, *lefts, *rights)


def row_terms(lefts, right, ids, in_order=False):
    tokens, n = right.shape
    k = sum(a.shape[1] for a in lefts)
    tile = 512
    half = k // 2

    def body(ids_ref, *refs):
        left_refs = refs[: len(lefts)]
        right_ref, mine_ref, theirs_ref, acc = refs[len(lefts) :]
        core = ids_ref[1]
        at = 0
        for ref in left_refs:
            width = ref.shape[1]
            if not in_order:
                acc[at : at + width, :] = mm_tn(ref[...], right_ref[...])
            else:
                total = None
                size = tokens // 4
                for m in range(4):
                    chip = jnp.bitwise_xor(ids_ref[0], m)
                    rows = right_ref[pl.ds(pl.multiple_of(chip * size, size), size), :]
                    term = mm_tn(ref[m * size : (m + 1) * size, :], rows)
                    total = term if total is None else total + term
                acc[at : at + width, :] = total
            at += width
        mine_ref[...] = acc[pl.ds(pl.multiple_of(core * half, 16), half), :].astype(bf16)
        theirs_ref[...] = acc[pl.ds(pl.multiple_of((1 - core) * half, 16), half), :].astype(bf16)

    out = pl.BlockSpec((half, tile), lambda i: (0, i))
    return pl.pallas_call(
        body,
        grid=(n // tile,),
        in_specs=[SMEM]
        + [pl.BlockSpec(a.shape, lambda i: (0, 0)) for a in lefts]
        + [pl.BlockSpec((tokens, tile), lambda i: (0, i))],
        out_specs=[out, out],
        out_shape=[jax.ShapeDtypeStruct((half, n), bf16)] * 2,
        scratch_shapes=[pltpu.VMEM((k, tile), f32)],
        compiler_params=params(),
        cost_estimate=cost(2 * tokens * k * n, 2 * (tokens * k + tokens * n + k * n)),
        name="row_terms",
    )(ids, *lefts, right)


def after(values, *earlier):
    if not earlier:
        return values
    return lax.optimization_barrier((values, earlier))[0]


def to_chip(a, nf, j):
    return lax.ppermute(a, "fsdp", [(i, i ^ (2 * j)) for i in range(nf)])


def swap_core(a, nf):
    return lax.ppermute(a, "fsdp", [(i, i ^ 1) for i in range(nf)])


RIGHT = [(0, 1), (1, 2), (2, 3)]
LEFT = [(1, 0), (2, 1), (3, 2)]
INWARD = [(0, 1), (3, 2)]
MIDDLE = [(1, 2), (2, 1)]
OUTWARD = [(1, 0), (2, 3)]
SWAP = [(0, 1), (1, 0), (2, 3), (3, 2)]


def along(a, pairs):
    return lax.ppermute(a, "rep", pairs)


def add16(a, b):
    return (a.astype(f32) + b.astype(f32)).astype(bf16)


def gather_small(a, nf):
    me = lax.axis_index("fsdp")
    out = a[None]
    bit = 1
    while bit < nf:
        other = lax.ppermute(out, "fsdp", [(i, i ^ bit) for i in range(nf)])
        upper = (me & bit) != 0
        out = jnp.concatenate(
            [jnp.where(upper, other, out), jnp.where(upper, out, other)], axis=0
        )
        bit *= 2
    return out


def sum_small(a, nf):
    me = lax.axis_index("fsdp")
    bit = nf // 2
    while bit:
        half = a.shape[0] // 2
        upper = (me & bit) != 0
        keep = jnp.where(upper, a[half:], a[:half])
        send = jnp.where(upper, a[:half], a[half:])
        got = lax.ppermute(send, "fsdp", [(i, i ^ bit) for i in range(nf)])
        a = keep + got
        bit //= 2
    return a[0], got


def sum_line(a):
    z = lax.axis_index("rep")
    a = a + along(a, INWARD)
    a = a + along(a, MIDDLE)
    return jnp.where(jnp.logical_or(z == 1, z == 2), a, along(a, OUTWARD))


class Line:
    def __init__(self, nz, ids):
        self.nz = nz
        self.ids = ids
        self.tokens = ()
        self.first = None
        self.second = None

    def step(self, new, *earlier):
        if self.nz != 4:
            return new and (new[0], (lax.psum(new[1], "rep"),) * 2)
        chunk = None if new is None else new[1]
        first = (None, None) if self.first is None else self.first[1:]
        second = (None, None) if self.second is None else self.second[1:]
        chunk, first, second, _, _ = lax.optimization_barrier(
            (chunk, first, second, self.tokens, earlier)
        )
        finished = next_first = next_second = None
        tokens = []
        values = []
        if self.first is not None or self.second is not None:
            if chunk is not None and self.second is None:
                values = [chunk] + line_values(self.ids, *first, None, None, None)
            else:
                values = line_values(self.ids, *first, *second, chunk)
        elif chunk is not None:
            values = [chunk]
        if chunk is not None or self.second is not None:
            got = along(values[0], OUTWARD if chunk is None else SWAP)
            tokens.append(got)
            if self.second is not None:
                finished = (self.second[0], (values[0], got))
            if chunk is not None:
                next_first = (new[0], chunk, got)
        if self.first is not None:
            met = along(values[-1], MIDDLE)
            tokens.append(met)
            next_second = (self.first[0], values[-1], met)
        self.first, self.second, self.tokens = next_first, next_second, tuple(tokens)
        self.sent = tuple(values)
        return finished


class Overlapped:
    def __init__(self, nz, ids):
        self.nz = nz
        self.ids = ids
        self.value = None
        self.new = None
        self.total = None
        self.inward = None
        self.met = []
        self.got = self.arriving = ()
        self.sent = ()
        self.done = {}

    def prepare(self, new, *earlier):
        if self.nz != 4:
            if new:
                self.done[new[0]] = (lax.psum(new[1], "rep"),) * 2
            return
        chunk = new and new[1]
        pair = (None, None)
        self.total = None
        if len(self.met) > 1 or (self.met and new is None):
            self.total, *pair = self.met.pop(0)
        chunk, pair, _ = lax.optimization_barrier((chunk, tuple(pair), (self.sent, earlier)))
        self.new = new and (new[0], chunk)
        self.value = chunk
        if self.total is not None:
            self.value = line_values(self.ids, None, None, *pair, chunk)[0]
            self.sent = self.value

    def step(self, *earlier):
        if self.nz != 4:
            return
        before = self.inward
        if self.value is not None:
            value = after(self.value, self.sent, self.got, earlier)
            got = along(value, OUTWARD if self.new is None else SWAP)
            self.got = got
            if self.total is not None:
                self.done[self.total] = (value, got)
        self.inward = self.new and (self.new[0], self.new[1], got)
        if before is not None:
            name, *pair = before
            pair = after(tuple(pair), self.sent, earlier)
            value = line_values(self.ids, *pair, None, None, None)[0]
            self.sent = (value,) + tuple(pair[2] for pair in self.met[-1:])
            self.met.append((name, value, along(value, MIDDLE)))
            self.arriving = (self.got, self.met[-1][2])


def gather_first(a, nf, *earlier):
    chips = nf // 2
    a = after(a, *earlier)
    if chips != 4:
        return [a] + [to_chip(a, nf, j) for j in range(1, chips)]
    return [a, to_chip(a, nf, 1), to_chip(a, nf, 2)]


def gather_second(parts, nf, *earlier):
    if nf != 8:
        return jnp.concatenate(parts, axis=0)
    a, one, two = parts
    half = a.shape[0] // 2
    low, high = after((one[:half], two[half:]), *earlier)
    return jnp.concatenate([a, one, two, to_chip(low, nf, 2), to_chip(high, nf, 1)], axis=0)


def scatter_first(a, nf, *earlier):
    chips = nf // 2
    n = a.shape[0] // chips
    parts = [a[j * n : (j + 1) * n] for j in range(chips)]
    if chips != 4:
        return [parts[0]] + [to_chip(parts[j], nf, j) for j in range(1, chips)]
    half = n // 2
    low, high, one, two = after(
        (parts[3][:half], parts[3][half:], parts[1][half:], parts[2][:half]), *earlier
    )
    low = to_chip(low, nf, 2)
    high = to_chip(high, nf, 1)
    one = to_chip(one, nf, 1)
    two = to_chip(two, nf, 2)
    return [
        parts[0],
        one,
        two,
        add16(parts[1][:half], low),
        add16(parts[2][half:], high),
    ]


def scatter_second(parts, nf, *earlier):
    if nf != 8:
        total = parts[0].astype(f32)
        for part in parts[1:]:
            total = total + part.astype(f32)
        return total
    own, one, two, one_low, two_high = parts
    one_low, two_high = after((one_low, two_high), *earlier)
    one_low = to_chip(one_low, nf, 1)
    two_high = to_chip(two_high, nf, 2)
    own = own.astype(f32)
    half = own.shape[0] // 2
    return jnp.concatenate(
        [
            own[:half] + one_low.astype(f32) + two.astype(f32),
            own[half:] + one.astype(f32) + two_high.astype(f32),
        ],
        axis=0,
    )


def rms_back(rows, r, gain, d_out):
    unit = rows * r
    d_unit = d_out * gain
    d_rows = r * (d_unit - unit * jnp.mean(d_unit * unit, axis=1, keepdims=True))
    return d_rows, jnp.sum(d_out * unit, axis=0)


def scale_of(rows):
    return lax.rsqrt(jnp.mean(rows * rows, axis=1, keepdims=True) + eps_norm)


def exchange(a, nf):
    groups = [[2 * c + k for c in range(nf // 2)] for k in range(2)]
    return lax.all_to_all(a, "fsdp", 0, 0, axis_index_groups=groups, tiled=True)


def column_blocks(w, widths, chips, groups, p):
    rows = w.shape[0]
    start = 0
    parts = []
    for width in widths:
        part = w[:, start : start + width].reshape(rows, chips, groups, width // (chips * groups))
        parts.append(part[:, :, p].transpose(1, 0, 2))
        start += width
    return jnp.concatenate(parts, axis=2)


def from_column_blocks(blocks, widths):
    chips, rows, _ = blocks.shape
    parts = []
    at = 0
    for width in widths:
        part = blocks[:, :, at : at + width // chips]
        parts.append(part.transpose(1, 0, 2).reshape(rows, width))
        at += width // chips
    return parts


def both_core_rows(own, nf):
    core = lax.axis_index("fsdp") % 2
    other = swap_core(own, nf)
    first = core == 0
    chips, rows, width = own.shape
    both = jnp.stack([jnp.where(first, own, other), jnp.where(first, other, own)], axis=1)
    return both.reshape(chips * 2 * rows, width)


def core_half(x, chips, which):
    tokens, width = x.shape
    x = x.reshape(tokens, chips, 2, width // (2 * chips))
    x = lax.dynamic_index_in_dim(x, which, 2, keepdims=False)
    return x.reshape(tokens, width // 2)


def column_gradient(left, right, nf, *earlier):
    core = lax.axis_index("fsdp") % 2
    chips = nf // 2
    theirs = mm_tn(core_half(left, chips, 1 - core), right).astype(bf16)
    got = swap_core(theirs, nf)
    mine = mm_tn(core_half(left, chips, core), right) + got.astype(f32)
    return mine.astype(bf16).reshape(chips, -1, right.shape[1])


def both_cores(w, nf, *earlier):
    core = lax.axis_index("fsdp") % 2
    other = swap_core(after(w, *earlier), nf)
    first = core == 0
    return jnp.concatenate([jnp.where(first, w, other), jnp.where(first, other, w)], axis=0)


def halves(a):
    core = lax.axis_index("fsdp") % 2
    rows = a.shape[0] // 2
    mine = lax.dynamic_slice(a, (core * rows, 0), (rows, a.shape[1]))
    theirs = lax.dynamic_slice(a, ((1 - core) * rows, 0), (rows, a.shape[1]))
    return mine, theirs


def sum_cores(a, nf):
    mine, theirs = halves(a)
    return add16(mine, swap_core(theirs, nf))


def as_rows(a):
    flat = a.reshape(-1)
    return jnp.pad(flat, (0, -flat.shape[0] % 128)).reshape(-1, 128)


def gather_pieces(parts, nf, *earlier):
    a, one, two = parts
    half = a.shape[0] // 2
    low, high = after((one[:half], two[half:]), *earlier)
    return [a, one, two, to_chip(low, nf, 2), to_chip(high, nf, 1)]


def scatter_start(parts, nf, *earlier):
    over_x, over_y = after((parts[0], parts[2]), *earlier)
    return [parts[1], to_chip(over_x, nf, 1), parts[3], to_chip(over_y, nf, 2)]


def scatter_middle(parts, nf, *earlier):
    stay_x, got_x, stay_y, got_y = after(parts, *earlier)
    over_y, over_x = scatter_add(stay_x, got_x, stay_y, got_y)
    return [stay_x, got_x, to_chip(over_y, nf, 2), stay_y, got_y, to_chip(over_x, nf, 1)]


def scatter_end(parts):
    size = parts[2].shape[0]
    parts = [p[:size].astype(f32) for p in parts]
    return jnp.concatenate([sum(parts[:3]), sum(parts[3:])], axis=1)


def local_fast(
    tokens,
    cotangent,
    lengths,
    slot_owner,
    gain_in,
    w_proj,
    w_decay,
    conv_weight,
    a_log,
    dt_bias,
    o_gain,
    w_out,
    gain_mid,
    w_gate_up,
    w_down,
    *,
    nf,
    nz,
):
    chips = nf // 2
    hl = H // chips
    pair = 2
    groups = hl // pair
    me = lax.axis_index("fsdp")
    rep = lax.axis_index("rep")
    held = jnp.sum(jnp.where(slot_owner == rep * nf + me, lengths, 0))
    ids = jnp.stack([me // 2, me % 2, rep, held]).astype(jnp.int32)
    shard = gain_in.shape[0]
    conv_shard = conv_weight.shape[1]
    hv = w_out.shape[0] * nf
    hk = (conv_shard * nf - hv) // 2
    ff = w_down.shape[0] * nf
    wide = ff // chips
    qk, vv = pair * DK, pair * DV
    span = 2 * qk + 2 * vv
    proj_widths = (hk, hk, hv, hv)

    def proj_table(p):
        table = []
        for c in range(chips):
            at = c * groups + p
            table.append(
                [
                    (at * qk, qk),
                    (hk + at * qk, qk),
                    (2 * hk + at * vv, vv),
                    (2 * hk + hv + at * vv, vv),
                ]
            )
        return table

    up_table = [
        [(s * ff + c * wide + at, 128) for at in range(0, wide, 128) for s in range(2)]
        for c in range(chips)
    ]
    plane = shard // nz

    vectors = [v.reshape(1, -1) for v in (gain_in, gain_mid, o_gain, a_log, dt_bias)]
    sizes = [v.shape[1] for v in vectors]
    small = lax.all_to_all(pack_small(conv_weight, vectors, nf), "fsdp", 0, 0, tiled=True)
    decay_pad = jnp.pad(w_decay, ((0, 0), (0, 128 - 2 * H)))
    plane_rows = pack_relative(w_proj, decay_pad, proj_table(0), True, ids)
    packed = pack_relative(w_proj, None, proj_table(1), False, ids)

    def spread(own, *earlier):
        sends = after(own[1:], *earlier)
        return [own[0]] + [to_chip(a, nf, j + 1) for j, a in enumerate(sends)]

    def swap_all(own, *earlier):
        return [swap_core(a, nf) for a in after(own, *earlier)]

    out_other = swap_core(w_out, nf)
    down_other = swap_core(w_down, nf)
    first_rows = spread(plane_rows)
    first = jnp.stack(after(first_rows, packed))
    tok = gather_first(tokens, nf, small, first_rows, out_other, down_other)
    sends = after(packed[1:], first_rows, out_other, down_other)
    own = [packed[0], to_chip(sends[0], nf, 1), to_chip(sends[1], nf, 2)]
    first = lax.all_gather(first, "rep", axis=0)
    gains, head_rows, gain_row, *conv_pair = unpack_small(small, sizes, ids, hk, qk, vv, groups)
    tok = gather_pieces(tok, nf, gains)
    own.append(to_chip(after(sends[2], tok[3:]), nf, 3))
    up_plane = pack_columns(after(w_gate_up, packed), None, up_table, plane, True, ids)

    live_own = (jnp.arange(TOK_DEV, dtype=jnp.int32) < held).astype(f32)[:, None]
    seeded = cotangent.astype(f32) * live_own
    d_ffn_own = seeded.astype(bf16)

    normed_in = norm_rows(after(tok, d_ffn_own), gains)
    first_other = swap_core(after(first, normed_in, up_plane, own[1], own[2]), nf)
    up_plane = exchange(after(up_plane, own[3]), nf)
    own = stack_blocks(own)
    other = swap_core(own, nf)
    projected = [project_planes(after(normed_in, own), first, first_other, ids)]

    def forward(p, *before):
        return mixer_forward(
            ids, after(projected[p], *before), projected[0], conv_pair[p], head_rows, gain_row,
            hl, pair, p,
        )

    gated0, *saved0 = forward(0, other)
    up_own = lax.all_gather(after(up_plane, gated0), "rep", axis=0)
    sends = after(d_ffn_own, gated0, up_plane)
    ffn_parts = [d_ffn_own] + [to_chip(sends, nf, j) for j in range(1, chips)]
    projected.append(project_planes(after(normed_in, gated0), own, other, ids))
    gated1, *saved1 = forward(1)
    gated = [gated0, gated1]
    saved = [saved0, saved1]
    branch_parts = scatter_start(times_rows(gated, w_out, out_other, ids), nf)
    d_ffn = jnp.concatenate(after(ffn_parts, branch_parts[0]), axis=0)
    pieces_in = [(first, first_other), (own, other)]
    down_chip = join_cores(w_down, after(down_other, branch_parts[0]), ids)
    out_chip = join_cores(w_out, after(out_other, branch_parts[0]), ids)
    branch_parts = scatter_middle(branch_parts, nf, d_ffn, down_chip, out_chip)

    middle, normed_own = middle_rows(branch_parts, tokens, gains, ids)
    normed_mid = gather_first(normed_own, nf)
    up_own = after(up_own, normed_mid)
    up_other = swap_core(up_own, nf)
    in_other = swap_core(after(normed_in, up_other), nf)
    normed_mid = jnp.concatenate(gather_pieces(normed_mid, nf), axis=0)
    hidden, d_gate_up = feed_forward(normed_mid, up_own, up_other, down_chip, d_ffn, ids)

    line = Overlapped(nz, ids)
    done = line.done

    d_up_other = swap_core(d_gate_up, nf)
    mid_other = swap_core(normed_mid, nf)
    mine, theirs = row_terms([hidden], after(d_ffn, mid_other), ids)
    theirs = swap_core(theirs, nf)
    half = mine.shape[0] // 2
    down0 = mine[:half] + theirs[:half]
    down1 = mine[half:] + theirs[half:]
    line.prepare(("down0", down0), down1)
    line.step()
    partial_mid = times_transposed(
        [(after(d_gate_up, down0, down1, d_up_other), up_own, up_other)], ids, False
    )
    mid_parts = scatter_start(partial_mid, nf)
    partial_ffn = times_rows(after([hidden], partial_mid), w_down, down_other, ids)
    line.prepare(("down1", down1), partial_ffn)
    line.step()
    mid_parts = scatter_middle(mid_parts, nf, line.sent)
    grad_up = column_terms(
        [normed_mid, mid_other],
        [after(d_gate_up, line.sent, mid_parts[0]), d_up_other],
        ids,
        True,
    )
    line.prepare(("up0", grad_up[0]))
    line.step(grad_up[0])
    d_middle, d_branch_own, g_gain_mid = middle_back(
        after(mid_parts, line.sent), middle, cotangent, gains, ids
    )
    branch_parts = gather_first(d_branch_own, nf)
    d_branch = gather_pieces(branch_parts, nf, line.sent)
    line.prepare(("up1", grad_up[1]), branch_parts)
    line.step()
    line.prepare(("up2", grad_up[2]))
    d_branch = jnp.concatenate(after(d_branch, line.sent), axis=0)
    d_gated = [mm_nt(d_branch, out_chip[p * vv : (p + 1) * vv]) for p in range(groups)]

    def backward(p, *before, more=None):
        return mixer_backward(
            ids, projected[p], projected[0], conv_pair[p], head_rows, gain_row, saved[p],
            after(d_gated[p], *before), hl, pair, p, more,
        )

    d_x1, d_dec, g_conv1, g_heads1 = backward(1, line.sent)
    arriving = line.arriving
    line.step(d_x1)
    line.prepare(("up3", grad_up[3]))
    d_x1_other = swap_core(after(d_x1, arriving), nf)
    mine, theirs = row_terms(gated, after(d_branch, line.sent), ids)
    half = mine.shape[0] // 2
    theirs = [swap_core(theirs[:half], nf), swap_core(theirs[half:], nf)]
    cols1 = column_terms([normed_in, in_other], [after(d_x1, mine), d_x1_other], ids, False)
    cols1_all = exchange(after(cols1, line.arriving), nf)
    grad_out = mine + jnp.concatenate(after(theirs, cols1), axis=0)
    line.step(cols1)
    d_x0, dec, g_conv0, g_heads0 = backward(0, line.sent, theirs, more=d_dec)
    arriving = line.arriving
    size = down0.shape[0]
    rest = grad_out.shape[0] - size
    line.prepare(("out0", grad_out[:size]), d_x0)
    line.step()
    d_x0_other = swap_core(after(d_x0, arriving, cols1_all), nf)
    cols0 = column_terms([normed_in, in_other], [after(d_x0, line.sent), d_x0_other], ids, False)
    bands0_all = exchange(after(cols0, line.arriving), nf)
    bands1 = cols1_all.reshape(-1, STREAM)
    at1 = size - rest
    line.prepare(("mix0", jnp.concatenate([grad_out[size:], bands1[:at1]], axis=0)), cols0)
    line.step()
    line.prepare(("p1", bands1[at1 : at1 + size]))
    right = [d_x0, d_x1]
    partial_in = times_transposed(
        [(after(right[p], line.sent),) + pieces_in[p] for p in range(groups)], ids, True
    )
    line.step(partial_in)
    bands0 = bands0_all.reshape(-1, STREAM)
    at1 += size
    left = bands1.shape[0] - at1
    at0 = size - left
    in_first = scatter_start(partial_in, nf, line.sent)
    grad_up = None
    for j in range(3):
        grad_up = place_blocks(
            grad_up, after(done["up%d" % j], line.sent), ids, j, (chips, shard, 2 * wide)
        )
    line.prepare(("mix1", jnp.concatenate([bands1[at1:], bands0[:at0]], axis=0)), grad_up)
    line.step()
    line.prepare(("p0", bands0[at0 : at0 + size]))
    in_sends = scatter_middle(in_first, nf, line.sent)
    grad_up = place_blocks(
        grad_up, after(done["up3"], line.sent, in_sends[0]), ids, 3, (chips, shard, 2 * wide)
    )
    arriving = line.arriving
    line.step(grad_up)
    line.prepare(("p0last", bands0[at0 + size :]))
    grad_up_all = exchange(after(grad_up, arriving, in_sends[2], in_sends[5]), nf)
    ffn_first = scatter_start(partial_ffn, nf, grad_up_all)
    grad_tokens, g_gain_in = tokens_back(after(in_sends, line.sent), tokens, d_middle, gains)
    blocks = pack_small_grads(
        [g_conv0, g_conv1],
        [g_heads0, g_heads1],
        g_gain_in,
        g_gain_mid,
        sizes,
        ids,
        nf,
        conv_shard,
        hk,
        qk,
        vv,
    )
    line.step(blocks)
    line.prepare(None)
    def tile_of(p, c, t):
        at = c * groups + p
        q_tiles, v_tiles = qk // 128, vv // 128
        if t < q_tiles:
            return at * q_tiles + t
        if t < 2 * q_tiles:
            return hk // 128 + at * q_tiles + t - q_tiles
        if t < 2 * q_tiles + v_tiles:
            return 2 * hk // 128 + at * v_tiles + t - 2 * q_tiles
        return (2 * hk + hv) // 128 + at * v_tiles + t - 2 * q_tiles - v_tiles

    each = span // 128
    bands = [(1, c, t) for c in range(chips) for t in range(each)]
    bands += [(0, c, t) for c in range(chips) for t in range(each + 1)]
    slots = [("mix0", n) for n in range(rest // 16, size // 16)]
    slots += [("p1", n) for n in range(size // 16)]
    slots += [("mix1", n) for n in range(size // 16)]
    slots += [("p0", n) for n in range(size // 16)]
    slots += [("p0last", n) for n in range(size // 16)]
    where = dict(zip(bands, slots))

    def place(grad_proj, name, *before):
        pairs = [
            (where[key][1], tile_of(*key))
            for key in bands
            if where[key][0] == name and key[2] < each and key[2] % 2 == 0
        ]
        return finish_projection(grad_proj, after(done[name], *before), ids, pairs, w_proj.shape)

    grad_proj = place(None, "mix0", line.sent)
    line.step(grad_proj)
    line.prepare(None)
    grad_up = finish_feed_forward(after(grad_up_all, line.sent))
    ffn_sends = scatter_middle(ffn_first, nf, grad_up)
    line.step(grad_up)
    line.prepare(None)
    grad_proj = place(grad_proj, "p1", line.sent)
    grad_proj = place(grad_proj, "mix1", line.sent)
    small_sum = lax.all_to_all(after(blocks, ffn_sends[2], ffn_sends[5]), "fsdp", 0, 0, tiled=True)
    output = (middle + live_own * scatter_end(after(ffn_sends, grad_proj))).astype(bf16)
    line.step(grad_proj, output)
    small_sum = lax.all_gather(jnp.sum(after(small_sum, line.sent), axis=0), "rep", axis=0)
    grad_proj = place(grad_proj, "p0", line.sent)
    small_sum = jnp.sum(small_sum, axis=0)
    done["p0last"] = after(done["p0last"], grad_proj)
    grad_proj = place(grad_proj, "p0last")
    middle_two = jnp.logical_or(rep == 1, rep == 2)

    def pick(name):
        return jnp.where(middle_two, *done[name])

    tail = pick("p0last")
    summed = small_sum
    lanes, _ = small_layout(sizes)
    s_gain_in, s_gain_mid, s_ogain, s_alog, s_bias = (
        summed[KCONV, lane : lane + width] for lane, width in zip(lanes, sizes)
    )
    grad_decay = 0.0
    for c in range(chips):
        name, n = where[(0, c, each)]
        band = tail if name == "p0last" else pick(name)
        band = band[16 * n : 16 * n + 16].astype(f32).reshape(16, shard // 16, 128)
        grad_decay = grad_decay + band.transpose(1, 0, 2).reshape(shard, 128)
    grad_decay = grad_decay[:, : 2 * H]
    grad_down = jnp.concatenate([pick("down0"), pick("down1")], axis=0).astype(f32)
    grad_out = jnp.concatenate([pick("out0"), pick("mix0")[:rest]], axis=0).astype(f32)
    return (
        output,
        grad_tokens,
        s_gain_in,
        grad_proj,
        grad_decay,
        summed[:KCONV, :conv_shard],
        s_alog,
        s_bias,
        s_ogain,
        grad_out,
        s_gain_mid,
        grad_up,
        grad_down,
    )


def local_general(
    tokens,
    cotangent,
    lengths,
    slot_owner,
    gain_in,
    w_proj,
    w_decay,
    conv_weight,
    a_log,
    dt_bias,
    o_gain,
    w_out,
    gain_mid,
    w_gate_up,
    w_down,
    *,
    nf,
    nz,
):
    chips = nf // 2
    hl = H // chips
    pair = 2 if hl % 2 == 0 else 1
    groups = hl // pair
    me = lax.axis_index("fsdp")
    rep = lax.axis_index("rep")
    chip, core = me // 2, me % 2
    ids = jnp.stack([chip, core, rep, rep]).astype(jnp.int32)
    d_model = tokens.shape[1]
    shard = gain_in.shape[0]
    conv_shard = conv_weight.shape[1]
    channels = conv_shard * nf
    hv = w_out.shape[0] * nf
    hk = (channels - hv) // 2
    ff = w_down.shape[0] * nf
    wide = ff // chips
    qk, vv = pair * DK, pair * DV
    span = 2 * qk + 2 * vv
    proj_widths = (hk, hk, hv, hv)
    up_widths = (ff, ff)

    def proj_blocks(w, dec, p):
        blocks = column_blocks(w, proj_widths, chips, groups, p)
        if p:
            return blocks
        extra = jnp.pad(dec, ((0, 0), (0, 128 - 2 * H)))
        extra = jnp.broadcast_to(extra, (chips,) + extra.shape)
        return jnp.concatenate([blocks, extra], axis=2)

    def plane_rows(w):
        rows = w.shape[0] // nz
        return lax.dynamic_slice(w, (rep * rows, 0), (rows, w.shape[1]))

    def over_planes(blocks):
        got = lax.all_gather(blocks, "rep", axis=0)
        return got.transpose(1, 0, 2, 3).reshape(chips, -1, blocks.shape[2])

    pieces = [conv_weight, gain_in, gain_mid, o_gain, a_log, dt_bias]
    rows = [as_rows(p) for p in pieces]
    counts = [r.shape[0] for r in rows]
    packed = jnp.concatenate(rows, axis=0)
    packed = jnp.pad(packed, ((0, -packed.shape[0] % 16), (0, 0)))

    plane_proj = plane_rows(w_proj)
    rest = [exchange(proj_blocks(plane_proj, None, p), nf) for p in range(1, groups)]
    first = exchange(proj_blocks(w_proj, w_decay, 0), nf)
    tok = gather_first(tokens, nf)
    small = gather_small(packed, nf)
    tokens_all = gather_second(tok, nf)
    rest = [over_planes(r) for r in rest]
    up_plane = exchange(
        after(column_blocks(plane_rows(w_gate_up), up_widths, chips, 1, 0), first), nf
    )
    up_own = over_planes(after(up_plane, *rest))

    device = rep * nf + me
    held = jnp.sum(jnp.where(slot_owner == device, lengths, 0))
    live_own = (jnp.arange(TOK_DEV, dtype=jnp.int32) < held).astype(f32)[:, None]

    small = small.astype(f32)
    split = []
    at = 0
    for p, count in zip(pieces, counts):
        split.append(
            small[:, at : at + count].reshape(nf, count * 128)[:, : p.size].reshape((nf,) + p.shape)
        )
        at += count
    conv_full = split[0].transpose(1, 0, 2).reshape(KCONV, channels)
    gain_in_full, gain_mid_full, ogain_full, alog_full, bias_full = (
        s.reshape(-1) for s in split[1:]
    )
    conv_pair = []
    for p in range(groups):
        blocks = column_blocks(conv_full, proj_widths[:3], chips, groups, p)
        mine = lax.dynamic_index_in_dim(blocks, chip, 0, keepdims=False)
        conv_pair.append(jnp.pad(mine, ((0, 8 - KCONV), (0, 0))))
    head_rows = jnp.stack([alog_full, bias_full])
    head_rows = jnp.pad(head_rows, ((0, 6), (0, 128 - H)))
    gain_row = jnp.pad(ogain_full[None, :], ((0, 7), (0, 0)))

    rows_in = tokens_all.astype(f32)
    normed_in = (rows_in * scale_of(rows_in) * gain_in_full).astype(bf16)
    seeded = cotangent.astype(f32) * live_own
    weight_in = [both_core_rows(first, nf)]
    out_chip = both_cores(w_out, nf, weight_in[0])
    down_chip = both_cores(w_down, nf, weight_in[0])
    weight_in += [both_core_rows(r, nf) for r in rest]
    ffn_parts = gather_first(seeded.astype(bf16), nf, up_plane)
    d_ffn = gather_second(ffn_parts, nf)
    projected = []
    gated = []
    saved = []
    for p in range(groups):
        projected.append(mm(normed_in, weight_in[p]))
        got = mixer_forward(
            ids, projected[p], projected[0], conv_pair[p], head_rows, gain_row, hl, pair, p
        )
        gated.append(got[0])
        saved.append(got[1:])
    gated = jnp.concatenate(gated, axis=1)
    branch_parts = scatter_first(mm(gated, out_chip).astype(bf16), nf, d_ffn)
    d_hidden = mm_nt(after(d_ffn, gated), down_chip)
    up_chip = both_core_rows(after(up_own, gated), nf)
    branch = scatter_second(branch_parts, nf)

    tokens32 = tokens.astype(f32)
    middle = tokens32 + live_own * branch
    r_mid = scale_of(middle)
    normed_own = (middle * r_mid * gain_mid_full).astype(bf16)
    normed_mid = gather_second(gather_first(normed_own, nf), nf)
    gate_up = mm(normed_mid, up_chip)
    gate, up = gate_up[:, :wide], gate_up[:, wide:]
    sig = jax.nn.sigmoid(gate)
    act = gate * sig
    hidden = (act * up).astype(bf16)
    d_gate_up = jnp.concatenate(
        [d_hidden * up * (sig * (1.0 + gate * (1.0 - sig))), d_hidden * act], axis=1
    ).astype(bf16)

    line = Line(nz, ids)
    done = {}

    def step(new, *earlier):
        for item in new or [None]:
            got = line.step(item, *earlier)
            if got is not None:
                done[got[0]] = got[1][0]

    grad_down = sum_cores(mm_tn(hidden, d_ffn).astype(bf16), nf)
    down_parts = jnp.split(grad_down, 2, axis=0)
    step([("down0", down_parts[0])])
    partial_mid = mm_nt(after(d_gate_up, down_parts[0]), up_chip).astype(bf16)
    mid_parts = scatter_first(partial_mid, nf)
    grad_up = column_gradient(normed_mid, after(d_gate_up, partial_mid), nf)
    step([("down1", down_parts[1])], grad_up)
    d_normed_mid = scatter_second(mid_parts, nf)
    d_mid, g_gain_mid = rms_back(middle, r_mid, gain_mid_full, d_normed_mid)
    d_middle = seeded + d_mid
    d_branch_own = (live_own * d_middle).astype(bf16)
    branch_parts = gather_first(d_branch_own, nf)
    partial_ffn = mm(after(hidden, d_branch_own), down_chip).astype(bf16)
    step([("up0", grad_up[0])], partial_ffn)
    d_branch = gather_second(branch_parts, nf)
    step([("up1", grad_up[1])], d_branch)
    d_gated = [mm_nt(d_branch, out_chip[p * vv : (p + 1) * vv]) for p in range(groups)]
    grad_out = sum_cores(mm_tn(gated, d_branch).astype(bf16), nf)
    d_x = [None] * groups
    d_dec = None
    g_conv = [None] * groups
    g_heads = None
    ups = [("up%d" % j, grad_up[j]) for j in range(2, chips)]
    for n, p in enumerate(reversed(range(groups))):
        d_x[p], dec, g_conv[p], heads = mixer_backward(
            ids, projected[p], projected[0], conv_pair[p], head_rows, gain_row, saved[p],
            d_gated[p], hl, pair, p,
        )
        d_dec = dec if d_dec is None else d_dec + dec
        g_heads = heads if g_heads is None else g_heads + heads
        step(ups[n : n + 1] if n + 1 < groups else ups[n:], d_x[p])
        if p:
            d_gated[p - 1] = after(d_gated[p - 1], d_x[p])
    d_dec = d_dec.astype(bf16)
    right = [jnp.concatenate([d_x[0], d_dec], axis=1)] + d_x[1:]
    grad_cols = [None] * groups
    for p in reversed(range(groups)):
        grad_cols[p] = exchange(column_gradient(normed_in, right[p], nf), nf)
    ffn_parts = scatter_first(partial_ffn, nf, grad_cols[0])
    step([("out", grad_out)], right[0])
    partial_in = mm_nt(right[0], weight_in[0])
    for p in range(1, groups):
        partial_in = partial_in + mm_nt(right[p], weight_in[p])
    partial_in = partial_in.astype(bf16)
    queue = []
    for p in reversed(range(groups)):
        size = 1 if p == 0 else 2
        for c in range(0, chips, size):
            queue.append(((p, c), grad_cols[p][c : c + size]))
    for n, item in enumerate(queue):
        if n == 1:
            ffn_branch = scatter_second(ffn_parts, nf, line.tokens)
            output = (middle + live_own * ffn_branch).astype(bf16)
            in_parts = scatter_first(partial_in, nf, ffn_branch)
        if n == 2:
            d_normed_in = scatter_second(in_parts, nf, line.tokens)
            d_rows, g_gain_in = rms_back(tokens32, scale_of(tokens32), gain_in_full, d_normed_in)
            grad_tokens = d_middle + d_rows
            ups = jnp.stack([done["up%d" % j] for j in range(chips)])
            grad_up = exchange(after(ups, d_normed_in), nf)
        step([item])

    g_conv = [g[:KCONV] for g in g_conv]
    blocks = jnp.concatenate(
        [g[:, a:b] for a, b in ((0, qk), (qk, 2 * qk), (2 * qk, 2 * qk + vv)) for g in g_conv],
        axis=1,
    )
    conv_grad = jnp.zeros((KCONV, chips, channels // chips), f32)
    conv_grad = lax.dynamic_update_slice(conv_grad, blocks[:, None], (0, chip, 0))
    conv_grad = jnp.concatenate(from_column_blocks(conv_grad.transpose(1, 0, 2), proj_widths[:3]), axis=1)
    heads_grad = g_heads[1:3, :H]
    parts = [
        conv_grad.reshape(KCONV, nf, conv_shard).transpose(1, 0, 2),
        g_gain_in.reshape(nf, shard),
        g_gain_mid.reshape(nf, shard),
        g_heads[0].reshape(nf, -1),
        heads_grad[0].reshape(nf, -1),
        heads_grad[1].reshape(nf, -1),
    ]
    flat = []
    for part in parts:
        part = part.reshape(nf, -1)
        flat.append(jnp.pad(part, ((0, 0), (0, -part.shape[1] % 128))))
    flat = jnp.concatenate(flat, axis=1)
    summed = lax.psum(sum_small(flat.reshape(nf, -1, 128), nf)[0], "rep").reshape(-1)
    grads = []
    at = 0
    for p in pieces:
        grads.append(summed[at : at + p.size].reshape(p.shape))
        at += p.size + (-p.size % 128)
    s_conv, s_gain_in, s_gain_mid, s_ogain, s_alog, s_bias = grads

    step([])
    step([])
    grad_up = jnp.concatenate(from_column_blocks(grad_up, up_widths), axis=1).astype(f32)
    wholes = []
    for p in range(groups):
        size = 1 if p == 0 else 2
        wholes.append(jnp.concatenate([done[(p, c)] for c in range(0, chips, size)], axis=0))
    parts = []
    at = 0
    for width in (qk, qk, vv, vv):
        part = jnp.stack([w[:, :, at : at + width] for w in wholes], axis=1)
        parts.append(part.transpose(2, 0, 1, 3).reshape(shard, -1))
        at += width
    grad_proj = jnp.concatenate(parts, axis=1).astype(f32)
    grad_decay = jnp.sum(wholes[0][:, :, span : span + 2 * H].astype(f32), axis=0)
    grad_down = jnp.concatenate([done["down0"], done["down1"]], axis=0).astype(f32)
    grad_out = done["out"].astype(f32)
    return (
        output,
        grad_tokens,
        s_gain_in,
        grad_proj,
        grad_decay,
        s_conv,
        s_alog,
        s_bias,
        s_ogain,
        grad_out,
        s_gain_mid,
        grad_up,
        grad_down,
    )


def solution(mesh):
    rows = P(("rep", "fsdp"), None)
    one = P("fsdp")
    two = P("fsdp", None)
    columns = P(None, "fsdp")
    in_specs = (rows, rows, P(), P(), one, two, two, columns, one, one, one, two, one, two, two)
    out_specs = (rows, rows, one, two, two, columns, one, one, one, two, one, two, two)
    nf, nz = mesh.shape["fsdp"], mesh.shape["rep"]
    body = partial(local_fast if (nf, nz) == (8, 4) else local_general, nf=nf, nz=nz)
    return jax.shard_map(body, mesh=mesh, in_specs=in_specs, out_specs=out_specs, check_vma=False)
```

```python
from functools import partial

import jax
import jax.numpy as jnp
from jax import lax
from jax.experimental import pallas as pl
from jax.experimental.pallas import tpu as pltpu
from jax.sharding import PartitionSpec as P

H = 16
DK = 128
DV = 256
KCONV = 4
BLOCK = 64
TOK_DEV = 256
eps_norm = 1e-05
eps_unit = 1e-06
bf16 = jnp.bfloat16
f32 = jnp.float32


def mm(a, b):
    return lax.dot_general(
        a.astype(bf16), b.astype(bf16), (((1,), (0,)), ((), ())), preferred_element_type=f32
    )


def mm_nt(a, b):
    return lax.dot_general(
        a.astype(bf16), b.astype(bf16), (((1,), (1,)), ((), ())), preferred_element_type=f32
    )


def mm_tn(a, b):
    return lax.dot_general(
        a.astype(bf16), b.astype(bf16), (((0,), (0,)), ((), ())), preferred_element_type=f32
    )


def mm_exact(a, b):
    return lax.dot_general(
        a, b, (((1,), (0,)), ((), ())), precision=lax.Precision.HIGHEST, preferred_element_type=f32
    )


def silu(v):
    return v * jax.nn.sigmoid(v)


def shifted_down(x, s):
    if s == 0:
        return x
    row = lax.broadcasted_iota(jnp.int32, x.shape, 0)
    return jnp.where(row >= s, pltpu.roll(x, s, 0), 0.0)


def shifted_up(x, s):
    if s == 0:
        return x
    n = x.shape[0]
    row = lax.broadcasted_iota(jnp.int32, x.shape, 0)
    return jnp.where(row < n - s, pltpu.roll(x, n - s, 0), 0.0)


def conv_forward(mixed, weight):
    out = weight[KCONV - 1 : KCONV, :] * mixed
    for s in range(1, KCONV):
        out = out + weight[KCONV - 1 - s : KCONV - s, :] * shifted_down(mixed, s)
    return out


def conv_backward(d_conv, mixed, weight):
    d_mixed = weight[KCONV - 1 : KCONV, :] * d_conv
    rows = [None] * KCONV
    rows[KCONV - 1] = jnp.sum(d_conv * mixed, axis=0, keepdims=True)
    for s in range(1, KCONV):
        up = shifted_up(d_conv, s)
        d_mixed = d_mixed + weight[KCONV - 1 - s : KCONV - s, :] * up
        rows[KCONV - 1 - s] = jnp.sum(up * mixed, axis=0, keepdims=True)
    return d_mixed, jnp.concatenate(rows, axis=0)


def block_masks(n):
    i = lax.broadcasted_iota(jnp.int32, (n, n), 0)
    j = lax.broadcasted_iota(jnp.int32, (n, n), 1)
    x = i ^ j
    same = x < BLOCK
    return x, i > j, jnp.logical_and(same, i >= j), jnp.logical_and(same, i > j), same


def decay_parts(dec, alog_row, bias_row):
    pre = dec + bias_row
    softplus = jnp.maximum(pre, 0.0) + jnp.log1p(jnp.exp(-jnp.abs(pre)))
    log_decay = -jnp.exp(alog_row) * softplus
    n = dec.shape[0]
    i = lax.broadcasted_iota(jnp.int32, (n, n), 0)
    j = lax.broadcasted_iota(jnp.int32, (n, n), 1)
    same = (i ^ j) < BLOCK
    lower = jnp.where(jnp.logical_and(same, i >= j), 1.0, 0.0)
    whole = jnp.where(same, 1.0, 0.0)
    running = mm_exact(lower, log_decay)
    total = mm_exact(whole, log_decay)
    return pre, log_decay, running, total


def lane_of(x, h):
    lane = lax.broadcasted_iota(jnp.int32, x.shape, 1)
    return jnp.sum(jnp.where(lane == h, x, 0.0), axis=1, keepdims=True)


def row_of(x, h):
    row = lax.broadcasted_iota(jnp.int32, x.shape, 0)
    return jnp.sum(jnp.where(row == h, x, 0.0), axis=0, keepdims=True)


def unit_rows(a, scale):
    r = lax.rsqrt(jnp.sum(a * a, axis=1, keepdims=True) + eps_unit)
    return a * r * scale, r


def inverse_blocks(lowers, x, below):
    eye = jnp.where(x == 0, 1.0, 0.0)
    inv = [eye - jnp.where(x == 1, low, 0.0) for low in lowers]
    level = 1
    while (2 << level) <= BLOCK:
        pick = lax.shift_right_logical(x, level) == 1
        half = [mm(jnp.where(pick, low, 0.0), t) for low, t in zip(lowers, inv)]
        inv = [t - mm(t, u) for t, u in zip(inv, half)]
        level += 1
    return inv


def forward_kernel(
    hl,
    pair,
    p,
    ids_ref,
    x_ref,
    dec_ref,
    conv_ref,
    head_ref,
    gain_ref,
    gated_ref,
    o_ref,
    u_ref,
    w_ref,
    inv_ref,
    s_ref,
):
    n = TOK_DEV
    qk, vv = pair * DK, pair * DV
    blocks = n // BLOCK
    x, below, on_below, strict, same = block_masks(n)
    dec = dec_ref[...]
    pre, log_decay, running, total = decay_parts(dec, head_ref[0:1, :], head_ref[1:2, :])
    running_t = running.T
    heads = range(pair)
    q = silu(conv_forward(x_ref[:, :qk], conv_ref[:, :qk]))
    k = silu(conv_forward(x_ref[:, qk : 2 * qk], conv_ref[:, qk : 2 * qk]))
    v = silu(conv_forward(x_ref[:, 2 * qk : 2 * qk + vv], conv_ref[:, 2 * qk :])).astype(bf16)
    qn, kn, vn, beta, b, tot, fade, low, score = [], [], [], [], [], [], [], [], []
    for i in heads:
        h = ids_ref[0] * hl + p * pair + i
        qn.append(unit_rows(q[:, i * DK : (i + 1) * DK], DK**-0.5)[0].astype(bf16))
        kn.append(unit_rows(k[:, i * DK : (i + 1) * DK], 1.0)[0].astype(bf16))
        vn.append(v[:, i * DV : (i + 1) * DV])
        beta.append(jax.nn.sigmoid(lane_of(dec, H + h)))
        b.append(lane_of(running, h))
        tot.append(lane_of(total, h))
        d = jnp.where(on_below, jnp.exp(jnp.where(on_below, b[i] - row_of(running_t, h), 0.0)), 0.0)
        both = mm_nt(jnp.concatenate([kn[i], qn[i]], axis=0), kn[i])
        low.append(jnp.where(strict, beta[i] * d * both[:n], 0.0))
        score.append((both[n:] * d).astype(bf16))
    inv = inverse_blocks(low, x, below)
    e = [jnp.exp(b[i]) for i in heads]
    fin = [jnp.exp(tot[i] - b[i]) for i in heads]
    grow = [jnp.exp(tot[i]) for i in heads]
    inv = [t.astype(bf16) for t in inv]
    right = [
        jnp.concatenate(
            [beta[i] * vn[i].astype(f32), (beta[i] * e[i]) * kn[i].astype(f32)], axis=1
        ).astype(bf16)
        for i in heads
    ]
    uw = [mm(inv[i], right[i]) for i in heads]
    w = [uw[i][:, DV:].astype(bf16) for i in heads]
    state = [jnp.zeros((DK, DV), f32) for i in heads]
    u_parts = [[] for i in heads]
    o_parts = [[] for i in heads]
    for c in range(blocks):
        lo, hi = c * BLOCK, (c + 1) * BLOCK
        for i in heads:
            sb = state[i].astype(bf16)
            s_ref[0, i, c * DK : (c + 1) * DK, :] = sb
            got = mm(jnp.concatenate([w[i][lo:hi], qn[i][lo:hi]], axis=0), sb)
            u = uw[i][lo:hi, :DV] - got[:BLOCK]
            u_parts[i].append(u)
            o_parts[i].append(e[i][lo:hi] * got[BLOCK:])
            if c < blocks - 1:
                state[i] = grow[i][lo : lo + 1] * state[i] + mm_tn(
                    kn[i][lo:hi], fin[i][lo:hi] * u
                )
    gain = gain_ref[0:1, :]
    for i in heads:
        u = jnp.concatenate(u_parts[i], axis=0).astype(bf16)
        out = jnp.concatenate(o_parts[i], axis=0) + mm(score[i], u)
        cols = slice(i * DV, (i + 1) * DV)
        o_ref[:, cols] = out
        u_ref[:, cols] = u
        w_ref[:, i * DK : (i + 1) * DK] = w[i]
        inv_ref[0, i] = inv[i]
        r = lax.rsqrt(jnp.mean(out * out, axis=1, keepdims=True) + eps_norm)
        gated_ref[:, cols] = (out * r * gain * silu(x_ref[:, 2 * qk + vv + i * DV : 2 * qk + vv + (i + 1) * DV])).astype(bf16)


def mixer_forward(ids, proj, dec, conv, head_rows, gain_row, hl, pair, p):
    tokens = proj.shape[0]
    slots = tokens // TOK_DEV
    qk = pair * DK
    vv = pair * DV
    spec = pl.BlockSpec
    n = TOK_DEV

    def body(*refs):
        forward_kernel(hl, pair, p, *refs)

    return pl.pallas_call(
        body,
        grid=(slots,),
        in_specs=[
            pl.BlockSpec(memory_space=pltpu.SMEM),
            spec((n, 2 * qk + 2 * vv), lambda s: (s, 0)),
            spec((n, 128), lambda s: (s, dec.shape[1] // 128 - 1)),
            spec((8, 2 * qk + vv), lambda s: (0, 0)),
            spec((8, 128), lambda s: (0, 0)),
            spec((8, DV), lambda s: (0, 0)),
        ],
        out_specs=[
            spec((n, vv), lambda s: (s, 0)),
            spec((n, vv), lambda s: (s, 0)),
            spec((n, vv), lambda s: (s, 0)),
            spec((n, qk), lambda s: (s, 0)),
            spec((1, pair, n, n), lambda s: (s, 0, 0, 0)),
            spec((1, pair, n // BLOCK * DK, DV), lambda s: (s, 0, 0, 0)),
        ],
        out_shape=[
            jax.ShapeDtypeStruct((tokens, vv), bf16),
            jax.ShapeDtypeStruct((tokens, vv), f32),
            jax.ShapeDtypeStruct((tokens, vv), bf16),
            jax.ShapeDtypeStruct((tokens, qk), bf16),
            jax.ShapeDtypeStruct((slots, pair, n, n), bf16),
            jax.ShapeDtypeStruct((slots, pair, n // BLOCK * DK, DV), bf16),
        ],
        compiler_params=pltpu.CompilerParams(vmem_limit_bytes=56 * 1024 * 1024),
        cost_estimate=pl.CostEstimate(flops=1, bytes_accessed=1, transcendentals=0),
        name="mixer_forward",
    )(ids, proj, dec, conv, head_rows, gain_row)


def backward_kernel(
    hl,
    pair,
    p,
    ids_ref,
    x_ref,
    dec_ref,
    conv_ref,
    head_ref,
    gain_ref,
    o_ref,
    u_ref,
    w_ref,
    inv_ref,
    s_ref,
    dy_ref,
    *refs,
):
    more_ref = refs[0] if len(refs) == 5 else None
    dx_out, ddec_out, conv_out, small_out = refs[-4:]
    slot = pl.program_id(0)
    n = TOK_DEV
    qk, vv = pair * DK, pair * DV
    q_at = slice(0, qk)
    k_at = slice(qk, 2 * qk)
    v_at = slice(2 * qk, 2 * qk + vv)
    blocks = n // BLOCK
    x, below, on_below, strict, same = block_masks(n)
    dec = dec_ref[...]
    alog_row = head_ref[0:1, :]
    pre, log_decay, running, total = decay_parts(dec, alog_row, head_ref[1:2, :])
    running_t = running.T
    heads = range(pair)
    qc = conv_forward(x_ref[:, q_at], conv_ref[:, q_at])
    kc = conv_forward(x_ref[:, k_at], conv_ref[:, k_at])
    vc = conv_forward(x_ref[:, v_at], conv_ref[:, v_at])
    q_sig = jax.nn.sigmoid(qc)
    k_sig = jax.nn.sigmoid(kc)
    v_sig = jax.nn.sigmoid(vc)
    q = qc * q_sig
    k = kc * k_sig
    v = (vc * v_sig).astype(bf16)
    gain = gain_ref[0:1, :]
    qn, kn, vn, qr, kr, beta, b, tot, d, sim, low, score = ([] for _ in range(12))
    d_out, u = [], []
    gain_rows = jnp.zeros((1, DV), f32)
    for i in heads:
        h = ids_ref[0] * hl + p * pair + i
        cols = slice(i * DV, (i + 1) * DV)
        kcols = slice(i * DK, (i + 1) * DK)
        rows_q, r_q = unit_rows(q[:, kcols], DK**-0.5)
        rows_k, r_k = unit_rows(k[:, kcols], 1.0)
        qr.append((rows_q, r_q))
        kr.append((rows_k, r_k))
        qn.append(rows_q.astype(bf16))
        kn.append(rows_k.astype(bf16))
        vn.append(v[:, cols])
        beta.append(jax.nn.sigmoid(lane_of(dec, H + h)))
        b.append(lane_of(running, h))
        tot.append(lane_of(total, h))
        d.append(
            jnp.where(on_below, jnp.exp(jnp.where(on_below, b[i] - row_of(running_t, h), 0.0)), 0.0)
        )
        both = mm_nt(jnp.concatenate([kn[i], qn[i]], axis=0), kn[i])
        sim.append(jnp.where(strict, d[i] * both[:n], 0.0))
        score.append(both[n:] * d[i])
        out = o_ref[:, cols]
        g_at = slice(2 * qk + vv + i * DV, 2 * qk + vv + (i + 1) * DV)
        gate = x_ref[:, g_at]
        dy = dy_ref[:, cols].astype(f32)
        r = lax.rsqrt(jnp.mean(out * out, axis=1, keepdims=True) + eps_norm)
        normed = out * r
        g_sig = jax.nn.sigmoid(gate)
        act = gate * g_sig
        d_act = dy * normed * gain
        dx_out[:, g_at] = (d_act * (g_sig * (1.0 + gate * (1.0 - g_sig)))).astype(bf16)
        gain_rows = gain_rows + jnp.sum(dy * normed * act, axis=0, keepdims=True)
        d_normed = dy * gain * act
        d_out.append(r * (d_normed - normed * jnp.mean(d_normed * normed, axis=1, keepdims=True)))
        u.append(u_ref[:, cols])
    e = [jnp.exp(b[i]) for i in heads]
    fin = [jnp.exp(tot[i] - b[i]) for i in heads]
    grow = [jnp.exp(tot[i]) for i in heads]
    d_out16 = [d_out[i].astype(bf16) for i in heads]
    score16 = [score[i].astype(bf16) for i in heads]
    d_u0 = [mm_tn(score16[i], d_out16[i]) for i in heads]
    d_state = [jnp.zeros((DK, DV), f32) for i in heads]
    d_u = [[None] * blocks for i in heads]
    dq_s = [[None] * blocks for i in heads]
    dk_s = [[None] * blocks for i in heads]
    fin_col = [[None] * blocks for i in heads]
    grow_col = [[None] * blocks for i in heads]
    e_out = [(e[i] * d_out[i]).astype(bf16) for i in heads]
    for c in reversed(range(blocks)):
        lo, hi = c * BLOCK, (c + 1) * BLOCK
        for i in heads:
            ds16 = d_state[i].astype(bf16)
            s16 = s_ref[0, i, c * DK : (c + 1) * DK, :]
            u_c = u[i][lo:hi].astype(f32)
            if c == blocks - 1:
                d_u[i][c] = d_u0[i][lo:hi]
                fin_col[i][c] = jnp.zeros((BLOCK, 1), f32)
                grow_col[i][c] = jnp.zeros((1, 1), f32)
                dk_s[i][c] = jnp.zeros((BLOCK, DK), f32)
            else:
                k_ds = mm(kn[i][lo:hi], ds16)
                add = fin[i][lo:hi] * k_ds
                d_u[i][c] = d_u0[i][lo:hi] + add
                fin_col[i][c] = jnp.sum(add * u_c, axis=1, keepdims=True)
                grow_col[i][c] = grow[i][lo : lo + 1] * jnp.sum(
                    jnp.sum(d_state[i] * s16.astype(f32), axis=1, keepdims=True),
                    axis=0,
                    keepdims=True,
                )
                dk_s[i][c] = mm_nt(fin[i][lo:hi] * u_c, ds16)
            if c > 0:
                step = mm_tn(
                    jnp.concatenate([qn[i][lo:hi], w_ref[lo:hi, i * DK : (i + 1) * DK]], axis=0),
                    jnp.concatenate([e_out[i][lo:hi], (-d_u[i][c]).astype(bf16)], axis=0),
                )
                d_state[i] = grow[i][lo : lo + 1] * d_state[i] + step
    lane = lax.broadcasted_iota(jnp.int32, (n, 128), 1)
    d_dec = jnp.zeros((n, 128), f32)
    d_log = jnp.zeros((n, 128), f32)
    dq_all, dk_all, dv_all = [], [], []
    ones = jnp.ones((n, 128), bf16)
    upper_i = lax.broadcasted_iota(jnp.int32, (n, n), 0)
    upper_j = lax.broadcasted_iota(jnp.int32, (n, n), 1)
    upper = jnp.where(jnp.logical_and((upper_i ^ upper_j) < BLOCK, upper_i <= upper_j), 1.0, 0.0)
    for i in heads:
        h = ids_ref[0] * hl + p * pair + i
        du = jnp.concatenate(d_u[i], axis=0)
        d_right = mm_tn(inv_ref[0, i], du)
        dr16 = d_right.astype(bf16)
        outer = mm_nt(jnp.concatenate([d_out16[i], dr16], axis=0), u[i])
        d_score = jnp.where(on_below, outer[:n], 0.0)
        d_low = jnp.where(strict, -outer[n:], 0.0)
        z16 = (-(beta[i] * e[i]) * d_right).astype(bf16)
        recalled = []
        for c in range(blocks):
            lo, hi = c * BLOCK, (c + 1) * BLOCK
            s16 = s_ref[0, i, c * DK : (c + 1) * DK, :]
            if c == 0:
                dq_s[i][c] = jnp.zeros((BLOCK, DK), f32)
                recalled.append(jnp.zeros((BLOCK, 2 * DV), f32))
                continue
            back = mm_nt(jnp.concatenate([e_out[i][lo:hi], z16[lo:hi]], axis=0), s16)
            dq_s[i][c] = back[:BLOCK]
            dk_s[i][c] = dk_s[i][c] + back[BLOCK:]
            got = mm(jnp.concatenate([kn[i][lo:hi], qn[i][lo:hi]], axis=0), s16)
            recalled.append(jnp.concatenate([got[:BLOCK], got[BLOCK:]], axis=1))
        recalled = jnp.concatenate(recalled, axis=0)
        k_s = recalled[:, :DV]
        q_s = recalled[:, DV:]
        d_a = (d_score * d[i]).astype(bf16)
        d_g = d_low * beta[i] * d[i]
        d_g16 = (d_g + d_g.T).astype(bf16)
        dq = jnp.concatenate(dq_s[i], axis=0) + mm(d_a, kn[i])
        dk = jnp.concatenate(dk_s[i], axis=0) + mm_tn(d_a, qn[i]) + mm(d_g16, kn[i])
        dv = beta[i] * d_right
        row_sum = jnp.sum(d_low * sim[i], axis=1, keepdims=True)
        keep = vn[i].astype(f32) - e[i] * k_s
        d_beta = row_sum + jnp.sum(d_right * keep, axis=1, keepdims=True)
        moved = (d_score * score[i] + d_low * beta[i] * sim[i]).astype(bf16)
        d_b = mm(moved, ones) - mm_tn(moved, ones)
        d_b_col = e[i] * jnp.sum(
            d_out[i] * q_s - (beta[i] * d_right) * k_s, axis=1, keepdims=True
        )
        fin_all = jnp.concatenate(fin_col[i], axis=0)
        d_b = jnp.where(lane == h, d_b + (d_b_col - fin_all), 0.0)
        tail = jnp.concatenate(
            [
                jnp.broadcast_to(
                    grow_col[i][c] + jnp.sum(fin_col[i][c], axis=0, keepdims=True), (BLOCK, 1)
                )
                for c in range(blocks)
            ],
            axis=0,
        )
        d_log = d_log + mm_exact(upper, d_b) + jnp.where(lane == h, tail, 0.0)
        d_dec = d_dec + jnp.where(lane == H + h, d_beta * beta[i] * (1.0 - beta[i]), 0.0)
        rows_q, r_q = qr[i]
        rows_k, r_k = kr[i]
        unit = rows_q * DK**0.5
        dq = (DK**-0.5) * r_q * (dq - unit * jnp.sum(dq * unit, axis=1, keepdims=True))
        dk = r_k * (dk - rows_k * jnp.sum(dk * rows_k, axis=1, keepdims=True))
        dq_all.append(dq)
        dk_all.append(dk)
        dv_all.append(dv)

    @pl.when(slot == 0)
    def _():
        conv_out[...] = jnp.zeros_like(conv_out)
        small_out[...] = jnp.zeros_like(small_out)

    def through_conv(d_active, conv, sig, at):
        d_conv = d_active * (sig * (1.0 + conv * (1.0 - sig)))
        d_mixed, d_weight = conv_backward(d_conv, x_ref[:, at], conv_ref[:, at])
        dx_out[:, at] = d_mixed.astype(bf16)
        conv_out[0:KCONV, at] += d_weight

    through_conv(jnp.concatenate(dq_all, axis=1), qc, q_sig, q_at)
    through_conv(jnp.concatenate(dk_all, axis=1), kc, k_sig, k_at)
    through_conv(jnp.concatenate(dv_all, axis=1), vc, v_sig, v_at)
    first = ids_ref[0] * hl + p * pair
    mine = jnp.logical_and(lane >= first, lane < first + pair)
    d_pre = jnp.where(mine, -jnp.exp(alog_row) * jax.nn.sigmoid(pre) * d_log, 0.0)
    ddec_out[...] = d_dec + d_pre
    if more_ref is not None:
        dx_out[:, 2 * qk + 2 * vv :] = (more_ref[...] + (d_dec + d_pre)).astype(bf16)

    small_out[0:1, :] += gain_rows
    small_out[1:2, 0:128] += jnp.sum(jnp.where(mine, d_log * log_decay, 0.0), axis=0, keepdims=True)
    small_out[2:3, 0:128] += jnp.sum(d_pre, axis=0, keepdims=True)


def mixer_backward(ids, proj, dec, conv, head_rows, gain_row, saved, d_gated, hl, pair, p, more=None):
    out, u, w, inv, states = saved
    tokens = proj.shape[0]
    slots = tokens // TOK_DEV
    qk = pair * DK
    vv = pair * DV
    spec = pl.BlockSpec
    n = TOK_DEV
    width = 2 * qk + 2 * vv + (128 if more is not None else 0)

    def body(*refs):
        backward_kernel(hl, pair, p, *refs)

    return pl.pallas_call(
        body,
        grid=(slots,),
        in_specs=[
            pl.BlockSpec(memory_space=pltpu.SMEM),
            spec((n, 2 * qk + 2 * vv), lambda s: (s, 0)),
            spec((n, 128), lambda s: (s, dec.shape[1] // 128 - 1)),
            spec((8, 2 * qk + vv), lambda s: (0, 0)),
            spec((8, 128), lambda s: (0, 0)),
            spec((8, DV), lambda s: (0, 0)),
            spec((n, vv), lambda s: (s, 0)),
            spec((n, vv), lambda s: (s, 0)),
            spec((n, qk), lambda s: (s, 0)),
            spec((1, pair, n, n), lambda s: (s, 0, 0, 0)),
            spec((1, pair, n // BLOCK * DK, DV), lambda s: (s, 0, 0, 0)),
            spec((n, vv), lambda s: (s, 0)),
        ]
        + ([spec((n, 128), lambda s: (s, 0))] if more is not None else []),
        out_specs=[
            spec((n, width), lambda s: (s, 0)),
            spec((n, 128), lambda s: (s, 0)),
            spec((8, 2 * qk + vv), lambda s: (0, 0)),
            spec((8, DV), lambda s: (0, 0)),
        ],
        out_shape=[
            jax.ShapeDtypeStruct((tokens, width), bf16),
            jax.ShapeDtypeStruct((tokens, 128), f32),
            jax.ShapeDtypeStruct((8, 2 * qk + vv), f32),
            jax.ShapeDtypeStruct((8, DV), f32),
        ],
        compiler_params=pltpu.CompilerParams(vmem_limit_bytes=56 * 1024 * 1024),
        cost_estimate=pl.CostEstimate(flops=1, bytes_accessed=1, transcendentals=0),
        name="mixer_backward",
    )(ids, proj, dec, conv, head_rows, gain_row, out, u, w, inv, states, d_gated, *([more] if more is not None else []))


VMEM_LIMIT = 58 * 1024 * 1024
ANY = pl.BlockSpec(memory_space=pl.ANY)
SMEM = pl.BlockSpec(memory_space=pltpu.SMEM)


def params(**more):
    return pltpu.CompilerParams(vmem_limit_bytes=VMEM_LIMIT, **more)


def cost(flops, moved):
    return pl.CostEstimate(flops=1, bytes_accessed=1, transcendentals=0)


def pack_columns(w, extra, table, rows, plane, ids):
    chips = len(table)
    width = sum(size for _, size in table[0])
    more = 0 if extra is None else extra.shape[1]

    def body(ids_ref, w_ref, *refs):
        out = refs[-1]
        for c in range(chips):
            at = 0
            for start, size in table[c]:
                out[c, :, at : at + size] = w_ref[:, start : start + size]
                at += size
            if more:
                out[c, :, at : at + more] = refs[0][...]

    def block(i, ids_ref):
        return (ids_ref[2] if plane else 0, 0)

    def whole(i, ids_ref):
        return (0, 0)

    return pl.pallas_call(
        body,
        grid_spec=pltpu.PrefetchScalarGridSpec(
            num_scalar_prefetch=1,
            grid=(1,),
            in_specs=[pl.BlockSpec((rows, w.shape[1]), block)]
            + ([pl.BlockSpec((rows, more), whole)] if more else []),
            out_specs=pl.BlockSpec((chips, rows, width + more), lambda i, ids_ref: (0, 0, 0)),
        ),
        out_shape=jax.ShapeDtypeStruct((chips, rows, width + more), bf16),
        compiler_params=params(),
        cost_estimate=cost(0, 2 * rows * w.shape[1] + 2 * chips * rows * (width + more)),
        name="pack_columns",
    )(ids, w, *([extra] if more else []))


def pack_relative(w, extra, table, plane, ids):
    rows = w.shape[0] // 4 if plane else w.shape[0]
    chips = len(table)
    more = 0 if extra is None else extra.shape[1]
    width = sum(size for _, size in table[0]) + more

    def body(ids_ref, w_ref, *refs):
        outs = refs[-chips:]
        for j in range(chips):
            c = jnp.bitwise_xor(ids_ref[0], j)
            at = 0
            for r, (start, size) in enumerate(table[0]):
                step = table[1][r][0] - start
                lane = pl.multiple_of(start + c * step, 128)
                outs[j][:, at : at + size] = w_ref[:, pl.ds(lane, size)]
                at += size
            if more:
                outs[j][:, at : at + more] = refs[0][...]

    def block(i, ids_ref):
        return (ids_ref[2] if plane else 0, 0)

    def whole(i, ids_ref):
        return (0, 0)

    return pl.pallas_call(
        body,
        grid_spec=pltpu.PrefetchScalarGridSpec(
            num_scalar_prefetch=1,
            grid=(1,),
            in_specs=[pl.BlockSpec((rows, w.shape[1]), block)]
            + ([pl.BlockSpec((rows, more), block)] if more else []),
            out_specs=[pl.BlockSpec((rows, width), whole)] * chips,
        ),
        out_shape=[jax.ShapeDtypeStruct((rows, width), bf16)] * chips,
        compiler_params=params(),
        cost_estimate=cost(0, 4 * rows * w.shape[1]),
        name="pack_relative",
    )(ids, w, *([extra] if more else []))


def scatter_add(stay_x, got_x, stay_y, got_y):
    rows, n = stay_x.shape
    block = pl.BlockSpec((rows // 2, n), lambda i: (1, 0))
    out = pl.BlockSpec((rows // 2, n), lambda i: (0, 0))

    def body(a_ref, b_ref, c_ref, d_ref, x_ref, y_ref):
        x_ref[...] = a_ref[...] + b_ref[...]
        y_ref[...] = c_ref[...] + d_ref[...]

    return pl.pallas_call(
        body,
        grid=(1,),
        in_specs=[block] * 4,
        out_specs=[out] * 2,
        out_shape=[jax.ShapeDtypeStruct((rows // 2, n), bf16)] * 2,
        compiler_params=params(),
        cost_estimate=cost(0, 0),
        name="scatter_add",
    )(stay_x, got_x, stay_y, got_y)


def parts_specs(parts):
    rows = parts[2].shape[0]
    return [pl.BlockSpec((rows, p.shape[1]), lambda i: (0, 0)) for p in parts]


def sum_parts(refs):
    halves = []
    for h in range(2):
        a, b, c = refs[3 * h : 3 * h + 3]
        halves.append(a[...].astype(f32) + b[...].astype(f32) + c[...].astype(f32))
    return jnp.concatenate(halves, axis=1)


def live_rows(ids_ref, rows):
    return lax.broadcasted_iota(jnp.int32, (rows, 1), 0) < ids_ref[3]


def middle_rows(parts, tokens, gains, ids):
    rows, d = tokens.shape

    def body(ids_ref, t_ref, g_ref, *refs):
        mid_ref, out_ref = refs[-2:]
        branch = jnp.where(live_rows(ids_ref, rows), sum_parts(refs[:6]), 0.0)
        mid = t_ref[...].astype(f32) + branch
        mid_ref[...] = mid
        r = lax.rsqrt(jnp.mean(mid * mid, axis=1, keepdims=True) + eps_norm)
        out_ref[...] = (mid * r * g_ref[1:2, :]).astype(bf16)

    whole = pl.BlockSpec((rows, d), lambda i: (0, 0))
    return pl.pallas_call(
        body,
        grid=(1,),
        in_specs=[SMEM, whole, pl.BlockSpec((8, d), lambda i: (0, 0))] + parts_specs(parts),
        out_specs=[whole, whole],
        out_shape=[jax.ShapeDtypeStruct((rows, d), f32), jax.ShapeDtypeStruct((rows, d), bf16)],
        compiler_params=params(),
        cost_estimate=cost(0, 0),
        name="middle_rows",
    )(ids, tokens, gains, *parts)


def rms_parts(unit, r, gain, d_out):
    d_unit = d_out * gain
    d_rows = r * (d_unit - unit * jnp.mean(d_unit * unit, axis=1, keepdims=True))
    return d_rows, jnp.sum(d_out * unit, axis=0, keepdims=True)


def middle_back(parts, middle, cotangent, gains, ids):
    rows, d = middle.shape

    def body(ids_ref, m_ref, c_ref, g_ref, *refs):
        d_ref, b_ref, s_ref = refs[-3:]
        mid = m_ref[...]
        r = lax.rsqrt(jnp.mean(mid * mid, axis=1, keepdims=True) + eps_norm)
        d_rows, s_ref[...] = rms_parts(mid * r, r, g_ref[1:2, :], sum_parts(refs[:6]))
        live = live_rows(ids_ref, rows)
        total = jnp.where(live, c_ref[...].astype(f32), 0.0) + d_rows
        d_ref[...] = total
        b_ref[...] = jnp.where(live, total, 0.0).astype(bf16)

    whole = pl.BlockSpec((rows, d), lambda i: (0, 0))
    return pl.pallas_call(
        body,
        grid=(1,),
        in_specs=[SMEM, whole, whole, pl.BlockSpec((8, d), lambda i: (0, 0))]
        + parts_specs(parts),
        out_specs=[whole, whole, pl.BlockSpec((1, d), lambda i: (0, 0))],
        out_shape=[
            jax.ShapeDtypeStruct((rows, d), f32),
            jax.ShapeDtypeStruct((rows, d), bf16),
            jax.ShapeDtypeStruct((1, d), f32),
        ],
        compiler_params=params(),
        cost_estimate=cost(0, 0),
        name="middle_back",
    )(ids, middle, cotangent, gains, *parts)


def tokens_back(parts, tokens, d_middle, gains):
    rows, d = tokens.shape

    def body(t_ref, m_ref, g_ref, *refs):
        d_ref, s_ref = refs[-2:]
        x = t_ref[...].astype(f32)
        r = lax.rsqrt(jnp.mean(x * x, axis=1, keepdims=True) + eps_norm)
        d_rows, s_ref[...] = rms_parts(x * r, r, g_ref[0:1, :], sum_parts(refs[:6]))
        d_ref[...] = m_ref[...] + d_rows

    whole = pl.BlockSpec((rows, d), lambda i: (0, 0))
    return pl.pallas_call(
        body,
        grid=(1,),
        in_specs=[whole, whole, pl.BlockSpec((8, d), lambda i: (0, 0))] + parts_specs(parts),
        out_specs=[whole, pl.BlockSpec((1, d), lambda i: (0, 0))],
        out_shape=[jax.ShapeDtypeStruct((rows, d), f32), jax.ShapeDtypeStruct((1, d), f32)],
        compiler_params=params(),
        cost_estimate=cost(0, 0),
        name="tokens_back",
    )(tokens, d_middle, gains, *parts)


def stack_blocks(parts):
    rows, n = parts[0].shape
    tile = n // 2

    def body(*refs):
        for j in range(len(parts)):
            refs[-1][0, j] = refs[j][...]

    return pl.pallas_call(
        body,
        grid=(2,),
        in_specs=[pl.BlockSpec((rows, tile), lambda i: (0, i))] * len(parts),
        out_specs=pl.BlockSpec((1, len(parts), rows, tile), lambda i: (0, 0, 0, i)),
        out_shape=jax.ShapeDtypeStruct((1, len(parts), rows, n), bf16),
        compiler_params=params(),
        cost_estimate=cost(0, 0),
        name="stack_blocks",
    )(*parts)


def join_cores(mine, theirs, ids):
    rows, n = mine.shape
    tile = 512

    def body(ids_ref, mine_ref, theirs_ref, o_ref):
        core = ids_ref[1]
        o_ref[pl.ds(pl.multiple_of(core * rows, 16), rows), :] = mine_ref[...]
        o_ref[pl.ds(pl.multiple_of((1 - core) * rows, 16), rows), :] = theirs_ref[...]

    return pl.pallas_call(
        body,
        grid=(n // tile,),
        in_specs=[SMEM] + [pl.BlockSpec((rows, tile), lambda i: (0, i))] * 2,
        out_specs=pl.BlockSpec((2 * rows, tile), lambda i: (0, i)),
        out_shape=jax.ShapeDtypeStruct((2 * rows, n), bf16),
        compiler_params=params(),
        cost_estimate=cost(0, 8 * rows * n),
        name="join_cores",
    )(ids, mine, theirs)


def norm_rows(parts, gain):
    d = parts[0].shape[1]
    total = sum(p.shape[0] for p in parts)

    def body(gain_ref, *refs):
        out = refs[-1]
        at = 0
        for ref in refs[:-1]:
            for m in range(0, ref.shape[0], 128):
                rows = ref[m : m + 128, :].astype(f32)
                r = lax.rsqrt(jnp.mean(rows * rows, axis=1, keepdims=True) + eps_norm)
                out[at : at + 128, :] = (rows * r * gain_ref[0:1, :]).astype(bf16)
                at += 128

    return pl.pallas_call(
        body,
        out_shape=jax.ShapeDtypeStruct((total, d), bf16),
        compiler_params=params(),
        cost_estimate=cost(8 * total * d, 4 * total * d),
        name="norm_rows",
    )(gain, *parts)


def small_layout(shapes):
    lanes = []
    at = 0
    for size in shapes:
        lanes.append(at)
        at += size + (-size % 128)
    return lanes, at


def pack_small(conv, vectors, nf):
    lanes, used = small_layout([v.shape[1] for v in vectors])
    channels = conv.shape[1]

    def body(conv_ref, *refs):
        out = refs[-1]
        out[...] = jnp.zeros_like(out)
        for d in range(nf):
            out[d, 0:KCONV, :] = conv_ref[...].astype(f32)
            for ref, lane in zip(refs[:-1], lanes):
                out[d, KCONV : KCONV + 1, lane : lane + ref.shape[1]] = ref[...].astype(f32)

    out = pl.pallas_call(
        body,
        out_shape=jax.ShapeDtypeStruct((nf, 8, channels), f32),
        compiler_params=params(),
        cost_estimate=cost(0, 0),
        name="pack_small",
    )(conv, *vectors)
    return out.astype(bf16)


def small_ranges(chip, hk, qk, vv, groups, p, conv_shard):
    at = chip * groups + p
    found = []
    for start, size in ((at * qk, qk), (hk + at * qk, qk), (2 * hk + at * vv, vv)):
        lane = pl.multiple_of(lax.rem(start, conv_shard), 128)
        found.append((lax.div(start, conv_shard), lane, size))
    return found


def unpack_small(gathered, sizes, ids, hk, qk, vv, groups):
    nf, _, conv_shard = gathered.shape
    lanes, _ = small_layout(sizes)
    d = nf * sizes[0]

    def body(ids_ref, g_ref, gains_ref, heads_ref, ogain_ref, *convs):
        gains_ref[...] = jnp.zeros_like(gains_ref)
        heads_ref[...] = jnp.zeros_like(heads_ref)
        ogain_ref[...] = jnp.zeros_like(ogain_ref)
        for n, out, row in (
            (0, gains_ref, 0),
            (1, gains_ref, 1),
            (2, ogain_ref, 0),
            (3, heads_ref, 0),
            (4, heads_ref, 1),
        ):
            size = sizes[n]
            for i in range(nf):
                out[row : row + 1, i * size : (i + 1) * size] = g_ref[
                    i, KCONV : KCONV + 1, lanes[n] : lanes[n] + size
                ]
        for p, out in enumerate(convs):
            at = 0
            for dev, lane, size in small_ranges(ids_ref[0], hk, qk, vv, groups, p, conv_shard):
                out[:, at : at + size] = g_ref[dev, :, pl.ds(lane, size)]
                at += size

    return pl.pallas_call(
        body,
        in_specs=[SMEM, pl.BlockSpec(memory_space=pltpu.VMEM)],
        out_shape=[
            jax.ShapeDtypeStruct((8, d), f32),
            jax.ShapeDtypeStruct((8, 128), f32),
            jax.ShapeDtypeStruct((8, nf * sizes[2]), f32),
        ]
        + [jax.ShapeDtypeStruct((8, 2 * qk + vv), f32)] * groups,
        compiler_params=params(),
        name="unpack_small",
    )(ids, gathered.astype(f32))


def pack_small_grads(g_conv, g_heads, gain_in, gain_mid, sizes, ids, nf, conv_shard, hk, qk, vv):
    lanes, _ = small_layout(sizes)
    groups = len(g_conv)

    def body(ids_ref, gin_ref, gmid_ref, *refs):
        out = refs[-1]
        out[...] = jnp.zeros_like(out)
        heads = refs[groups][...]
        for ref in refs[groups + 1 : -1]:
            heads = heads + ref[...]
        for n, row in (
            (0, gin_ref[0:1, :]),
            (1, gmid_ref[0:1, :]),
            (2, heads[0:1, :]),
            (3, heads[1:2, :]),
            (4, heads[2:3, :]),
        ):
            size = sizes[n]
            for i in range(nf):
                out[i, KCONV : KCONV + 1, lanes[n] : lanes[n] + size] = row[
                    :, i * size : (i + 1) * size
                ]
        for p in range(groups):
            at = 0
            for dev, lane, size in small_ranges(ids_ref[0], hk, qk, vv, groups, p, conv_shard):
                out[dev, 0:KCONV, pl.ds(lane, size)] = refs[p][0:KCONV, at : at + size]
                at += size

    vmem = pl.BlockSpec(memory_space=pltpu.VMEM)
    return pl.pallas_call(
        body,
        in_specs=[SMEM] + [vmem] * (2 + 2 * groups),
        out_shape=jax.ShapeDtypeStruct((nf, 8, conv_shard), f32),
        compiler_params=params(),
        name="pack_small_grads",
    )(ids, gain_in, gain_mid, *g_conv, *g_heads)


def line_values(ids, chunk, got, pair, met, new):
    rows, n = chunk.shape if chunk is not None else (new if new is not None else pair).shape
    steps = 2
    args = [a for a in (chunk, got, pair, met, new) if a is not None]
    count = (pair is not None or new is not None) + (chunk is not None)

    def body(ids_ref, *refs):
        refs = list(refs)
        outs = refs[len(args) :]
        if chunk is not None:
            outs[-1][...] = refs.pop(0)[...] + refs.pop(0)[...]
        if pair is not None:
            total = refs.pop(0)[...] + refs.pop(0)[...]
            if new is not None:
                middle = jnp.logical_or(ids_ref[2] == 1, ids_ref[2] == 2)
                total = jnp.where(middle, total, refs.pop(0)[...])
            outs[0][...] = total

    block = pl.BlockSpec((rows // steps, n), lambda i: (i, 0))
    return list(pl.pallas_call(
        body,
        grid=(steps,),
        in_specs=[SMEM] + [block] * len(args),
        out_specs=[block] * count,
        out_shape=[jax.ShapeDtypeStruct((rows, n), bf16)] * count,
        compiler_params=params(),
        cost_estimate=cost(0, 0),
        name="line_values",
    )(ids, *args))


def place_blocks(whole, pair_values, ids, c, shape):
    t, last = pair_values
    rows, n = shape[1:]
    old = [] if whole is None else [whole]
    tiles = n // 128

    def body(ids_ref, t_ref, last_ref, *refs):
        out = refs[-1]
        middle = jnp.logical_or(ids_ref[2] == 1, ids_ref[2] == 2)
        for k in range(tiles):
            band = slice(16 * k, 16 * k + 16)
            value = jnp.where(middle, t_ref[band, :], last_ref[band, :])
            for s in range(rows // 16):
                out[0, 16 * s : 16 * s + 16, 128 * k : 128 * k + 128] = value[
                    :, 128 * s : 128 * s + 128
                ]

    vmem = pl.BlockSpec(t.shape, lambda i: (0, 0))
    return pl.pallas_call(
        body,
        grid=(1,),
        in_specs=[SMEM, vmem, vmem] + [ANY] * len(old),
        out_specs=pl.BlockSpec((1, rows, n), lambda i: (c, 0, 0)),
        out_shape=jax.ShapeDtypeStruct(shape, bf16),
        input_output_aliases={3: 0} if old else {},
        compiler_params=params(),
        cost_estimate=cost(0, 6 * rows * n),
        name="place_blocks",
    )(ids, t, last, *old)


def finish_projection(whole, pair_values, ids, bands, shape):
    t, last = pair_values
    rows = shape[0]
    old = [] if whole is None else [whole]
    table = jnp.array([b for b, _ in bands] + [c // 2 for _, c in bands], jnp.int32)
    count = len(bands)

    def body(table_ref, ids_ref, t_ref, last_ref, *refs):
        middle = jnp.logical_or(ids_ref[2] == 1, ids_ref[2] == 2)
        at = pl.multiple_of(16 * table_ref[pl.program_id(0)], 16)
        value = jnp.where(middle, t_ref[pl.ds(at, 32), :], last_ref[pl.ds(at, 32), :])
        for k in range(2):
            for s in range(rows // 16):
                refs[-1][16 * s : 16 * s + 16, 128 * k : 128 * k + 128] = value[
                    16 * k : 16 * k + 16, 128 * s : 128 * s + 128
                ].astype(f32)

    def whole_chunk(i, table_ref):
        return (0, 0)

    return pl.pallas_call(
        body,
        grid_spec=pltpu.PrefetchScalarGridSpec(
            num_scalar_prefetch=1,
            grid=(count,),
            in_specs=[SMEM] + [pl.BlockSpec(t.shape, whole_chunk)] * 2 + [ANY] * len(old),
            out_specs=pl.BlockSpec((rows, 256), lambda i, table_ref: (0, table_ref[count + i])),
        ),
        out_shape=jax.ShapeDtypeStruct(shape, f32),
        input_output_aliases={4: 0} if old else {},
        compiler_params=params(),
        cost_estimate=cost(0, 8 * rows * 256 * count),
        name="finish_projection",
    )(table, ids, t, last, *old)


def finish_feed_forward(blocks):
    chips, rows, n = blocks.shape
    wide = n // 2

    def body(x_ref, o_ref):
        which = pl.program_id(1)
        for s in range(2):

            @pl.when(which == s)
            def _():
                for at in range(0, wide, 128):
                    start = 2 * at + 128 * s
                    o_ref[:, at : at + 128] = x_ref[0, :, start : start + 128].astype(f32)

    return pl.pallas_call(
        body,
        grid=(chips, 2),
        in_specs=[pl.BlockSpec((1, rows, n), lambda c, s: (c, 0, 0))],
        out_specs=pl.BlockSpec((rows, wide), lambda c, s: (0, s * chips + c)),
        out_shape=jax.ShapeDtypeStruct((rows, chips * n), f32),
        compiler_params=params(),
        cost_estimate=cost(0, 6 * chips * rows * n),
        name="finish_feed_forward",
    )(blocks)


def fill_rows(w_ref, own_ref, other_ref, core, chip=0):
    planes, chips, rows, _ = own_ref.shape
    for z in range(planes):
        for j in range(chips):
            c = jnp.bitwise_xor(chip, j)
            for ref, k in ((own_ref, core), (other_ref, 1 - core)):
                at = pl.multiple_of((2 * c + k) * planes * rows + z * rows, rows)
                w_ref[pl.ds(at, rows), :] = ref[z, j]


def project_planes(x, own, other, ids):
    tokens, k = x.shape
    planes, chips, rows, n = own.shape
    tile = 256

    def body(ids_ref, x_ref, own_ref, other_ref, o_ref, w_ref):
        fill_rows(w_ref, own_ref, other_ref, ids_ref[1], ids_ref[0])
        o_ref[...] = jnp.dot(x_ref[...], w_ref[...], preferred_element_type=f32)

    return pl.pallas_call(
        body,
        grid=(pl.cdiv(n, tile),),
        in_specs=[SMEM, pl.BlockSpec((tokens, k), lambda i: (0, 0))]
        + [pl.BlockSpec((planes, chips, rows, tile), lambda i: (0, 0, 0, i))] * 2,
        out_specs=pl.BlockSpec((tokens, tile), lambda i: (0, i)),
        out_shape=jax.ShapeDtypeStruct((tokens, n), f32),
        scratch_shapes=[pltpu.VMEM((k, tile), bf16)],
        compiler_params=params(),
        cost_estimate=cost(2 * tokens * k * n, 2 * tokens * k + 2 * k * n + 4 * tokens * n),
        name="project",
    )(ids, x, own, other)


def project(x, own, other, ids):
    tokens, k = x.shape
    rows, n = own[0].shape
    chips = len(own)
    tile = 256

    def body(ids_ref, x_ref, *refs):
        o_ref, w_ref = refs[2 * chips :]
        for j in range(chips):
            c = jnp.bitwise_xor(ids_ref[0], j)
            for ref, core in ((refs[j], ids_ref[1]), (refs[chips + j], 1 - ids_ref[1])):
                at = pl.multiple_of((2 * c + core) * rows, rows)
                w_ref[pl.ds(at, rows), :] = ref[...]
        o_ref[...] = jnp.dot(x_ref[...], w_ref[...], preferred_element_type=f32)

    return pl.pallas_call(
        body,
        grid=(pl.cdiv(n, tile),),
        in_specs=[SMEM, pl.BlockSpec((tokens, k), lambda i: (0, 0))]
        + [pl.BlockSpec((rows, tile), lambda i: (0, i))] * (2 * chips),
        out_specs=pl.BlockSpec((tokens, tile), lambda i: (0, i)),
        out_shape=jax.ShapeDtypeStruct((tokens, n), f32),
        scratch_shapes=[pltpu.VMEM((k, tile), bf16)],
        compiler_params=params(),
        cost_estimate=cost(2 * tokens * k * n, 2 * tokens * k + 2 * k * n + 4 * tokens * n),
        name="project",
    )(ids, x, *own, *other)


def feed_forward(x, own, other, down, d_ffn, ids):
    tokens, k = x.shape
    planes, chips, rows, n = own.shape
    wide = n // 2
    tile = 512

    def body(ids_ref, x_ref, own_ref, other_ref, down_ref, d_ref, h_ref, g_ref, w_ref):
        fill_rows(w_ref, own_ref, other_ref, ids_ref[1])
        for m in range(0, tokens, 256):
            rows_at = slice(m, m + 256)
            both = jnp.dot(x_ref[rows_at, :], w_ref[...], preferred_element_type=f32)
            d_hidden = mm_nt(d_ref[rows_at, :], down_ref[...])
            for s in range(tile // 256):
                gate = both[:, 256 * s : 256 * s + 128]
                up = both[:, 256 * s + 128 : 256 * s + 256]
                dh = d_hidden[:, 128 * s : 128 * s + 128]
                sig = jax.nn.sigmoid(gate)
                act = gate * sig
                h_ref[rows_at, 128 * s : 128 * s + 128] = (act * up).astype(bf16)
                g_ref[rows_at, 256 * s : 256 * s + 128] = (
                    dh * up * (sig * (1.0 + gate * (1.0 - sig)))
                ).astype(bf16)
                g_ref[rows_at, 256 * s + 128 : 256 * s + 256] = (dh * act).astype(bf16)

    return pl.pallas_call(
        body,
        grid=(pl.cdiv(n, tile),),
        in_specs=[
            SMEM,
            pl.BlockSpec((tokens, k), lambda i: (0, 0)),
            pl.BlockSpec((planes, chips, rows, tile), lambda i: (0, 0, 0, i)),
            pl.BlockSpec((planes, chips, rows, tile), lambda i: (0, 0, 0, i)),
            pl.BlockSpec((tile // 2, k), lambda i: (i, 0)),
            pl.BlockSpec((tokens, k), lambda i: (0, 0)),
        ],
        out_specs=[
            pl.BlockSpec((tokens, tile // 2), lambda i: (0, i)),
            pl.BlockSpec((tokens, tile), lambda i: (0, i)),
        ],
        out_shape=[
            jax.ShapeDtypeStruct((tokens, wide), bf16),
            jax.ShapeDtypeStruct((tokens, n), bf16),
        ],
        scratch_shapes=[pltpu.VMEM((k, tile), bf16)],
        compiler_params=params(),
        cost_estimate=cost(3 * tokens * k * n, 4 * tokens * k + 3 * k * n + 3 * tokens * n),
        name="feed_forward",
    )(ids, x, own, other, down, d_ffn)


def halves_of(i, tiles):
    half = tiles // 2
    return jnp.minimum(i, half - 1), jnp.maximum(i - half, 0)


def scatter_outputs(tokens, n, tile, refs=None):
    size = tokens // 2
    tiles = n // tile
    first = pl.BlockSpec((size, tile), lambda i, *ids: (0, halves_of(i, tiles)[0]))
    second = pl.BlockSpec((size, tile), lambda i, *ids: (0, halves_of(i, tiles)[1]))
    return [first, first, second, second], [jax.ShapeDtypeStruct((size, n // 2), bf16)] * 4


def write_scattered(outs, total_ref, tiles):
    size = total_ref.shape[0] // 4
    i = pl.program_id(0)

    for half, rows in ((0, ((1, 3), (0, 2))), (1, ((2, 3), (0, 1)))):

        @pl.when((i < tiles // 2) if half == 0 else (i >= tiles // 2))
        def _():
            for out, chips in zip(outs[2 * half : 2 * half + 2], rows):
                for n, m in enumerate(chips):
                    out[n * size : (n + 1) * size, :] = total_ref[m * size : (m + 1) * size, :]


def times_rows(lefts, mine, theirs, ids):
    tokens = lefts[0].shape[0]
    half, n = mine.shape
    tile = 256
    specs, shapes = scatter_outputs(tokens, n, tile)

    def body(ids_ref, *refs):
        left_refs = refs[: len(lefts)]
        mine_ref, theirs_ref = refs[len(lefts) : len(lefts) + 2]
        outs = refs[len(lefts) + 2 : -2]
        right_ref, total_ref = refs[-2:]
        core = ids_ref[1]
        right_ref[pl.ds(pl.multiple_of(core * half, 16), half), :] = mine_ref[...]
        right_ref[pl.ds(pl.multiple_of((1 - core) * half, 16), half), :] = theirs_ref[...]
        total = None
        at = 0
        for ref in left_refs:
            width = ref.shape[1]
            term = jnp.dot(ref[...], right_ref[at : at + width, :], preferred_element_type=f32)
            total = term if total is None else total + term
            at += width
        total_ref[...] = total.astype(bf16)
        write_scattered(outs, total_ref, n // tile)

    return pl.pallas_call(
        body,
        grid=(n // tile,),
        in_specs=[SMEM]
        + [pl.BlockSpec(a.shape, lambda i: (0, 0)) for a in lefts]
        + [pl.BlockSpec((half, tile), lambda i: (0, i))] * 2,
        out_specs=specs,
        out_shape=shapes,
        scratch_shapes=[pltpu.VMEM((2 * half, tile), bf16), pltpu.VMEM((tokens, tile), bf16)],
        compiler_params=params(),
        cost_estimate=cost(4 * tokens * half * n, 2 * (tokens * half + half * n + tokens * n)),
        name="times_rows",
    )(ids, *lefts, mine, theirs)


def times_transposed(pairs, ids, relative):
    tokens = pairs[0][0].shape[0]
    planes, chips, rows, _ = pairs[0][1].shape
    rows *= planes
    total_n = sum(left.shape[1] for left, own, other in pairs)
    k = 2 * chips * rows
    specs_out, shapes = scatter_outputs(tokens, k, rows)

    def body(ids_ref, *refs):
        count = len(pairs)
        outs = refs[3 * count : 3 * count + 4]
        piece_refs = refs[3 * count + 4 : -1]
        total_ref = refs[-1]
        mine = pl.program_id(0) % 2 == ids_ref[1]

        def choose(which):
            for n in range(count):
                piece = refs[3 * n + which][:, 0]
                piece_refs[n][...] = piece.reshape(rows, piece.shape[2])

        @pl.when(mine)
        def _():
            choose(1)

        @pl.when(jnp.logical_not(mine))
        def _():
            choose(2)

        total = None
        for n in range(count):
            term = mm_nt(refs[3 * n][...], piece_refs[n][...])
            total = term if total is None else total + term
        total_ref[...] = total.astype(bf16)
        write_scattered(outs, total_ref, 2 * chips)

    def piece_at(i, ids_ref):
        c = lax.div(i, 2)
        if relative:
            c = jnp.bitwise_xor(c, ids_ref[0])
        return (0, c, 0, 0)

    specs = []
    args = []
    for left, own, other in pairs:
        specs.append(pl.BlockSpec(left.shape, lambda i, ids_ref: (0, 0)))
        block = (own.shape[0], 1) + own.shape[2:]
        specs += [pl.BlockSpec(block, piece_at)] * 2
        args += [left, own, other]
    return pl.pallas_call(
        body,
        grid_spec=pltpu.PrefetchScalarGridSpec(
            num_scalar_prefetch=1,
            grid=(2 * chips,),
            in_specs=specs,
            out_specs=specs_out,
            scratch_shapes=[pltpu.VMEM((rows, own.shape[3]), bf16) for _, own, _ in pairs]
            + [pltpu.VMEM((tokens, rows), bf16)],
        ),
        out_shape=shapes,
        compiler_params=params(),
        cost_estimate=cost(
            2 * tokens * k * total_n, 2 * (tokens * k + k * total_n + tokens * total_n)
        ),
        name="times_transposed",
    )(ids, *args)


STREAM = 2048


def pack_bands(value, out, rows, tiles):
    for t in range(tiles):
        for s in range(rows // 16):
            out[16 * t : 16 * t + 16, 128 * s : 128 * s + 128] = value[
                16 * s : 16 * s + 16, 128 * t : 128 * t + 128
            ]


def column_terms(lefts, rights, ids, split):
    tokens, k = lefts[0].shape
    n = rights[0].shape[1]
    chips = 4
    rows = k // (2 * chips)
    tiles = n // 128

    def body(ids_ref, a_ref, b_ref, ra_ref, rb_ref, *refs):
        total_ref = refs[-1]
        total = mm_tn(a_ref[...], ra_ref[...]) + mm_tn(b_ref[...], rb_ref[...])
        if not split:
            total_ref[...] = total.astype(bf16)
            pack_bands(total_ref, refs[0].at[0], rows, tiles)
            return
        total_ref[...] = total.astype(bf16)
        for c in range(chips):

            @pl.when(pl.program_id(0) == c)
            def _():
                pack_bands(total_ref, refs[c], rows, tiles)

    def column(i, ids_ref):
        return (0, 2 * i + ids_ref[1])

    def whole(i, ids_ref):
        return (0, 0)

    if split:
        out_specs = [pl.BlockSpec((16 * tiles, STREAM), whole)] * chips
        out_shape = [jax.ShapeDtypeStruct((16 * tiles, STREAM), bf16)] * chips
    else:
        out_specs = pl.BlockSpec((1, 16 * tiles, STREAM), lambda i, ids_ref: (i, 0, 0))
        out_shape = jax.ShapeDtypeStruct((chips, 16 * tiles, STREAM), bf16)
    return pl.pallas_call(
        body,
        grid_spec=pltpu.PrefetchScalarGridSpec(
            num_scalar_prefetch=1,
            grid=(chips,),
            in_specs=[pl.BlockSpec((tokens, rows), column)] * 2
            + [pl.BlockSpec((tokens, n), whole)] * 2,
            out_specs=out_specs,
            scratch_shapes=[pltpu.VMEM((rows, n), bf16)],
        ),
        out_shape=out_shape,
        compiler_params=params(),
        cost_estimate=cost(2 * tokens * k * n, 4 * (tokens * k + tokens * n + k * n)),
        name="column_terms",
    )(ids, *lefts, *rights)


def row_terms(lefts, right, ids, in_order=False):
    tokens, n = right.shape
    k = sum(a.shape[1] for a in lefts)
    tile = 512
    half = k // 2

    def body(ids_ref, *refs):
        left_refs = refs[: len(lefts)]
        right_ref, mine_ref, theirs_ref, acc = refs[len(lefts) :]
        core = ids_ref[1]
        at = 0
        for ref in left_refs:
            width = ref.shape[1]
            if not in_order:
                acc[at : at + width, :] = mm_tn(ref[...], right_ref[...])
            else:
                total = None
                size = tokens // 4
                for m in range(4):
                    chip = jnp.bitwise_xor(ids_ref[0], m)
                    rows = right_ref[pl.ds(pl.multiple_of(chip * size, size), size), :]
                    term = mm_tn(ref[m * size : (m + 1) * size, :], rows)
                    total = term if total is None else total + term
                acc[at : at + width, :] = total
            at += width
        mine_ref[...] = acc[pl.ds(pl.multiple_of(core * half, 16), half), :].astype(bf16)
        theirs_ref[...] = acc[pl.ds(pl.multiple_of((1 - core) * half, 16), half), :].astype(bf16)

    out = pl.BlockSpec((half, tile), lambda i: (0, i))
    return pl.pallas_call(
        body,
        grid=(n // tile,),
        in_specs=[SMEM]
        + [pl.BlockSpec(a.shape, lambda i: (0, 0)) for a in lefts]
        + [pl.BlockSpec((tokens, tile), lambda i: (0, i))],
        out_specs=[out, out],
        out_shape=[jax.ShapeDtypeStruct((half, n), bf16)] * 2,
        scratch_shapes=[pltpu.VMEM((k, tile), f32)],
        compiler_params=params(),
        cost_estimate=cost(2 * tokens * k * n, 2 * (tokens * k + tokens * n + k * n)),
        name="row_terms",
    )(ids, *lefts, right)


def after(values, *earlier):
    if not earlier:
        return values
    return lax.optimization_barrier((values, earlier))[0]


def to_chip(a, nf, j):
    return lax.ppermute(a, "fsdp", [(i, i ^ (2 * j)) for i in range(nf)])


def swap_core(a, nf):
    return lax.ppermute(a, "fsdp", [(i, i ^ 1) for i in range(nf)])


RIGHT = [(0, 1), (1, 2), (2, 3)]
LEFT = [(1, 0), (2, 1), (3, 2)]
INWARD = [(0, 1), (3, 2)]
MIDDLE = [(1, 2), (2, 1)]
OUTWARD = [(1, 0), (2, 3)]
SWAP = [(0, 1), (1, 0), (2, 3), (3, 2)]


def along(a, pairs):
    return lax.ppermute(a, "rep", pairs)


def add16(a, b):
    return (a.astype(f32) + b.astype(f32)).astype(bf16)


def gather_small(a, nf):
    me = lax.axis_index("fsdp")
    out = a[None]
    bit = 1
    while bit < nf:
        other = lax.ppermute(out, "fsdp", [(i, i ^ bit) for i in range(nf)])
        upper = (me & bit) != 0
        out = jnp.concatenate(
            [jnp.where(upper, other, out), jnp.where(upper, out, other)], axis=0
        )
        bit *= 2
    return out


def sum_small(a, nf):
    me = lax.axis_index("fsdp")
    bit = nf // 2
    while bit:
        half = a.shape[0] // 2
        upper = (me & bit) != 0
        keep = jnp.where(upper, a[half:], a[:half])
        send = jnp.where(upper, a[:half], a[half:])
        got = lax.ppermute(send, "fsdp", [(i, i ^ bit) for i in range(nf)])
        a = keep + got
        bit //= 2
    return a[0], got


def sum_line(a):
    z = lax.axis_index("rep")
    a = a + along(a, INWARD)
    a = a + along(a, MIDDLE)
    return jnp.where(jnp.logical_or(z == 1, z == 2), a, along(a, OUTWARD))


class Line:
    def __init__(self, nz, ids):
        self.nz = nz
        self.ids = ids
        self.tokens = ()
        self.first = None
        self.second = None

    def step(self, new, *earlier):
        if self.nz != 4:
            return new and (new[0], (lax.psum(new[1], "rep"),) * 2)
        chunk = None if new is None else new[1]
        first = (None, None) if self.first is None else self.first[1:]
        second = (None, None) if self.second is None else self.second[1:]
        chunk, first, second, _, _ = lax.optimization_barrier(
            (chunk, first, second, self.tokens, earlier)
        )
        finished = next_first = next_second = None
        tokens = []
        values = []
        if self.first is not None or self.second is not None:
            if chunk is not None and self.second is None:
                values = [chunk] + line_values(self.ids, *first, None, None, None)
            else:
                values = line_values(self.ids, *first, *second, chunk)
        elif chunk is not None:
            values = [chunk]
        if chunk is not None or self.second is not None:
            got = along(values[0], OUTWARD if chunk is None else SWAP)
            tokens.append(got)
            if self.second is not None:
                finished = (self.second[0], (values[0], got))
            if chunk is not None:
                next_first = (new[0], chunk, got)
        if self.first is not None:
            met = along(values[-1], MIDDLE)
            tokens.append(met)
            next_second = (self.first[0], values[-1], met)
        self.first, self.second, self.tokens = next_first, next_second, tuple(tokens)
        self.sent = tuple(values)
        return finished


class Overlapped:
    def __init__(self, nz, ids):
        self.nz = nz
        self.ids = ids
        self.value = None
        self.new = None
        self.total = None
        self.inward = None
        self.met = []
        self.got = self.arriving = ()
        self.sent = ()
        self.done = {}

    def prepare(self, new, *earlier):
        if self.nz != 4:
            if new:
                self.done[new[0]] = (lax.psum(new[1], "rep"),) * 2
            return
        chunk = new and new[1]
        pair = (None, None)
        self.total = None
        if len(self.met) > 1 or (self.met and new is None):
            self.total, *pair = self.met.pop(0)
        chunk, pair, _ = lax.optimization_barrier((chunk, tuple(pair), (self.sent, earlier)))
        self.new = new and (new[0], chunk)
        self.value = chunk
        if self.total is not None:
            self.value = line_values(self.ids, None, None, *pair, chunk)[0]
            self.sent = self.value

    def step(self, *earlier):
        if self.nz != 4:
            return
        before = self.inward
        if self.value is not None:
            value = after(self.value, self.sent, self.got, earlier)
            got = along(value, OUTWARD if self.new is None else SWAP)
            self.got = got
            if self.total is not None:
                self.done[self.total] = (value, got)
        self.inward = self.new and (self.new[0], self.new[1], got)
        if before is not None:
            name, *pair = before
            pair = after(tuple(pair), self.sent, earlier)
            value = line_values(self.ids, *pair, None, None, None)[0]
            self.sent = (value,) + tuple(pair[2] for pair in self.met[-1:])
            self.met.append((name, value, along(value, MIDDLE)))
            self.arriving = (self.got, self.met[-1][2])


def gather_first(a, nf, *earlier):
    chips = nf // 2
    a = after(a, *earlier)
    if chips != 4:
        return [a] + [to_chip(a, nf, j) for j in range(1, chips)]
    return [a, to_chip(a, nf, 1), to_chip(a, nf, 2)]


def gather_second(parts, nf, *earlier):
    if nf != 8:
        return jnp.concatenate(parts, axis=0)
    a, one, two = parts
    half = a.shape[0] // 2
    low, high = after((one[:half], two[half:]), *earlier)
    return jnp.concatenate([a, one, two, to_chip(low, nf, 2), to_chip(high, nf, 1)], axis=0)


def scatter_first(a, nf, *earlier):
    chips = nf // 2
    n = a.shape[0] // chips
    parts = [a[j * n : (j + 1) * n] for j in range(chips)]
    if chips != 4:
        return [parts[0]] + [to_chip(parts[j], nf, j) for j in range(1, chips)]
    half = n // 2
    low, high, one, two = after(
        (parts[3][:half], parts[3][half:], parts[1][half:], parts[2][:half]), *earlier
    )
    low = to_chip(low, nf, 2)
    high = to_chip(high, nf, 1)
    one = to_chip(one, nf, 1)
    two = to_chip(two, nf, 2)
    return [
        parts[0],
        one,
        two,
        add16(parts[1][:half], low),
        add16(parts[2][half:], high),
    ]


def scatter_second(parts, nf, *earlier):
    if nf != 8:
        total = parts[0].astype(f32)
        for part in parts[1:]:
            total = total + part.astype(f32)
        return total
    own, one, two, one_low, two_high = parts
    one_low, two_high = after((one_low, two_high), *earlier)
    one_low = to_chip(one_low, nf, 1)
    two_high = to_chip(two_high, nf, 2)
    own = own.astype(f32)
    half = own.shape[0] // 2
    return jnp.concatenate(
        [
            own[:half] + one_low.astype(f32) + two.astype(f32),
            own[half:] + one.astype(f32) + two_high.astype(f32),
        ],
        axis=0,
    )


def rms_back(rows, r, gain, d_out):
    unit = rows * r
    d_unit = d_out * gain
    d_rows = r * (d_unit - unit * jnp.mean(d_unit * unit, axis=1, keepdims=True))
    return d_rows, jnp.sum(d_out * unit, axis=0)


def scale_of(rows):
    return lax.rsqrt(jnp.mean(rows * rows, axis=1, keepdims=True) + eps_norm)


def exchange(a, nf):
    groups = [[2 * c + k for c in range(nf // 2)] for k in range(2)]
    return lax.all_to_all(a, "fsdp", 0, 0, axis_index_groups=groups, tiled=True)


def column_blocks(w, widths, chips, groups, p):
    rows = w.shape[0]
    start = 0
    parts = []
    for width in widths:
        part = w[:, start : start + width].reshape(rows, chips, groups, width // (chips * groups))
        parts.append(part[:, :, p].transpose(1, 0, 2))
        start += width
    return jnp.concatenate(parts, axis=2)


def from_column_blocks(blocks, widths):
    chips, rows, _ = blocks.shape
    parts = []
    at = 0
    for width in widths:
        part = blocks[:, :, at : at + width // chips]
        parts.append(part.transpose(1, 0, 2).reshape(rows, width))
        at += width // chips
    return parts


def both_core_rows(own, nf):
    core = lax.axis_index("fsdp") % 2
    other = swap_core(own, nf)
    first = core == 0
    chips, rows, width = own.shape
    both = jnp.stack([jnp.where(first, own, other), jnp.where(first, other, own)], axis=1)
    return both.reshape(chips * 2 * rows, width)


def core_half(x, chips, which):
    tokens, width = x.shape
    x = x.reshape(tokens, chips, 2, width // (2 * chips))
    x = lax.dynamic_index_in_dim(x, which, 2, keepdims=False)
    return x.reshape(tokens, width // 2)


def column_gradient(left, right, nf, *earlier):
    core = lax.axis_index("fsdp") % 2
    chips = nf // 2
    theirs = mm_tn(core_half(left, chips, 1 - core), right).astype(bf16)
    got = swap_core(theirs, nf)
    mine = mm_tn(core_half(left, chips, core), right) + got.astype(f32)
    return mine.astype(bf16).reshape(chips, -1, right.shape[1])


def both_cores(w, nf, *earlier):
    core = lax.axis_index("fsdp") % 2
    other = swap_core(after(w, *earlier), nf)
    first = core == 0
    return jnp.concatenate([jnp.where(first, w, other), jnp.where(first, other, w)], axis=0)


def halves(a):
    core = lax.axis_index("fsdp") % 2
    rows = a.shape[0] // 2
    mine = lax.dynamic_slice(a, (core * rows, 0), (rows, a.shape[1]))
    theirs = lax.dynamic_slice(a, ((1 - core) * rows, 0), (rows, a.shape[1]))
    return mine, theirs


def sum_cores(a, nf):
    mine, theirs = halves(a)
    return add16(mine, swap_core(theirs, nf))


def as_rows(a):
    flat = a.reshape(-1)
    return jnp.pad(flat, (0, -flat.shape[0] % 128)).reshape(-1, 128)


def gather_pieces(parts, nf, *earlier):
    a, one, two = parts
    half = a.shape[0] // 2
    low, high = after((one[:half], two[half:]), *earlier)
    return [a, one, two, to_chip(low, nf, 2), to_chip(high, nf, 1)]


def scatter_start(parts, nf, *earlier):
    over_x, over_y = after((parts[0], parts[2]), *earlier)
    return [parts[1], to_chip(over_x, nf, 1), parts[3], to_chip(over_y, nf, 2)]


def scatter_middle(parts, nf, *earlier):
    stay_x, got_x, stay_y, got_y = after(parts, *earlier)
    over_y, over_x = scatter_add(stay_x, got_x, stay_y, got_y)
    return [stay_x, got_x, to_chip(over_y, nf, 2), stay_y, got_y, to_chip(over_x, nf, 1)]


def scatter_end(parts):
    size = parts[2].shape[0]
    parts = [p[:size].astype(f32) for p in parts]
    return jnp.concatenate([sum(parts[:3]), sum(parts[3:])], axis=1)


def local_fast(
    tokens,
    cotangent,
    lengths,
    slot_owner,
    gain_in,
    w_proj,
    w_decay,
    conv_weight,
    a_log,
    dt_bias,
    o_gain,
    w_out,
    gain_mid,
    w_gate_up,
    w_down,
    *,
    nf,
    nz,
):
    chips = nf // 2
    hl = H // chips
    pair = 2
    groups = hl // pair
    me = lax.axis_index("fsdp")
    rep = lax.axis_index("rep")
    held = jnp.sum(jnp.where(slot_owner == rep * nf + me, lengths, 0))
    ids = jnp.stack([me // 2, me % 2, rep, held]).astype(jnp.int32)
    shard = gain_in.shape[0]
    conv_shard = conv_weight.shape[1]
    hv = w_out.shape[0] * nf
    hk = (conv_shard * nf - hv) // 2
    ff = w_down.shape[0] * nf
    wide = ff // chips
    qk, vv = pair * DK, pair * DV
    span = 2 * qk + 2 * vv
    proj_widths = (hk, hk, hv, hv)

    def proj_table(p):
        table = []
        for c in range(chips):
            at = c * groups + p
            table.append(
                [
                    (at * qk, qk),
                    (hk + at * qk, qk),
                    (2 * hk + at * vv, vv),
                    (2 * hk + hv + at * vv, vv),
                ]
            )
        return table

    up_table = [
        [(s * ff + c * wide + at, 128) for at in range(0, wide, 128) for s in range(2)]
        for c in range(chips)
    ]
    plane = shard // nz

    vectors = [v.reshape(1, -1) for v in (gain_in, gain_mid, o_gain, a_log, dt_bias)]
    sizes = [v.shape[1] for v in vectors]
    small = lax.all_to_all(pack_small(conv_weight, vectors, nf), "fsdp", 0, 0, tiled=True)
    decay_pad = jnp.pad(w_decay, ((0, 0), (0, 128 - 2 * H)))
    plane_rows = pack_relative(w_proj, decay_pad, proj_table(0), True, ids)
    packed = pack_relative(w_proj, None, proj_table(1), False, ids)

    def spread(own, *earlier):
        sends = after(own[1:], *earlier)
        return [own[0]] + [to_chip(a, nf, j + 1) for j, a in enumerate(sends)]

    def swap_all(own, *earlier):
        return [swap_core(a, nf) for a in after(own, *earlier)]

    out_other = swap_core(w_out, nf)
    down_other = swap_core(w_down, nf)
    first_rows = spread(plane_rows)
    first = jnp.stack(after(first_rows, packed))
    tok = gather_first(tokens, nf, small, first_rows, out_other, down_other)
    sends = after(packed[1:], first_rows, out_other, down_other)
    own = [packed[0], to_chip(sends[0], nf, 1), to_chip(sends[1], nf, 2)]
    first = lax.all_gather(first, "rep", axis=0)
    gains, head_rows, gain_row, *conv_pair = unpack_small(small, sizes, ids, hk, qk, vv, groups)
    tok = gather_pieces(tok, nf, gains)
    own.append(to_chip(after(sends[2], tok[3:]), nf, 3))
    up_plane = pack_columns(after(w_gate_up, packed), None, up_table, plane, True, ids)

    live_own = (jnp.arange(TOK_DEV, dtype=jnp.int32) < held).astype(f32)[:, None]
    seeded = cotangent.astype(f32) * live_own
    d_ffn_own = seeded.astype(bf16)

    normed_in = norm_rows(after(tok, d_ffn_own), gains)
    first_other = swap_core(after(first, normed_in, up_plane, own[1], own[2]), nf)
    up_plane = exchange(after(up_plane, own[3]), nf)
    own = stack_blocks(own)
    other = swap_core(own, nf)
    projected = [project_planes(after(normed_in, own), first, first_other, ids)]

    def forward(p, *before):
        return mixer_forward(
            ids, after(projected[p], *before), projected[0], conv_pair[p], head_rows, gain_row,
            hl, pair, p,
        )

    gated0, *saved0 = forward(0, other)
    up_own = lax.all_gather(after(up_plane, gated0), "rep", axis=0)
    sends = after(d_ffn_own, gated0, up_plane)
    ffn_parts = [d_ffn_own] + [to_chip(sends, nf, j) for j in range(1, chips)]
    projected.append(project_planes(after(normed_in, gated0), own, other, ids))
    gated1, *saved1 = forward(1)
    gated = [gated0, gated1]
    saved = [saved0, saved1]
    branch_parts = scatter_start(times_rows(gated, w_out, out_other, ids), nf)
    d_ffn = jnp.concatenate(after(ffn_parts, branch_parts[0]), axis=0)
    pieces_in = [(first, first_other), (own, other)]
    down_chip = join_cores(w_down, after(down_other, branch_parts[0]), ids)
    out_chip = join_cores(w_out, after(out_other, branch_parts[0]), ids)
    branch_parts = scatter_middle(branch_parts, nf, d_ffn, down_chip, out_chip)

    middle, normed_own = middle_rows(branch_parts, tokens, gains, ids)
    normed_mid = gather_first(normed_own, nf)
    up_own = after(up_own, normed_mid)
    up_other = swap_core(up_own, nf)
    in_other = swap_core(after(normed_in, up_other), nf)
    normed_mid = jnp.concatenate(gather_pieces(normed_mid, nf), axis=0)
    hidden, d_gate_up = feed_forward(normed_mid, up_own, up_other, down_chip, d_ffn, ids)

    line = Overlapped(nz, ids)
    done = line.done

    d_up_other = swap_core(d_gate_up, nf)
    mid_other = swap_core(normed_mid, nf)
    mine, theirs = row_terms([hidden], after(d_ffn, mid_other), ids)
    theirs = swap_core(theirs, nf)
    half = mine.shape[0] // 2
    down0 = mine[:half] + theirs[:half]
    down1 = mine[half:] + theirs[half:]
    line.prepare(("down0", down0), down1)
    line.step()
    partial_mid = times_transposed(
        [(after(d_gate_up, down0, down1, d_up_other), up_own, up_other)], ids, False
    )
    mid_parts = scatter_start(partial_mid, nf)
    partial_ffn = times_rows(after([hidden], partial_mid), w_down, down_other, ids)
    line.prepare(("down1", down1), partial_ffn)
    line.step()
    mid_parts = scatter_middle(mid_parts, nf, line.sent)
    grad_up = column_terms(
        [normed_mid, mid_other],
        [after(d_gate_up, line.sent, mid_parts[0]), d_up_other],
        ids,
        True,
    )
    line.prepare(("up0", grad_up[0]))
    line.step(grad_up[0])
    d_middle, d_branch_own, g_gain_mid = middle_back(
        after(mid_parts, line.sent), middle, cotangent, gains, ids
    )
    branch_parts = gather_first(d_branch_own, nf)
    d_branch = gather_pieces(branch_parts, nf, line.sent)
    line.prepare(("up1", grad_up[1]), branch_parts)
    line.step()
    line.prepare(("up2", grad_up[2]))
    d_branch = jnp.concatenate(after(d_branch, line.sent), axis=0)
    d_gated = [mm_nt(d_branch, out_chip[p * vv : (p + 1) * vv]) for p in range(groups)]

    def backward(p, *before, more=None):
        return mixer_backward(
            ids, projected[p], projected[0], conv_pair[p], head_rows, gain_row, saved[p],
            after(d_gated[p], *before), hl, pair, p, more,
        )

    d_x1, d_dec, g_conv1, g_heads1 = backward(1, line.sent)
    arriving = line.arriving
    line.step(d_x1)
    line.prepare(("up3", grad_up[3]))
    d_x1_other = swap_core(after(d_x1, arriving), nf)
    mine, theirs = row_terms(gated, after(d_branch, line.sent), ids)
    theirs = swap_core(theirs, nf)
    cols1 = column_terms([normed_in, in_other], [after(d_x1, mine), d_x1_other], ids, False)
    cols1_all = exchange(after(cols1, line.arriving), nf)
    grad_out = mine + after(theirs, cols1)
    line.step(cols1)
    d_x0, dec, g_conv0, g_heads0 = backward(0, line.sent, theirs, more=d_dec)
    arriving = line.arriving
    size = down0.shape[0]
    rest = grad_out.shape[0] - size
    line.prepare(("out0", grad_out[:size]), d_x0)
    line.step()
    d_x0_other = swap_core(after(d_x0, arriving, cols1_all), nf)
    cols0 = column_terms([normed_in, in_other], [after(d_x0, line.sent), d_x0_other], ids, False)
    bands0_all = exchange(after(cols0, line.arriving), nf)
    bands1 = cols1_all.reshape(-1, STREAM)
    at1 = size - rest
    line.prepare(("mix0", jnp.concatenate([grad_out[size:], bands1[:at1]], axis=0)), cols0)
    line.step()
    line.prepare(("p1", bands1[at1 : at1 + size]))
    right = [d_x0, d_x1]
    partial_in = times_transposed(
        [(after(right[p], line.sent),) + pieces_in[p] for p in range(groups)], ids, True
    )
    line.step(partial_in)
    bands0 = bands0_all.reshape(-1, STREAM)
    at1 += size
    left = bands1.shape[0] - at1
    at0 = size - left
    in_first = scatter_start(partial_in, nf, line.sent)
    grad_up = None
    for j in range(3):
        grad_up = place_blocks(
            grad_up, after(done["up%d" % j], line.sent), ids, j, (chips, shard, 2 * wide)
        )
    line.prepare(("mix1", jnp.concatenate([bands1[at1:], bands0[:at0]], axis=0)), grad_up)
    line.step()
    line.prepare(("p0", bands0[at0 : at0 + size]))
    in_sends = scatter_middle(in_first, nf, line.sent)
    grad_up = place_blocks(
        grad_up, after(done["up3"], line.sent, in_sends[0]), ids, 3, (chips, shard, 2 * wide)
    )
    arriving = line.arriving
    line.step(grad_up)
    line.prepare(("p0last", bands0[at0 + size :]))
    grad_up_all = exchange(after(grad_up, arriving, in_sends[2], in_sends[5]), nf)
    ffn_first = scatter_start(partial_ffn, nf, grad_up_all)
    grad_tokens, g_gain_in = tokens_back(after(in_sends, line.sent), tokens, d_middle, gains)
    blocks = pack_small_grads(
        [g_conv0, g_conv1],
        [g_heads0, g_heads1],
        g_gain_in,
        g_gain_mid,
        sizes,
        ids,
        nf,
        conv_shard,
        hk,
        qk,
        vv,
    )
    line.step(blocks)
    line.prepare(None)
    def tile_of(p, c, t):
        at = c * groups + p
        q_tiles, v_tiles = qk // 128, vv // 128
        if t < q_tiles:
            return at * q_tiles + t
        if t < 2 * q_tiles:
            return hk // 128 + at * q_tiles + t - q_tiles
        if t < 2 * q_tiles + v_tiles:
            return 2 * hk // 128 + at * v_tiles + t - 2 * q_tiles
        return (2 * hk + hv) // 128 + at * v_tiles + t - 2 * q_tiles - v_tiles

    each = span // 128
    bands = [(1, c, t) for c in range(chips) for t in range(each)]
    bands += [(0, c, t) for c in range(chips) for t in range(each + 1)]
    slots = [("mix0", n) for n in range(rest // 16, size // 16)]
    slots += [("p1", n) for n in range(size // 16)]
    slots += [("mix1", n) for n in range(size // 16)]
    slots += [("p0", n) for n in range(size // 16)]
    slots += [("p0last", n) for n in range(size // 16)]
    where = dict(zip(bands, slots))

    def place(grad_proj, name, *before):
        pairs = [
            (where[key][1], tile_of(*key))
            for key in bands
            if where[key][0] == name and key[2] < each and key[2] % 2 == 0
        ]
        return finish_projection(grad_proj, after(done[name], *before), ids, pairs, w_proj.shape)

    grad_proj = place(None, "mix0", line.sent)
    line.step(grad_proj)
    line.prepare(None)
    grad_up = finish_feed_forward(after(grad_up_all, line.sent))
    ffn_sends = scatter_middle(ffn_first, nf, grad_up)
    line.step(grad_up)
    line.prepare(None)
    grad_proj = place(grad_proj, "p1", line.sent)
    grad_proj = place(grad_proj, "mix1", line.sent)
    small_sum = lax.all_to_all(after(blocks, ffn_sends[2], ffn_sends[5]), "fsdp", 0, 0, tiled=True)
    output = (middle + live_own * scatter_end(after(ffn_sends, grad_proj))).astype(bf16)
    line.step(grad_proj, output)
    small_sum = lax.all_gather(jnp.sum(after(small_sum, line.sent), axis=0), "rep", axis=0)
    grad_proj = place(grad_proj, "p0", line.sent)
    small_sum = jnp.sum(small_sum, axis=0)
    done["p0last"] = after(done["p0last"], grad_proj)
    grad_proj = place(grad_proj, "p0last")
    middle_two = jnp.logical_or(rep == 1, rep == 2)

    def pick(name):
        return jnp.where(middle_two, *done[name])

    tail = pick("p0last")
    summed = small_sum
    lanes, _ = small_layout(sizes)
    s_gain_in, s_gain_mid, s_ogain, s_alog, s_bias = (
        summed[KCONV, lane : lane + width] for lane, width in zip(lanes, sizes)
    )
    grad_decay = 0.0
    for c in range(chips):
        name, n = where[(0, c, each)]
        band = tail if name == "p0last" else pick(name)
        band = band[16 * n : 16 * n + 16].astype(f32).reshape(16, shard // 16, 128)
        grad_decay = grad_decay + band.transpose(1, 0, 2).reshape(shard, 128)
    grad_decay = grad_decay[:, : 2 * H]
    grad_down = jnp.concatenate([pick("down0"), pick("down1")], axis=0).astype(f32)
    grad_out = jnp.concatenate([pick("out0"), pick("mix0")[:rest]], axis=0).astype(f32)
    return (
        output,
        grad_tokens,
        s_gain_in,
        grad_proj,
        grad_decay,
        summed[:KCONV, :conv_shard],
        s_alog,
        s_bias,
        s_ogain,
        grad_out,
        s_gain_mid,
        grad_up,
        grad_down,
    )


def local_general(
    tokens,
    cotangent,
    lengths,
    slot_owner,
    gain_in,
    w_proj,
    w_decay,
    conv_weight,
    a_log,
    dt_bias,
    o_gain,
    w_out,
    gain_mid,
    w_gate_up,
    w_down,
    *,
    nf,
    nz,
):
    chips = nf // 2
    hl = H // chips
    pair = 2 if hl % 2 == 0 else 1
    groups = hl // pair
    me = lax.axis_index("fsdp")
    rep = lax.axis_index("rep")
    chip, core = me // 2, me % 2
    ids = jnp.stack([chip, core, rep, rep]).astype(jnp.int32)
    d_model = tokens.shape[1]
    shard = gain_in.shape[0]
    conv_shard = conv_weight.shape[1]
    channels = conv_shard * nf
    hv = w_out.shape[0] * nf
    hk = (channels - hv) // 2
    ff = w_down.shape[0] * nf
    wide = ff // chips
    qk, vv = pair * DK, pair * DV
    span = 2 * qk + 2 * vv
    proj_widths = (hk, hk, hv, hv)
    up_widths = (ff, ff)

    def proj_blocks(w, dec, p):
        blocks = column_blocks(w, proj_widths, chips, groups, p)
        if p:
            return blocks
        extra = jnp.pad(dec, ((0, 0), (0, 128 - 2 * H)))
        extra = jnp.broadcast_to(extra, (chips,) + extra.shape)
        return jnp.concatenate([blocks, extra], axis=2)

    def plane_rows(w):
        rows = w.shape[0] // nz
        return lax.dynamic_slice(w, (rep * rows, 0), (rows, w.shape[1]))

    def over_planes(blocks):
        got = lax.all_gather(blocks, "rep", axis=0)
        return got.transpose(1, 0, 2, 3).reshape(chips, -1, blocks.shape[2])

    pieces = [conv_weight, gain_in, gain_mid, o_gain, a_log, dt_bias]
    rows = [as_rows(p) for p in pieces]
    counts = [r.shape[0] for r in rows]
    packed = jnp.concatenate(rows, axis=0)
    packed = jnp.pad(packed, ((0, -packed.shape[0] % 16), (0, 0)))

    plane_proj = plane_rows(w_proj)
    rest = [exchange(proj_blocks(plane_proj, None, p), nf) for p in range(1, groups)]
    first = exchange(proj_blocks(w_proj, w_decay, 0), nf)
    tok = gather_first(tokens, nf)
    small = gather_small(packed, nf)
    tokens_all = gather_second(tok, nf)
    rest = [over_planes(r) for r in rest]
    up_plane = exchange(
        after(column_blocks(plane_rows(w_gate_up), up_widths, chips, 1, 0), first), nf
    )
    up_own = over_planes(after(up_plane, *rest))

    device = rep * nf + me
    held = jnp.sum(jnp.where(slot_owner == device, lengths, 0))
    live_own = (jnp.arange(TOK_DEV, dtype=jnp.int32) < held).astype(f32)[:, None]

    small = small.astype(f32)
    split = []
    at = 0
    for p, count in zip(pieces, counts):
        split.append(
            small[:, at : at + count].reshape(nf, count * 128)[:, : p.size].reshape((nf,) + p.shape)
        )
        at += count
    conv_full = split[0].transpose(1, 0, 2).reshape(KCONV, channels)
    gain_in_full, gain_mid_full, ogain_full, alog_full, bias_full = (
        s.reshape(-1) for s in split[1:]
    )
    conv_pair = []
    for p in range(groups):
        blocks = column_blocks(conv_full, proj_widths[:3], chips, groups, p)
        mine = lax.dynamic_index_in_dim(blocks, chip, 0, keepdims=False)
        conv_pair.append(jnp.pad(mine, ((0, 8 - KCONV), (0, 0))))
    head_rows = jnp.stack([alog_full, bias_full])
    head_rows = jnp.pad(head_rows, ((0, 6), (0, 128 - H)))
    gain_row = jnp.pad(ogain_full[None, :], ((0, 7), (0, 0)))

    rows_in = tokens_all.astype(f32)
    normed_in = (rows_in * scale_of(rows_in) * gain_in_full).astype(bf16)
    seeded = cotangent.astype(f32) * live_own
    weight_in = [both_core_rows(first, nf)]
    out_chip = both_cores(w_out, nf, weight_in[0])
    down_chip = both_cores(w_down, nf, weight_in[0])
    weight_in += [both_core_rows(r, nf) for r in rest]
    ffn_parts = gather_first(seeded.astype(bf16), nf, up_plane)
    d_ffn = gather_second(ffn_parts, nf)
    projected = []
    gated = []
    saved = []
    for p in range(groups):
        projected.append(mm(normed_in, weight_in[p]))
        got = mixer_forward(
            ids, projected[p], projected[0], conv_pair[p], head_rows, gain_row, hl, pair, p
        )
        gated.append(got[0])
        saved.append(got[1:])
    gated = jnp.concatenate(gated, axis=1)
    branch_parts = scatter_first(mm(gated, out_chip).astype(bf16), nf, d_ffn)
    d_hidden = mm_nt(after(d_ffn, gated), down_chip)
    up_chip = both_core_rows(after(up_own, gated), nf)
    branch = scatter_second(branch_parts, nf)

    tokens32 = tokens.astype(f32)
    middle = tokens32 + live_own * branch
    r_mid = scale_of(middle)
    normed_own = (middle * r_mid * gain_mid_full).astype(bf16)
    normed_mid = gather_second(gather_first(normed_own, nf), nf)
    gate_up = mm(normed_mid, up_chip)
    gate, up = gate_up[:, :wide], gate_up[:, wide:]
    sig = jax.nn.sigmoid(gate)
    act = gate * sig
    hidden = (act * up).astype(bf16)
    d_gate_up = jnp.concatenate(
        [d_hidden * up * (sig * (1.0 + gate * (1.0 - sig))), d_hidden * act], axis=1
    ).astype(bf16)

    line = Line(nz, ids)
    done = {}

    def step(new, *earlier):
        for item in new or [None]:
            got = line.step(item, *earlier)
            if got is not None:
                done[got[0]] = got[1][0]

    grad_down = sum_cores(mm_tn(hidden, d_ffn).astype(bf16), nf)
    down_parts = jnp.split(grad_down, 2, axis=0)
    step([("down0", down_parts[0])])
    partial_mid = mm_nt(after(d_gate_up, down_parts[0]), up_chip).astype(bf16)
    mid_parts = scatter_first(partial_mid, nf)
    grad_up = column_gradient(normed_mid, after(d_gate_up, partial_mid), nf)
    step([("down1", down_parts[1])], grad_up)
    d_normed_mid = scatter_second(mid_parts, nf)
    d_mid, g_gain_mid = rms_back(middle, r_mid, gain_mid_full, d_normed_mid)
    d_middle = seeded + d_mid
    d_branch_own = (live_own * d_middle).astype(bf16)
    branch_parts = gather_first(d_branch_own, nf)
    partial_ffn = mm(after(hidden, d_branch_own), down_chip).astype(bf16)
    step([("up0", grad_up[0])], partial_ffn)
    d_branch = gather_second(branch_parts, nf)
    step([("up1", grad_up[1])], d_branch)
    d_gated = [mm_nt(d_branch, out_chip[p * vv : (p + 1) * vv]) for p in range(groups)]
    grad_out = sum_cores(mm_tn(gated, d_branch).astype(bf16), nf)
    d_x = [None] * groups
    d_dec = None
    g_conv = [None] * groups
    g_heads = None
    ups = [("up%d" % j, grad_up[j]) for j in range(2, chips)]
    for n, p in enumerate(reversed(range(groups))):
        d_x[p], dec, g_conv[p], heads = mixer_backward(
            ids, projected[p], projected[0], conv_pair[p], head_rows, gain_row, saved[p],
            d_gated[p], hl, pair, p,
        )
        d_dec = dec if d_dec is None else d_dec + dec
        g_heads = heads if g_heads is None else g_heads + heads
        step(ups[n : n + 1] if n + 1 < groups else ups[n:], d_x[p])
        if p:
            d_gated[p - 1] = after(d_gated[p - 1], d_x[p])
    d_dec = d_dec.astype(bf16)
    right = [jnp.concatenate([d_x[0], d_dec], axis=1)] + d_x[1:]
    grad_cols = [None] * groups
    for p in reversed(range(groups)):
        grad_cols[p] = exchange(column_gradient(normed_in, right[p], nf), nf)
    ffn_parts = scatter_first(partial_ffn, nf, grad_cols[0])
    step([("out", grad_out)], right[0])
    partial_in = mm_nt(right[0], weight_in[0])
    for p in range(1, groups):
        partial_in = partial_in + mm_nt(right[p], weight_in[p])
    partial_in = partial_in.astype(bf16)
    queue = []
    for p in reversed(range(groups)):
        size = 1 if p == 0 else 2
        for c in range(0, chips, size):
            queue.append(((p, c), grad_cols[p][c : c + size]))
    for n, item in enumerate(queue):
        if n == 1:
            ffn_branch = scatter_second(ffn_parts, nf, line.tokens)
            output = (middle + live_own * ffn_branch).astype(bf16)
            in_parts = scatter_first(partial_in, nf, ffn_branch)
        if n == 2:
            d_normed_in = scatter_second(in_parts, nf, line.tokens)
            d_rows, g_gain_in = rms_back(tokens32, scale_of(tokens32), gain_in_full, d_normed_in)
            grad_tokens = d_middle + d_rows
            ups = jnp.stack([done["up%d" % j] for j in range(chips)])
            grad_up = exchange(after(ups, d_normed_in), nf)
        step([item])

    g_conv = [g[:KCONV] for g in g_conv]
    blocks = jnp.concatenate(
        [g[:, a:b] for a, b in ((0, qk), (qk, 2 * qk), (2 * qk, 2 * qk + vv)) for g in g_conv],
        axis=1,
    )
    conv_grad = jnp.zeros((KCONV, chips, channels // chips), f32)
    conv_grad = lax.dynamic_update_slice(conv_grad, blocks[:, None], (0, chip, 0))
    conv_grad = jnp.concatenate(from_column_blocks(conv_grad.transpose(1, 0, 2), proj_widths[:3]), axis=1)
    heads_grad = g_heads[1:3, :H]
    parts = [
        conv_grad.reshape(KCONV, nf, conv_shard).transpose(1, 0, 2),
        g_gain_in.reshape(nf, shard),
        g_gain_mid.reshape(nf, shard),
        g_heads[0].reshape(nf, -1),
        heads_grad[0].reshape(nf, -1),
        heads_grad[1].reshape(nf, -1),
    ]
    flat = []
    for part in parts:
        part = part.reshape(nf, -1)
        flat.append(jnp.pad(part, ((0, 0), (0, -part.shape[1] % 128))))
    flat = jnp.concatenate(flat, axis=1)
    summed = lax.psum(sum_small(flat.reshape(nf, -1, 128), nf)[0], "rep").reshape(-1)
    grads = []
    at = 0
    for p in pieces:
        grads.append(summed[at : at + p.size].reshape(p.shape))
        at += p.size + (-p.size % 128)
    s_conv, s_gain_in, s_gain_mid, s_ogain, s_alog, s_bias = grads

    step([])
    step([])
    grad_up = jnp.concatenate(from_column_blocks(grad_up, up_widths), axis=1).astype(f32)
    wholes = []
    for p in range(groups):
        size = 1 if p == 0 else 2
        wholes.append(jnp.concatenate([done[(p, c)] for c in range(0, chips, size)], axis=0))
    parts = []
    at = 0
    for width in (qk, qk, vv, vv):
        part = jnp.stack([w[:, :, at : at + width] for w in wholes], axis=1)
        parts.append(part.transpose(2, 0, 1, 3).reshape(shard, -1))
        at += width
    grad_proj = jnp.concatenate(parts, axis=1).astype(f32)
    grad_decay = jnp.sum(wholes[0][:, :, span : span + 2 * H].astype(f32), axis=0)
    grad_down = jnp.concatenate([done["down0"], done["down1"]], axis=0).astype(f32)
    grad_out = done["out"].astype(f32)
    return (
        output,
        grad_tokens,
        s_gain_in,
        grad_proj,
        grad_decay,
        s_conv,
        s_alog,
        s_bias,
        s_ogain,
        grad_out,
        s_gain_mid,
        grad_up,
        grad_down,
    )


def solution(mesh):
    rows = P(("rep", "fsdp"), None)
    one = P("fsdp")
    two = P("fsdp", None)
    columns = P(None, "fsdp")
    in_specs = (rows, rows, P(), P(), one, two, two, columns, one, one, one, two, one, two, two)
    out_specs = (rows, rows, one, two, two, columns, one, one, one, two, one, two, two)
    nf, nz = mesh.shape["fsdp"], mesh.shape["rep"]
    body = partial(local_fast if (nf, nz) == (8, 4) else local_general, nf=nf, nz=nz)
    return jax.shard_map(body, mesh=mesh, in_specs=in_specs, out_specs=out_specs, check_vma=False)
```
